512 devices in a mesh: gx: 64 (over y, z_lo, core), gy: 8 (over x, z_hi).
Axes of the slice: x: 4, y: 8, z: 8 (z_hi: 2, z_lo: 4; z = z_hi * 4 + z_lo), core: 2. Of those that a mesh axis runs over, the one named last changes fastest.
Arguments:
- populations: float32 [19, 768, 3072], P(None, 'gx', 'gy'), may hold values from 0.02 to 0.1
- phase_field: float32 [768, 3072], P('gx', 'gy'), may hold values from -1 to 1
- plane_shifts: int32 [4, 16], replicated, may hold values from 0 to 127
Outputs:
- populations_out: float32 [19, 768, 3072], P(None, 'gx', 'gy')
- phase_out: float32 [768, 3072], P('gx', 'gy')
The draws below stay inside these ranges and needn't reach their ends.
All inputs are finite; a program needn't handle non-finite values.
Results may differ from the reference program's by a relative error of at most 0.0001.
Values sent between devices are 32-bit elements; how exact they have to be, the bound alone decides.
A program may use at most 64 MiB of HBM per device.

```python
import jax
import jax.numpy as jnp
from jax import lax

VELOCITIES = 19
PLANES = 16
STEPS = 4
NZ = 24
NX = 768
NY = 128


def with_ends(result, own_key, smallest, high):
    spot = [jax.random.randint(jax.random.fold_in(own_key, axis), (), 0, length) for axis, length in enumerate(result.shape)]
    main_axis = result.shape.index(max(result.shape))
    next_to = spot[:main_axis] + [(spot[main_axis] + 1) % result.shape[main_axis]] + spot[main_axis + 1:]
    return result.at[tuple(spot)].set(smallest).at[tuple(next_to)].set(high)


def levels(rng, shape, cuts, smallest, largest):
    def one(dim, blocks):
        heights = jax.random.uniform(jax.random.fold_in(jax.random.fold_in(rng, 6), dim), (blocks,), jnp.float32, smallest / len(cuts), largest / len(cuts))
        return jnp.repeat(jnp.exp(heights), shape[dim] // blocks).reshape((-1,) + (1,) * (len(shape) - dim - 1))

    factor_of = one(*cuts[0])
    for cut in cuts[1:]:
        factor_of = factor_of * one(*cut)
    return factor_of


def setup_inputs(seed: int = 0) -> dict:
    splits = jax.random.split(jax.random.key(seed), 4)
    populations = jnp.clip(0.02 + 0.08 * jax.random.uniform(splits[0], (VELOCITIES, NX, NY * NZ), jnp.float32) ** levels(splits[0], (VELOCITIES, NX, NY * NZ), ((1, 64), (2, 8)), -0.2, 0.2), 0.02, 0.1)
    phase_field = jnp.clip(jax.random.uniform(splits[1], (NX, NY * NZ), jnp.float32, -1.0, 1.0) * levels(splits[1], (NX, NY * NZ), ((0, 64), (1, 8)), -0.4, 0.0), -1.0, 1.0)
    plane_shifts = with_ends(jax.random.randint(splits[2], (STEPS, PLANES), 0, NY), jax.random.fold_in(splits[2], 1), 0, NY - 1).astype(jnp.int32)
    return {"populations": populations, "phase_field": phase_field, "plane_shifts": plane_shifts}


lattice_vel = ((0, 0, 0), (1, 0, 0), (-1, 0, 0), (0, 1, 0), (0, -1, 0), (0, 0, 1), (0, 0, -1),
               (1, 1, 0), (-1, -1, 0), (1, -1, 0), (-1, 1, 0), (1, 0, 1), (-1, 0, -1), (1, 0, -1),
               (-1, 0, 1), (0, 1, 1), (0, -1, -1), (0, 1, -1), (0, -1, 1))
weights = (1.0 / 3.0,) + (1.0 / 18.0,) * 6 + (1.0 / 36.0,) * 12
plus_slots = (1, 7, 9, 11, 13)
minus_slots = (2, 8, 10, 12, 14)
side_slots = (3, 4, 7, 8, 9, 10, 15, 16, 17, 18)
relax_rate = 0.8
coupling = 0.01
bulk_coeff = 0.5
stiffness = 0.5
mobility = 0.02
far_weight = 0.25


def roll_cells(field, shift, depth):
    position = lax.broadcasted_iota(jnp.int32, (field.shape[-1],), 0) % depth
    if shift == 1:
        return jnp.where(position == 0, jnp.roll(field, 1 - depth, -1), jnp.roll(field, 1, -1))
    if shift == -1:
        return jnp.where(position == depth - 1, jnp.roll(field, depth - 1, -1), jnp.roll(field, -1, -1))
    return field


def laplace(extended, depth):
    core = extended[1:-1, depth:-depth]
    total = extended[2:, depth:-depth] + extended[:-2, depth:-depth]
    total = total + extended[1:-1, 2 * depth:] + extended[1:-1, :-2 * depth]
    return total + roll_cells(core, 1, depth) + roll_cells(core, -1, depth) - 6.0 * core


def gradient(extended, depth):
    core = extended[1:-1, depth:-depth]
    along_x = 0.5 * (extended[2:, depth:-depth] - extended[:-2, depth:-depth])
    along_y = 0.5 * (extended[1:-1, 2 * depth:] - extended[1:-1, :-2 * depth])
    along_z = 0.5 * (roll_cells(core, -1, depth) - roll_cells(core, 1, depth))
    return (along_x, along_y, along_z)


def update_cells(current, phase_ext, depth):
    inner = phase_ext[1:-1, depth:-depth]
    chem_pot = bulk_coeff * (inner * inner * inner - inner) - stiffness * laplace(phase_ext, depth)
    phase_core = phase_ext[2:-2, 2 * depth:-2 * depth]
    push = gradient(chem_pot, depth)
    slope = gradient(inner, depth)
    density = jnp.sum(current, axis=0)
    flow = []
    for axis in range(3):
        total = jnp.zeros_like(density)
        for slot in range(19):
            if lattice_vel[slot][axis] != 0:
                total = total + lattice_vel[slot][axis] * current[slot]
        flow.append(total / density)
    drift = [flow[axis] - coupling * phase_core * push[axis] / (relax_rate * density) for axis in range(3)]
    speed_sq = drift[0] * drift[0] + drift[1] * drift[1] + drift[2] * drift[2]
    post = []
    for slot in range(19):
        along = jnp.zeros_like(density)
        for axis in range(3):
            if lattice_vel[slot][axis] != 0:
                along = along + lattice_vel[slot][axis] * drift[axis]
        balance = weights[slot] * density * (1.0 + 3.0 * along + 4.5 * along * along - 1.5 * speed_sq)
        post.append(current[slot] + relax_rate * (balance - current[slot]))
    advect = flow[0] * slope[0] + flow[1] * slope[1] + flow[2] * slope[2]
    phase_next = phase_core - advect + mobility * laplace(chem_pot, depth)
    return jnp.stack(post), phase_next


def stream_cells(post, from_left, from_right, beside, depth):
    rows = post.shape[2] // depth
    outputs = []
    for slot in range(19):
        step_x, step_y, step_z = lattice_vel[slot]
        low = (1 - step_y) * depth
        high = (1 - step_y + rows) * depth
        if step_y == 0:
            middle = post[slot]
        else:
            middle = beside[slot][:, low:high]
        if step_x == 1:
            middle = jnp.concatenate([from_left[slot][:, low:high], middle[:-1]], 0)
        elif step_x == -1:
            middle = jnp.concatenate([middle[1:], from_right[slot][:, low:high]], 0)
        outputs.append(roll_cells(middle, step_z, depth))
    return jnp.stack(outputs)


def slide(strip, shift, near_w, far_w):
    near_rows = jnp.roll(strip, shift * NZ, axis=-1)
    far_rows = jnp.roll(strip, (shift + 1) * NZ, axis=-1)
    return near_w * near_rows + far_w * far_rows


def pad_rows(field, margin):
    return jnp.concatenate([field[..., -margin * NZ:], field, field[..., :margin * NZ]], -1)


def reference(populations, phase_field, plane_shifts):
    width_x = populations.shape[1]
    segment = width_x // PLANES
    near = (1.0 - far_weight, far_weight)
    far = (far_weight, 1.0 - far_weight)
    current = populations
    phase = phase_field
    for step in range(STEPS):
        shifts = plane_shifts[step].astype(jnp.int32)

        def lows_of(index):
            return shifts[(index + PLANES - 1) % PLANES], -shifts[index] - 1

        def collide(index, buffers):
            post_all, phase_all = buffers
            start = (index * segment).astype(jnp.int32)
            low_left, low_right = lows_of(index)
            below = lax.dynamic_slice_in_dim(phase, (start + width_x - 2) % width_x, 2, 0)
            above = lax.dynamic_slice_in_dim(phase, (start + segment) % width_x, 2, 0)
            own = lax.dynamic_slice_in_dim(phase, start, segment, 0)
            phase_ext = jnp.concatenate([pad_rows(slide(below, low_left, near[0], far[0]), 2), pad_rows(own, 2),
                                         pad_rows(slide(above, low_right, near[1], far[1]), 2)], 0)
            post, phase_next = update_cells(lax.dynamic_slice_in_dim(current, start, segment, 1), phase_ext, NZ)
            return (lax.dynamic_update_slice_in_dim(post_all, post, start, 1),
                    lax.dynamic_update_slice_in_dim(phase_all, phase_next, start, 0))

        post_all, phase_new = lax.fori_loop(0, PLANES, collide, (jnp.zeros_like(current), jnp.zeros_like(phase)))

        def stream(index, buffer):
            start = (index * segment).astype(jnp.int32)
            low_left, low_right = lows_of(index)
            below = lax.dynamic_slice_in_dim(post_all, (start + width_x - 1) % width_x, 1, 1)
            above = lax.dynamic_slice_in_dim(post_all, (start + segment) % width_x, 1, 1)
            own = lax.dynamic_slice_in_dim(post_all, start, segment, 1)
            below = pad_rows(slide(below, low_left, near[0], far[0]), 1)
            above = pad_rows(slide(above, low_right, near[1], far[1]), 1)
            sides = pad_rows(own, 1)
            from_left = {slot: below[slot] for slot in plus_slots}
            from_right = {slot: above[slot] for slot in minus_slots}
            beside = {slot: sides[slot] for slot in side_slots}
            moved = stream_cells(own, from_left, from_right, beside, NZ)
            return lax.dynamic_update_slice_in_dim(buffer, moved, start, 1)

        current = lax.fori_loop(0, PLANES, stream, jnp.zeros_like(current))
        phase = phase_new
    return current, phase
```

```python
import functools

import jax
import jax.numpy as jnp
from jax import lax
from jax.experimental import pallas as pl
from jax.experimental.pallas import tpu as pltpu
from jax.sharding import PartitionSpec as P

STEPS = 4
NZ = 24
ROWS = 12
WIDE = 384
SPAN = 4
MESH = pl.DeviceIdType.MESH

lattice_vel = (
    (0, 0, 0),
    (1, 0, 0),
    (-1, 0, 0),
    (0, 1, 0),
    (0, -1, 0),
    (0, 0, 1),
    (0, 0, -1),
    (1, 1, 0),
    (-1, -1, 0),
    (1, -1, 0),
    (-1, 1, 0),
    (1, 0, 1),
    (-1, 0, -1),
    (1, 0, -1),
    (-1, 0, 1),
    (0, 1, 1),
    (0, -1, -1),
    (0, 1, -1),
    (0, -1, 1),
)
relax_rate = 0.8
coupling = 0.01
mobility = 0.02

up_slots = (1, 11, 13, 7, 9)
down_slots = (2, 12, 14, 10, 8)
plus_y = (3, 7, 10, 15, 17)
minus_y = (4, 8, 9, 16, 18)


def rolled(value, shift, axis):
    size = value.shape[axis]
    shift = shift % size
    return value if shift == 0 else pltpu.roll(value, shift, axis)


def moved_yz(value, step_y, step_z, place):
    if step_z == 0:
        return rolled(value, step_y * NZ, 1)
    edge = 0 if step_z == 1 else NZ - 1
    inner = rolled(value, step_y * NZ + step_z, 1)
    wrap = rolled(value, step_y * NZ + step_z - step_z * NZ, 1)
    return jnp.where(place == edge, wrap, inner)


def kernel(
    shifts, f_in, p_in, f_out, p_out,
    f, ext, from_x, from_y, from_corner, to_x, to_y, to_corner, ring, send_sem, recv_sem,
):
    count_x, count_y = lax.axis_size("gx"), lax.axis_size("gy")
    gx, gy = lax.axis_index("gx"), lax.axis_index("gy")
    above, below = lax.rem(gx + 1, count_x), lax.rem(gx + count_x - 1, count_x)
    front, back = lax.rem(gy + 1, count_y), lax.rem(gy + count_y - 1, count_y)
    planes = count_x // SPAN
    left_plane = lax.rem(gx, SPAN) == 0
    right_plane = lax.rem(gx, SPAN) == SPAN - 1
    left_slot = lax.rem(gx // SPAN + planes - 1, planes)
    right_slot = gx // SPAN
    blocks = 3 * count_y

    def signal(x, y):
        pl.semaphore_signal(barrier, inc=1, device_id=(x, y), device_id_type=MESH)

    barrier = pltpu.get_barrier_semaphore()
    signal(gx, front)
    signal(gx, back)
    for is_plane, side in ((left_plane, below), (right_plane, above)):
        @pl.when(is_plane)
        def _(side=side):
            for y in range(count_y):
                signal(side, y)

        @pl.when(jnp.logical_not(is_plane))
        def _(side=side):
            signal(side, gy)
            signal(side, front)
            signal(side, back)

    lane = lax.broadcasted_iota(jnp.int32, (16, WIDE), 1)
    place = lax.rem(lane, NZ)
    lane4 = lax.broadcasted_iota(jnp.int32, (16, 512), 1)
    place4 = lax.rem(jnp.where(lane4 < 448, lane4, lane4 - 464), NZ)
    lane1 = lax.broadcasted_iota(jnp.int32, (16, 128), 1)

    def pack_phase(r):
        for b in range(3):
            cut = slice(b * 128, b * 128 + 128)
            to_x[r, 0, b, 5:7, :] = ext[10:12, cut]
            to_x[r, 1, b, 5:7, :] = ext[0:2, cut]
        to_y[r, 0, 12:24, :] = ext[0:12, 256:384]
        to_y[r, 1, 12:24, :] = ext[0:12, 0:128]
        to_corner[r, 0, 1:2, :] = ext[11:12, 256:384]
        to_corner[r, 1, 1:2, :] = ext[11:12, 0:128]
        to_corner[r, 2, 1:2, :] = ext[0:1, 256:384]
        to_corner[r, 3, 1:2, :] = ext[0:1, 0:128]

    def remote(src, dst, r, kind, x, y):
        return pltpu.make_async_remote_copy(
            src_ref=src, dst_ref=dst, send_sem=send_sem.at[r, kind], recv_sem=recv_sem.at[r, kind],
            device_id=(x, y), device_id_type=MESH,
        )

    def send(r):
        for kind, is_plane, side in ((0, right_plane, above), (1, left_plane, below)):
            @pl.when(is_plane)
            def _(kind=kind, side=side):
                for y in range(count_y):
                    remote(to_x.at[r, kind], from_x.at[r, kind, pl.ds(gy * 3, 3)], r, kind, side, y).start()

            @pl.when(jnp.logical_not(is_plane))
            def _(kind=kind, side=side):
                for k, y in ((2 * kind, front), (2 * kind + 1, back)):
                    remote(to_corner.at[r, k], from_corner.at[r, k], r, 4 + k, side, y).start()
                remote(to_x.at[r, kind], from_x.at[r, kind, pl.ds(0, 3)], r, kind, side, gy).start()
        remote(to_y.at[r, 0], from_y.at[r, 0], r, 2, gx, front).start()
        remote(to_y.at[r, 1], from_y.at[r, 1], r, 3, gx, back).start()

    def wait_for(ref, sem):
        pltpu.make_async_copy(ref, ref, sem).wait()

    def wait_sent(r):
        for kind, is_plane in ((0, right_plane), (1, left_plane)):
            @pl.when(is_plane)
            def _(kind=kind):
                wait_for(from_x.at[r, kind], send_sem.at[r, kind])

            @pl.when(jnp.logical_not(is_plane))
            def _(kind=kind):
                for k in (2 * kind, 2 * kind + 1):
                    wait_for(to_corner.at[r, k], send_sem.at[r, 4 + k])
                wait_for(to_x.at[r, kind], send_sem.at[r, kind])
        for k in (0, 1):
            wait_for(to_y.at[r, k], send_sem.at[r, 2 + k])

    def close_ring(r, kind):
        for b in range(blocks + 4):
            ring[b] = from_x[r, kind, b % blocks]

    def view(kind, shift):
        low = shift if kind == 0 else -shift - 1
        near, far = (0.75, 0.25) if kind == 0 else (0.25, 0.75)
        start = ((gy * 16 - low - 3) & (16 * count_y - 1)) * NZ
        first, offset = start >> 7, start & 127
        window = jnp.concatenate([ring[first + i] for i in range(5)], axis=1)
        window = pltpu.roll(window, 640 - 3 * NZ - offset, 1)
        return near * window + far * rolled(window, NZ, 1)

    def receive(r, step):
        slots_of = (up_slots, down_slots)
        edges = (0, ROWS - 1)
        for k in (0, 1):
            wait_for(from_y.at[r, k], recv_sem.at[r, 2 + k])
        for k, slots in ((0, plus_y), (1, minus_y)):
            packed = from_y[r, k, 0:16]
            cut = slice(0, 128) if k == 0 else slice(256, 384)
            keep = lane1 < NZ if k == 0 else lane1 >= 128 - NZ
            for i, slot in enumerate(slots):
                part = rolled(packed, -i * NZ if k == 0 else i * NZ, 1)
                f[slot, :, cut] = jnp.where(keep, part, f[slot, :, cut])
        ext[0:12, 384:512] = jnp.where(lane1[:12] < 64, from_y[r, 1, 12:24], from_y[r, 0, 12:24])
        row = lax.broadcasted_iota(jnp.int32, (8, WIDE), 0)
        lane8 = lax.broadcasted_iota(jnp.int32, (8, WIDE), 1)
        for kind, is_plane, place_of in ((0, left_plane, left_slot), (1, right_plane, right_slot)):
            outer = 14 - 2 * kind
            near_row = 15 - 3 * kind

            @pl.when(is_plane)
            def _(kind=kind, place_of=place_of, outer=outer):
                wait_for(from_x.at[r, kind], recv_sem.at[r, kind])
                close_ring(r, kind)
                rows = lax.broadcasted_iota(jnp.int32, (8, 640), 0)
                strip = view(kind, shifts[step, place_of])
                strip = jnp.where(
                    rows == 3, rolled(strip, NZ, 1), jnp.where(rows == 4, rolled(strip, -NZ, 1), strip)
                )
                for i, slot in enumerate(slots_of[kind]):
                    f[slot, edges[kind]:edges[kind] + 1, :] = strip[i:i + 1, :WIDE]
                phase = view(kind, shifts[jnp.minimum(step + 1, STEPS - 1), place_of])
                ext[outer:outer + 2, 0:WIDE] = phase[5:7, 0:WIDE]
                ext[outer:outer + 2, WIDE:512] = jnp.where(
                    lane1[:2] < 64, phase[5:7, 384:512], phase[5:7, 512:640]
                )

            @pl.when(jnp.logical_not(is_plane))
            def _(kind=kind, outer=outer, near_row=near_row):
                for k in (2 * kind, 2 * kind + 1):
                    wait_for(from_corner.at[r, k], recv_sem.at[r, 4 + k])
                wait_for(from_x.at[r, kind, pl.ds(0, 3)], recv_sem.at[r, kind])
                strip = jnp.concatenate([from_x[r, kind, b] for b in range(3)], axis=1)
                first, last = from_corner[r, 2 * kind], from_corner[r, 2 * kind + 1]
                plus = rolled(strip, NZ, 1)
                minus = rolled(strip, -NZ, 1)
                for i in range(3):
                    slot = slots_of[kind][i]
                    f[slot, edges[kind]:edges[kind] + 1, :] = strip[i:i + 1]
                head = jnp.where(lane1[:1] < NZ, first[0:1], plus[3:4, 0:128])
                tail = jnp.where(lane1[:1] >= 128 - NZ, last[0:1], minus[4:5, 256:384])
                e = edges[kind]
                f[slots_of[kind][3], e:e + 1, 0:128] = head
                f[slots_of[kind][3], e:e + 1, 128:384] = plus[3:4, 128:384]
                f[slots_of[kind][4], e:e + 1, 0:256] = minus[4:5, 0:256]
                f[slots_of[kind][4], e:e + 1, 256:384] = tail
                ext[outer:outer + 2, 0:WIDE] = strip[5:7]
                ext[near_row:near_row + 1, WIDE:512] = jnp.where(lane1[:1] < 64, last[1:2], first[1:2])

    def advance(r):
        p = ext[...]
        px, mx = rolled(p, -1, 0), rolled(p, 1, 0)
        py, my = rolled(p, -NZ, 1), rolled(p, NZ, 1)
        pz, mz = moved_yz(p, 0, -1, place4), moved_yz(p, 0, 1, place4)
        chem = 0.5 * (p * p * p - p) - 0.5 * (px + mx + py + my + pz + mz - 6.0 * p)
        slope = [0.5 * (a - b)[:, :WIDE] for a, b in ((px, mx), (py, my), (pz, mz))]
        px, mx = rolled(chem, -1, 0)[:, :WIDE], rolled(chem, 1, 0)[:, :WIDE]
        py, my = rolled(chem, -NZ, 1)[:, :WIDE], rolled(chem, NZ, 1)[:, :WIDE]
        pz, mz = moved_yz(chem, 0, -1, place4)[:, :WIDE], moved_yz(chem, 0, 1, place4)[:, :WIDE]
        bend = px + mx + py + my + pz + mz - 6.0 * chem[:, :WIDE]
        own = p[:, :WIDE]
        density = f[0]
        for slot in range(1, 19):
            density = density + f[slot]
        inverse = 1.0 / density
        scaled = (-0.5 * coupling / relax_rate) * own
        next_phase = own + mobility * bend
        drift = []
        for axis, push in enumerate((px - mx, py - my, pz - mz)):
            total = None
            for slot in range(1, 19, 2):
                sign = lattice_vel[slot][axis]
                if sign != 0:
                    pair = f[slot] - f[slot + 1]
                    if total is None:
                        total = pair
                    else:
                        total = total + pair if sign == 1 else total - pair
            next_phase = next_phase - total * inverse * slope[axis]
            drift.append((total + scaled * push) * inverse)
        ext[0:12, 0:WIDE] = next_phase[:12]
        base = 1.0 - 1.5 * (drift[0] * drift[0] + drift[1] * drift[1] + drift[2] * drift[2])
        weight = relax_rate / 36.0 * density
        keep = 1.0 - relax_rate
        packs = {}

        def put(slot, post):
            step_x, step_y, step_z = lattice_vel[slot]
            value = rolled(post, step_x, 0)
            moved = moved_yz(value, step_y, step_z, place)
            f[slot] = moved
            if step_x != 0:
                kind = 0 if step_x == 1 else 1
                i = (up_slots, down_slots)[kind].index(slot)
                line = 12 if step_x == 1 else 15
                shown = value if step_y != 0 else moved
                for b in range(3):
                    to_x[r, kind, b, i:i + 1, :] = shown[line:line + 1, b * 128:b * 128 + 128]
                if step_y != 0:
                    k = 2 * kind + (0 if step_y == 1 else 1)
                    cut = slice(0, 128) if step_y == 1 else slice(256, 384)
                    to_corner[r, k, 0:1, :] = moved[line:line + 1, cut]
            if step_y == 1:
                i = plus_y.index(slot)
                part = rolled(moved[:, 0:128], i * NZ, 1)
                packs[0] = part if i == 0 else jnp.where(lane1 >= i * NZ, part, packs[0])
            if step_y == -1:
                i = minus_y.index(slot)
                part = rolled(moved[:, 256:384], -i * NZ, 1)
                packs[1] = part if i == 0 else jnp.where(lane1 < 128 - i * NZ, part, packs[1])

        put(0, keep * f[0] + 12.0 * weight * base)
        for slot in range(1, 19, 2):
            along = None
            for axis in range(3):
                sign = lattice_vel[slot][axis]
                if sign != 0:
                    if along is None:
                        along = drift[axis]
                    else:
                        along = along + drift[axis] if sign == 1 else along - drift[axis]
            scale = 2.0 * weight if slot < 7 else weight
            even = scale * (base + 4.5 * along * along)
            odd = scale * (3.0 * along)
            here, there = f[slot], f[slot + 1]
            put(slot, keep * here + (even + odd))
            put(slot + 1, keep * there + (even - odd))
        to_y[r, 0, 0:12, :] = packs[0][:12]
        to_y[r, 1, 0:12, :] = packs[1][:12]
        pack_phase(r)

    for slot in range(19):
        f[slot, 0:12, :] = f_in[slot]
        f[slot, 12:16, :] = jnp.ones((4, WIDE), jnp.float32)
    ext[...] = jnp.zeros_like(ext)
    ext[0:12, 0:WIDE] = p_in[...]
    pack_phase(0)
    pl.semaphore_wait(barrier, jnp.where(left_plane | right_plane, 5 + count_y, 8))
    send(0)
    for k in (0, 1):
        wait_for(from_y.at[0, k], recv_sem.at[0, 2 + k])
    ext[0:12, 384:512] = jnp.where(lane1[:12] < 64, from_y[0, 1, 12:24], from_y[0, 0, 12:24])
    for kind, is_plane, place_of in ((0, left_plane, left_slot), (1, right_plane, right_slot)):
        outer = 14 - 2 * kind
        near_row = 15 - 3 * kind

        @pl.when(is_plane)
        def _(kind=kind, place_of=place_of, outer=outer):
            wait_for(from_x.at[0, kind], recv_sem.at[0, kind])
            close_ring(0, kind)
            phase = view(kind, shifts[0, place_of])
            ext[outer:outer + 2, 0:WIDE] = phase[5:7, 0:WIDE]
            ext[outer:outer + 2, WIDE:512] = jnp.where(
                lane1[:2] < 64, phase[5:7, 384:512], phase[5:7, 512:640]
            )

        @pl.when(jnp.logical_not(is_plane))
        def _(kind=kind, outer=outer, near_row=near_row):
            for k in (2 * kind, 2 * kind + 1):
                wait_for(from_corner.at[0, k], recv_sem.at[0, 4 + k])
            wait_for(from_x.at[0, kind, pl.ds(0, 3)], recv_sem.at[0, kind])
            first, last = from_corner[0, 2 * kind], from_corner[0, 2 * kind + 1]
            for b in range(3):
                ext[outer:outer + 2, b * 128:b * 128 + 128] = from_x[0, kind, b, 5:7, :]
            ext[near_row:near_row + 1, WIDE:512] = jnp.where(lane1[:1] < 64, last[1:2], first[1:2])

    def body(step, carry):
        advance(step + 1)
        send(step + 1)
        wait_sent(step)
        receive(step + 1, step)
        return carry

    lax.fori_loop(0, STEPS, body, 0)
    for slot in range(19):
        f_out[slot] = f[slot, 0:12, :]
    p_out[...] = ext[0:12, 0:WIDE]
    wait_sent(STEPS)


def on_device(populations, phase_field, plane_shifts):
    blocks = 3 * lax.axis_size("gy")
    rounds = STEPS + 1
    vmem = pl.BlockSpec(memory_space=pltpu.VMEM)
    return pl.pallas_call(
        kernel,
        out_shape=(
            jax.ShapeDtypeStruct(populations.shape, jnp.float32),
            jax.ShapeDtypeStruct(phase_field.shape, jnp.float32),
        ),
        in_specs=[pl.BlockSpec(memory_space=pltpu.SMEM), vmem, vmem],
        out_specs=(vmem, vmem),
        scratch_shapes=[
            pltpu.VMEM((19, 16, WIDE), jnp.float32),
            pltpu.VMEM((16, 512), jnp.float32),
            pltpu.VMEM((rounds, 2, blocks, 8, 128), jnp.float32),
            pltpu.VMEM((rounds, 2, 24, 128), jnp.float32),
            pltpu.VMEM((rounds, 4, 8, 128), jnp.float32),
            pltpu.VMEM((rounds, 2, 3, 8, 128), jnp.float32),
            pltpu.VMEM((rounds, 2, 24, 128), jnp.float32),
            pltpu.VMEM((rounds, 4, 8, 128), jnp.float32),
            pltpu.VMEM((blocks + 4, 8, 128), jnp.float32),
            pltpu.SemaphoreType.DMA((rounds, 8)),
            pltpu.SemaphoreType.DMA((rounds, 8)),
        ],
        compiler_params=pltpu.CompilerParams(
            collective_id=0, has_side_effects=True, vmem_limit_bytes=32 * 1024 * 1024
        ),
    )(plane_shifts, populations, phase_field)


def solution(mesh):
    return jax.shard_map(
        on_device,
        mesh=mesh,
        in_specs=(P(None, "gx", "gy"), P("gx", "gy"), P()),
        out_specs=(P(None, "gx", "gy"), P("gx", "gy")),
        check_vma=False,
    )
```

```python
import functools

import jax
import jax.numpy as jnp
from jax import lax
from jax.experimental import pallas as pl
from jax.experimental.pallas import tpu as pltpu
from jax.sharding import PartitionSpec as P

STEPS = 4
NZ = 24
ROWS = 12
WIDE = 384
SPAN = 4
MESH = pl.DeviceIdType.MESH

lattice_vel = (
    (0, 0, 0),
    (1, 0, 0),
    (-1, 0, 0),
    (0, 1, 0),
    (0, -1, 0),
    (0, 0, 1),
    (0, 0, -1),
    (1, 1, 0),
    (-1, -1, 0),
    (1, -1, 0),
    (-1, 1, 0),
    (1, 0, 1),
    (-1, 0, -1),
    (1, 0, -1),
    (-1, 0, 1),
    (0, 1, 1),
    (0, -1, -1),
    (0, 1, -1),
    (0, -1, 1),
)
relax_rate = 0.8
coupling = 0.01
mobility = 0.02

up_slots = (1, 11, 13, 7, 9)
down_slots = (2, 12, 14, 10, 8)
plus_y = (3, 7, 10, 15, 17)
minus_y = (4, 8, 9, 16, 18)


def rolled(value, shift, axis):
    size = value.shape[axis]
    shift = shift % size
    return value if shift == 0 else pltpu.roll(value, shift, axis)


def moved_yz(value, step_y, step_z, place):
    if step_z == 0:
        return rolled(value, step_y * NZ, 1)
    edge = 0 if step_z == 1 else NZ - 1
    inner = rolled(value, step_y * NZ + step_z, 1)
    wrap = rolled(value, step_y * NZ + step_z - step_z * NZ, 1)
    return jnp.where(place == edge, wrap, inner)


def differences(value, place):
    return (
        (rolled(value, -1, 0), rolled(value, 1, 0)),
        (rolled(value, -NZ, 1), rolled(value, NZ, 1)),
        (moved_yz(value, 0, -1, place), moved_yz(value, 0, 1, place)),
    )


def bulk(p, around):
    total = around[0][0] + around[0][1] + around[1][0] + around[1][1] + around[2][0] + around[2][1]
    return 0.5 * (p * p * p - p) - 0.5 * (total - 6.0 * p)


def bent(chem, around):
    total = around[0][0] + around[0][1] + around[1][0] + around[1][1] + around[2][0] + around[2][1]
    return total - 6.0 * chem


def relaxed(here, weight, along, drift):
    square = drift[0] * drift[0] + drift[1] * drift[1] + drift[2] * drift[2]
    return (1.0 - relax_rate) * here + weight * (
        1.0 - 1.5 * square + 3.0 * along + 4.5 * along * along
    )


def strip_post(kind, here, density, drift, place):
    sign = 1.0 - 2.0 * kind
    row = lax.broadcasted_iota(jnp.int32, here.shape, 0)
    full = [jnp.broadcast_to(d, here.shape) for d in drift]
    along = sign * full[0]
    along = along + jnp.where(row == 3, full[1], jnp.where(row == 4, -full[1], 0.0))
    along = along + jnp.where(row == 1, sign * full[2], jnp.where(row == 2, -sign * full[2], 0.0))
    weight = jnp.where(row == 0, 2.0, 1.0) * (relax_rate / 36.0) * density
    post = relaxed(here, weight, along, full)
    first, second = (1, -1) if kind == 0 else (-1, 1)
    return jnp.where(
        row == 1, moved_yz(post, 0, first, place), jnp.where(row == 2, moved_yz(post, 0, second, place), post)
    )


def strip_moved(strip):
    row = lax.broadcasted_iota(jnp.int32, strip.shape, 0)
    return jnp.where(row == 3, rolled(strip, NZ, 1), jnp.where(row == 4, rolled(strip, -NZ, 1), strip))


def packed_post(k, here, density, drift, lane1):
    def spread(value):
        out = rolled(value, NZ if k == 0 else 104, 1)
        first = out
        for i in range(1, 5):
            if k == 0:
                out = jnp.where(lane1 >= i * NZ, rolled(first, i * NZ, 1), out)
            else:
                out = jnp.where(lane1 < 128 - i * NZ, rolled(first, -i * NZ, 1), out)
        return out

    slots = plus_y if k == 0 else minus_y
    group = lane1 // NZ if k == 0 else (127 - lane1) // NZ
    density, drift = spread(density), [spread(d) for d in drift]

    def chosen(axis, value):
        out = jnp.zeros_like(value)
        for i, slot in enumerate(slots):
            if lattice_vel[slot][axis] != 0:
                out = jnp.where(group == i, lattice_vel[slot][axis] * value, out)
        return out

    along = chosen(0, drift[0]) + chosen(1, drift[1]) + chosen(2, drift[2])
    weight = jnp.where(group == 0, 2.0, 1.0) * (relax_rate / 36.0) * density
    post = relaxed(here, weight, along, drift)
    place = lax.rem(lane1, NZ) if k == 0 else lax.rem(lane1 + 16, NZ)
    out = post
    for i, slot in enumerate(slots):
        step_x, _, step_z = lattice_vel[slot]
        if step_x != 0 or step_z != 0:
            out = jnp.where(group == i, moved_yz(rolled(post, step_x, 0), 0, step_z, place), out)
    return out


def kernel(
    shifts, f_in, p_in, f_out, p_out,
    f, ext, from_x, from_y, from_corner, to_x, to_y, to_corner, ring,
    e_p, e_r, e_u, ring_b, ring_a,
    wide_x, wide_y, wide_corner, wide_a, out_x, out_y, out_corner, out_a,
    send_sem, recv_sem,
):
    count_x, count_y = lax.axis_size("gx"), lax.axis_size("gy")
    gx, gy = lax.axis_index("gx"), lax.axis_index("gy")
    above, below = lax.rem(gx + 1, count_x), lax.rem(gx + count_x - 1, count_x)
    front, back = lax.rem(gy + 1, count_y), lax.rem(gy + count_y - 1, count_y)
    planes = count_x // SPAN
    left_plane = lax.rem(gx, SPAN) == 0
    right_plane = lax.rem(gx, SPAN) == SPAN - 1
    left_slot = lax.rem(gx // SPAN + planes - 1, planes)
    right_slot = gx // SPAN
    blocks = 3 * count_y

    def signal(x, y):
        pl.semaphore_signal(barrier, inc=1, device_id=(x, y), device_id_type=MESH)

    barrier = pltpu.get_barrier_semaphore()
    any_plane = left_plane | right_plane
    signal(gx, front)
    signal(gx, back)

    @pl.when(any_plane)
    def _():
        for j in range(2, count_y - 1):
            signal(gx, lax.rem(gy + j, count_y))

    for is_plane, side in ((left_plane, below), (right_plane, above)):
        @pl.when(is_plane)
        def _(side=side):
            for y in range(count_y):
                signal(side, y)

        @pl.when(jnp.logical_not(is_plane))
        def _(side=side):
            signal(side, gy)
            signal(side, front)
            signal(side, back)

    lane = lax.broadcasted_iota(jnp.int32, (16, WIDE), 1)
    place = lax.rem(lane, NZ)
    lane4 = lax.broadcasted_iota(jnp.int32, (16, 512), 1)
    place4 = lax.rem(jnp.where(lane4 < 448, lane4, lane4 - 464), NZ)
    lane1 = lax.broadcasted_iota(jnp.int32, (16, 128), 1)
    lane5 = lax.broadcasted_iota(jnp.int32, (24, 640), 1)
    place5 = lax.rem(jnp.where(lane5 < 512, lane5, lane5 + 8), NZ)
    place6 = lax.rem(lax.broadcasted_iota(jnp.int32, (8, 768), 1), NZ)

    def pack_phase(r):
        for b in range(3):
            cut = slice(b * 128, b * 128 + 128)
            to_x[r, 0, b, 5:7, :] = ext[10:12, cut]
            to_x[r, 1, b, 5:7, :] = ext[0:2, cut]
        to_y[r, 0, 12:24, :] = ext[0:12, 256:384]
        to_y[r, 1, 12:24, :] = ext[0:12, 0:128]
        to_corner[r, 0, 1:2, :] = ext[11:12, 256:384]
        to_corner[r, 1, 1:2, :] = ext[11:12, 0:128]
        to_corner[r, 2, 1:2, :] = ext[0:1, 256:384]
        to_corner[r, 3, 1:2, :] = ext[0:1, 0:128]

    def remote(src, dst, r, kind, x, y):
        return pltpu.make_async_remote_copy(
            src_ref=src, dst_ref=dst, send_sem=send_sem.at[r, kind], recv_sem=recv_sem.at[r, kind],
            device_id=(x, y), device_id_type=MESH,
        )

    def send(r):
        for kind, is_plane, side in ((0, right_plane, above), (1, left_plane, below)):
            @pl.when(is_plane)
            def _(kind=kind, side=side):
                for y in range(count_y):
                    remote(to_x.at[r, kind], from_x.at[r, kind, pl.ds(gy * 3, 3)], r, kind, side, y).start()

            @pl.when(jnp.logical_not(is_plane))
            def _(kind=kind, side=side):
                for k, y in ((2 * kind, front), (2 * kind + 1, back)):
                    remote(to_corner.at[r, k], from_corner.at[r, k], r, 4 + k, side, y).start()
                remote(to_x.at[r, kind], from_x.at[r, kind, pl.ds(0, 3)], r, kind, side, gy).start()
        remote(to_y.at[r, 0], from_y.at[r, 0], r, 2, gx, front).start()
        remote(to_y.at[r, 1], from_y.at[r, 1], r, 3, gx, back).start()

    def wait_for(ref, sem):
        pltpu.make_async_copy(ref, ref, sem).wait()

    def wait_sent(r):
        for kind, is_plane in ((0, right_plane), (1, left_plane)):
            @pl.when(is_plane)
            def _(kind=kind):
                wait_for(from_x.at[r, kind], send_sem.at[r, kind])

            @pl.when(jnp.logical_not(is_plane))
            def _(kind=kind):
                for k in (2 * kind, 2 * kind + 1):
                    wait_for(to_corner.at[r, k], send_sem.at[r, 4 + k])
                wait_for(to_x.at[r, kind], send_sem.at[r, kind])
        for k in (0, 1):
            wait_for(to_y.at[r, k], send_sem.at[r, 2 + k])

    def window_of(held, turn):
        start = ((gy * 16 - turn - 4) & (16 * count_y - 1)) * NZ
        first, offset = start >> 7, start & 127
        window = jnp.concatenate([held[first + i] for i in range(6)], axis=1)
        return pltpu.roll(window, 768 - 4 * NZ - offset, 1)

    def view_b(kind, shift):
        return window_of(ring_b, shift if kind == 0 else -shift - 1)

    def close_ring(r, kind):
        for b in range(blocks + 4):
            ring[b] = from_x[r, kind, b % blocks]

    def view(kind, shift):
        low = shift if kind == 0 else -shift - 1
        near, far = (0.75, 0.25) if kind == 0 else (0.25, 0.75)
        start = ((gy * 16 - low - 3) & (16 * count_y - 1)) * NZ
        first, offset = start >> 7, start & 127
        window = jnp.concatenate([ring[first + i] for i in range(5)], axis=1)
        window = pltpu.roll(window, 640 - 3 * NZ - offset, 1)
        return near * window + far * rolled(window, NZ, 1)

    def patch_y(k, packed):
        cut = slice(0, 128) if k == 0 else slice(256, 384)
        keep = lane1 < NZ if k == 0 else lane1 >= 128 - NZ
        for i, slot in enumerate(plus_y if k == 0 else minus_y):
            part = rolled(packed, -i * NZ if k == 0 else i * NZ, 1)
            f[slot, :, cut] = jnp.where(keep, part, f[slot, :, cut])

    def patch_x(kind, strip):
        edge = 0 if kind == 0 else ROWS - 1
        for i, slot in enumerate(up_slots if kind == 0 else down_slots):
            f[slot, edge:edge + 1, :] = strip[i:i + 1, :WIDE]

    def receive(r, step):
        slots_of = (up_slots, down_slots)
        edges = (0, ROWS - 1)
        for k in (0, 1):
            wait_for(from_y.at[r, k], recv_sem.at[r, 2 + k])
        for k in (0, 1):
            patch_y(k, from_y[r, k, 0:16])
        ext[0:12, 384:512] = jnp.where(lane1[:12] < 64, from_y[r, 1, 12:24], from_y[r, 0, 12:24])
        for kind, is_plane, place_of in ((0, left_plane, left_slot), (1, right_plane, right_slot)):
            outer = 14 - 2 * kind
            near_row = 15 - 3 * kind

            @pl.when(is_plane)
            def _(kind=kind, place_of=place_of, outer=outer):
                wait_for(from_x.at[r, kind], recv_sem.at[r, kind])
                close_ring(r, kind)
                patch_x(kind, strip_moved(view(kind, shifts[step, place_of])))
                phase = view(kind, shifts[jnp.minimum(step + 1, STEPS - 1), place_of])
                ext[outer:outer + 2, 0:WIDE] = phase[5:7, 0:WIDE]
                ext[outer:outer + 2, WIDE:512] = jnp.where(
                    lane1[:2] < 64, phase[5:7, 384:512], phase[5:7, 512:640]
                )

            @pl.when(jnp.logical_not(is_plane))
            def _(kind=kind, outer=outer, near_row=near_row):
                for k in (2 * kind, 2 * kind + 1):
                    wait_for(from_corner.at[r, k], recv_sem.at[r, 4 + k])
                wait_for(from_x.at[r, kind, pl.ds(0, 3)], recv_sem.at[r, kind])
                strip = jnp.concatenate([from_x[r, kind, b] for b in range(3)], axis=1)
                first, last = from_corner[r, 2 * kind], from_corner[r, 2 * kind + 1]
                plus = rolled(strip, NZ, 1)
                minus = rolled(strip, -NZ, 1)
                for i in range(3):
                    slot = slots_of[kind][i]
                    f[slot, edges[kind]:edges[kind] + 1, :] = strip[i:i + 1]
                head = jnp.where(lane1[:1] < NZ, first[0:1], plus[3:4, 0:128])
                tail = jnp.where(lane1[:1] >= 128 - NZ, last[0:1], minus[4:5, 256:384])
                e = edges[kind]
                f[slots_of[kind][3], e:e + 1, 0:128] = head
                f[slots_of[kind][3], e:e + 1, 128:384] = plus[3:4, 128:384]
                f[slots_of[kind][4], e:e + 1, 0:256] = minus[4:5, 0:256]
                f[slots_of[kind][4], e:e + 1, 256:384] = tail
                ext[outer:outer + 2, 0:WIDE] = strip[5:7]
                ext[near_row:near_row + 1, WIDE:512] = jnp.where(lane1[:1] < 64, last[1:2], first[1:2])

    def momentum():
        density = f[0]
        for slot in range(1, 19):
            density = density + f[slot]
        totals = []
        for axis in range(3):
            total = None
            for slot in range(1, 19, 2):
                sign = lattice_vel[slot][axis]
                if sign != 0:
                    pair = f[slot] - f[slot + 1]
                    if total is None:
                        total = pair
                    else:
                        total = total + pair if sign == 1 else total - pair
            totals.append(total)
        return density, totals

    def advance(r):
        p = ext[...]
        around = differences(p, place4)
        chem = bulk(p, around)
        slope = [0.5 * (a - b)[:, :WIDE] for a, b in around]
        around = [(a[:, :WIDE], b[:, :WIDE]) for a, b in differences(chem, place4)]
        bend = bent(chem[:, :WIDE], around)
        own = p[:, :WIDE]
        density, totals = momentum()
        inverse = 1.0 / density
        scaled = (-0.5 * coupling / relax_rate) * own
        next_phase = own + mobility * bend
        drift = []
        for axis in range(3):
            next_phase = next_phase - totals[axis] * inverse * slope[axis]
            drift.append((totals[axis] + scaled * (around[axis][0] - around[axis][1])) * inverse)
        ext[0:12, 0:WIDE] = next_phase[:12]
        collide(density, drift, r)
        pack_phase(r)

    def collide(density, drift, r):
        base = 1.0 - 1.5 * (drift[0] * drift[0] + drift[1] * drift[1] + drift[2] * drift[2])
        weight = relax_rate / 36.0 * density
        keep = 1.0 - relax_rate
        packs = {}

        def put(slot, post):
            step_x, step_y, step_z = lattice_vel[slot]
            value = rolled(post, step_x, 0)
            moved = moved_yz(value, step_y, step_z, place)
            f[slot] = moved
            if r is None:
                return
            if step_x != 0:
                kind = 0 if step_x == 1 else 1
                i = (up_slots, down_slots)[kind].index(slot)
                line = 12 if step_x == 1 else 15
                shown = value if step_y != 0 else moved
                for b in range(3):
                    to_x[r, kind, b, i:i + 1, :] = shown[line:line + 1, b * 128:b * 128 + 128]
                if step_y != 0:
                    k = 2 * kind + (0 if step_y == 1 else 1)
                    cut = slice(0, 128) if step_y == 1 else slice(256, 384)
                    to_corner[r, k, 0:1, :] = moved[line:line + 1, cut]
            if step_y == 1:
                i = plus_y.index(slot)
                part = rolled(moved[:, 0:128], i * NZ, 1)
                packs[0] = part if i == 0 else jnp.where(lane1 >= i * NZ, part, packs[0])
            if step_y == -1:
                i = minus_y.index(slot)
                part = rolled(moved[:, 256:384], -i * NZ, 1)
                packs[1] = part if i == 0 else jnp.where(lane1 < 128 - i * NZ, part, packs[1])

        put(0, keep * f[0] + 12.0 * weight * base)
        for slot in range(1, 19, 2):
            along = None
            for axis in range(3):
                sign = lattice_vel[slot][axis]
                if sign != 0:
                    if along is None:
                        along = drift[axis]
                    else:
                        along = along + drift[axis] if sign == 1 else along - drift[axis]
            scale = 2.0 * weight if slot < 7 else weight
            even = scale * (base + 4.5 * along * along)
            odd = scale * (3.0 * along)
            here, there = f[slot], f[slot + 1]
            put(slot, keep * here + (even + odd))
            put(slot + 1, keep * there + (even - odd))
        if r is not None:
            to_y[r, 0, 0:12, :] = packs[0][:12]
            to_y[r, 1, 0:12, :] = packs[1][:12]

    for slot in range(19):
        f[slot, 0:12, :] = f_in[slot]
        f[slot, 12:16, :] = jnp.ones((4, WIDE), jnp.float32)
    ext[...] = jnp.zeros_like(ext)
    sides = ((0, left_plane, left_slot), (1, right_plane, right_slot))
    e_p[...] = jnp.zeros_like(e_p)
    e_r[...] = jnp.ones_like(e_r)
    e_u[...] = jnp.zeros_like(e_u)
    e_p[0:12, 0:WIDE] = p_in[...]
    density, totals = momentum()
    e_r[0:12, 0:WIDE] = density[:12]
    for axis in range(3):
        e_u[axis, 0:12, 0:WIDE] = (totals[axis] / density)[:12]

    for kind in (0, 1):
        edge, second, low = ((11, 10, 8), (0, 1, 0))[kind]
        for b in range(3):
            cut = slice(b * 128, b * 128 + 128)
            out_x[kind, b, 0:4, :] = e_p[low:low + 4, cut]
            out_x[kind, b, 4:5, :] = e_r[edge:edge + 1, cut]
            for axis in range(3):
                out_x[kind, b, 5 + axis:6 + axis, :] = e_u[axis, edge:edge + 1, cut]
                out_x[kind, b, 13 + axis:14 + axis, :] = e_u[axis, second:second + 1, cut]
            for i, slot in enumerate(up_slots if kind == 0 else down_slots):
                out_x[kind, b, 8 + i:9 + i, :] = f[slot, edge:edge + 1, cut]
        third = (9, 0)[kind]
        for k in (2 * kind, 2 * kind + 1):
            cut = slice(256, 384) if k % 2 == 0 else slice(0, 128)
            out_corner[k, 0:3, :] = e_p[third:third + 3, cut]
            out_corner[k, 3:4, :] = e_r[edge:edge + 1, cut]
            for axis in range(3):
                out_corner[k, 4 + axis:5 + axis, :] = e_u[axis, edge:edge + 1, cut]
            slot = (up_slots if kind == 0 else down_slots)[3 + k % 2]
            out_corner[k, 7:8, :] = f[slot, edge:edge + 1, cut]
    for k in (0, 1):
        cut = slice(256, 384) if k == 0 else slice(0, 128)
        low = lane1[:12] < 64
        if k == 0:
            pair = lambda a, b: jnp.where(low, pltpu.roll(b, 64, 1), a)
        else:
            pair = lambda a, b: jnp.where(low, a, pltpu.roll(b, 64, 1))
        packed = None
        for i, slot in enumerate(plus_y if k == 0 else minus_y):
            block = f[slot, :, cut]
            part = rolled(block, NZ + i * NZ if k == 0 else -NZ - i * NZ, 1)
            if i == 0:
                packed = part
            else:
                packed = jnp.where(lane1 >= i * NZ if k == 0 else lane1 < 128 - i * NZ, part, packed)
        out_y[k, 0:12, :] = packed[:12]
        out_y[k, 12:24, :] = e_p[0:12, cut]
        out_y[k, 24:36, :] = pair(e_r[0:12, cut], e_u[0, 0:12, cut])
        out_y[k, 36:48, :] = pair(e_u[1, 0:12, cut], e_u[2, 0:12, cut])

    @pl.when(left_plane)
    def _():
        for b in range(3):
            out_a[2 * b:2 * b + 2, :] = e_p[0:2, b * 128:b * 128 + 128]

    @pl.when(right_plane)
    def _():
        for b in range(3):
            out_a[2 * b:2 * b + 2, :] = e_p[10:12, b * 128:b * 128 + 128]

    pl.semaphore_wait(barrier, jnp.where(any_plane, 5 + count_y + max(count_y - 3, 0), 8))

    for kind, is_plane, side in ((0, right_plane, above), (1, left_plane, below)):
        @pl.when(is_plane)
        def _(kind=kind, side=side):
            for y in range(count_y):
                remote(out_x.at[kind], wide_x.at[kind, pl.ds(gy * 3, 3)], 0, kind, side, y).start()

        @pl.when(jnp.logical_not(is_plane))
        def _(kind=kind, side=side):
            for k, y in ((2 * kind, front), (2 * kind + 1, back)):
                remote(out_corner.at[k], wide_corner.at[k], 0, 4 + k, side, y).start()
            remote(out_x.at[kind], wide_x.at[kind, pl.ds(0, 3)], 0, kind, side, gy).start()

    @pl.when(any_plane)
    def _():
        for j in range(1, count_y):
            remote(out_a, wide_a.at[j - 1], 0, 8, gx, lax.rem(gy + j, count_y)).start()

    remote(out_y.at[0], wide_y.at[0], 0, 2, gx, front).start()
    remote(out_y.at[1], wide_y.at[1], 0, 3, gx, back).start()

    for k in (0, 1):
        wait_for(wide_y.at[k], recv_sem.at[0, 2 + k])
        cut = slice(512, 640) if k == 0 else slice(384, 512)
        e_p[0:12, cut] = wide_y[k, 12:24]
        e_r[0:12, cut] = wide_y[k, 24:36]
        e_u[0, 0:12, cut] = pltpu.roll(wide_y[k, 24:36], 64, 1)
        e_u[1, 0:12, cut] = wide_y[k, 36:48]
        e_u[2, 0:12, cut] = pltpu.roll(wide_y[k, 36:48], 64, 1)
    for kind, is_plane, place_of in sides:
        low = (20, 12)[kind]
        edge, second, third = ((23, 22, 21), (12, 13, 12))[kind]

        @pl.when(is_plane)
        def _(kind=kind, place_of=place_of):
            wait_for(wide_x.at[kind], recv_sem.at[0, kind])
            wait_for(wide_a.at[pl.ds(0, count_y - 1)], recv_sem.at[0, 8])
            for b in range(blocks + 5):
                ring_b[b] = wide_x[kind, b % blocks]
            a_row = (4, 6)[kind]
            for j in range(count_y):
                source = lax.rem(gy + count_y - j, count_y)
                for b in range(3):
                    piece = out_a[2 * b:2 * b + 2, :] if j == 0 else wide_a[j - 1, 2 * b:2 * b + 2, :]
                    ring_a[source * 3 + b, a_row:a_row + 2, :] = piece
            for b in range(5):
                ring_a[blocks + b] = ring_a[b]
            shift = shifts[0, place_of]
            near = view_b(kind, shift)[0:8]
            phase = (near * 0.75 + rolled(near, NZ, 1) * 0.25) if kind == 0 else (
                near * 0.25 + rolled(near, NZ, 1) * 0.75)
            row, at = ((22, 2), (12, 0))[kind]
            e_p[row:row + 2, 0:512] = phase[at:at + 2, 0:512]
            e_p[row:row + 2, 512:640] = phase[at:at + 2, 640:768]

        @pl.when(jnp.logical_not(is_plane))
        def _(kind=kind, low=low, edge=edge, second=second, third=third):
            for k in (2 * kind, 2 * kind + 1):
                wait_for(wide_corner.at[k], recv_sem.at[0, 4 + k])
                cut = slice(512, 640) if k % 2 == 0 else slice(384, 512)
                e_p[third:third + 3, cut] = wide_corner[k, 0:3]
                e_r[edge:edge + 1, cut] = wide_corner[k, 3:4]
                for axis in range(3):
                    e_u[axis, edge:edge + 1, cut] = wide_corner[k, 4 + axis:5 + axis]
            wait_for(wide_x.at[kind, pl.ds(0, 3)], recv_sem.at[0, kind])
            for b in range(3):
                cut = slice(b * 128, b * 128 + 128)
                e_p[low:low + 4, cut] = wide_x[kind, b, 0:4]
                e_r[edge:edge + 1, cut] = wide_x[kind, b, 4:5]
                for axis in range(3):
                    e_u[axis, edge:edge + 1, cut] = wide_x[kind, b, 5 + axis:6 + axis]
                    e_u[axis, second:second + 1, cut] = wide_x[kind, b, 13 + axis:14 + axis]

    p = e_p[...]
    around = differences(p, place5)
    chem = bulk(p, around)
    slope = [0.5 * (a - b) for a, b in around]
    around = differences(chem, place5)
    next_phase = p + mobility * bent(chem, around)
    scaled = (-0.5 * coupling / relax_rate) * p / e_r[...]
    drift = []
    for axis in range(3):
        flow = e_u[axis]
        next_phase = next_phase - flow * slope[axis]
        drift.append(flow + scaled * (around[axis][0] - around[axis][1]))
    for top, at, size in ((0, 0, 12), (12, 12, 2), (14, 22, 2)):
        ext[top:top + size, 0:WIDE] = next_phase[at:at + size, 0:WIDE]
        ext[top:top + size, WIDE:512] = jnp.where(
            lane1[:size] < 64, next_phase[at:at + size, 384:512], next_phase[at:at + size, 512:640]
        )
    collide(e_r[0:16, 0:WIDE], [d[0:16, 0:WIDE] for d in drift], None)
    for k in (0, 1):
        cut = slice(512, 640) if k == 0 else slice(384, 512)
        patch_y(k, packed_post(k, wide_y[k, 0:16], e_r[0:16, cut], [d[0:16, cut] for d in drift], lane1))
    for kind, is_plane, place_of in sides:
        @pl.when(is_plane)
        def _(kind=kind, place_of=place_of):
            first = shifts[0, place_of]
            row = lax.broadcasted_iota(jnp.int32, (8, 768), 0)
            edge, at, outer = ((3, 2, 14), (0, 0, 12))[kind]
            weights_of = ((0.75, 0.25), (0.25, 0.75))[kind]
            for step in (0, 1):
                shift = shifts[step, place_of]
                both = view_b(kind, shift)
                turn = shift - first if kind == 0 else first - shift - 1
                own = window_of(ring_a, turn)
                own = 0.75 * own + 0.25 * rolled(own, -NZ if kind == 0 else NZ, 1)
                far_p = jnp.where(row < 4, both[0:8], own)
                around = differences(far_p, place6)
                chem = bulk(far_p, around)
                slope = [0.5 * (a - b) for a, b in around]
                around = differences(chem, place6)
                if step == 0:
                    density = both[4:5]
                    scaled = (-0.5 * coupling / relax_rate) * far_p[edge:edge + 1] / density
                    drift = [
                        both[5 + axis:6 + axis]
                        + scaled * (around[axis][0] - around[axis][1])[edge:edge + 1]
                        for axis in range(3)
                    ]
                    strip = strip_post(kind, both[8:16], density, drift, place6)
                    strip = weights_of[0] * strip + weights_of[1] * rolled(strip, NZ, 1)
                    patch_x(kind, strip_moved(strip))
                else:
                    after = far_p + mobility * bent(chem, around)
                    for axis in range(3):
                        flow = jnp.where(row == edge, both[5 + axis:6 + axis], both[13 + axis:14 + axis])
                        after = after - flow * slope[axis]
                    after = weights_of[0] * after + weights_of[1] * rolled(after, NZ, 1)
                    ext[outer:outer + 2, 0:WIDE] = after[at:at + 2, 0:WIDE]
                    ext[outer:outer + 2, WIDE:512] = jnp.where(
                        lane1[:2] < 64, after[at:at + 2, 384:512], after[at:at + 2, 640:768]
                    )

        @pl.when(jnp.logical_not(is_plane))
        def _(kind=kind):
            edge = (23, 12)[kind]
            strip = jnp.concatenate(
                [wide_x[kind, b, 8:16] for b in range(3)]
                + [jnp.broadcast_to(wide_corner[2 * kind + i, 7:8], (8, 128)) for i in (1, 0)],
                axis=1,
            )
            strip = strip_post(
                kind, strip, e_r[edge:edge + 1, :], [d[edge:edge + 1] for d in drift], place5[:8]
            )
            patch_x(kind, strip_moved(strip))

    for kind, is_plane in ((0, right_plane), (1, left_plane)):
        @pl.when(is_plane)
        def _(kind=kind):
            wait_for(wide_x.at[kind], send_sem.at[0, kind])
            wait_for(wide_a.at[pl.ds(0, count_y - 1)], send_sem.at[0, 8])

        @pl.when(jnp.logical_not(is_plane))
        def _(kind=kind):
            for k in (2 * kind, 2 * kind + 1):
                wait_for(out_corner.at[k], send_sem.at[0, 4 + k])
            wait_for(out_x.at[kind], send_sem.at[0, kind])
    for k in (0, 1):
        wait_for(out_y.at[k], send_sem.at[0, 2 + k])

    def body(step, carry):
        advance(step)
        send(step)
        receive(step, step)
        wait_sent(step)
        return carry

    lax.fori_loop(1, STEPS, body, 0)
    for slot in range(19):
        f_out[slot] = f[slot, 0:12, :]
    p_out[...] = ext[0:12, 0:WIDE]


def on_device(populations, phase_field, plane_shifts):
    blocks = 3 * lax.axis_size("gy")
    rounds = STEPS
    vmem = pl.BlockSpec(memory_space=pltpu.VMEM)
    return pl.pallas_call(
        kernel,
        out_shape=(
            jax.ShapeDtypeStruct(populations.shape, jnp.float32),
            jax.ShapeDtypeStruct(phase_field.shape, jnp.float32),
        ),
        in_specs=[pl.BlockSpec(memory_space=pltpu.SMEM), vmem, vmem],
        out_specs=(vmem, vmem),
        scratch_shapes=[
            pltpu.VMEM((19, 16, WIDE), jnp.float32),
            pltpu.VMEM((16, 512), jnp.float32),
            pltpu.VMEM((rounds, 2, blocks, 8, 128), jnp.float32),
            pltpu.VMEM((rounds, 2, 24, 128), jnp.float32),
            pltpu.VMEM((rounds, 4, 8, 128), jnp.float32),
            pltpu.VMEM((rounds, 2, 3, 8, 128), jnp.float32),
            pltpu.VMEM((rounds, 2, 24, 128), jnp.float32),
            pltpu.VMEM((rounds, 4, 8, 128), jnp.float32),
            pltpu.VMEM((blocks + 4, 8, 128), jnp.float32),
            pltpu.VMEM((24, 640), jnp.float32),
            pltpu.VMEM((24, 640), jnp.float32),
            pltpu.VMEM((3, 24, 640), jnp.float32),
            pltpu.VMEM((blocks + 5, 16, 128), jnp.float32),
            pltpu.VMEM((blocks + 5, 8, 128), jnp.float32),
            pltpu.VMEM((2, blocks, 16, 128), jnp.float32),
            pltpu.VMEM((2, 48, 128), jnp.float32),
            pltpu.VMEM((4, 8, 128), jnp.float32),
            pltpu.VMEM((lax.axis_size("gy") - 1, 8, 128), jnp.float32),
            pltpu.VMEM((2, 3, 16, 128), jnp.float32),
            pltpu.VMEM((2, 48, 128), jnp.float32),
            pltpu.VMEM((4, 8, 128), jnp.float32),
            pltpu.VMEM((8, 128), jnp.float32),
            pltpu.SemaphoreType.DMA((rounds, 9)),
            pltpu.SemaphoreType.DMA((rounds, 9)),
        ],
        compiler_params=pltpu.CompilerParams(
            collective_id=0, has_side_effects=True, vmem_limit_bytes=32 * 1024 * 1024
        ),
    )(plane_shifts, populations, phase_field)


def solution(mesh):
    return jax.shard_map(
        on_device,
        mesh=mesh,
        in_specs=(P(None, "gx", "gy"), P("gx", "gy"), P()),
        out_specs=(P(None, "gx", "gy"), P("gx", "gy")),
        check_vma=False,
    )
```

```python
import functools

import jax
import jax.numpy as jnp
from jax import lax
from jax.experimental import pallas as pl
from jax.experimental.pallas import tpu as pltpu
from jax.sharding import PartitionSpec as P

STEPS = 4
NZ = 24
ROWS = 12
WIDE = 384
SPAN = 4
MESH = pl.DeviceIdType.MESH

lattice_vel = (
    (0, 0, 0),
    (1, 0, 0),
    (-1, 0, 0),
    (0, 1, 0),
    (0, -1, 0),
    (0, 0, 1),
    (0, 0, -1),
    (1, 1, 0),
    (-1, -1, 0),
    (1, -1, 0),
    (-1, 1, 0),
    (1, 0, 1),
    (-1, 0, -1),
    (1, 0, -1),
    (-1, 0, 1),
    (0, 1, 1),
    (0, -1, -1),
    (0, 1, -1),
    (0, -1, 1),
)
relax_rate = 0.8
coupling = 0.01
mobility = 0.02

up_slots = (1, 11, 13, 7, 9)
down_slots = (2, 12, 14, 10, 8)
plus_y = (3, 7, 10, 15, 17)
minus_y = (4, 8, 9, 16, 18)


def rolled(value, shift, axis):
    size = value.shape[axis]
    shift = shift % size
    return value if shift == 0 else pltpu.roll(value, shift, axis)


def moved_yz(value, step_y, step_z, place):
    if step_z == 0:
        return rolled(value, step_y * NZ, 1)
    edge = 0 if step_z == 1 else NZ - 1
    inner = rolled(value, step_y * NZ + step_z, 1)
    wrap = rolled(value, step_y * NZ + step_z - step_z * NZ, 1)
    return jnp.where(place == edge, wrap, inner)


def differences(value, place):
    return (
        (rolled(value, -1, 0), rolled(value, 1, 0)),
        (rolled(value, -NZ, 1), rolled(value, NZ, 1)),
        (moved_yz(value, 0, -1, place), moved_yz(value, 0, 1, place)),
    )


def bulk(p, around):
    total = around[0][0] + around[0][1] + around[1][0] + around[1][1] + around[2][0] + around[2][1]
    return 0.5 * (p * p * p - p) - 0.5 * (total - 6.0 * p)


def bent(chem, around):
    total = around[0][0] + around[0][1] + around[1][0] + around[1][1] + around[2][0] + around[2][1]
    return total - 6.0 * chem


def relaxed(here, weight, along, drift):
    square = drift[0] * drift[0] + drift[1] * drift[1] + drift[2] * drift[2]
    return (1.0 - relax_rate) * here + weight * (
        1.0 - 1.5 * square + 3.0 * along + 4.5 * along * along
    )


def strip_post(kind, here, density, drift, place):
    sign = 1.0 - 2.0 * kind
    row = lax.broadcasted_iota(jnp.int32, here.shape, 0)
    full = [jnp.broadcast_to(d, here.shape) for d in drift]
    along = sign * full[0]
    along = along + jnp.where(row == 3, full[1], jnp.where(row == 4, -full[1], 0.0))
    along = along + jnp.where(row == 1, sign * full[2], jnp.where(row == 2, -sign * full[2], 0.0))
    weight = jnp.where(row == 0, 2.0, 1.0) * (relax_rate / 36.0) * density
    post = relaxed(here, weight, along, full)
    first, second = (1, -1) if kind == 0 else (-1, 1)
    return jnp.where(
        row == 1, moved_yz(post, 0, first, place), jnp.where(row == 2, moved_yz(post, 0, second, place), post)
    )


def strip_moved(strip):
    row = lax.broadcasted_iota(jnp.int32, strip.shape, 0)
    return jnp.where(row == 3, rolled(strip, NZ, 1), jnp.where(row == 4, rolled(strip, -NZ, 1), strip))


def packed_post(k, here, density, drift, lane1):
    def spread(value):
        out = rolled(value, NZ if k == 0 else 104, 1)
        first = out
        for i in range(1, 5):
            if k == 0:
                out = jnp.where(lane1 >= i * NZ, rolled(first, i * NZ, 1), out)
            else:
                out = jnp.where(lane1 < 128 - i * NZ, rolled(first, -i * NZ, 1), out)
        return out

    slots = plus_y if k == 0 else minus_y
    group = lane1 // NZ if k == 0 else (127 - lane1) // NZ
    density, drift = spread(density), [spread(d) for d in drift]

    def chosen(axis, value):
        out = jnp.zeros_like(value)
        for i, slot in enumerate(slots):
            if lattice_vel[slot][axis] != 0:
                out = jnp.where(group == i, lattice_vel[slot][axis] * value, out)
        return out

    along = chosen(0, drift[0]) + chosen(1, drift[1]) + chosen(2, drift[2])
    weight = jnp.where(group == 0, 2.0, 1.0) * (relax_rate / 36.0) * density
    post = relaxed(here, weight, along, drift)
    place = lax.rem(lane1, NZ) if k == 0 else lax.rem(lane1 + 16, NZ)
    out = post
    for i, slot in enumerate(slots):
        step_x, _, step_z = lattice_vel[slot]
        if step_x != 0 or step_z != 0:
            out = jnp.where(group == i, moved_yz(rolled(post, step_x, 0), 0, step_z, place), out)
    return out


def lanes_of_y(k):
    groups = [NZ * i if k == 0 else 104 - NZ * i for i in range(5)]
    return groups, (120 if k == 0 else 0), ((104, 80) if k == 0 else (0, 24))


def with_phase(k, packed, phase):
    groups, spare, (first, second) = lanes_of_y(k)
    lane = lax.broadcasted_iota(jnp.int32, (8, 128), 1)
    upper = lax.broadcasted_iota(jnp.int32, (8, 128), 0) >= 4
    in_spare = (lane >= spare) & (lane < spare + 8)
    top, low = phase[0:8], phase[8:16]
    top_down, low_down = rolled(top, 4, 0), rolled(low, 4, 0)
    head, tail = packed[0:8], packed[8:16]
    pieces = ((top_down, first), (top, first), (low_down, first), (top_down, second), (top, second))
    for start, (piece, at) in zip(groups, pieces):
        here = upper & (lane >= start) & (lane < start + NZ)
        tail = jnp.where(here, rolled(piece, start - at, 1), tail)
    parts = [
        rolled(low, spare - second, 1),
        rolled(low_down, spare - second - 8, 1),
        rolled(low, spare - second - 16, 1),
    ]
    head = jnp.where(in_spare, jnp.where(upper, parts[1], parts[0]), head)
    tail = jnp.where(in_spare & jnp.logical_not(upper), parts[2], tail)
    return jnp.concatenate([head, tail], axis=0)


def phase_part(k, message):
    groups, spare, (first, second) = lanes_of_y(k)
    lane = lax.broadcasted_iota(jnp.int32, (8, 128), 1)
    upper = lax.broadcasted_iota(jnp.int32, (8, 128), 0) >= 4
    in_first = (lane >= first) & (lane < first + NZ)
    head, tail = message[0:8], message[8:16]
    head_up, tail_up = rolled(head, 4, 0), rolled(tail, 4, 0)

    def picked(near, far):
        return jnp.where(in_first, rolled(near[0], first - near[1], 1), rolled(far[0], second - far[1], 1))

    top = jnp.where(
        upper,
        picked((tail, groups[1]), (tail, groups[4])),
        picked((tail_up, groups[0]), (tail_up, groups[3])),
    )
    far = jnp.where(
        lane < second + 8,
        rolled(head, second - spare, 1),
        jnp.where(
            lane < second + 16,
            rolled(head_up, second + 8 - spare, 1),
            rolled(tail, second + 16 - spare, 1),
        ),
    )
    low = jnp.where(in_first, rolled(tail_up, first - groups[2], 1), far)
    return jnp.concatenate([top, low], axis=0)


def kernel(
    shifts, f_in, p_in, f_out, p_out,
    f, ext, got, got_corner, to_x, to_y, to_corner, ring,
    e_p, e_r, e_u, ring_b, ring_a, wide, out_x, out_y, out_corner, out_a,
    send_sem, near_sem, plane_sem, corner_sem, corner_send,
):
    count_x, count_y = lax.axis_size("gx"), lax.axis_size("gy")
    gx, gy = lax.axis_index("gx"), lax.axis_index("gy")
    above, below = lax.rem(gx + 1, count_x), lax.rem(gx + count_x - 1, count_x)
    front, back = lax.rem(gy + 1, count_y), lax.rem(gy + count_y - 1, count_y)
    planes = count_x // SPAN
    left_plane = lax.rem(gx, SPAN) == 0
    right_plane = lax.rem(gx, SPAN) == SPAN - 1
    left_slot = lax.rem(gx // SPAN + planes - 1, planes)
    right_slot = gx // SPAN
    any_plane = left_plane | right_plane
    blocks = 3 * count_y
    sides = ((0, left_plane, left_slot), (1, right_plane, right_slot))

    def signal(x, y):
        pl.semaphore_signal(barrier, inc=1, device_id=(x, y), device_id_type=MESH)

    barrier = pltpu.get_barrier_semaphore()
    any_plane = left_plane | right_plane
    def far_first():
        half = count_y // 2
        order = [(half // 2, 1), (half // 2, 0)]
        for dx in range(half // 2 - 1, -1, -1):
            order += [(d, z) for z in (1, 0) for d in sorted({dx, (half - dx) % half})]
        return [2 * lax.rem(gy // 2 + dx, half) + lax.rem(gy + dz, 2) for dx, dz in dict.fromkeys(order)]

    for is_plane, side in ((left_plane, below), (right_plane, above)):
        @pl.when(is_plane)
        def _(side=side):
            for y in far_first():
                signal(side, y)
            for j in range(2, count_y - 1):
                signal(gx, lax.rem(gy + j, count_y))

    signal(gx, front)
    signal(gx, back)
    for is_plane, side in ((left_plane, below), (right_plane, above)):
        @pl.when(jnp.logical_not(is_plane))
        def _(side=side):
            signal(side, front)
            signal(side, back)
            signal(side, gy)

    lane = lax.broadcasted_iota(jnp.int32, (16, WIDE), 1)
    place = lax.rem(lane, NZ)
    lane4 = lax.broadcasted_iota(jnp.int32, (16, 512), 1)
    place4 = lax.rem(jnp.where(lane4 < 448, lane4, lane4 - 464), NZ)
    lane1 = lax.broadcasted_iota(jnp.int32, (16, 128), 1)
    lane5 = lax.broadcasted_iota(jnp.int32, (24, 640), 1)
    place5 = lax.rem(jnp.where(lane5 < 512, lane5, lane5 + 8), NZ)
    place6 = lax.rem(lax.broadcasted_iota(jnp.int32, (8, 768), 1), NZ)

    def pack_phase(r):
        for b in range(3):
            cut = slice(b * 128, b * 128 + 128)
            to_x[r, 0, 8 * b + 5:8 * b + 7, :] = ext[10:12, cut]
            to_x[r, 1, 8 * b + 5:8 * b + 7, :] = ext[0:2, cut]

    def remote(src, dst, r, sem, x, y, sent=send_sem):
        pltpu.make_async_remote_copy(
            src_ref=src, dst_ref=dst, send_sem=sent.at[r], recv_sem=sem.at[r],
            device_id=(x, y), device_id_type=MESH,
        ).start()

    def rows_of(wide_round):
        y_rows, strip, corners = (48, 48, 16) if wide_round else (16, 24, 0)
        return y_rows, strip, 2 * y_rows, strip + corners

    def side_start(kind, wide_round, on_left_plane):
        _, _, first, size = rows_of(wide_round)
        return first if kind == 0 else jnp.where(on_left_plane, first, first + size)

    def land(buffer, start, size):
        return buffer.at[pl.ds(start, size)]

    def landing(r):
        return wide if r is None else got.at[r]

    def send_x(r, strips, corners):
        buffer = landing(r)
        _, strip, first, size = rows_of(r is None)
        n = 0 if r is None else r
        for kind, is_plane, side in ((0, right_plane, above), (1, left_plane, below)):
            @pl.when(is_plane)
            def _(kind=kind, side=side):
                place = pl.multiple_of(first + size + gy * strip, 8)
                for y in far_first():
                    remote(strips(kind), land(buffer, place, strip), n, plane_sem, side, y)

            @pl.when(jnp.logical_not(is_plane))
            def _(kind=kind, side=side):
                place = side_start(kind, r is None, lax.rem(side, SPAN) == 0)
                for k, y in ((0, front), (1, back)):
                    if r is None:
                        spot = land(buffer, pl.multiple_of(place + strip + 8 * k, 8), 8)
                        remote(corners(2 * kind + k), spot, n, near_sem, side, y)
                    else:
                        spot = got_corner.at[r, 2 * kind + k]
                        remote(corners(2 * kind + k), spot, n, corner_sem, side, y, corner_send)
                remote(strips(kind), land(buffer, pl.multiple_of(place, 8), strip), n, near_sem, side, gy)

    def send_y(r, messages):
        size = rows_of(r is None)[0]
        n = 0 if r is None else r
        for k, y in ((0, front), (1, back)):
            remote(messages(k), land(landing(r), k * size, size), n, near_sem, gx, y)

    def wait_for(ref, sem):
        pltpu.make_async_copy(ref, ref, sem).wait()

    def run_of(r):
        _, strip, first, size = rows_of(r is None)
        return first + size, first + 2 * size, count_y * strip + (8 * (count_y - 1) if r is None else 0)

    def wait_corners(r, sem):
        for is_kind, start, size in (
            (left_plane, 2, 2), (right_plane, 0, 2), (jnp.logical_not(any_plane), 0, 4)
        ):
            @pl.when(is_kind)
            def _(start=start, size=size):
                wait_for(got_corner.at[r, pl.ds(start, size)], sem.at[r])

    def wait_sent(r):
        buffer, n = landing(r), 0 if r is None else r
        short, near, crossing = run_of(r)

        @pl.when(any_plane)
        def _():
            wait_for(land(buffer, 0, short + crossing), send_sem.at[n])

        @pl.when(jnp.logical_not(any_plane))
        def _():
            wait_for(land(buffer, 0, near), send_sem.at[n])

        if r is not None:
            wait_corners(r, corner_send)

    def wait_near(r):
        buffer, n = landing(r), 0 if r is None else r
        short, near, _ = run_of(r)

        @pl.when(any_plane)
        def _():
            wait_for(land(buffer, 0, short), near_sem.at[n])

        @pl.when(jnp.logical_not(any_plane))
        def _():
            wait_for(land(buffer, 0, near), near_sem.at[n])

        if r is not None:
            wait_corners(r, corner_sem)

    def wait_plane(r):
        short, _, crossing = run_of(r)
        wait_for(land(landing(r), short, crossing), plane_sem.at[0 if r is None else r])

    def window_of(held, turn):
        start = ((gy * 16 - turn - 4) & (16 * count_y - 1)) * NZ
        first, offset = start >> 7, start & 127
        window = jnp.concatenate([held[first + i] for i in range(6)], axis=1)
        return pltpu.roll(window, 768 - 4 * NZ - offset, 1)

    def view_b(kind, shift):
        return window_of(ring_b, shift if kind == 0 else -shift - 1)

    def close_ring(r):
        first = run_of(r)[0]
        for b in range(blocks + 4):
            row = first + 8 * (b % blocks)
            ring[b] = got[r, row:row + 8]

    def view(kind, shift):
        low = shift if kind == 0 else -shift - 1
        near, far = (0.75, 0.25) if kind == 0 else (0.25, 0.75)
        start = ((gy * 16 - low - 3) & (16 * count_y - 1)) * NZ
        first, offset = start >> 7, start & 127
        window = jnp.concatenate([ring[first + i] for i in range(5)], axis=1)
        window = pltpu.roll(window, 640 - 3 * NZ - offset, 1)
        return near * window + far * rolled(window, NZ, 1)

    def patch_y(k, packed):
        cut = slice(0, 128) if k == 0 else slice(256, 384)
        keep = lane1 < NZ if k == 0 else lane1 >= 128 - NZ
        for i, slot in enumerate(plus_y if k == 0 else minus_y):
            part = rolled(packed, -i * NZ if k == 0 else i * NZ, 1)
            f[slot, :, cut] = jnp.where(keep, part, f[slot, :, cut])

    def patch_x(kind, strip):
        edge = 0 if kind == 0 else ROWS - 1
        for i, slot in enumerate(up_slots if kind == 0 else down_slots):
            f[slot, edge:edge + 1, :] = strip[i:i + 1, :WIDE]

    def receive(r, step):
        wait_near(r)
        for k in (0, 1):
            patch_y(k, got[r, 16 * k:16 * k + 16])
        ext[0:12, 384:512] = jnp.where(
            lane1 < 64, phase_part(1, got[r, 16:32]), phase_part(0, got[r, 0:16])
        )[:12]
        for kind, is_plane, _ in sides:
            @pl.when(jnp.logical_not(is_plane))
            def _(kind=kind):
                outer = 14 - 2 * kind
                near_row = 15 - 3 * kind
                e = (0, ROWS - 1)[kind]
                place = pl.multiple_of(side_start(kind, False, left_plane), 8)
                strip = jnp.concatenate([got[r, pl.ds(place + 8 * b, 8)] for b in range(3)], axis=1)
                first, last = got_corner[r, 2 * kind], got_corner[r, 2 * kind + 1]
                plus = rolled(strip, NZ, 1)
                minus = rolled(strip, -NZ, 1)
                slots = up_slots if kind == 0 else down_slots
                for i in range(3):
                    f[slots[i], e:e + 1, :] = strip[i:i + 1]
                head = jnp.where(lane1[:1] < NZ, first, plus[3:4, 0:128])
                tail = jnp.where(lane1[:1] >= 128 - NZ, last, minus[4:5, 256:384])
                f[slots[3], e:e + 1, 0:128] = head
                f[slots[3], e:e + 1, 128:384] = plus[3:4, 128:384]
                f[slots[4], e:e + 1, 0:256] = minus[4:5, 0:256]
                f[slots[4], e:e + 1, 256:384] = tail
                ext[outer:outer + 2, 0:WIDE] = strip[5:7]
                ext[near_row:near_row + 1, WIDE:512] = jnp.where(lane1[:1] < 64, last, first)

        for kind, is_plane, place_of in sides:
            @pl.when(is_plane)
            def _(kind=kind, place_of=place_of):
                outer = 14 - 2 * kind
                wait_plane(r)
                close_ring(r)
                patch_x(kind, strip_moved(view(kind, shifts[step, place_of])))
                phase = view(kind, shifts[jnp.minimum(step + 1, STEPS - 1), place_of])
                ext[outer:outer + 2, 0:WIDE] = phase[5:7, 0:WIDE]
                ext[outer:outer + 2, WIDE:512] = jnp.where(
                    lane1[:2] < 64, phase[5:7, 384:512], phase[5:7, 512:640]
                )

    def momentum():
        density = f[0]
        for slot in range(1, 19):
            density = density + f[slot]
        totals = []
        for axis in range(3):
            total = None
            for slot in range(1, 19, 2):
                sign = lattice_vel[slot][axis]
                if sign != 0:
                    pair = f[slot] - f[slot + 1]
                    if total is None:
                        total = pair
                    else:
                        total = total + pair if sign == 1 else total - pair
            totals.append(total)
        return density, totals

    def advance(r):
        p = ext[...]
        around = differences(p, place4)
        chem = bulk(p, around)
        slope = [0.5 * (a - b)[:, :WIDE] for a, b in around]
        around = [(a[:, :WIDE], b[:, :WIDE]) for a, b in differences(chem, place4)]
        bend = bent(chem[:, :WIDE], around)
        own = p[:, :WIDE]
        density, totals = momentum()
        inverse = 1.0 / density
        scaled = (-0.5 * coupling / relax_rate) * own
        next_phase = own + mobility * bend
        drift = []
        for axis in range(3):
            next_phase = next_phase - totals[axis] * inverse * slope[axis]
            drift.append((totals[axis] + scaled * (around[axis][0] - around[axis][1])) * inverse)
        ext[0:12, 0:WIDE] = next_phase[:12]
        pack_phase(r)
        collide(density, drift, r)

    def collide(density, drift, r):
        base = 1.0 - 1.5 * (drift[0] * drift[0] + drift[1] * drift[1] + drift[2] * drift[2])
        weight = relax_rate / 36.0 * density
        keep = 1.0 - relax_rate
        packs = {}

        def put(slot, post):
            step_x, step_y, step_z = lattice_vel[slot]
            value = rolled(post, step_x, 0)
            moved = moved_yz(value, step_y, step_z, place)
            f[slot] = moved
            if r is None:
                return
            if step_x != 0:
                kind = 0 if step_x == 1 else 1
                i = (up_slots, down_slots)[kind].index(slot)
                line = 12 if step_x == 1 else 15
                shown = value if step_y != 0 else moved
                for b in range(3):
                    to_x[r, kind, 8 * b + i:8 * b + i + 1, :] = shown[line:line + 1, b * 128:b * 128 + 128]
                if step_y != 0:
                    k = 2 * kind + (0 if step_y == 1 else 1)
                    cut = slice(0, 128) if step_y == 1 else slice(256, 384)
                    edge = 11 if step_x == 1 else 0
                    own = ext[edge:edge + 1, slice(256, 384) if step_y == 1 else slice(0, 128)]
                    post_row = moved[line:line + 1, cut]
                    low = lane1[:1] < 64
                    to_corner[r, k] = (
                        jnp.where(low, post_row, own) if step_y == 1 else jnp.where(low, own, post_row)
                    )
            if step_y == 1:
                i = plus_y.index(slot)
                part = rolled(moved[:, 0:128], i * NZ, 1)
                mine = (lane1 >= i * NZ) & (lane1 < i * NZ + NZ)
                packs[0] = jnp.where(mine, part, packs[0]) if 0 in packs else part
            if step_y == -1:
                i = minus_y.index(slot)
                part = rolled(moved[:, 256:384], -i * NZ, 1)
                mine = (lane1 < 128 - i * NZ) & (lane1 >= 128 - NZ - i * NZ)
                packs[1] = jnp.where(mine, part, packs[1]) if 1 in packs else part

        def put_pair(slot):
            along = None
            for axis in range(3):
                sign = lattice_vel[slot][axis]
                if sign != 0:
                    if along is None:
                        along = drift[axis]
                    else:
                        along = along + drift[axis] if sign == 1 else along - drift[axis]
            scale = 2.0 * weight if slot < 7 else weight
            even = scale * (base + 4.5 * along * along)
            odd = scale * (3.0 * along)
            here, there = f[slot], f[slot + 1]
            put(slot, keep * here + (even + odd))
            put(slot + 1, keep * there + (even - odd))

        for slot in (1, 7, 9, 11, 13):
            put_pair(slot)
        if r is not None:
            send_x(r, lambda kind: to_x.at[r, kind], lambda k: to_corner.at[r, k])
        for slot in (3, 15, 17):
            put_pair(slot)
        if r is not None:
            for k in (0, 1):
                to_y[r, k] = with_phase(k, packs[k], ext[0:16, 256:384] if k == 0 else ext[0:16, 0:128])
            send_y(r, lambda k: to_y.at[r, k])
        put_pair(5)
        put(0, keep * f[0] + 12.0 * weight * base)

    for slot in range(19):
        f[slot, 0:12, :] = f_in[slot]
        f[slot, 12:16, :] = jnp.ones((4, WIDE), jnp.float32)
    ext[...] = jnp.zeros_like(ext)
    e_p[...] = jnp.zeros_like(e_p)
    e_r[...] = jnp.ones_like(e_r)
    e_u[...] = jnp.zeros_like(e_u)
    e_p[0:12, 0:WIDE] = p_in[...]
    density, totals = momentum()
    e_r[0:12, 0:WIDE] = density[:12]
    for axis in range(3):
        e_u[axis, 0:12, 0:WIDE] = (totals[axis] / density)[:12]

    for kind in (0, 1):
        edge, second, low = ((11, 10, 8), (0, 1, 0))[kind]
        for b in range(3):
            cut = slice(b * 128, b * 128 + 128)
            out_x[kind, 16 * b:16 * b + 4, :] = e_p[low:low + 4, cut]
            out_x[kind, 16 * b + 4:16 * b + 5, :] = e_r[edge:edge + 1, cut]
            for axis in range(3):
                out_x[kind, 16 * b + 5 + axis:16 * b + 6 + axis, :] = e_u[axis, edge:edge + 1, cut]
                out_x[kind, 16 * b + 13 + axis:16 * b + 14 + axis, :] = e_u[axis, second:second + 1, cut]
            for i, slot in enumerate(up_slots if kind == 0 else down_slots):
                out_x[kind, 16 * b + 8 + i:16 * b + 9 + i, :] = f[slot, edge:edge + 1, cut]
        third = (9, 0)[kind]
        for k in (2 * kind, 2 * kind + 1):
            cut = slice(256, 384) if k % 2 == 0 else slice(0, 128)
            out_corner[k, 0:3, :] = e_p[third:third + 3, cut]
            out_corner[k, 3:4, :] = e_r[edge:edge + 1, cut]
            for axis in range(3):
                out_corner[k, 4 + axis:5 + axis, :] = e_u[axis, edge:edge + 1, cut]
            slot = (up_slots if kind == 0 else down_slots)[3 + k % 2]
            out_corner[k, 7:8, :] = f[slot, edge:edge + 1, cut]
    for k in (0, 1):
        cut = slice(256, 384) if k == 0 else slice(0, 128)
        low = lane1[:12] < 64
        if k == 0:
            pair = lambda a, b: jnp.where(low, pltpu.roll(b, 64, 1), a)
        else:
            pair = lambda a, b: jnp.where(low, a, pltpu.roll(b, 64, 1))
        packed = None
        for i, slot in enumerate(plus_y if k == 0 else minus_y):
            block = f[slot, :, cut]
            part = rolled(block, NZ + i * NZ if k == 0 else -NZ - i * NZ, 1)
            if i == 0:
                packed = part
            else:
                packed = jnp.where(lane1 >= i * NZ if k == 0 else lane1 < 128 - i * NZ, part, packed)
        out_y[k, 0:12, :] = packed[:12]
        out_y[k, 12:24, :] = e_p[0:12, cut]
        out_y[k, 24:36, :] = pair(e_r[0:12, cut], e_u[0, 0:12, cut])
        out_y[k, 36:48, :] = pair(e_u[1, 0:12, cut], e_u[2, 0:12, cut])

    @pl.when(left_plane)
    def _():
        for b in range(3):
            out_a[2 * b:2 * b + 2, :] = e_p[0:2, b * 128:b * 128 + 128]

    @pl.when(right_plane)
    def _():
        for b in range(3):
            out_a[2 * b:2 * b + 2, :] = e_p[10:12, b * 128:b * 128 + 128]

    pl.semaphore_wait(barrier, jnp.where(any_plane, 5 + count_y + max(count_y - 3, 0), 8))

    send_x(None, lambda kind: out_x.at[kind], lambda k: out_corner.at[k])

    @pl.when(any_plane)
    def _():
        start = run_of(None)[0] + count_y * 48
        for j in range(1, count_y):
            remote(out_a, land(wide, start + 8 * (j - 1), 8), 0, plane_sem, gx, lax.rem(gy + j, count_y))

    send_y(None, lambda k: out_y.at[k])

    wait_near(None)
    for k in (0, 1):
        at = 48 * k
        cut = slice(512, 640) if k == 0 else slice(384, 512)
        e_p[0:12, cut] = wide[at + 12:at + 24]
        e_r[0:12, cut] = wide[at + 24:at + 36]
        e_u[0, 0:12, cut] = pltpu.roll(wide[at + 24:at + 36], 64, 1)
        e_u[1, 0:12, cut] = wide[at + 36:at + 48]
        e_u[2, 0:12, cut] = pltpu.roll(wide[at + 36:at + 48], 64, 1)
    for kind, is_plane, place_of in sides:
        low = (20, 12)[kind]
        edge, second, third = ((23, 22, 21), (12, 13, 12))[kind]

        @pl.when(jnp.logical_not(is_plane))
        def _(kind=kind, low=low, edge=edge, second=second, third=third):
            place = pl.multiple_of(side_start(kind, True, left_plane), 8)
            for k in (0, 1):
                corner = wide[pl.ds(place + 48 + 8 * k, 8)]
                cut = slice(512, 640) if k == 0 else slice(384, 512)
                e_p[third:third + 3, cut] = corner[0:3]
                e_r[edge:edge + 1, cut] = corner[3:4]
                for axis in range(3):
                    e_u[axis, edge:edge + 1, cut] = corner[4 + axis:5 + axis]
            for b in range(3):
                cut = slice(b * 128, b * 128 + 128)
                strip = wide[pl.ds(place + 16 * b, 16)]
                e_p[low:low + 4, cut] = strip[0:4]
                e_r[edge:edge + 1, cut] = strip[4:5]
                for axis in range(3):
                    e_u[axis, edge:edge + 1, cut] = strip[5 + axis:6 + axis]
                    e_u[axis, second:second + 1, cut] = strip[13 + axis:14 + axis]

    for kind, is_plane, place_of in sides:
        @pl.when(is_plane)
        def _(kind=kind, place_of=place_of):
            wait_plane(None)
            start = run_of(None)[0]
            for b in range(blocks + 5):
                row = start + 16 * (b % blocks)
                ring_b[b] = wide[row:row + 16]
            start = start + 16 * blocks
            a_row = (4, 6)[kind]
            for j in range(count_y):
                source = lax.rem(gy + count_y - j, count_y)
                for b in range(3):
                    row = start + 8 * (j - 1) + 2 * b
                    piece = out_a[2 * b:2 * b + 2, :] if j == 0 else wide[row:row + 2]
                    ring_a[source * 3 + b, a_row:a_row + 2, :] = piece
            for b in range(5):
                ring_a[blocks + b] = ring_a[b]
            shift = shifts[0, place_of]
            near = view_b(kind, shift)[0:8]
            phase = (near * 0.75 + rolled(near, NZ, 1) * 0.25) if kind == 0 else (
                near * 0.25 + rolled(near, NZ, 1) * 0.75)
            row, at = ((22, 2), (12, 0))[kind]
            e_p[row:row + 2, 0:512] = phase[at:at + 2, 0:512]
            e_p[row:row + 2, 512:640] = phase[at:at + 2, 640:768]

    p = e_p[...]
    around = differences(p, place5)
    chem = bulk(p, around)
    slope = [0.5 * (a - b) for a, b in around]
    around = differences(chem, place5)
    next_phase = p + mobility * bent(chem, around)
    scaled = (-0.5 * coupling / relax_rate) * p / e_r[...]
    drift = []
    for axis in range(3):
        flow = e_u[axis]
        next_phase = next_phase - flow * slope[axis]
        drift.append(flow + scaled * (around[axis][0] - around[axis][1]))
    for top, at, size in ((0, 0, 12), (12, 12, 2), (14, 22, 2)):
        ext[top:top + size, 0:WIDE] = next_phase[at:at + size, 0:WIDE]
        ext[top:top + size, WIDE:512] = jnp.where(
            lane1[:size] < 64, next_phase[at:at + size, 384:512], next_phase[at:at + size, 512:640]
        )
    collide(e_r[0:16, 0:WIDE], [d[0:16, 0:WIDE] for d in drift], None)
    for k in (0, 1):
        cut = slice(512, 640) if k == 0 else slice(384, 512)
        patch_y(k, packed_post(k, wide[48 * k:48 * k + 16], e_r[0:16, cut], [d[0:16, cut] for d in drift], lane1))
    for kind, is_plane, place_of in sides:
        @pl.when(is_plane)
        def _(kind=kind, place_of=place_of):
            first = shifts[0, place_of]
            row = lax.broadcasted_iota(jnp.int32, (8, 768), 0)
            edge, at, outer = ((3, 2, 14), (0, 0, 12))[kind]
            weights_of = ((0.75, 0.25), (0.25, 0.75))[kind]
            for step in (0, 1):
                shift = shifts[step, place_of]
                both = view_b(kind, shift)
                turn = shift - first if kind == 0 else first - shift - 1
                own = window_of(ring_a, turn)
                own = 0.75 * own + 0.25 * rolled(own, -NZ if kind == 0 else NZ, 1)
                far_p = jnp.where(row < 4, both[0:8], own)
                around = differences(far_p, place6)
                chem = bulk(far_p, around)
                slope = [0.5 * (a - b) for a, b in around]
                around = differences(chem, place6)
                if step == 0:
                    density = both[4:5]
                    scaled = (-0.5 * coupling / relax_rate) * far_p[edge:edge + 1] / density
                    drift = [
                        both[5 + axis:6 + axis]
                        + scaled * (around[axis][0] - around[axis][1])[edge:edge + 1]
                        for axis in range(3)
                    ]
                    strip = strip_post(kind, both[8:16], density, drift, place6)
                    strip = weights_of[0] * strip + weights_of[1] * rolled(strip, NZ, 1)
                    patch_x(kind, strip_moved(strip))
                else:
                    after = far_p + mobility * bent(chem, around)
                    for axis in range(3):
                        flow = jnp.where(row == edge, both[5 + axis:6 + axis], both[13 + axis:14 + axis])
                        after = after - flow * slope[axis]
                    after = weights_of[0] * after + weights_of[1] * rolled(after, NZ, 1)
                    ext[outer:outer + 2, 0:WIDE] = after[at:at + 2, 0:WIDE]
                    ext[outer:outer + 2, WIDE:512] = jnp.where(
                        lane1[:2] < 64, after[at:at + 2, 384:512], after[at:at + 2, 640:768]
                    )

        @pl.when(jnp.logical_not(is_plane))
        def _(kind=kind):
            edge = (23, 12)[kind]
            place = pl.multiple_of(side_start(kind, True, left_plane), 8)
            strip = jnp.concatenate(
                [wide[pl.ds(place + 16 * b + 8, 8)] for b in range(3)]
                + [jnp.broadcast_to(wide[pl.ds(place + 48 + 8 * i, 8)][7:8], (8, 128)) for i in (1, 0)],
                axis=1,
            )
            strip = strip_post(
                kind, strip, e_r[edge:edge + 1, :], [d[edge:edge + 1] for d in drift], place5[:8]
            )
            patch_x(kind, strip_moved(strip))

    def body(step, carry):
        advance(step)

        @pl.when(step == 1)
        def _():
            wait_sent(None)

        @pl.when(step > 1)
        def _():
            wait_sent(step - 1)

        receive(step, step)
        return carry

    lax.fori_loop(1, STEPS, body, 0)
    for slot in range(19):
        f_out[slot] = f[slot, 0:12, :]
    p_out[...] = ext[0:12, 0:WIDE]
    wait_sent(STEPS - 1)


def on_device(populations, phase_field, plane_shifts):
    blocks = 3 * lax.axis_size("gy")
    rounds = STEPS
    vmem = pl.BlockSpec(memory_space=pltpu.VMEM)
    return pl.pallas_call(
        kernel,
        out_shape=(
            jax.ShapeDtypeStruct(populations.shape, jnp.float32),
            jax.ShapeDtypeStruct(phase_field.shape, jnp.float32),
        ),
        in_specs=[pl.BlockSpec(memory_space=pltpu.SMEM), vmem, vmem],
        out_specs=(vmem, vmem),
        scratch_shapes=[
            pltpu.VMEM((19, 16, WIDE), jnp.float32),
            pltpu.VMEM((16, 512), jnp.float32),
            pltpu.VMEM((rounds, 56 + 8 * blocks, 128), jnp.float32),
            pltpu.VMEM((rounds, 4, 1, 128), jnp.float32),
            pltpu.VMEM((rounds, 2, 24, 128), jnp.float32),
            pltpu.VMEM((rounds, 2, 16, 128), jnp.float32),
            pltpu.VMEM((rounds, 4, 1, 128), jnp.float32),
            pltpu.VMEM((blocks + 4, 8, 128), jnp.float32),
            pltpu.VMEM((24, 640), jnp.float32),
            pltpu.VMEM((24, 640), jnp.float32),
            pltpu.VMEM((3, 24, 640), jnp.float32),
            pltpu.VMEM((blocks + 5, 16, 128), jnp.float32),
            pltpu.VMEM((blocks + 5, 8, 128), jnp.float32),
            pltpu.VMEM((160 + 16 * blocks + 8 * (lax.axis_size("gy") - 1), 128), jnp.float32),
            pltpu.VMEM((2, 48, 128), jnp.float32),
            pltpu.VMEM((2, 48, 128), jnp.float32),
            pltpu.VMEM((4, 8, 128), jnp.float32),
            pltpu.VMEM((8, 128), jnp.float32),
            pltpu.SemaphoreType.DMA((rounds,)),
            pltpu.SemaphoreType.DMA((rounds,)),
            pltpu.SemaphoreType.DMA((rounds,)),
            pltpu.SemaphoreType.DMA((rounds,)),
            pltpu.SemaphoreType.DMA((rounds,)),
        ],
        compiler_params=pltpu.CompilerParams(
            collective_id=0, has_side_effects=True, vmem_limit_bytes=32 * 1024 * 1024
        ),
    )(plane_shifts, populations, phase_field)


def solution(mesh):
    return jax.shard_map(
        on_device,
        mesh=mesh,
        in_specs=(P(None, "gx", "gy"), P("gx", "gy"), P()),
        out_specs=(P(None, "gx", "gy"), P("gx", "gy")),
        check_vma=False,
    )
```

```python
import functools

import jax
import jax.numpy as jnp
from jax import lax
from jax.experimental import pallas as pl
from jax.experimental.pallas import tpu as pltpu
from jax.sharding import PartitionSpec as P

STEPS = 4
NZ = 24
ROWS = 12
WIDE = 384
SPAN = 4
MESH = pl.DeviceIdType.MESH

lattice_vel = (
    (0, 0, 0),
    (1, 0, 0),
    (-1, 0, 0),
    (0, 1, 0),
    (0, -1, 0),
    (0, 0, 1),
    (0, 0, -1),
    (1, 1, 0),
    (-1, -1, 0),
    (1, -1, 0),
    (-1, 1, 0),
    (1, 0, 1),
    (-1, 0, -1),
    (1, 0, -1),
    (-1, 0, 1),
    (0, 1, 1),
    (0, -1, -1),
    (0, 1, -1),
    (0, -1, 1),
)
relax_rate = 0.8
coupling = 0.01
mobility = 0.02

up_slots = (1, 11, 13, 7, 9)
down_slots = (2, 12, 14, 10, 8)
plus_y = (3, 7, 10, 15, 17)
minus_y = (4, 8, 9, 16, 18)


zero_x = (0, 3, 4, 5, 6, 15, 16, 17, 18)
near_x = (up_slots + zero_x, down_slots + zero_x)
zero_y = tuple(slot for slot in range(19) if lattice_vel[slot][1] == 0)
near_y = (plus_y + zero_y, minus_y + zero_y)
y_units = tuple(
    tuple((slot, 1) for slot in near_y[k]) + tuple((slot, 2) for slot in (plus_y, minus_y)[k])
    + ((None, 1), (None, 2), (None, 3))
    for k in (0, 1)
)


def corner_units(kind, k):
    step = (1 - 2 * kind, 1 - 2 * k)
    units = []
    for deep in ((1, 1), (2, 1), (1, 2), (2, 2)):
        for slot in range(19):
            if all(
                lattice_vel[slot][axis] == step[axis] or (deep[axis] == 1 and lattice_vel[slot][axis] == 0)
                for axis in (0, 1)
            ):
                units.append((slot,) + deep)
    return tuple(units) + tuple((None, x, y) for x in (1, 2, 3) for y in range(1, 5 - x))


def lane_of(k, depth):
    return 128 - NZ * depth if k == 0 else NZ * (depth - 1)


def rolled(value, shift, axis):
    size = value.shape[axis]
    shift = shift % size
    return value if shift == 0 else pltpu.roll(value, shift, axis)


def moved_yz(value, step_y, step_z, place):
    if step_z == 0:
        return rolled(value, step_y * NZ, 1)
    edge = 0 if step_z == 1 else NZ - 1
    inner = rolled(value, step_y * NZ + step_z, 1)
    wrap = rolled(value, step_y * NZ + step_z - step_z * NZ, 1)
    return jnp.where(place == edge, wrap, inner)


def differences(value, place):
    return (
        (rolled(value, -1, 0), rolled(value, 1, 0)),
        (rolled(value, -NZ, 1), rolled(value, NZ, 1)),
        (moved_yz(value, 0, -1, place), moved_yz(value, 0, 1, place)),
    )


def bulk(p, around):
    total = around[0][0] + around[0][1] + around[1][0] + around[1][1] + around[2][0] + around[2][1]
    return 0.5 * (p * p * p - p) - 0.5 * (total - 6.0 * p)


def bent(chem, around):
    total = around[0][0] + around[0][1] + around[1][0] + around[1][1] + around[2][0] + around[2][1]
    return total - 6.0 * chem


def relaxed(here, weight, along, drift):
    square = drift[0] * drift[0] + drift[1] * drift[1] + drift[2] * drift[2]
    return (1.0 - relax_rate) * here + weight * (
        1.0 - 1.5 * square + 3.0 * along + 4.5 * along * along
    )


def strip_post(kind, here, density, drift, place):
    sign = 1.0 - 2.0 * kind
    row = lax.broadcasted_iota(jnp.int32, here.shape, 0)
    full = [jnp.broadcast_to(d, here.shape) for d in drift]
    along = sign * full[0]
    along = along + jnp.where(row == 3, full[1], jnp.where(row == 4, -full[1], 0.0))
    along = along + jnp.where(row == 1, sign * full[2], jnp.where(row == 2, -sign * full[2], 0.0))
    weight = jnp.where(row == 0, 2.0, 1.0) * (relax_rate / 36.0) * density
    post = relaxed(here, weight, along, full)
    return strip_along_z(kind, post, place)


def strip_along_z(kind, strip, place):
    row = lax.broadcasted_iota(jnp.int32, strip.shape, 0)
    first, second = (1, -1) if kind == 0 else (-1, 1)
    return jnp.where(
        row == 1, moved_yz(strip, 0, first, place), jnp.where(row == 2, moved_yz(strip, 0, second, place), strip)
    )


def strip_moved(strip):
    row = lax.broadcasted_iota(jnp.int32, strip.shape, 0)
    return jnp.where(row == 3, rolled(strip, NZ, 1), jnp.where(row == 4, rolled(strip, -NZ, 1), strip))


def packed_post(k, here, density, drift, lane1):
    def spread(value):
        out = rolled(value, NZ if k == 0 else 104, 1)
        first = out
        for i in range(1, 5):
            if k == 0:
                out = jnp.where(lane1 >= i * NZ, rolled(first, i * NZ, 1), out)
            else:
                out = jnp.where(lane1 < 128 - i * NZ, rolled(first, -i * NZ, 1), out)
        return out

    slots = plus_y if k == 0 else minus_y
    group = lane1 // NZ if k == 0 else (127 - lane1) // NZ
    density, drift = spread(density), [spread(d) for d in drift]

    def chosen(axis, value):
        out = jnp.zeros_like(value)
        for i, slot in enumerate(slots):
            if lattice_vel[slot][axis] != 0:
                out = jnp.where(group == i, lattice_vel[slot][axis] * value, out)
        return out

    along = chosen(0, drift[0]) + chosen(1, drift[1]) + chosen(2, drift[2])
    weight = jnp.where(group == 0, 2.0, 1.0) * (relax_rate / 36.0) * density
    post = relaxed(here, weight, along, drift)
    place = lax.rem(lane1, NZ) if k == 0 else lax.rem(lane1 + 16, NZ)
    out = post
    for i, slot in enumerate(slots):
        step_x, _, step_z = lattice_vel[slot]
        if step_x != 0 or step_z != 0:
            out = jnp.where(group == i, moved_yz(rolled(post, step_x, 0), 0, step_z, place), out)
    return out


def lanes_of_y(k):
    groups = [NZ * i if k == 0 else 104 - NZ * i for i in range(5)]
    return groups, (120 if k == 0 else 0), ((104, 80) if k == 0 else (0, 24))


def with_phase(k, packed, phase):
    groups, spare, (first, second) = lanes_of_y(k)
    lane = lax.broadcasted_iota(jnp.int32, (8, 128), 1)
    upper = lax.broadcasted_iota(jnp.int32, (8, 128), 0) >= 4
    in_spare = (lane >= spare) & (lane < spare + 8)
    top, low = phase[0:8], phase[8:16]
    top_down, low_down = rolled(top, 4, 0), rolled(low, 4, 0)
    head, tail = packed[0:8], packed[8:16]
    pieces = ((top_down, first), (top, first), (low_down, first), (top_down, second), (top, second))
    for start, (piece, at) in zip(groups, pieces):
        here = upper & (lane >= start) & (lane < start + NZ)
        tail = jnp.where(here, rolled(piece, start - at, 1), tail)
    parts = [
        rolled(low, spare - second, 1),
        rolled(low_down, spare - second - 8, 1),
        rolled(low, spare - second - 16, 1),
    ]
    head = jnp.where(in_spare, jnp.where(upper, parts[1], parts[0]), head)
    tail = jnp.where(in_spare & jnp.logical_not(upper), parts[2], tail)
    return jnp.concatenate([head, tail], axis=0)


def phase_part(k, message):
    groups, spare, (first, second) = lanes_of_y(k)
    lane = lax.broadcasted_iota(jnp.int32, (8, 128), 1)
    upper = lax.broadcasted_iota(jnp.int32, (8, 128), 0) >= 4
    in_first = (lane >= first) & (lane < first + NZ)
    head, tail = message[0:8], message[8:16]
    head_up, tail_up = rolled(head, 4, 0), rolled(tail, 4, 0)

    def picked(near, far):
        return jnp.where(in_first, rolled(near[0], first - near[1], 1), rolled(far[0], second - far[1], 1))

    top = jnp.where(
        upper,
        picked((tail, groups[1]), (tail, groups[4])),
        picked((tail_up, groups[0]), (tail_up, groups[3])),
    )
    far = jnp.where(
        lane < second + 8,
        rolled(head, second - spare, 1),
        jnp.where(
            lane < second + 16,
            rolled(head_up, second + 8 - spare, 1),
            rolled(tail, second + 16 - spare, 1),
        ),
    )
    low = jnp.where(in_first, rolled(tail_up, first - groups[2], 1), far)
    return jnp.concatenate([top, low], axis=0)


def kernel(
    shifts, f_in, p_in, f_out, p_out,
    f, ext, got, got_corner, to_x, to_y, to_corner, ring,
    e_p, e_r, e_u, ring_b, ring_a, wide, out_x, out_y, out_corner, out_a,
    fx, chem_x, tile_a, ring_e, ring_o, last, last_x, last_y, last_corner, last_a,
    send_sem, near_sem, plane_sem, corner_sem, corner_send,
):
    count_x, count_y = lax.axis_size("gx"), lax.axis_size("gy")
    gx, gy = lax.axis_index("gx"), lax.axis_index("gy")
    above, below = lax.rem(gx + 1, count_x), lax.rem(gx + count_x - 1, count_x)
    front, back = lax.rem(gy + 1, count_y), lax.rem(gy + count_y - 1, count_y)
    planes = count_x // SPAN
    left_plane = lax.rem(gx, SPAN) == 0
    right_plane = lax.rem(gx, SPAN) == SPAN - 1
    left_slot = lax.rem(gx // SPAN + planes - 1, planes)
    right_slot = gx // SPAN
    any_plane = left_plane | right_plane
    blocks = 3 * count_y
    sides = ((0, left_plane, left_slot), (1, right_plane, right_slot))

    def signal(x, y):
        pl.semaphore_signal(barrier, inc=1, device_id=(x, y), device_id_type=MESH)

    barrier = pltpu.get_barrier_semaphore()
    any_plane = left_plane | right_plane
    def far_first():
        half = count_y // 2
        order = [(half // 2, 1), (half // 2, 0)]
        for dx in range(half // 2 - 1, -1, -1):
            order += [(d, z) for z in (1, 0) for d in sorted({dx, (half - dx) % half})]
        return [2 * lax.rem(gy // 2 + dx, half) + lax.rem(gy + dz, 2) for dx, dz in dict.fromkeys(order)]

    for is_plane, side in ((left_plane, below), (right_plane, above)):
        @pl.when(is_plane)
        def _(side=side):
            for y in far_first():
                signal(side, y)
            for j in range(2, count_y - 1):
                signal(gx, lax.rem(gy + j, count_y))

    signal(gx, front)
    signal(gx, back)
    for is_plane, side in ((left_plane, below), (right_plane, above)):
        @pl.when(jnp.logical_not(is_plane))
        def _(side=side):
            signal(side, front)
            signal(side, back)
            signal(side, gy)

    lane = lax.broadcasted_iota(jnp.int32, (16, WIDE), 1)
    place = lax.rem(lane, NZ)
    lane4 = lax.broadcasted_iota(jnp.int32, (16, 512), 1)
    place4 = lax.rem(jnp.where(lane4 < 448, lane4, lane4 - 464), NZ)
    lane1 = lax.broadcasted_iota(jnp.int32, (16, 128), 1)
    lane5 = lax.broadcasted_iota(jnp.int32, (24, 640), 1)
    place5 = lax.rem(jnp.where(lane5 < 512, lane5, lane5 + 8), NZ)
    place6 = lax.rem(lax.broadcasted_iota(jnp.int32, (8, 768), 1), NZ)

    def pack_phase(r):
        for b in range(3):
            cut = slice(b * 128, b * 128 + 128)
            to_x[0, 8 * b + 5:8 * b + 7, :] = ext[10:12, cut]
            to_x[1, 8 * b + 5:8 * b + 7, :] = ext[0:2, cut]

    def remote(src, dst, r, sem, x, y, sent=send_sem):
        pltpu.make_async_remote_copy(
            src_ref=src, dst_ref=dst, send_sem=sent.at[r], recv_sem=sem.at[r],
            device_id=(x, y), device_id_type=MESH,
        ).start()

    def rows_of(r):
        y_rows, strip, corners = {0: (48, 48, 16), 1: (16, 24, 0), 2: (64, 72, 16)}[r]
        return y_rows, strip, 2 * y_rows, strip + corners

    def side_start(kind, r, on_left_plane):
        _, _, first, size = rows_of(r)
        return first if kind == 0 else jnp.where(on_left_plane, first, first + size)

    def land(buffer, start, size):
        return buffer.at[pl.ds(start, size)]

    def landing(r):
        return {0: wide, 1: got, 2: last}[r]

    def send_x(r, strips, corners):
        buffer = landing(r)
        _, strip, first, size = rows_of(r)
        n = r
        for kind, is_plane, side in ((0, right_plane, above), (1, left_plane, below)):
            @pl.when(is_plane)
            def _(kind=kind, side=side):
                place = pl.multiple_of(first + size + gy * strip, 8)
                for y in far_first():
                    remote(strips(kind), land(buffer, place, strip), n, plane_sem, side, y)

            @pl.when(jnp.logical_not(is_plane))
            def _(kind=kind, side=side):
                place = side_start(kind, r, lax.rem(side, SPAN) == 0)
                for k, y in ((0, front), (1, back)):
                    if r != 1:
                        spot = land(buffer, pl.multiple_of(place + strip + 8 * k, 8), 8)
                        remote(corners(2 * kind + k), spot, n, near_sem, side, y)
                    else:
                        spot = got_corner.at[2 * kind + k]
                        remote(corners(2 * kind + k), spot, n, corner_sem, side, y, corner_send)
                remote(strips(kind), land(buffer, pl.multiple_of(place, 8), strip), n, near_sem, side, gy)

    def send_y(r, messages):
        size = rows_of(r)[0]
        n = r
        for k, y in ((0, front), (1, back)):
            remote(messages(k), land(landing(r), k * size, size), n, near_sem, gx, y)

    def wait_for(ref, sem):
        pltpu.make_async_copy(ref, ref, sem).wait()

    def run_of(r):
        _, strip, first, size = rows_of(r)
        return first + size, first + 2 * size, count_y * strip + (8, 0, 24)[r] * (count_y - 1)

    def wait_corners(r, sem):
        for is_kind, start, size in (
            (left_plane, 2, 2), (right_plane, 0, 2), (jnp.logical_not(any_plane), 0, 4)
        ):
            @pl.when(is_kind)
            def _(start=start, size=size):
                wait_for(got_corner.at[pl.ds(start, size)], sem.at[r])

    def wait_sent(r):
        buffer, n = landing(r), r
        short, near, crossing = run_of(r)

        @pl.when(any_plane)
        def _():
            wait_for(land(buffer, 0, short + crossing), send_sem.at[n])

        @pl.when(jnp.logical_not(any_plane))
        def _():
            wait_for(land(buffer, 0, near), send_sem.at[n])

        if r == 1:
            wait_corners(r, corner_send)

    def wait_near(r):
        buffer, n = landing(r), r
        short, near, _ = run_of(r)

        @pl.when(any_plane)
        def _():
            wait_for(land(buffer, 0, short), near_sem.at[n])

        @pl.when(jnp.logical_not(any_plane))
        def _():
            wait_for(land(buffer, 0, near), near_sem.at[n])

        if r == 1:
            wait_corners(r, corner_sem)

    def wait_plane(r):
        short, _, crossing = run_of(r)
        wait_for(land(landing(r), short, crossing), plane_sem.at[r])

    def window_of(held, turn):
        start = ((gy * 16 - turn - 4) & (16 * count_y - 1)) * NZ
        first, offset = start >> 7, start & 127
        window = jnp.concatenate([held[first + i] for i in range(6)], axis=1)
        return pltpu.roll(window, 768 - 4 * NZ - offset, 1)

    def view_b(kind, shift):
        return window_of(ring_b, shift if kind == 0 else -shift - 1)

    def close_ring(r):
        first = run_of(r)[0]
        for b in range(blocks + 4):
            row = first + 8 * (b % blocks)
            ring[b] = got[row:row + 8]

    def view(kind, shift):
        low = shift if kind == 0 else -shift - 1
        near, far = (0.75, 0.25) if kind == 0 else (0.25, 0.75)
        start = ((gy * 16 - low - 3) & (16 * count_y - 1)) * NZ
        first, offset = start >> 7, start & 127
        window = jnp.concatenate([ring[first + i] for i in range(5)], axis=1)
        window = pltpu.roll(window, 640 - 3 * NZ - offset, 1)
        return near * window + far * rolled(window, NZ, 1)

    def patch_y(k, packed):
        cut = slice(0, 128) if k == 0 else slice(256, 384)
        keep = lane1 < NZ if k == 0 else lane1 >= 128 - NZ
        for i, slot in enumerate(plus_y if k == 0 else minus_y):
            part = rolled(packed, -i * NZ if k == 0 else i * NZ, 1)
            f[slot, :, cut] = jnp.where(keep, part, f[slot, :, cut])

    def patch_x(kind, strip):
        edge = 0 if kind == 0 else ROWS - 1
        for i, slot in enumerate(up_slots if kind == 0 else down_slots):
            f[slot, edge:edge + 1, :] = strip[i:i + 1, :WIDE]

    def receive(r, step):
        wait_near(r)
        for k in (0, 1):
            patch_y(k, got[16 * k:16 * k + 16])
        ext[0:12, 384:512] = jnp.where(
            lane1 < 64, phase_part(1, got[16:32]), phase_part(0, got[0:16])
        )[:12]
        for kind, is_plane, _ in sides:
            @pl.when(jnp.logical_not(is_plane))
            def _(kind=kind):
                outer = 14 - 2 * kind
                near_row = 15 - 3 * kind
                e = (0, ROWS - 1)[kind]
                place = pl.multiple_of(side_start(kind, 1, left_plane), 8)
                strip = jnp.concatenate([got[pl.ds(place + 8 * b, 8)] for b in range(3)], axis=1)
                first, last = got_corner[2 * kind], got_corner[2 * kind + 1]
                plus = rolled(strip, NZ, 1)
                minus = rolled(strip, -NZ, 1)
                slots = up_slots if kind == 0 else down_slots
                for i in range(3):
                    f[slots[i], e:e + 1, :] = strip[i:i + 1]
                head = jnp.where(lane1[:1] < NZ, first, plus[3:4, 0:128])
                tail = jnp.where(lane1[:1] >= 128 - NZ, last, minus[4:5, 256:384])
                f[slots[3], e:e + 1, 0:128] = head
                f[slots[3], e:e + 1, 128:384] = plus[3:4, 128:384]
                f[slots[4], e:e + 1, 0:256] = minus[4:5, 0:256]
                f[slots[4], e:e + 1, 256:384] = tail
                ext[outer:outer + 2, 0:WIDE] = strip[5:7]
                ext[near_row:near_row + 1, WIDE:512] = jnp.where(lane1[:1] < 64, last, first)

        for kind, is_plane, place_of in sides:
            @pl.when(is_plane)
            def _(kind=kind, place_of=place_of):
                outer = 14 - 2 * kind
                wait_plane(r)
                close_ring(r)
                patch_x(kind, strip_moved(view(kind, shifts[step, place_of])))
                phase = view(kind, shifts[jnp.minimum(step + 1, STEPS - 1), place_of])
                ext[outer:outer + 2, 0:WIDE] = phase[5:7, 0:WIDE]
                ext[outer:outer + 2, WIDE:512] = jnp.where(
                    lane1[:2] < 64, phase[5:7, 384:512], phase[5:7, 512:640]
                )

    def momentum(f):
        density = f[0]
        for slot in range(1, 19):
            density = density + f[slot]
        totals = []
        for axis in range(3):
            total = None
            for slot in range(1, 19, 2):
                sign = lattice_vel[slot][axis]
                if sign != 0:
                    pair = f[slot] - f[slot + 1]
                    if total is None:
                        total = pair
                    else:
                        total = total + pair if sign == 1 else total - pair
            totals.append(total)
        return density, totals

    def advance(r):
        p = ext[...]
        around = differences(p, place4)
        chem = bulk(p, around)
        slope = [0.5 * (a - b)[:, :WIDE] for a, b in around]
        around = [(a[:, :WIDE], b[:, :WIDE]) for a, b in differences(chem, place4)]
        bend = bent(chem[:, :WIDE], around)
        own = p[:, :WIDE]
        density, totals = momentum(f)
        inverse = 1.0 / density
        scaled = (-0.5 * coupling / relax_rate) * own
        next_phase = own + mobility * bend
        drift = []
        for axis in range(3):
            next_phase = next_phase - totals[axis] * inverse * slope[axis]
            drift.append((totals[axis] + scaled * (around[axis][0] - around[axis][1])) * inverse)
        ext[0:12, 0:WIDE] = next_phase[:12]
        if r == 1:
            pack_phase(r)
        collide(density, drift, r, lambda slot: f[slot])

    def collide(density, drift, r, source):
        base = 1.0 - 1.5 * (drift[0] * drift[0] + drift[1] * drift[1] + drift[2] * drift[2])
        weight = relax_rate / 36.0 * density
        keep = 1.0 - relax_rate
        packs = {}

        def put(slot, post):
            step_x, step_y, step_z = lattice_vel[slot]
            if r == 2:
                fx[slot, :, 0:WIDE] = post
                return
            value = rolled(post, step_x, 0)
            moved = moved_yz(value, step_y, step_z, place)
            f[slot] = moved
            if r is None:
                return
            if step_x != 0:
                kind = 0 if step_x == 1 else 1
                i = (up_slots, down_slots)[kind].index(slot)
                line = 12 if step_x == 1 else 15
                shown = value if step_y != 0 else moved
                for b in range(3):
                    to_x[kind, 8 * b + i:8 * b + i + 1, :] = shown[line:line + 1, b * 128:b * 128 + 128]
                if step_y != 0:
                    k = 2 * kind + (0 if step_y == 1 else 1)
                    cut = slice(0, 128) if step_y == 1 else slice(256, 384)
                    edge = 11 if step_x == 1 else 0
                    own = ext[edge:edge + 1, slice(256, 384) if step_y == 1 else slice(0, 128)]
                    post_row = moved[line:line + 1, cut]
                    low = lane1[:1] < 64
                    to_corner[k] = (
                        jnp.where(low, post_row, own) if step_y == 1 else jnp.where(low, own, post_row)
                    )
            if step_y == 1:
                i = plus_y.index(slot)
                part = rolled(moved[:, 0:128], i * NZ, 1)
                mine = (lane1 >= i * NZ) & (lane1 < i * NZ + NZ)
                packs[0] = jnp.where(mine, part, packs[0]) if 0 in packs else part
            if step_y == -1:
                i = minus_y.index(slot)
                part = rolled(moved[:, 256:384], -i * NZ, 1)
                mine = (lane1 < 128 - i * NZ) & (lane1 >= 128 - NZ - i * NZ)
                packs[1] = jnp.where(mine, part, packs[1]) if 1 in packs else part

        def put_pair(slot):
            along = None
            for axis in range(3):
                sign = lattice_vel[slot][axis]
                if sign != 0:
                    if along is None:
                        along = drift[axis]
                    else:
                        along = along + drift[axis] if sign == 1 else along - drift[axis]
            scale = 2.0 * weight if slot < 7 else weight
            even = scale * (base + 4.5 * along * along)
            odd = scale * (3.0 * along)
            here, there = source(slot), source(slot + 1)
            put(slot, keep * here + (even + odd))
            put(slot + 1, keep * there + (even - odd))

        for slot in (1, 7, 9, 11, 13):
            put_pair(slot)
        if r == 1:
            send_x(r, lambda kind: to_x.at[kind], lambda k: to_corner.at[k])
        for slot in (3, 15, 17):
            put_pair(slot)
        if r == 1:
            for k in (0, 1):
                to_y[k] = with_phase(k, packs[k], ext[0:16, 256:384] if k == 0 else ext[0:16, 0:128])
            send_y(r, lambda k: to_y.at[k])
        put_pair(5)
        put(0, keep * source(0) + 12.0 * weight * base)

    for slot in range(19):
        f[slot, 0:12, :] = f_in[slot]
        f[slot, 12:16, :] = jnp.ones((4, WIDE), jnp.float32)
    ext[...] = jnp.zeros_like(ext)
    e_p[...] = jnp.zeros_like(e_p)
    e_r[...] = jnp.ones_like(e_r)
    e_u[...] = jnp.zeros_like(e_u)
    e_p[0:12, 0:WIDE] = p_in[...]
    density, totals = momentum(f)
    e_r[0:12, 0:WIDE] = density[:12]
    for axis in range(3):
        e_u[axis, 0:12, 0:WIDE] = (totals[axis] / density)[:12]

    for kind in (0, 1):
        edge, second, low = ((11, 10, 8), (0, 1, 0))[kind]
        for b in range(3):
            cut = slice(b * 128, b * 128 + 128)
            out_x[kind, 16 * b:16 * b + 4, :] = e_p[low:low + 4, cut]
            out_x[kind, 16 * b + 4:16 * b + 5, :] = e_r[edge:edge + 1, cut]
            for axis in range(3):
                out_x[kind, 16 * b + 5 + axis:16 * b + 6 + axis, :] = e_u[axis, edge:edge + 1, cut]
                out_x[kind, 16 * b + 13 + axis:16 * b + 14 + axis, :] = e_u[axis, second:second + 1, cut]
            for i, slot in enumerate(up_slots if kind == 0 else down_slots):
                out_x[kind, 16 * b + 8 + i:16 * b + 9 + i, :] = f[slot, edge:edge + 1, cut]
        third = (9, 0)[kind]
        for k in (2 * kind, 2 * kind + 1):
            cut = slice(256, 384) if k % 2 == 0 else slice(0, 128)
            out_corner[k, 0:3, :] = e_p[third:third + 3, cut]
            out_corner[k, 3:4, :] = e_r[edge:edge + 1, cut]
            for axis in range(3):
                out_corner[k, 4 + axis:5 + axis, :] = e_u[axis, edge:edge + 1, cut]
            slot = (up_slots if kind == 0 else down_slots)[3 + k % 2]
            out_corner[k, 7:8, :] = f[slot, edge:edge + 1, cut]
    for k in (0, 1):
        cut = slice(256, 384) if k == 0 else slice(0, 128)
        low = lane1[:12] < 64
        if k == 0:
            pair = lambda a, b: jnp.where(low, pltpu.roll(b, 64, 1), a)
        else:
            pair = lambda a, b: jnp.where(low, a, pltpu.roll(b, 64, 1))
        packed = None
        for i, slot in enumerate(plus_y if k == 0 else minus_y):
            block = f[slot, :, cut]
            part = rolled(block, NZ + i * NZ if k == 0 else -NZ - i * NZ, 1)
            if i == 0:
                packed = part
            else:
                packed = jnp.where(lane1 >= i * NZ if k == 0 else lane1 < 128 - i * NZ, part, packed)
        out_y[k, 0:12, :] = packed[:12]
        out_y[k, 12:24, :] = e_p[0:12, cut]
        out_y[k, 24:36, :] = pair(e_r[0:12, cut], e_u[0, 0:12, cut])
        out_y[k, 36:48, :] = pair(e_u[1, 0:12, cut], e_u[2, 0:12, cut])

    @pl.when(left_plane)
    def _():
        for b in range(3):
            out_a[2 * b:2 * b + 2, :] = e_p[0:2, b * 128:b * 128 + 128]

    @pl.when(right_plane)
    def _():
        for b in range(3):
            out_a[2 * b:2 * b + 2, :] = e_p[10:12, b * 128:b * 128 + 128]

    pl.semaphore_wait(barrier, jnp.where(any_plane, 5 + count_y + max(count_y - 3, 0), 8))

    send_x(0, lambda kind: out_x.at[kind], lambda k: out_corner.at[k])

    @pl.when(any_plane)
    def _():
        start = run_of(0)[0] + count_y * 48
        for j in range(1, count_y):
            remote(out_a, land(wide, start + 8 * (j - 1), 8), 0, plane_sem, gx, lax.rem(gy + j, count_y))

    send_y(0, lambda k: out_y.at[k])

    wait_near(0)
    for k in (0, 1):
        at = 48 * k
        cut = slice(512, 640) if k == 0 else slice(384, 512)
        e_p[0:12, cut] = wide[at + 12:at + 24]
        e_r[0:12, cut] = wide[at + 24:at + 36]
        e_u[0, 0:12, cut] = pltpu.roll(wide[at + 24:at + 36], 64, 1)
        e_u[1, 0:12, cut] = wide[at + 36:at + 48]
        e_u[2, 0:12, cut] = pltpu.roll(wide[at + 36:at + 48], 64, 1)
    for kind, is_plane, place_of in sides:
        low = (20, 12)[kind]
        edge, second, third = ((23, 22, 21), (12, 13, 12))[kind]

        @pl.when(jnp.logical_not(is_plane))
        def _(kind=kind, low=low, edge=edge, second=second, third=third):
            place = pl.multiple_of(side_start(kind, 0, left_plane), 8)
            for k in (0, 1):
                corner = wide[pl.ds(place + 48 + 8 * k, 8)]
                cut = slice(512, 640) if k == 0 else slice(384, 512)
                e_p[third:third + 3, cut] = corner[0:3]
                e_r[edge:edge + 1, cut] = corner[3:4]
                for axis in range(3):
                    e_u[axis, edge:edge + 1, cut] = corner[4 + axis:5 + axis]
            for b in range(3):
                cut = slice(b * 128, b * 128 + 128)
                strip = wide[pl.ds(place + 16 * b, 16)]
                e_p[low:low + 4, cut] = strip[0:4]
                e_r[edge:edge + 1, cut] = strip[4:5]
                for axis in range(3):
                    e_u[axis, edge:edge + 1, cut] = strip[5 + axis:6 + axis]
                    e_u[axis, second:second + 1, cut] = strip[13 + axis:14 + axis]

    for kind, is_plane, place_of in sides:
        @pl.when(is_plane)
        def _(kind=kind, place_of=place_of):
            wait_plane(0)
            start = run_of(0)[0]
            for b in range(blocks + 5):
                row = start + 16 * (b % blocks)
                ring_b[b] = wide[row:row + 16]
            start = start + 16 * blocks
            a_row = (4, 6)[kind]
            for j in range(count_y):
                source = lax.rem(gy + count_y - j, count_y)
                for b in range(3):
                    row = start + 8 * (j - 1) + 2 * b
                    piece = out_a[2 * b:2 * b + 2, :] if j == 0 else wide[row:row + 2]
                    ring_a[source * 3 + b, a_row:a_row + 2, :] = piece
            for b in range(5):
                ring_a[blocks + b] = ring_a[b]
            shift = shifts[0, place_of]
            near = view_b(kind, shift)[0:8]
            phase = (near * 0.75 + rolled(near, NZ, 1) * 0.25) if kind == 0 else (
                near * 0.25 + rolled(near, NZ, 1) * 0.75)
            row, at = ((22, 2), (12, 0))[kind]
            e_p[row:row + 2, 0:512] = phase[at:at + 2, 0:512]
            e_p[row:row + 2, 512:640] = phase[at:at + 2, 640:768]

    p = e_p[...]
    around = differences(p, place5)
    chem = bulk(p, around)
    slope = [0.5 * (a - b) for a, b in around]
    around = differences(chem, place5)
    next_phase = p + mobility * bent(chem, around)
    scaled = (-0.5 * coupling / relax_rate) * p / e_r[...]
    drift = []
    for axis in range(3):
        flow = e_u[axis]
        next_phase = next_phase - flow * slope[axis]
        drift.append(flow + scaled * (around[axis][0] - around[axis][1]))
    for top, at, size in ((0, 0, 12), (12, 12, 2), (14, 22, 2)):
        ext[top:top + size, 0:WIDE] = next_phase[at:at + size, 0:WIDE]
        ext[top:top + size, WIDE:512] = jnp.where(
            lane1[:size] < 64, next_phase[at:at + size, 384:512], next_phase[at:at + size, 512:640]
        )
    collide(e_r[0:16, 0:WIDE], [d[0:16, 0:WIDE] for d in drift], None, lambda slot: f[slot])
    for k in (0, 1):
        cut = slice(512, 640) if k == 0 else slice(384, 512)
        patch_y(k, packed_post(k, wide[48 * k:48 * k + 16], e_r[0:16, cut], [d[0:16, cut] for d in drift], lane1))
    for kind, is_plane, place_of in sides:
        @pl.when(is_plane)
        def _(kind=kind, place_of=place_of):
            first = shifts[0, place_of]
            row = lax.broadcasted_iota(jnp.int32, (8, 768), 0)
            edge, at, outer = ((3, 2, 14), (0, 0, 12))[kind]
            weights_of = ((0.75, 0.25), (0.25, 0.75))[kind]
            for step in (0, 1):
                shift = shifts[step, place_of]
                both = view_b(kind, shift)
                turn = shift - first if kind == 0 else first - shift - 1
                own = window_of(ring_a, turn)
                own = 0.75 * own + 0.25 * rolled(own, -NZ if kind == 0 else NZ, 1)
                far_p = jnp.where(row < 4, both[0:8], own)
                around = differences(far_p, place6)
                chem = bulk(far_p, around)
                slope = [0.5 * (a - b) for a, b in around]
                around = differences(chem, place6)
                if step == 0:
                    density = both[4:5]
                    scaled = (-0.5 * coupling / relax_rate) * far_p[edge:edge + 1] / density
                    drift = [
                        both[5 + axis:6 + axis]
                        + scaled * (around[axis][0] - around[axis][1])[edge:edge + 1]
                        for axis in range(3)
                    ]
                    strip = strip_post(kind, both[8:16], density, drift, place6)
                    strip = weights_of[0] * strip + weights_of[1] * rolled(strip, NZ, 1)
                    patch_x(kind, strip_moved(strip))
                else:
                    after = far_p + mobility * bent(chem, around)
                    for axis in range(3):
                        flow = jnp.where(row == edge, both[5 + axis:6 + axis], both[13 + axis:14 + axis])
                        after = after - flow * slope[axis]
                    after = weights_of[0] * after + weights_of[1] * rolled(after, NZ, 1)
                    ext[outer:outer + 2, 0:WIDE] = after[at:at + 2, 0:WIDE]
                    ext[outer:outer + 2, WIDE:512] = jnp.where(
                        lane1[:2] < 64, after[at:at + 2, 384:512], after[at:at + 2, 640:768]
                    )

        @pl.when(jnp.logical_not(is_plane))
        def _(kind=kind):
            edge = (23, 12)[kind]
            place = pl.multiple_of(side_start(kind, 0, left_plane), 8)
            strip = jnp.concatenate(
                [wide[pl.ds(place + 16 * b + 8, 8)] for b in range(3)]
                + [jnp.broadcast_to(wide[pl.ds(place + 48 + 8 * i, 8)][7:8], (8, 128)) for i in (1, 0)],
                axis=1,
            )
            strip = strip_post(
                kind, strip, e_r[edge:edge + 1, :], [d[edge:edge + 1] for d in drift], place5[:8]
            )
            patch_x(kind, strip_moved(strip))

    advance(1)
    wait_sent(0)
    receive(1, 1)

    advance(2)
    lane_low = lane1 < 64
    y_cut = (slice(256, 384), slice(0, 128))
    for kind in (0, 1):
        edge, second, low = ((11, 10, 9), (0, 1, 0))[kind]
        inward = (up_slots, down_slots)[kind]
        for b in range(3):
            cut = slice(b * 128, b * 128 + 128)
            for i, slot in enumerate(near_x[kind]):
                last_x[kind, 24 * b + i:24 * b + i + 1, :] = fx[slot, edge:edge + 1, cut]
            for i, slot in enumerate(inward):
                last_x[kind, 24 * b + 14 + i:24 * b + 15 + i, :] = fx[slot, second:second + 1, cut]
            last_x[kind, 24 * b + 19:24 * b + 22, :] = ext[low:low + 3, cut]
        for k in (0, 1):
            units = corner_units(kind, k)
            for i in range(0, len(units), 5):
                line = None
                for j, (slot, deep_x, deep_y) in enumerate(units[i:i + 5]):
                    row = 12 - deep_x if kind == 0 else deep_x - 1
                    part = ext[row:row + 1, y_cut[k]] if slot is None else fx[slot, row:row + 1, y_cut[k]]
                    part = rolled(part, NZ * j - lane_of(k, deep_y), 1)
                    line = part if j == 0 else jnp.where(lane1[:1] >= NZ * j, part, line)
                last_corner[2 * kind + k, i // 5:i // 5 + 1, :] = line
    for is_plane, edge, slots in ((left_plane, 0, down_slots), (right_plane, 11, up_slots)):
        @pl.when(is_plane)
        def _(edge=edge, slots=slots):
            for b in range(3):
                for i, slot in enumerate(slots):
                    last_a[8 * b + i:8 * b + i + 1, :] = fx[slot, edge:edge + 1, b * 128:b * 128 + 128]

    send_x(2, lambda kind: last_x.at[kind], lambda k: last_corner.at[k])

    @pl.when(any_plane)
    def _():
        start = run_of(2)[0] + count_y * 72
        for j in range(1, count_y):
            remote(last_a, land(last, start + 24 * (j - 1), 24), 2, plane_sem, gx, lax.rem(gy + j, count_y))

    for k in (0, 1):
        for i in range(0, len(y_units[k]), 5):
            line = None
            for j, (slot, deep) in enumerate(y_units[k][i:i + 5]):
                part = ext[0:16, y_cut[k]] if slot is None else fx[slot, :, y_cut[k]]
                part = rolled(part, NZ * j - lane_of(k, deep), 1)
                line = part if j == 0 else jnp.where(lane1 >= NZ * j, part, line)
            last_y[k, 12 * (i // 5):12 * (i // 5) + 12, :] = line[:12]
    send_y(2, lambda k: last_y.at[k])
    e_p[0:12, 0:WIDE] = ext[0:12, 0:WIDE]
    wait_sent(1)

    wait_near(2)

    def unit_of_y(k, slot, deep):
        place = y_units[k].index((slot, deep))
        row = 64 * k + 12 * (place // 5)
        return rolled(last[row:row + 12], lane_of(k, deep) - NZ * (place % 5), 1)

    lane12 = lane1[:12]
    for slot in range(19):
        step_y = lattice_vel[slot][1]
        if step_y == 0:
            rim = jnp.where(lane12 < 64, unit_of_y(1, slot, 1), unit_of_y(0, slot, 1))
        elif step_y == 1:
            rim = jnp.where(lane12 >= 104, unit_of_y(0, slot, 1), unit_of_y(0, slot, 2))
        else:
            rim = jnp.where(lane12 < NZ, unit_of_y(1, slot, 1), unit_of_y(1, slot, 2))
        fx[slot, 0:12, 384:512] = rim
    e_p[0:12, 384:512] = jnp.where(
        lane12 < NZ, unit_of_y(1, None, 1),
        jnp.where(lane12 < 2 * NZ, unit_of_y(1, None, 2), unit_of_y(1, None, 3)),
    )
    e_p[0:12, 512:640] = jnp.where(
        lane12 >= 104, unit_of_y(0, None, 1),
        jnp.where(lane12 >= 80, unit_of_y(0, None, 2), unit_of_y(0, None, 3)),
    )
    for kind, is_plane, place_of in sides:
        @pl.when(jnp.logical_not(is_plane))
        def _(kind=kind):
            place = pl.multiple_of(side_start(kind, 2, left_plane), 8)
            rows = ((15, 14), (12, 13))[kind]
            low = (21, 12)[kind]
            inward = (up_slots, down_slots)[kind]
            for b in range(3):
                cut = slice(b * 128, b * 128 + 128)
                strip = last[pl.ds(place + 24 * b, 24)]
                for i, slot in enumerate(near_x[kind]):
                    fx[slot, rows[0]:rows[0] + 1, cut] = strip[i:i + 1]
                for i, slot in enumerate(inward):
                    fx[slot, rows[1]:rows[1] + 1, cut] = strip[14 + i:15 + i]
                e_p[low:low + 3, cut] = strip[19:22]
            found = {}
            for k in (0, 1):
                corner = last[pl.ds(place + 72 + 8 * k, 8)]
                for i, (slot, deep_x, deep_y) in enumerate(corner_units(kind, k)):
                    part = corner[i // 5:i // 5 + 1]
                    part = rolled(part, lane_of(k, deep_y) - NZ * (i % 5), 1)
                    found.setdefault((slot, deep_x), []).append((k, deep_y, part))
            for (slot, deep_x), parts in found.items():
                line = {}
                for k, deep_y, part in parts:
                    start = lane_of(k, deep_y)
                    here = (lane1[:1] >= start) & (lane1[:1] < start + NZ)
                    at = k if slot is None else 0
                    line[at] = jnp.where(here, part, line[at]) if at in line else part
                if slot is None:
                    row = 24 - deep_x if kind == 0 else 11 + deep_x
                    e_p[row:row + 1, 512:640] = line[0]
                    e_p[row:row + 1, 384:512] = line[1]
                else:
                    row = rows[deep_x - 1]
                    fx[slot, row:row + 1, 384:512] = line[0]

    def mixed(kind, value):
        near, far = ((0.75, 0.25), (0.25, 0.75))[kind]
        return near * value + far * rolled(value, NZ, 1)

    for kind, is_plane, place_of in sides:
        @pl.when(is_plane)
        def _(kind=kind, place_of=place_of):
            wait_plane(2)
            start = run_of(2)[0]
            for b in range(blocks + 5):
                row = start + 24 * (b % blocks)
                ring_e[b] = last[row:row + 24]
            start = start + 24 * blocks
            for j in range(count_y):
                source = lax.rem(gy + count_y - j, count_y)
                for b in range(3):
                    row = start + 24 * (j - 1) + 8 * b
                    ring_o[source * 3 + b] = last_a[8 * b:8 * b + 8, :] if j == 0 else last[row:row + 8]
            for b in range(5):
                ring_o[blocks + b] = ring_o[b]
            row = (15, 12)[kind]
            shift = shifts[2, place_of]
            strip = mixed(kind, window_of(ring_e, shift if kind == 0 else -shift - 1)[0:8])
            for i, slot in enumerate((up_slots, down_slots)[kind]):
                fx[slot, row:row + 1, 0:384] = strip[i:i + 1, 0:384]
                fx[slot, row:row + 1, 384:512] = jnp.where(
                    lane1[:1] < 64, strip[i:i + 1, 384:512], strip[i:i + 1, 640:768]
                )
            shift = shifts[3, place_of]
            phase = mixed(kind, window_of(ring_e, shift if kind == 0 else -shift - 1)[16:24])
            row, at = ((22, 4), (12, 3))[kind]
            e_p[row:row + 2, 0:512] = phase[at:at + 2, 0:512]
            e_p[row:row + 2, 512:640] = phase[at:at + 2, 640:768]

    def narrowed(to, value):
        for top, at, size in ((0, 0, 12), (12, 12, 2), (14, 22, 2)):
            to[top:top + size, 0:WIDE] = value[at:at + size, 0:WIDE]
            to[top:top + size, WIDE:512] = jnp.where(
                lane1[:size] < 64, value[at:at + size, 384:512], value[at:at + size, 512:640]
            )

    for slot in range(19):
        step_x, step_y, step_z = lattice_vel[slot]
        fx[slot] = moved_yz(rolled(fx[slot], step_x, 0), step_y, step_z, place4)
    p = e_p[...]
    narrowed(ext, p)
    narrowed(chem_x, bulk(p, differences(p, place5)))
    density, totals = momentum(fx)
    inverse = 1.0 / density
    p, chem = ext[...], chem_x[...]
    around = differences(p, place4)
    slope = [0.5 * (a - b)[:, :WIDE] for a, b in around]
    around = differences(chem, place4)
    next_phase = (p + mobility * bent(chem, around))[:, :WIDE]
    scaled = (-0.5 * coupling / relax_rate) * p
    drift = []
    for axis in range(3):
        next_phase = next_phase - (totals[axis] * inverse)[:, :WIDE] * slope[axis]
        drift.append((totals[axis] + scaled * (around[axis][0] - around[axis][1])) * inverse)
    p_out[...] = next_phase[:12]
    collide(density[:, :WIDE], [d[:, :WIDE] for d in drift], None, lambda slot: fx[slot, :, 0:WIDE])
    for k in (0, 1):
        here = None
        for i, slot in enumerate((plus_y, minus_y)[k]):
            part = rolled(fx[slot, :, 384:512], NZ + NZ * i if k == 0 else 104 - NZ * i, 1)
            if i == 0:
                here = part
            else:
                here = jnp.where(lane1 >= NZ * i if k == 0 else lane1 < 128 - NZ * i, part, here)
        rim = [d[:, 384:512] for d in drift]
        patch_y(k, packed_post(k, here, density[:, 384:512], rim, lane1))
    for kind, is_plane, place_of in sides:
        @pl.when(is_plane)
        def _(kind=kind, place_of=place_of):
            before, shift = shifts[2, place_of], shifts[3, place_of]
            edge, top, a_row, own_row = ((3, -2, 4, 0), (0, -3, 6, 10))[kind]
            far = window_of(ring_e, shift if kind == 0 else -shift - 1)
            inner = strip_moved(strip_along_z(kind, far[14:22], place6))
            turn = shift - before if kind == 0 else before - shift - 1
            outer = window_of(ring_o, turn)
            outer = 0.75 * outer + 0.25 * rolled(outer, -NZ if kind == 0 else NZ, 1)
            outer = strip_moved(strip_along_z(1 - kind, outer, place6))
            total = [None] * 4
            sign = 1.0 - 2.0 * kind
            for tile, way in ((inner, sign), (outer, -sign)):
                r = [tile[i:i + 1] for i in range(5)]
                whole = r[0] + r[1] + r[2] + r[3] + r[4]
                found = (whole, way * whole, r[3] - r[4], way * (r[1] - r[2]))
                total = [b if a is None else a + b for a, b in zip(total, found)]
            for i, slot in enumerate(zero_x):
                _, step_y, step_z = lattice_vel[slot]
                line = moved_yz(far[5 + i:6 + i], step_y, step_z, place6[:1])
                total[0] = total[0] + line
                if step_y != 0:
                    total[2] = total[2] + step_y * line
                if step_z != 0:
                    total[3] = total[3] + step_z * line
            tile_a[...] = jnp.zeros_like(tile_a)
            tile_a[a_row:a_row + 2, 0:512] = e_p[own_row:own_row + 2, 0:512]
            tile_a[a_row:a_row + 2, 640:768] = e_p[own_row:own_row + 2, 512:640]
            own = tile_a[...]
            ahead = rolled(own, -NZ, 1)
            own = 0.75 * own + 0.25 * ahead if kind == 0 else 0.25 * own + 0.75 * ahead
            row = lax.broadcasted_iota(jnp.int32, (8, 768), 0)
            far_p = jnp.where(row < 4, rolled(far[16:24], top, 0), own)
            around = differences(bulk(far_p, differences(far_p, place6)), place6)
            inverse = 1.0 / total[0]
            scaled = (-0.5 * coupling / relax_rate) * far_p[edge:edge + 1]
            drift = [
                (total[1 + axis] + scaled * (around[axis][0] - around[axis][1])[edge:edge + 1]) * inverse
                for axis in range(3)
            ]
            strip = mixed(kind, strip_post(kind, inner, total[0], drift, place6))
            patch_x(kind, strip_moved(strip))

        @pl.when(jnp.logical_not(is_plane))
        def _(kind=kind):
            row = (15, 12)[kind]
            inward = (up_slots, down_slots)[kind]
            lines = [fx[slot, row:row + 1, :] for slot in inward]
            strip = jnp.concatenate(lines + lines[:1] * 3, axis=0)
            strip = strip_post(
                kind, strip, density[row:row + 1], [d[row:row + 1] for d in drift], place4[:8]
            )
            patch_x(kind, strip_moved(strip))

    wait_sent(2)
    for slot in range(19):
        f_out[slot] = f[slot, 0:12, :]


def on_device(populations, phase_field, plane_shifts):
    blocks = 3 * lax.axis_size("gy")
    rounds = 3
    vmem = pl.BlockSpec(memory_space=pltpu.VMEM)
    return pl.pallas_call(
        kernel,
        out_shape=(
            jax.ShapeDtypeStruct(populations.shape, jnp.float32),
            jax.ShapeDtypeStruct(phase_field.shape, jnp.float32),
        ),
        in_specs=[pl.BlockSpec(memory_space=pltpu.SMEM), vmem, vmem],
        out_specs=(vmem, vmem),
        scratch_shapes=[
            pltpu.VMEM((19, 16, WIDE), jnp.float32),
            pltpu.VMEM((16, 512), jnp.float32),
            pltpu.VMEM((56 + 8 * blocks, 128), jnp.float32),
            pltpu.VMEM((4, 1, 128), jnp.float32),
            pltpu.VMEM((2, 24, 128), jnp.float32),
            pltpu.VMEM((2, 16, 128), jnp.float32),
            pltpu.VMEM((4, 1, 128), jnp.float32),
            pltpu.VMEM((blocks + 4, 8, 128), jnp.float32),
            pltpu.VMEM((24, 640), jnp.float32),
            pltpu.VMEM((24, 640), jnp.float32),
            pltpu.VMEM((3, 24, 640), jnp.float32),
            pltpu.VMEM((blocks + 5, 16, 128), jnp.float32),
            pltpu.VMEM((blocks + 5, 8, 128), jnp.float32),
            pltpu.VMEM((160 + 16 * blocks + 8 * (lax.axis_size("gy") - 1), 128), jnp.float32),
            pltpu.VMEM((2, 48, 128), jnp.float32),
            pltpu.VMEM((2, 48, 128), jnp.float32),
            pltpu.VMEM((4, 8, 128), jnp.float32),
            pltpu.VMEM((8, 128), jnp.float32),
            pltpu.VMEM((19, 16, 512), jnp.float32),
            pltpu.VMEM((16, 512), jnp.float32),
            pltpu.VMEM((8, 768), jnp.float32),
            pltpu.VMEM((blocks + 5, 24, 128), jnp.float32),
            pltpu.VMEM((blocks + 5, 8, 128), jnp.float32),
            pltpu.VMEM((304 + 24 * blocks + 24 * (lax.axis_size("gy") - 1), 128), jnp.float32),
            pltpu.VMEM((2, 72, 128), jnp.float32),
            pltpu.VMEM((2, 64, 128), jnp.float32),
            pltpu.VMEM((4, 8, 128), jnp.float32),
            pltpu.VMEM((24, 128), jnp.float32),
            pltpu.SemaphoreType.DMA((rounds,)),
            pltpu.SemaphoreType.DMA((rounds,)),
            pltpu.SemaphoreType.DMA((rounds,)),
            pltpu.SemaphoreType.DMA((rounds,)),
            pltpu.SemaphoreType.DMA((rounds,)),
        ],
        compiler_params=pltpu.CompilerParams(
            collective_id=0, has_side_effects=True, vmem_limit_bytes=32 * 1024 * 1024
        ),
    )(plane_shifts, populations, phase_field)


def solution(mesh):
    return jax.shard_map(
        on_device,
        mesh=mesh,
        in_specs=(P(None, "gx", "gy"), P("gx", "gy"), P()),
        out_specs=(P(None, "gx", "gy"), P("gx", "gy")),
        check_vma=False,
    )
```

```python
import functools

import jax
import jax.numpy as jnp
from jax import lax
from jax.experimental import pallas as pl
from jax.experimental.pallas import tpu as pltpu
from jax.sharding import PartitionSpec as P

STEPS = 4
NZ = 24
ROWS = 12
WIDE = 384
SPAN = 4
MESH = pl.DeviceIdType.MESH

lattice_vel = (
    (0, 0, 0),
    (1, 0, 0),
    (-1, 0, 0),
    (0, 1, 0),
    (0, -1, 0),
    (0, 0, 1),
    (0, 0, -1),
    (1, 1, 0),
    (-1, -1, 0),
    (1, -1, 0),
    (-1, 1, 0),
    (1, 0, 1),
    (-1, 0, -1),
    (1, 0, -1),
    (-1, 0, 1),
    (0, 1, 1),
    (0, -1, -1),
    (0, 1, -1),
    (0, -1, 1),
)
relax_rate = 0.8
coupling = 0.01
mobility = 0.02

up_slots = (1, 11, 13, 7, 9)
down_slots = (2, 12, 14, 10, 8)
plus_y = (3, 7, 10, 15, 17)
minus_y = (4, 8, 9, 16, 18)


x_groups = ((0, 5, 6), (3, 15, 17), (4, 18, 16))
y_groups = ((0, 5, 6), (1, 11, 13), (2, 14, 12))
folded_x = tuple((first, slot) for first, *pair in x_groups for slot in pair)
folded_y = tuple((first, slot) for first, *pair in y_groups for slot in pair)
near_y = tuple(slots + tuple(slot for _, slot in folded_y) for slots in (plus_y, minus_y))
y_units = tuple(
    tuple((slot, 1) for slot in near_y[k]) + tuple((slot, 2) for slot in (plus_y, minus_y)[k])
    + ((None, 1), (None, 2), (None, 3))
    for k in (0, 1)
)


def corner_units(kind, k):
    step = (1 - 2 * kind, 1 - 2 * k)
    units = []
    for deep in ((1, 1), (2, 1), (1, 2), (2, 2)):
        for slot in range(19):
            if all(
                lattice_vel[slot][axis] == step[axis] or (deep[axis] == 1 and lattice_vel[slot][axis] == 0)
                for axis in (0, 1)
            ):
                units.append((slot,) + deep)
    return tuple(units) + tuple((None, x, y) for x in (1, 2, 3) for y in range(1, 5 - x))


def lane_of(k, depth):
    return 128 - NZ * depth if k == 0 else NZ * (depth - 1)


def rolled(value, shift, axis):
    size = value.shape[axis]
    shift = shift % size
    return value if shift == 0 else pltpu.roll(value, shift, axis)


def moved_yz(value, step_y, step_z, place):
    if step_z == 0:
        return rolled(value, step_y * NZ, 1)
    edge = 0 if step_z == 1 else NZ - 1
    inner = rolled(value, step_y * NZ + step_z, 1)
    wrap = rolled(value, step_y * NZ + step_z - step_z * NZ, 1)
    return jnp.where(place == edge, wrap, inner)


def differences(value, place):
    return (
        (rolled(value, -1, 0), rolled(value, 1, 0)),
        (rolled(value, -NZ, 1), rolled(value, NZ, 1)),
        (moved_yz(value, 0, -1, place), moved_yz(value, 0, 1, place)),
    )


def bulk(p, around):
    total = around[0][0] + around[0][1] + around[1][0] + around[1][1] + around[2][0] + around[2][1]
    return 0.5 * (p * p * p - p) - 0.5 * (total - 6.0 * p)


def bent(chem, around):
    total = around[0][0] + around[0][1] + around[1][0] + around[1][1] + around[2][0] + around[2][1]
    return total - 6.0 * chem


def relaxed(here, weight, along, drift):
    square = drift[0] * drift[0] + drift[1] * drift[1] + drift[2] * drift[2]
    return (1.0 - relax_rate) * here + weight * (
        1.0 - 1.5 * square + 3.0 * along + 4.5 * along * along
    )


def strip_post(kind, here, density, drift, place):
    sign = 1.0 - 2.0 * kind
    row = lax.broadcasted_iota(jnp.int32, here.shape, 0)
    full = [jnp.broadcast_to(d, here.shape) for d in drift]
    along = sign * full[0]
    along = along + jnp.where(row == 3, full[1], jnp.where(row == 4, -full[1], 0.0))
    along = along + jnp.where(row == 1, sign * full[2], jnp.where(row == 2, -sign * full[2], 0.0))
    weight = jnp.where(row == 0, 2.0, 1.0) * (relax_rate / 36.0) * density
    post = relaxed(here, weight, along, full)
    return strip_along_z(kind, post, place)


def strip_along_z(kind, strip, place):
    row = lax.broadcasted_iota(jnp.int32, strip.shape, 0)
    first, second = (1, -1) if kind == 0 else (-1, 1)
    return jnp.where(
        row == 1, moved_yz(strip, 0, first, place), jnp.where(row == 2, moved_yz(strip, 0, second, place), strip)
    )


def strip_moved(strip):
    row = lax.broadcasted_iota(jnp.int32, strip.shape, 0)
    return jnp.where(row == 3, rolled(strip, NZ, 1), jnp.where(row == 4, rolled(strip, -NZ, 1), strip))


def packed_post(k, here, density, drift, lane1):
    def spread(value):
        out = rolled(value, NZ if k == 0 else 104, 1)
        first = out
        for i in range(1, 5):
            if k == 0:
                out = jnp.where(lane1 >= i * NZ, rolled(first, i * NZ, 1), out)
            else:
                out = jnp.where(lane1 < 128 - i * NZ, rolled(first, -i * NZ, 1), out)
        return out

    slots = plus_y if k == 0 else minus_y
    group = lane1 // NZ if k == 0 else (127 - lane1) // NZ
    density, drift = spread(density), [spread(d) for d in drift]

    def chosen(axis, value):
        out = jnp.zeros_like(value)
        for i, slot in enumerate(slots):
            if lattice_vel[slot][axis] != 0:
                out = jnp.where(group == i, lattice_vel[slot][axis] * value, out)
        return out

    along = chosen(0, drift[0]) + chosen(1, drift[1]) + chosen(2, drift[2])
    weight = jnp.where(group == 0, 2.0, 1.0) * (relax_rate / 36.0) * density
    post = relaxed(here, weight, along, drift)
    place = lax.rem(lane1, NZ) if k == 0 else lax.rem(lane1 + 16, NZ)
    out = post
    for i, slot in enumerate(slots):
        step_x, _, step_z = lattice_vel[slot]
        if step_x != 0 or step_z != 0:
            out = jnp.where(group == i, moved_yz(rolled(post, step_x, 0), 0, step_z, place), out)
    return out


def lanes_of_y(k):
    groups = [NZ * i if k == 0 else 104 - NZ * i for i in range(5)]
    return groups, (120 if k == 0 else 0), ((104, 80) if k == 0 else (0, 24))


def with_phase(k, packed, phase):
    groups, spare, (first, second) = lanes_of_y(k)
    lane = lax.broadcasted_iota(jnp.int32, (8, 128), 1)
    upper = lax.broadcasted_iota(jnp.int32, (8, 128), 0) >= 4
    in_spare = (lane >= spare) & (lane < spare + 8)
    top, low = phase[0:8], phase[8:16]
    top_down, low_down = rolled(top, 4, 0), rolled(low, 4, 0)
    head, tail = packed[0:8], packed[8:16]
    pieces = ((top_down, first), (top, first), (low_down, first), (top_down, second), (top, second))
    for start, (piece, at) in zip(groups, pieces):
        here = upper & (lane >= start) & (lane < start + NZ)
        tail = jnp.where(here, rolled(piece, start - at, 1), tail)
    parts = [
        rolled(low, spare - second, 1),
        rolled(low_down, spare - second - 8, 1),
        rolled(low, spare - second - 16, 1),
    ]
    head = jnp.where(in_spare, jnp.where(upper, parts[1], parts[0]), head)
    tail = jnp.where(in_spare & jnp.logical_not(upper), parts[2], tail)
    return jnp.concatenate([head, tail], axis=0)


def phase_part(k, message):
    groups, spare, (first, second) = lanes_of_y(k)
    lane = lax.broadcasted_iota(jnp.int32, (8, 128), 1)
    upper = lax.broadcasted_iota(jnp.int32, (8, 128), 0) >= 4
    in_first = (lane >= first) & (lane < first + NZ)
    head, tail = message[0:8], message[8:16]
    head_up, tail_up = rolled(head, 4, 0), rolled(tail, 4, 0)

    def picked(near, far):
        return jnp.where(in_first, rolled(near[0], first - near[1], 1), rolled(far[0], second - far[1], 1))

    top = jnp.where(
        upper,
        picked((tail, groups[1]), (tail, groups[4])),
        picked((tail_up, groups[0]), (tail_up, groups[3])),
    )
    far = jnp.where(
        lane < second + 8,
        rolled(head, second - spare, 1),
        jnp.where(
            lane < second + 16,
            rolled(head_up, second + 8 - spare, 1),
            rolled(tail, second + 16 - spare, 1),
        ),
    )
    low = jnp.where(in_first, rolled(tail_up, first - groups[2], 1), far)
    return jnp.concatenate([top, low], axis=0)


def kernel(
    shifts, f_in, p_in, f_out, p_out,
    f, ext, got, got_corner, to_x, to_y, to_corner, ring,
    e_p, e_r, e_u, ring_b, ring_a, wide, out_x, out_y, out_corner, out_a,
    fx, chem_x, tile_a, ring_e, ring_o, last, last_x, last_y, last_corner, last_a,
    send_sem, near_sem, plane_sem, corner_sem, corner_send,
):
    count_x, count_y = lax.axis_size("gx"), lax.axis_size("gy")
    gx, gy = lax.axis_index("gx"), lax.axis_index("gy")
    above, below = lax.rem(gx + 1, count_x), lax.rem(gx + count_x - 1, count_x)
    front, back = lax.rem(gy + 1, count_y), lax.rem(gy + count_y - 1, count_y)
    planes = count_x // SPAN
    left_plane = lax.rem(gx, SPAN) == 0
    right_plane = lax.rem(gx, SPAN) == SPAN - 1
    left_slot = lax.rem(gx // SPAN + planes - 1, planes)
    right_slot = gx // SPAN
    any_plane = left_plane | right_plane
    blocks = 3 * count_y
    sides = ((0, left_plane, left_slot), (1, right_plane, right_slot))

    def signal(x, y):
        pl.semaphore_signal(barrier, inc=1, device_id=(x, y), device_id_type=MESH)

    barrier = pltpu.get_barrier_semaphore()
    any_plane = left_plane | right_plane
    def far_first():
        half = count_y // 2
        order = [(half // 2, 1), (half // 2, 0)]
        for dx in range(half // 2 - 1, -1, -1):
            order += [(d, z) for z in (1, 0) for d in sorted({dx, (half - dx) % half})]
        return [2 * lax.rem(gy // 2 + dx, half) + lax.rem(gy + dz, 2) for dx, dz in dict.fromkeys(order)]

    for is_plane, side in ((left_plane, below), (right_plane, above)):
        @pl.when(is_plane)
        def _(side=side):
            for y in far_first():
                signal(side, y)
            for j in range(2, count_y - 1):
                signal(gx, lax.rem(gy + j, count_y))

    signal(gx, front)
    signal(gx, back)
    for is_plane, side in ((left_plane, below), (right_plane, above)):
        @pl.when(jnp.logical_not(is_plane))
        def _(side=side):
            signal(side, front)
            signal(side, back)
            signal(side, gy)

    lane = lax.broadcasted_iota(jnp.int32, (16, WIDE), 1)
    place = lax.rem(lane, NZ)
    lane4 = lax.broadcasted_iota(jnp.int32, (16, 512), 1)
    place4 = lax.rem(jnp.where(lane4 < 448, lane4, lane4 - 464), NZ)
    lane1 = lax.broadcasted_iota(jnp.int32, (16, 128), 1)
    lane5 = lax.broadcasted_iota(jnp.int32, (24, 640), 1)
    place5 = lax.rem(jnp.where(lane5 < 512, lane5, lane5 + 8), NZ)
    place6 = lax.rem(lax.broadcasted_iota(jnp.int32, (8, 768), 1), NZ)

    def pack_phase(r):
        for b in range(3):
            cut = slice(b * 128, b * 128 + 128)
            to_x[0, 8 * b + 5:8 * b + 7, :] = ext[10:12, cut]
            to_x[1, 8 * b + 5:8 * b + 7, :] = ext[0:2, cut]

    def remote(src, dst, r, sem, x, y, sent=send_sem):
        pltpu.make_async_remote_copy(
            src_ref=src, dst_ref=dst, send_sem=sent.at[r], recv_sem=sem.at[r],
            device_id=(x, y), device_id_type=MESH,
        ).start()

    def rows_of(r):
        y_rows, strip, corners = {0: (48, 48, 16), 1: (16, 24, 0), 2: (48, 64, 16)}[r]
        return y_rows, strip, 2 * y_rows, strip + corners

    def side_start(kind, r, on_left_plane):
        _, _, first, size = rows_of(r)
        return first if kind == 0 else jnp.where(on_left_plane, first, first + size)

    def land(buffer, start, size):
        return buffer.at[pl.ds(start, size)]

    def landing(r):
        return {0: wide, 1: got, 2: last}[r]

    def send_x(r, strips, corners):
        buffer = landing(r)
        _, strip, first, size = rows_of(r)
        n = r
        for kind, is_plane, side in ((0, right_plane, above), (1, left_plane, below)):
            @pl.when(is_plane)
            def _(kind=kind, side=side):
                place = pl.multiple_of(first + size + gy * strip, 8)
                for y in far_first():
                    remote(strips(kind), land(buffer, place, strip), n, plane_sem, side, y)

            @pl.when(jnp.logical_not(is_plane))
            def _(kind=kind, side=side):
                place = side_start(kind, r, lax.rem(side, SPAN) == 0)
                for k, y in ((0, front), (1, back)):
                    if r != 1:
                        spot = land(buffer, pl.multiple_of(place + strip + 8 * k, 8), 8)
                        remote(corners(2 * kind + k), spot, n, near_sem, side, y)
                    else:
                        spot = got_corner.at[2 * kind + k]
                        remote(corners(2 * kind + k), spot, n, corner_sem, side, y, corner_send)
                remote(strips(kind), land(buffer, pl.multiple_of(place, 8), strip), n, near_sem, side, gy)

    def send_y(r, messages):
        size = rows_of(r)[0]
        n = r
        for k, y in ((0, front), (1, back)):
            remote(messages(k), land(landing(r), k * size, size), n, near_sem, gx, y)

    def wait_for(ref, sem):
        pltpu.make_async_copy(ref, ref, sem).wait()

    def run_of(r):
        _, strip, first, size = rows_of(r)
        return first + size, first + 2 * size, count_y * strip + (8, 0, 16)[r] * (count_y - 1)

    def wait_corners(r, sem):
        for is_kind, start, size in (
            (left_plane, 2, 2), (right_plane, 0, 2), (jnp.logical_not(any_plane), 0, 4)
        ):
            @pl.when(is_kind)
            def _(start=start, size=size):
                wait_for(got_corner.at[pl.ds(start, size)], sem.at[r])

    def wait_sent(r):
        buffer, n = landing(r), r
        short, near, crossing = run_of(r)

        @pl.when(any_plane)
        def _():
            wait_for(land(buffer, 0, short + crossing), send_sem.at[n])

        @pl.when(jnp.logical_not(any_plane))
        def _():
            wait_for(land(buffer, 0, near), send_sem.at[n])

        if r == 1:
            wait_corners(r, corner_send)

    def wait_near(r):
        buffer, n = landing(r), r
        short, near, _ = run_of(r)

        @pl.when(any_plane)
        def _():
            wait_for(land(buffer, 0, short), near_sem.at[n])

        @pl.when(jnp.logical_not(any_plane))
        def _():
            wait_for(land(buffer, 0, near), near_sem.at[n])

        if r == 1:
            wait_corners(r, corner_sem)

    def wait_plane(r):
        short, _, crossing = run_of(r)
        wait_for(land(landing(r), short, crossing), plane_sem.at[r])

    def window_of(held, turn):
        start = ((gy * 16 - turn - 4) & (16 * count_y - 1)) * NZ
        first, offset = start >> 7, start & 127
        window = jnp.concatenate([held[first + i] for i in range(6)], axis=1)
        return pltpu.roll(window, 768 - 4 * NZ - offset, 1)

    def view_b(kind, shift):
        return window_of(ring_b, shift if kind == 0 else -shift - 1)

    def close_ring(r):
        first = run_of(r)[0]
        for b in range(blocks + 4):
            row = first + 8 * (b % blocks)
            ring[b] = got[row:row + 8]

    def view(kind, shift):
        low = shift if kind == 0 else -shift - 1
        near, far = (0.75, 0.25) if kind == 0 else (0.25, 0.75)
        start = ((gy * 16 - low - 3) & (16 * count_y - 1)) * NZ
        first, offset = start >> 7, start & 127
        window = jnp.concatenate([ring[first + i] for i in range(5)], axis=1)
        window = pltpu.roll(window, 640 - 3 * NZ - offset, 1)
        return near * window + far * rolled(window, NZ, 1)

    def patch_y(k, packed):
        cut = slice(0, 128) if k == 0 else slice(256, 384)
        keep = lane1 < NZ if k == 0 else lane1 >= 128 - NZ
        for i, slot in enumerate(plus_y if k == 0 else minus_y):
            part = rolled(packed, -i * NZ if k == 0 else i * NZ, 1)
            f[slot, :, cut] = jnp.where(keep, part, f[slot, :, cut])

    def patch_x(kind, strip):
        edge = 0 if kind == 0 else ROWS - 1
        for i, slot in enumerate(up_slots if kind == 0 else down_slots):
            f[slot, edge:edge + 1, :] = strip[i:i + 1, :WIDE]

    def receive(r, step):
        wait_near(r)
        for k in (0, 1):
            patch_y(k, got[16 * k:16 * k + 16])
        ext[0:12, 384:512] = jnp.where(
            lane1 < 64, phase_part(1, got[16:32]), phase_part(0, got[0:16])
        )[:12]
        for kind, is_plane, _ in sides:
            @pl.when(jnp.logical_not(is_plane))
            def _(kind=kind):
                outer = 14 - 2 * kind
                near_row = 15 - 3 * kind
                e = (0, ROWS - 1)[kind]
                place = pl.multiple_of(side_start(kind, 1, left_plane), 8)
                strip = jnp.concatenate([got[pl.ds(place + 8 * b, 8)] for b in range(3)], axis=1)
                first, last = got_corner[2 * kind], got_corner[2 * kind + 1]
                plus = rolled(strip, NZ, 1)
                minus = rolled(strip, -NZ, 1)
                slots = up_slots if kind == 0 else down_slots
                for i in range(3):
                    f[slots[i], e:e + 1, :] = strip[i:i + 1]
                head = jnp.where(lane1[:1] < NZ, first, plus[3:4, 0:128])
                tail = jnp.where(lane1[:1] >= 128 - NZ, last, minus[4:5, 256:384])
                f[slots[3], e:e + 1, 0:128] = head
                f[slots[3], e:e + 1, 128:384] = plus[3:4, 128:384]
                f[slots[4], e:e + 1, 0:256] = minus[4:5, 0:256]
                f[slots[4], e:e + 1, 256:384] = tail
                ext[outer:outer + 2, 0:WIDE] = strip[5:7]
                ext[near_row:near_row + 1, WIDE:512] = jnp.where(lane1[:1] < 64, last, first)

        for kind, is_plane, place_of in sides:
            @pl.when(is_plane)
            def _(kind=kind, place_of=place_of):
                outer = 14 - 2 * kind
                wait_plane(r)
                close_ring(r)
                patch_x(kind, strip_moved(view(kind, shifts[step, place_of])))
                phase = view(kind, shifts[jnp.minimum(step + 1, STEPS - 1), place_of])
                ext[outer:outer + 2, 0:WIDE] = phase[5:7, 0:WIDE]
                ext[outer:outer + 2, WIDE:512] = jnp.where(
                    lane1[:2] < 64, phase[5:7, 384:512], phase[5:7, 512:640]
                )

    def momentum(f):
        density = f[0]
        for slot in range(1, 19):
            density = density + f[slot]
        totals = []
        for axis in range(3):
            total = None
            for slot in range(1, 19, 2):
                sign = lattice_vel[slot][axis]
                if sign != 0:
                    pair = f[slot] - f[slot + 1]
                    if total is None:
                        total = pair
                    else:
                        total = total + pair if sign == 1 else total - pair
            totals.append(total)
        return density, totals

    def advance(r):
        p = ext[...]
        around = differences(p, place4)
        chem = bulk(p, around)
        slope = [0.5 * (a - b)[:, :WIDE] for a, b in around]
        around = [(a[:, :WIDE], b[:, :WIDE]) for a, b in differences(chem, place4)]
        bend = bent(chem[:, :WIDE], around)
        own = p[:, :WIDE]
        density, totals = momentum(f)
        inverse = 1.0 / density
        scaled = (-0.5 * coupling / relax_rate) * own
        next_phase = own + mobility * bend
        drift = []
        for axis in range(3):
            next_phase = next_phase - totals[axis] * inverse * slope[axis]
            drift.append((totals[axis] + scaled * (around[axis][0] - around[axis][1])) * inverse)
        ext[0:12, 0:WIDE] = next_phase[:12]
        if r == 1:
            pack_phase(r)
        collide(density, drift, r, lambda slot: f[slot])

    def collide(density, drift, r, source):
        base = 1.0 - 1.5 * (drift[0] * drift[0] + drift[1] * drift[1] + drift[2] * drift[2])
        weight = relax_rate / 36.0 * density
        keep = 1.0 - relax_rate
        packs = {}

        def put(slot, post):
            step_x, step_y, step_z = lattice_vel[slot]
            if r == 2:
                fx[slot, :, 0:WIDE] = post
                return
            value = rolled(post, step_x, 0)
            moved = moved_yz(value, step_y, step_z, place)
            f[slot] = moved
            if r is None:
                return
            if step_x != 0:
                kind = 0 if step_x == 1 else 1
                i = (up_slots, down_slots)[kind].index(slot)
                line = 12 if step_x == 1 else 15
                shown = value if step_y != 0 else moved
                for b in range(3):
                    to_x[kind, 8 * b + i:8 * b + i + 1, :] = shown[line:line + 1, b * 128:b * 128 + 128]
                if step_y != 0:
                    k = 2 * kind + (0 if step_y == 1 else 1)
                    cut = slice(0, 128) if step_y == 1 else slice(256, 384)
                    edge = 11 if step_x == 1 else 0
                    own = ext[edge:edge + 1, slice(256, 384) if step_y == 1 else slice(0, 128)]
                    post_row = moved[line:line + 1, cut]
                    low = lane1[:1] < 64
                    to_corner[k] = (
                        jnp.where(low, post_row, own) if step_y == 1 else jnp.where(low, own, post_row)
                    )
            if step_y == 1:
                i = plus_y.index(slot)
                part = rolled(moved[:, 0:128], i * NZ, 1)
                mine = (lane1 >= i * NZ) & (lane1 < i * NZ + NZ)
                packs[0] = jnp.where(mine, part, packs[0]) if 0 in packs else part
            if step_y == -1:
                i = minus_y.index(slot)
                part = rolled(moved[:, 256:384], -i * NZ, 1)
                mine = (lane1 < 128 - i * NZ) & (lane1 >= 128 - NZ - i * NZ)
                packs[1] = jnp.where(mine, part, packs[1]) if 1 in packs else part

        def put_pair(slot):
            along = None
            for axis in range(3):
                sign = lattice_vel[slot][axis]
                if sign != 0:
                    if along is None:
                        along = drift[axis]
                    else:
                        along = along + drift[axis] if sign == 1 else along - drift[axis]
            scale = 2.0 * weight if slot < 7 else weight
            even = scale * (base + 4.5 * along * along)
            odd = scale * (3.0 * along)
            here, there = source(slot), source(slot + 1)
            put(slot, keep * here + (even + odd))
            put(slot + 1, keep * there + (even - odd))

        for slot in (1, 7, 9, 11, 13):
            put_pair(slot)
        if r == 1:
            send_x(r, lambda kind: to_x.at[kind], lambda k: to_corner.at[k])
        for slot in (3, 15, 17):
            put_pair(slot)
        if r == 1:
            for k in (0, 1):
                to_y[k] = with_phase(k, packs[k], ext[0:16, 256:384] if k == 0 else ext[0:16, 0:128])
            send_y(r, lambda k: to_y.at[k])
        put_pair(5)
        put(0, keep * source(0) + 12.0 * weight * base)

    for slot in range(19):
        f[slot, 0:12, :] = f_in[slot]
        f[slot, 12:16, :] = jnp.ones((4, WIDE), jnp.float32)
    ext[...] = jnp.zeros_like(ext)
    e_p[...] = jnp.zeros_like(e_p)
    e_r[...] = jnp.ones_like(e_r)
    e_u[...] = jnp.zeros_like(e_u)
    e_p[0:12, 0:WIDE] = p_in[...]
    density, totals = momentum(f)
    e_r[0:12, 0:WIDE] = density[:12]
    for axis in range(3):
        e_u[axis, 0:12, 0:WIDE] = (totals[axis] / density)[:12]

    for kind in (0, 1):
        edge, second, low = ((11, 10, 8), (0, 1, 0))[kind]
        for b in range(3):
            cut = slice(b * 128, b * 128 + 128)
            out_x[kind, 16 * b:16 * b + 4, :] = e_p[low:low + 4, cut]
            out_x[kind, 16 * b + 4:16 * b + 5, :] = e_r[edge:edge + 1, cut]
            for axis in range(3):
                out_x[kind, 16 * b + 5 + axis:16 * b + 6 + axis, :] = e_u[axis, edge:edge + 1, cut]
                out_x[kind, 16 * b + 13 + axis:16 * b + 14 + axis, :] = e_u[axis, second:second + 1, cut]
            for i, slot in enumerate(up_slots if kind == 0 else down_slots):
                out_x[kind, 16 * b + 8 + i:16 * b + 9 + i, :] = f[slot, edge:edge + 1, cut]
        third = (9, 0)[kind]
        for k in (2 * kind, 2 * kind + 1):
            cut = slice(256, 384) if k % 2 == 0 else slice(0, 128)
            out_corner[k, 0:3, :] = e_p[third:third + 3, cut]
            out_corner[k, 3:4, :] = e_r[edge:edge + 1, cut]
            for axis in range(3):
                out_corner[k, 4 + axis:5 + axis, :] = e_u[axis, edge:edge + 1, cut]
            slot = (up_slots if kind == 0 else down_slots)[3 + k % 2]
            out_corner[k, 7:8, :] = f[slot, edge:edge + 1, cut]
    for k in (0, 1):
        cut = slice(256, 384) if k == 0 else slice(0, 128)
        low = lane1[:12] < 64
        if k == 0:
            pair = lambda a, b: jnp.where(low, pltpu.roll(b, 64, 1), a)
        else:
            pair = lambda a, b: jnp.where(low, a, pltpu.roll(b, 64, 1))
        packed = None
        for i, slot in enumerate(plus_y if k == 0 else minus_y):
            block = f[slot, :, cut]
            part = rolled(block, NZ + i * NZ if k == 0 else -NZ - i * NZ, 1)
            if i == 0:
                packed = part
            else:
                packed = jnp.where(lane1 >= i * NZ if k == 0 else lane1 < 128 - i * NZ, part, packed)
        out_y[k, 0:12, :] = packed[:12]
        out_y[k, 12:24, :] = e_p[0:12, cut]
        out_y[k, 24:36, :] = pair(e_r[0:12, cut], e_u[0, 0:12, cut])
        out_y[k, 36:48, :] = pair(e_u[1, 0:12, cut], e_u[2, 0:12, cut])

    @pl.when(left_plane)
    def _():
        for b in range(3):
            out_a[2 * b:2 * b + 2, :] = e_p[0:2, b * 128:b * 128 + 128]

    @pl.when(right_plane)
    def _():
        for b in range(3):
            out_a[2 * b:2 * b + 2, :] = e_p[10:12, b * 128:b * 128 + 128]

    pl.semaphore_wait(barrier, jnp.where(any_plane, 5 + count_y + max(count_y - 3, 0), 8))

    send_x(0, lambda kind: out_x.at[kind], lambda k: out_corner.at[k])

    @pl.when(any_plane)
    def _():
        start = run_of(0)[0] + count_y * 48
        for j in range(1, count_y):
            remote(out_a, land(wide, start + 8 * (j - 1), 8), 0, plane_sem, gx, lax.rem(gy + j, count_y))

    send_y(0, lambda k: out_y.at[k])

    wait_near(0)
    for k in (0, 1):
        at = 48 * k
        cut = slice(512, 640) if k == 0 else slice(384, 512)
        e_p[0:12, cut] = wide[at + 12:at + 24]
        e_r[0:12, cut] = wide[at + 24:at + 36]
        e_u[0, 0:12, cut] = pltpu.roll(wide[at + 24:at + 36], 64, 1)
        e_u[1, 0:12, cut] = wide[at + 36:at + 48]
        e_u[2, 0:12, cut] = pltpu.roll(wide[at + 36:at + 48], 64, 1)
    for kind, is_plane, place_of in sides:
        low = (20, 12)[kind]
        edge, second, third = ((23, 22, 21), (12, 13, 12))[kind]

        @pl.when(jnp.logical_not(is_plane))
        def _(kind=kind, low=low, edge=edge, second=second, third=third):
            place = pl.multiple_of(side_start(kind, 0, left_plane), 8)
            for k in (0, 1):
                corner = wide[pl.ds(place + 48 + 8 * k, 8)]
                cut = slice(512, 640) if k == 0 else slice(384, 512)
                e_p[third:third + 3, cut] = corner[0:3]
                e_r[edge:edge + 1, cut] = corner[3:4]
                for axis in range(3):
                    e_u[axis, edge:edge + 1, cut] = corner[4 + axis:5 + axis]
            for b in range(3):
                cut = slice(b * 128, b * 128 + 128)
                strip = wide[pl.ds(place + 16 * b, 16)]
                e_p[low:low + 4, cut] = strip[0:4]
                e_r[edge:edge + 1, cut] = strip[4:5]
                for axis in range(3):
                    e_u[axis, edge:edge + 1, cut] = strip[5 + axis:6 + axis]
                    e_u[axis, second:second + 1, cut] = strip[13 + axis:14 + axis]

    for kind, is_plane, place_of in sides:
        @pl.when(is_plane)
        def _(kind=kind, place_of=place_of):
            wait_plane(0)
            start = run_of(0)[0]
            for b in range(blocks + 5):
                row = start + 16 * (b % blocks)
                ring_b[b] = wide[row:row + 16]
            start = start + 16 * blocks
            a_row = (4, 6)[kind]
            for j in range(count_y):
                source = lax.rem(gy + count_y - j, count_y)
                for b in range(3):
                    row = start + 8 * (j - 1) + 2 * b
                    piece = out_a[2 * b:2 * b + 2, :] if j == 0 else wide[row:row + 2]
                    ring_a[source * 3 + b, a_row:a_row + 2, :] = piece
            for b in range(5):
                ring_a[blocks + b] = ring_a[b]
            shift = shifts[0, place_of]
            near = view_b(kind, shift)[0:8]
            phase = (near * 0.75 + rolled(near, NZ, 1) * 0.25) if kind == 0 else (
                near * 0.25 + rolled(near, NZ, 1) * 0.75)
            row, at = ((22, 2), (12, 0))[kind]
            e_p[row:row + 2, 0:512] = phase[at:at + 2, 0:512]
            e_p[row:row + 2, 512:640] = phase[at:at + 2, 640:768]

    p = e_p[...]
    around = differences(p, place5)
    chem = bulk(p, around)
    slope = [0.5 * (a - b) for a, b in around]
    around = differences(chem, place5)
    next_phase = p + mobility * bent(chem, around)
    scaled = (-0.5 * coupling / relax_rate) * p / e_r[...]
    drift = []
    for axis in range(3):
        flow = e_u[axis]
        next_phase = next_phase - flow * slope[axis]
        drift.append(flow + scaled * (around[axis][0] - around[axis][1]))
    for top, at, size in ((0, 0, 12), (12, 12, 2), (14, 22, 2)):
        ext[top:top + size, 0:WIDE] = next_phase[at:at + size, 0:WIDE]
        ext[top:top + size, WIDE:512] = jnp.where(
            lane1[:size] < 64, next_phase[at:at + size, 384:512], next_phase[at:at + size, 512:640]
        )
    collide(e_r[0:16, 0:WIDE], [d[0:16, 0:WIDE] for d in drift], None, lambda slot: f[slot])
    for k in (0, 1):
        cut = slice(512, 640) if k == 0 else slice(384, 512)
        patch_y(k, packed_post(k, wide[48 * k:48 * k + 16], e_r[0:16, cut], [d[0:16, cut] for d in drift], lane1))
    for kind, is_plane, place_of in sides:
        @pl.when(is_plane)
        def _(kind=kind, place_of=place_of):
            first = shifts[0, place_of]
            row = lax.broadcasted_iota(jnp.int32, (8, 768), 0)
            edge, at, outer = ((3, 2, 14), (0, 0, 12))[kind]
            weights_of = ((0.75, 0.25), (0.25, 0.75))[kind]
            for step in (0, 1):
                shift = shifts[step, place_of]
                both = view_b(kind, shift)
                turn = shift - first if kind == 0 else first - shift - 1
                own = window_of(ring_a, turn)
                own = 0.75 * own + 0.25 * rolled(own, -NZ if kind == 0 else NZ, 1)
                far_p = jnp.where(row < 4, both[0:8], own)
                around = differences(far_p, place6)
                chem = bulk(far_p, around)
                slope = [0.5 * (a - b) for a, b in around]
                around = differences(chem, place6)
                if step == 0:
                    density = both[4:5]
                    scaled = (-0.5 * coupling / relax_rate) * far_p[edge:edge + 1] / density
                    drift = [
                        both[5 + axis:6 + axis]
                        + scaled * (around[axis][0] - around[axis][1])[edge:edge + 1]
                        for axis in range(3)
                    ]
                    strip = strip_post(kind, both[8:16], density, drift, place6)
                    strip = weights_of[0] * strip + weights_of[1] * rolled(strip, NZ, 1)
                    patch_x(kind, strip_moved(strip))
                else:
                    after = far_p + mobility * bent(chem, around)
                    for axis in range(3):
                        flow = jnp.where(row == edge, both[5 + axis:6 + axis], both[13 + axis:14 + axis])
                        after = after - flow * slope[axis]
                    after = weights_of[0] * after + weights_of[1] * rolled(after, NZ, 1)
                    ext[outer:outer + 2, 0:WIDE] = after[at:at + 2, 0:WIDE]
                    ext[outer:outer + 2, WIDE:512] = jnp.where(
                        lane1[:2] < 64, after[at:at + 2, 384:512], after[at:at + 2, 640:768]
                    )

        @pl.when(jnp.logical_not(is_plane))
        def _(kind=kind):
            edge = (23, 12)[kind]
            place = pl.multiple_of(side_start(kind, 0, left_plane), 8)
            strip = jnp.concatenate(
                [wide[pl.ds(place + 16 * b + 8, 8)] for b in range(3)]
                + [jnp.broadcast_to(wide[pl.ds(place + 48 + 8 * i, 8)][7:8], (8, 128)) for i in (1, 0)],
                axis=1,
            )
            strip = strip_post(
                kind, strip, e_r[edge:edge + 1, :], [d[edge:edge + 1] for d in drift], place5[:8]
            )
            patch_x(kind, strip_moved(strip))

    advance(1)
    wait_sent(0)
    receive(1, 1)

    advance(2)
    y_cut = (slice(256, 384), slice(0, 128))
    lines = [fx[group[0], edge:edge + 1, 0:WIDE] for edge in (11, 0) for group in x_groups]
    halves = 0.5 * jnp.concatenate(lines + lines[:2], axis=0)
    ahead, behind = moved_yz(halves, 0, -1, place[:8]), moved_yz(halves, 0, 1, place[:8])
    for kind in (0, 1):
        edge, second, low = ((11, 10, 9), (0, 1, 0))[kind]
        inward = (up_slots, down_slots)[kind]
        for b in range(3):
            cut = slice(b * 128, b * 128 + 128)
            for i, slot in enumerate(inward):
                last_x[kind, 19 * b + i:19 * b + i + 1, :] = fx[slot, edge:edge + 1, cut]
                last_x[kind, 19 * b + 11 + i:19 * b + 12 + i, :] = fx[slot, second:second + 1, cut]
            for i, (first, slot) in enumerate(folded_x):
                at = x_groups.index(next(g for g in x_groups if g[0] == first)) + 3 * kind
                half = (ahead if lattice_vel[slot][2] == 1 else behind)[at:at + 1, cut]
                last_x[kind, 19 * b + 5 + i:19 * b + 6 + i, :] = fx[slot, edge:edge + 1, cut] + half
            last_x[kind, 19 * b + 16:19 * b + 19, :] = ext[low:low + 3, cut]
        for k in (0, 1):
            units = corner_units(kind, k)
            for i in range(0, len(units), 5):
                line = None
                for j, (slot, deep_x, deep_y) in enumerate(units[i:i + 5]):
                    row = 12 - deep_x if kind == 0 else deep_x - 1
                    part = ext[row:row + 1, y_cut[k]] if slot is None else fx[slot, row:row + 1, y_cut[k]]
                    part = rolled(part, NZ * j - lane_of(k, deep_y), 1)
                    line = part if j == 0 else jnp.where(lane1[:1] >= NZ * j, part, line)
                last_corner[2 * kind + k, i // 5:i // 5 + 1, :] = line
    for is_plane, edge, slots in ((left_plane, 0, down_slots), (right_plane, 11, up_slots)):
        @pl.when(is_plane)
        def _(edge=edge, slots=slots):
            for b in range(3):
                for i, slot in enumerate(slots):
                    last_a[5 * b + i:5 * b + i + 1, :] = fx[slot, edge:edge + 1, b * 128:b * 128 + 128]

    send_x(2, lambda kind: last_x.at[kind], lambda k: last_corner.at[k])

    @pl.when(any_plane)
    def _():
        start = run_of(2)[0] + count_y * 64
        for j in range(1, count_y):
            remote(last_a, land(last, start + 16 * (j - 1), 16), 2, plane_sem, gx, lax.rem(gy + j, count_y))

    for k in (0, 1):
        spots = lax.rem(lane1 + (16 if k == 0 else 0), NZ)
        for i in range(0, len(y_units[k]), 5):
            line = None
            for j, (slot, deep) in enumerate(y_units[k][i:i + 5]):
                part = ext[0:16, y_cut[k]] if slot is None else fx[slot, :, y_cut[k]]
                for first, folded in folded_y:
                    if folded == slot:
                        part = part + moved_yz(0.5 * fx[first, :, y_cut[k]], 0, -lattice_vel[slot][2], spots)
                part = rolled(part, NZ * j - lane_of(k, deep), 1)
                line = part if j == 0 else jnp.where(lane1 >= NZ * j, part, line)
            last_y[k, 12 * (i // 5):12 * (i // 5) + 12, :] = line[:12]
    send_y(2, lambda k: last_y.at[k])
    e_p[0:12, 0:WIDE] = ext[0:12, 0:WIDE]
    wait_sent(1)

    wait_near(2)

    def unit_of_y(k, slot, deep):
        place = y_units[k].index((slot, deep))
        row = 48 * k + 12 * (place // 5)
        return rolled(last[row:row + 12], lane_of(k, deep) - NZ * (place % 5), 1)

    lane12 = lane1[:12]
    for slot in range(19):
        step_y = lattice_vel[slot][1]
        if any(slot == group[0] for group in y_groups):
            rim = jnp.zeros((12, 128), jnp.float32)
        elif step_y == 0:
            rim = jnp.where(lane12 < 64, unit_of_y(1, slot, 1), unit_of_y(0, slot, 1))
        elif step_y == 1:
            rim = jnp.where(lane12 >= 104, unit_of_y(0, slot, 1), unit_of_y(0, slot, 2))
        else:
            rim = jnp.where(lane12 < NZ, unit_of_y(1, slot, 1), unit_of_y(1, slot, 2))
        fx[slot, 0:12, 384:512] = rim
    e_p[0:12, 384:512] = jnp.where(
        lane12 < NZ, unit_of_y(1, None, 1),
        jnp.where(lane12 < 2 * NZ, unit_of_y(1, None, 2), unit_of_y(1, None, 3)),
    )
    e_p[0:12, 512:640] = jnp.where(
        lane12 >= 104, unit_of_y(0, None, 1),
        jnp.where(lane12 >= 80, unit_of_y(0, None, 2), unit_of_y(0, None, 3)),
    )
    for kind, is_plane, place_of in sides:
        @pl.when(jnp.logical_not(is_plane))
        def _(kind=kind):
            place = pl.multiple_of(side_start(kind, 2, left_plane), 8)
            rows = ((15, 14), (12, 13))[kind]
            low = (21, 12)[kind]
            inward = (up_slots, down_slots)[kind]
            whole = last[pl.ds(place, 64)]
            for group in x_groups:
                fx[group[0], rows[0]:rows[0] + 1, 0:WIDE] = jnp.zeros((1, WIDE), jnp.float32)
            for b in range(3):
                cut = slice(b * 128, b * 128 + 128)
                strip = whole[19 * b:19 * b + 19]
                for i, slot in enumerate(inward):
                    fx[slot, rows[0]:rows[0] + 1, cut] = strip[i:i + 1]
                    fx[slot, rows[1]:rows[1] + 1, cut] = strip[11 + i:12 + i]
                for i, (_, slot) in enumerate(folded_x):
                    fx[slot, rows[0]:rows[0] + 1, cut] = strip[5 + i:6 + i]
                e_p[low:low + 3, cut] = strip[16:19]
            found = {}
            for k in (0, 1):
                corner = last[pl.ds(place + 64 + 8 * k, 8)]
                for i, (slot, deep_x, deep_y) in enumerate(corner_units(kind, k)):
                    part = corner[i // 5:i // 5 + 1]
                    part = rolled(part, lane_of(k, deep_y) - NZ * (i % 5), 1)
                    found.setdefault((slot, deep_x), []).append((k, deep_y, part))
            for (slot, deep_x), parts in found.items():
                line = {}
                for k, deep_y, part in parts:
                    start = lane_of(k, deep_y)
                    here = (lane1[:1] >= start) & (lane1[:1] < start + NZ)
                    at = k if slot is None else 0
                    line[at] = jnp.where(here, part, line[at]) if at in line else part
                if slot is None:
                    row = 24 - deep_x if kind == 0 else 11 + deep_x
                    e_p[row:row + 1, 512:640] = line[0]
                    e_p[row:row + 1, 384:512] = line[1]
                else:
                    row = rows[deep_x - 1]
                    fx[slot, row:row + 1, 384:512] = line[0]

    def mixed(kind, value):
        near, far = ((0.75, 0.25), (0.25, 0.75))[kind]
        return near * value + far * rolled(value, NZ, 1)

    for kind, is_plane, place_of in sides:
        @pl.when(is_plane)
        def _(kind=kind, place_of=place_of):
            wait_plane(2)
            start = run_of(2)[0]
            for b in range(blocks + 5):
                row = start + 64 * (b % blocks // 3) + 19 * (b % 3)
                ring_e[b, 0:19] = last[row:row + 19]
            start = start + 64 * count_y
            for j in range(count_y):
                source = lax.rem(gy + count_y - j, count_y)
                for b in range(3):
                    row = start + 16 * (j - 1) + 5 * b
                    ring_o[source * 3 + b, 0:5] = last_a[5 * b:5 * b + 5, :] if j == 0 else last[row:row + 5]
            for b in range(5):
                ring_o[blocks + b] = ring_o[b]
            row = (15, 12)[kind]
            shift = shifts[2, place_of]
            strip = mixed(kind, window_of(ring_e, shift if kind == 0 else -shift - 1)[0:8])
            for i, slot in enumerate((up_slots, down_slots)[kind]):
                fx[slot, row:row + 1, 0:384] = strip[i:i + 1, 0:384]
                fx[slot, row:row + 1, 384:512] = jnp.where(
                    lane1[:1] < 64, strip[i:i + 1, 384:512], strip[i:i + 1, 640:768]
                )
            shift = shifts[3, place_of]
            phase = mixed(kind, window_of(ring_e, shift if kind == 0 else -shift - 1)[16:24])
            row, at = ((22, 1), (12, 0))[kind]
            e_p[row:row + 2, 0:512] = phase[at:at + 2, 0:512]
            e_p[row:row + 2, 512:640] = phase[at:at + 2, 640:768]

    def narrowed(to, value):
        for top, at, size in ((0, 0, 12), (12, 12, 2), (14, 22, 2)):
            to[top:top + size, 0:WIDE] = value[at:at + size, 0:WIDE]
            to[top:top + size, WIDE:512] = jnp.where(
                lane1[:size] < 64, value[at:at + size, 384:512], value[at:at + size, 512:640]
            )

    for slot in range(19):
        step_x, step_y, step_z = lattice_vel[slot]
        fx[slot] = moved_yz(rolled(fx[slot], step_x, 0), step_y, step_z, place4)
    p = e_p[...]
    narrowed(ext, p)
    narrowed(chem_x, bulk(p, differences(p, place5)))
    density, totals = momentum(fx)
    inverse = 1.0 / density
    p, chem = ext[...], chem_x[...]
    around = differences(p, place4)
    slope = [0.5 * (a - b)[:, :WIDE] for a, b in around]
    around = differences(chem, place4)
    next_phase = (p + mobility * bent(chem, around))[:, :WIDE]
    scaled = (-0.5 * coupling / relax_rate) * p
    drift = []
    for axis in range(3):
        next_phase = next_phase - (totals[axis] * inverse)[:, :WIDE] * slope[axis]
        drift.append((totals[axis] + scaled * (around[axis][0] - around[axis][1])) * inverse)
    p_out[...] = next_phase[:12]
    collide(density[:, :WIDE], [d[:, :WIDE] for d in drift], None, lambda slot: fx[slot, :, 0:WIDE])
    for k in (0, 1):
        here = None
        for i, slot in enumerate((plus_y, minus_y)[k]):
            part = rolled(fx[slot, :, 384:512], NZ + NZ * i if k == 0 else 104 - NZ * i, 1)
            if i == 0:
                here = part
            else:
                here = jnp.where(lane1 >= NZ * i if k == 0 else lane1 < 128 - NZ * i, part, here)
        rim = [d[:, 384:512] for d in drift]
        patch_y(k, packed_post(k, here, density[:, 384:512], rim, lane1))
    for kind, is_plane, place_of in sides:
        @pl.when(is_plane)
        def _(kind=kind, place_of=place_of):
            before, shift = shifts[2, place_of], shifts[3, place_of]
            edge, top, a_row, own_row = ((3, 1, 4, 0), (0, 0, 6, 10))[kind]
            far = window_of(ring_e, shift if kind == 0 else -shift - 1)
            inner = strip_moved(strip_along_z(kind, far[11:19], place6))
            turn = shift - before if kind == 0 else before - shift - 1
            outer = window_of(ring_o, turn)
            outer = 0.75 * outer + 0.25 * rolled(outer, -NZ if kind == 0 else NZ, 1)
            outer = strip_moved(strip_along_z(1 - kind, outer, place6))
            total = [None] * 4
            sign = 1.0 - 2.0 * kind
            for tile, way in ((inner, sign), (outer, -sign)):
                r = [tile[i:i + 1] for i in range(5)]
                whole = r[0] + r[1] + r[2] + r[3] + r[4]
                found = (whole, way * whole, r[3] - r[4], way * (r[1] - r[2]))
                total = [b if a is None else a + b for a, b in zip(total, found)]
            for i, (_, slot) in enumerate(folded_x):
                _, step_y, step_z = lattice_vel[slot]
                line = moved_yz(far[5 + i:6 + i], step_y, step_z, place6[:1])
                total[0] = total[0] + line
                if step_y != 0:
                    total[2] = total[2] + step_y * line
                if step_z != 0:
                    total[3] = total[3] + step_z * line
            tile_a[...] = jnp.zeros_like(tile_a)
            tile_a[a_row:a_row + 2, 0:512] = e_p[own_row:own_row + 2, 0:512]
            tile_a[a_row:a_row + 2, 640:768] = e_p[own_row:own_row + 2, 512:640]
            own = tile_a[...]
            ahead = rolled(own, -NZ, 1)
            own = 0.75 * own + 0.25 * ahead if kind == 0 else 0.25 * own + 0.75 * ahead
            row = lax.broadcasted_iota(jnp.int32, (8, 768), 0)
            far_p = jnp.where(row < 4, rolled(far[16:24], top, 0), own)
            around = differences(bulk(far_p, differences(far_p, place6)), place6)
            inverse = 1.0 / total[0]
            scaled = (-0.5 * coupling / relax_rate) * far_p[edge:edge + 1]
            drift = [
                (total[1 + axis] + scaled * (around[axis][0] - around[axis][1])[edge:edge + 1]) * inverse
                for axis in range(3)
            ]
            strip = mixed(kind, strip_post(kind, inner, total[0], drift, place6))
            patch_x(kind, strip_moved(strip))

        @pl.when(jnp.logical_not(is_plane))
        def _(kind=kind):
            row = (15, 12)[kind]
            inward = (up_slots, down_slots)[kind]
            lines = [fx[slot, row:row + 1, :] for slot in inward]
            strip = jnp.concatenate(lines + lines[:1] * 3, axis=0)
            strip = strip_post(
                kind, strip, density[row:row + 1], [d[row:row + 1] for d in drift], place4[:8]
            )
            patch_x(kind, strip_moved(strip))

    wait_sent(2)
    for slot in range(19):
        f_out[slot] = f[slot, 0:12, :]


def on_device(populations, phase_field, plane_shifts):
    blocks = 3 * lax.axis_size("gy")
    rounds = 3
    vmem = pl.BlockSpec(memory_space=pltpu.VMEM)
    return pl.pallas_call(
        kernel,
        out_shape=(
            jax.ShapeDtypeStruct(populations.shape, jnp.float32),
            jax.ShapeDtypeStruct(phase_field.shape, jnp.float32),
        ),
        in_specs=[pl.BlockSpec(memory_space=pltpu.SMEM), vmem, vmem],
        out_specs=(vmem, vmem),
        scratch_shapes=[
            pltpu.VMEM((19, 16, WIDE), jnp.float32),
            pltpu.VMEM((16, 512), jnp.float32),
            pltpu.VMEM((56 + 8 * blocks, 128), jnp.float32),
            pltpu.VMEM((4, 1, 128), jnp.float32),
            pltpu.VMEM((2, 24, 128), jnp.float32),
            pltpu.VMEM((2, 16, 128), jnp.float32),
            pltpu.VMEM((4, 1, 128), jnp.float32),
            pltpu.VMEM((blocks + 4, 8, 128), jnp.float32),
            pltpu.VMEM((24, 640), jnp.float32),
            pltpu.VMEM((24, 640), jnp.float32),
            pltpu.VMEM((3, 24, 640), jnp.float32),
            pltpu.VMEM((blocks + 5, 16, 128), jnp.float32),
            pltpu.VMEM((blocks + 5, 8, 128), jnp.float32),
            pltpu.VMEM((160 + 16 * blocks + 8 * (lax.axis_size("gy") - 1), 128), jnp.float32),
            pltpu.VMEM((2, 48, 128), jnp.float32),
            pltpu.VMEM((2, 48, 128), jnp.float32),
            pltpu.VMEM((4, 8, 128), jnp.float32),
            pltpu.VMEM((8, 128), jnp.float32),
            pltpu.VMEM((19, 16, 512), jnp.float32),
            pltpu.VMEM((16, 512), jnp.float32),
            pltpu.VMEM((8, 768), jnp.float32),
            pltpu.VMEM((blocks + 5, 24, 128), jnp.float32),
            pltpu.VMEM((blocks + 5, 8, 128), jnp.float32),
            pltpu.VMEM((256 + 64 * lax.axis_size("gy") + 16 * (lax.axis_size("gy") - 1), 128), jnp.float32),
            pltpu.VMEM((2, 64, 128), jnp.float32),
            pltpu.VMEM((2, 48, 128), jnp.float32),
            pltpu.VMEM((4, 8, 128), jnp.float32),
            pltpu.VMEM((16, 128), jnp.float32),
            pltpu.SemaphoreType.DMA((rounds,)),
            pltpu.SemaphoreType.DMA((rounds,)),
            pltpu.SemaphoreType.DMA((rounds,)),
            pltpu.SemaphoreType.DMA((rounds,)),
            pltpu.SemaphoreType.DMA((rounds,)),
        ],
        compiler_params=pltpu.CompilerParams(
            collective_id=0, has_side_effects=True, vmem_limit_bytes=32 * 1024 * 1024
        ),
    )(plane_shifts, populations, phase_field)


def solution(mesh):
    return jax.shard_map(
        on_device,
        mesh=mesh,
        in_specs=(P(None, "gx", "gy"), P("gx", "gy"), P()),
        out_specs=(P(None, "gx", "gy"), P("gx", "gy")),
        check_vma=False,
    )
```

```python
import functools

import jax
import jax.numpy as jnp
from jax import lax
from jax.experimental import pallas as pl
from jax.experimental.pallas import tpu as pltpu
from jax.sharding import PartitionSpec as P

STEPS = 4
NZ = 24
ROWS = 12
WIDE = 384
SPAN = 4
MESH = pl.DeviceIdType.MESH

lattice_vel = (
    (0, 0, 0),
    (1, 0, 0),
    (-1, 0, 0),
    (0, 1, 0),
    (0, -1, 0),
    (0, 0, 1),
    (0, 0, -1),
    (1, 1, 0),
    (-1, -1, 0),
    (1, -1, 0),
    (-1, 1, 0),
    (1, 0, 1),
    (-1, 0, -1),
    (1, 0, -1),
    (-1, 0, 1),
    (0, 1, 1),
    (0, -1, -1),
    (0, 1, -1),
    (0, -1, 1),
)
relax_rate = 0.8
coupling = 0.01
mobility = 0.02

up_slots = (1, 11, 13, 7, 9)
down_slots = (2, 12, 14, 10, 8)
plus_y = (3, 7, 10, 15, 17)
minus_y = (4, 8, 9, 16, 18)


x_groups = ((0, 5, 6), (3, 15, 17), (4, 18, 16))
y_groups = ((0, 5, 6), (1, 11, 13), (2, 14, 12))
folded_x = tuple((first, slot) for first, *pair in x_groups for slot in pair)
folded_y = tuple((first, slot) for first, *pair in y_groups for slot in pair)
near_y = tuple(slots + tuple(slot for _, slot in folded_y) for slots in (plus_y, minus_y))
y_units = tuple(
    tuple((slot, 1) for slot in near_y[k]) + tuple((slot, 2) for slot in (plus_y, minus_y)[k])
    + ((None, 1), (None, 2), (None, 3))
    for k in (0, 1)
)


def corner_units(kind, k):
    step = (1 - 2 * kind, 1 - 2 * k)
    units = []
    for deep in ((1, 1), (2, 1), (1, 2), (2, 2)):
        for slot in range(19):
            if all(
                lattice_vel[slot][axis] == step[axis] or (deep[axis] == 1 and lattice_vel[slot][axis] == 0)
                for axis in (0, 1)
            ):
                units.append((slot,) + deep)
    return tuple(units) + tuple((None, x, y) for x in (1, 2, 3) for y in range(1, 5 - x))


first_units = tuple(("p", x, y) for x in (1, 2, 3) for y in range(1, 5 - x)) + tuple(
    (what, 1, 1) for what in ("r", 0, 1, 2, "f")
)


def lane_of(k, depth):
    return 128 - NZ * depth if k == 0 else NZ * (depth - 1)


def rolled(value, shift, axis):
    size = value.shape[axis]
    shift = shift % size
    return value if shift == 0 else pltpu.roll(value, shift, axis)


def moved_yz(value, step_y, step_z, place):
    if step_z == 0:
        return rolled(value, step_y * NZ, 1)
    edge = 0 if step_z == 1 else NZ - 1
    inner = rolled(value, step_y * NZ + step_z, 1)
    wrap = rolled(value, step_y * NZ + step_z - step_z * NZ, 1)
    return jnp.where(place == edge, wrap, inner)


def differences(value, place):
    return (
        (rolled(value, -1, 0), rolled(value, 1, 0)),
        (rolled(value, -NZ, 1), rolled(value, NZ, 1)),
        (moved_yz(value, 0, -1, place), moved_yz(value, 0, 1, place)),
    )


def bulk(p, around):
    total = around[0][0] + around[0][1] + around[1][0] + around[1][1] + around[2][0] + around[2][1]
    return 0.5 * (p * p * p - p) - 0.5 * (total - 6.0 * p)


def bent(chem, around):
    total = around[0][0] + around[0][1] + around[1][0] + around[1][1] + around[2][0] + around[2][1]
    return total - 6.0 * chem


def relaxed(here, weight, along, drift):
    square = drift[0] * drift[0] + drift[1] * drift[1] + drift[2] * drift[2]
    return (1.0 - relax_rate) * here + weight * (
        1.0 - 1.5 * square + 3.0 * along + 4.5 * along * along
    )


def strip_post(kind, here, density, drift, place):
    sign = 1.0 - 2.0 * kind
    row = lax.broadcasted_iota(jnp.int32, here.shape, 0)
    full = [jnp.broadcast_to(d, here.shape) for d in drift]
    along = sign * full[0]
    along = along + jnp.where(row == 3, full[1], jnp.where(row == 4, -full[1], 0.0))
    along = along + jnp.where(row == 1, sign * full[2], jnp.where(row == 2, -sign * full[2], 0.0))
    weight = jnp.where(row == 0, 2.0, 1.0) * (relax_rate / 36.0) * density
    post = relaxed(here, weight, along, full)
    return strip_along_z(kind, post, place)


def strip_along_z(kind, strip, place):
    row = lax.broadcasted_iota(jnp.int32, strip.shape, 0)
    first, second = (1, -1) if kind == 0 else (-1, 1)
    return jnp.where(
        row == 1, moved_yz(strip, 0, first, place), jnp.where(row == 2, moved_yz(strip, 0, second, place), strip)
    )


def strip_moved(strip):
    row = lax.broadcasted_iota(jnp.int32, strip.shape, 0)
    return jnp.where(row == 3, rolled(strip, NZ, 1), jnp.where(row == 4, rolled(strip, -NZ, 1), strip))


def packed_post(k, here, density, drift, lane1):
    def spread(value):
        out = rolled(value, NZ if k == 0 else 104, 1)
        first = out
        for i in range(1, 5):
            if k == 0:
                out = jnp.where(lane1 >= i * NZ, rolled(first, i * NZ, 1), out)
            else:
                out = jnp.where(lane1 < 128 - i * NZ, rolled(first, -i * NZ, 1), out)
        return out

    slots = plus_y if k == 0 else minus_y
    group = lane1 // NZ if k == 0 else (127 - lane1) // NZ
    density, drift = spread(density), [spread(d) for d in drift]

    def chosen(axis, value):
        out = jnp.zeros_like(value)
        for i, slot in enumerate(slots):
            if lattice_vel[slot][axis] != 0:
                out = jnp.where(group == i, lattice_vel[slot][axis] * value, out)
        return out

    along = chosen(0, drift[0]) + chosen(1, drift[1]) + chosen(2, drift[2])
    weight = jnp.where(group == 0, 2.0, 1.0) * (relax_rate / 36.0) * density
    post = relaxed(here, weight, along, drift)
    place = lax.rem(lane1, NZ) if k == 0 else lax.rem(lane1 + 16, NZ)
    out = post
    for i, slot in enumerate(slots):
        step_x, _, step_z = lattice_vel[slot]
        if step_x != 0 or step_z != 0:
            out = jnp.where(group == i, moved_yz(rolled(post, step_x, 0), 0, step_z, place), out)
    return out


def lanes_of_y(k):
    groups = [NZ * i if k == 0 else 104 - NZ * i for i in range(5)]
    return groups, (120 if k == 0 else 0), ((104, 80) if k == 0 else (0, 24))


def with_phase(k, packed, phase):
    groups, spare, (first, second) = lanes_of_y(k)
    lane = lax.broadcasted_iota(jnp.int32, (8, 128), 1)
    upper = lax.broadcasted_iota(jnp.int32, (8, 128), 0) >= 4
    in_spare = (lane >= spare) & (lane < spare + 8)
    top, low = phase[0:8], phase[8:16]
    top_down, low_down = rolled(top, 4, 0), rolled(low, 4, 0)
    head, tail = packed[0:8], packed[8:16]
    pieces = ((top_down, first), (top, first), (low_down, first), (top_down, second), (top, second))
    for start, (piece, at) in zip(groups, pieces):
        here = upper & (lane >= start) & (lane < start + NZ)
        tail = jnp.where(here, rolled(piece, start - at, 1), tail)
    parts = [
        rolled(low, spare - second, 1),
        rolled(low_down, spare - second - 8, 1),
        rolled(low, spare - second - 16, 1),
    ]
    head = jnp.where(in_spare, jnp.where(upper, parts[1], parts[0]), head)
    tail = jnp.where(in_spare & jnp.logical_not(upper), parts[2], tail)
    return jnp.concatenate([head, tail], axis=0)


def phase_part(k, message):
    groups, spare, (first, second) = lanes_of_y(k)
    lane = lax.broadcasted_iota(jnp.int32, (8, 128), 1)
    upper = lax.broadcasted_iota(jnp.int32, (8, 128), 0) >= 4
    in_first = (lane >= first) & (lane < first + NZ)
    head, tail = message[0:8], message[8:16]
    head_up, tail_up = rolled(head, 4, 0), rolled(tail, 4, 0)

    def picked(near, far):
        return jnp.where(in_first, rolled(near[0], first - near[1], 1), rolled(far[0], second - far[1], 1))

    top = jnp.where(
        upper,
        picked((tail, groups[1]), (tail, groups[4])),
        picked((tail_up, groups[0]), (tail_up, groups[3])),
    )
    far = jnp.where(
        lane < second + 8,
        rolled(head, second - spare, 1),
        jnp.where(
            lane < second + 16,
            rolled(head_up, second + 8 - spare, 1),
            rolled(tail, second + 16 - spare, 1),
        ),
    )
    low = jnp.where(in_first, rolled(tail_up, first - groups[2], 1), far)
    return jnp.concatenate([top, low], axis=0)


def kernel(
    shifts, f_in, p_in, f_out, p_out,
    f, ext, to_x, to_y, to_corner, ring,
    e_p, e_r, e_u, ring_b, ring_a, out_x, out_y, out_corner, out_a,
    fx, chem_x, tile_a, ring_e, ring_o, last_x, last_y, last_corner, last_a,
    *landings_and_semaphores,
):
    count_x, count_y = lax.axis_size("gx"), lax.axis_size("gy")
    gx, gy = lax.axis_index("gx"), lax.axis_index("gy")
    above, below = lax.rem(gx + 1, count_x), lax.rem(gx + count_x - 1, count_x)
    front, back = lax.rem(gy + 1, count_y), lax.rem(gy + count_y - 1, count_y)
    planes = count_x // SPAN
    left_plane = lax.rem(gx, SPAN) == 0
    right_plane = lax.rem(gx, SPAN) == SPAN - 1
    left_slot = lax.rem(gx // SPAN + planes - 1, planes)
    right_slot = gx // SPAN
    any_plane = left_plane | right_plane
    blocks = 3 * count_y
    sides = ((0, left_plane, left_slot), (1, right_plane, right_slot))

    def signal(x, y):
        pl.semaphore_signal(barrier, inc=1, device_id=(x, y), device_id_type=MESH)

    barrier = pltpu.get_barrier_semaphore()
    any_plane = left_plane | right_plane
    def far_first():
        half = count_y // 2
        order = [(half // 2, 1), (half // 2, 0)]
        for dx in range(half // 2 - 1, -1, -1):
            order += [(d, z) for z in (1, 0) for d in sorted({dx, (half - dx) % half})]
        return [2 * lax.rem(gy // 2 + dx, half) + lax.rem(gy + dz, 2) for dx, dz in dict.fromkeys(order)]

    for is_plane, side in ((left_plane, below), (right_plane, above)):
        @pl.when(is_plane)
        def _(side=side):
            for y in far_first():
                signal(side, y)
            for j in range(2, count_y - 1):
                signal(gx, lax.rem(gy + j, count_y))

    signal(gx, front)
    signal(gx, back)
    for is_plane, side in ((left_plane, below), (right_plane, above)):
        @pl.when(jnp.logical_not(is_plane))
        def _(side=side):
            signal(side, front)
            signal(side, back)
            signal(side, gy)

    lane = lax.broadcasted_iota(jnp.int32, (16, WIDE), 1)
    place = lax.rem(lane, NZ)
    lane4 = lax.broadcasted_iota(jnp.int32, (16, 512), 1)
    place4 = lax.rem(jnp.where(lane4 < 448, lane4, lane4 - 464), NZ)
    lane1 = lax.broadcasted_iota(jnp.int32, (16, 128), 1)
    lane5 = lax.broadcasted_iota(jnp.int32, (24, 640), 1)
    place5 = lax.rem(jnp.where(lane5 < 512, lane5, lane5 + 8), NZ)
    place6 = lax.rem(lax.broadcasted_iota(jnp.int32, (8, 768), 1), NZ)

    def pack_phase(r):
        for b in range(3):
            cut = slice(b * 128, b * 128 + 128)
            to_x[0, 7 * b + 5:7 * b + 7, :] = ext[10:12, cut]
            to_x[1, 7 * b + 5:7 * b + 7, :] = ext[0:2, cut]

    *landings, sent, arrived = landings_and_semaphores
    brought = (
        dict(zip(("y", "side", "corner", "plane", "around"), landings[0:5])),
        dict(zip(("y", "side", "corner", "plane"), landings[5:9])),
        dict(zip(("y", "side", "corner", "plane", "around"), landings[9:14])),
    )
    names = ("y", "side", "corner", "plane", "around")

    def remote(src, r, name, index, x, y):
        pltpu.make_async_remote_copy(
            src_ref=src, dst_ref=brought[r][name].at[index],
            send_sem=sent.at[r, names.index(name)], recv_sem=arrived.at[r, names.index(name)],
            device_id=(x, y), device_id_type=MESH,
        ).start()

    def send_x(r, strips):
        for kind, is_plane, side in ((0, right_plane, above), (1, left_plane, below)):
            @pl.when(is_plane)
            def _(kind=kind, side=side):
                for y in far_first():
                    remote(strips.at[kind], r, "plane", gy, side, y)

    def send_sides(r, strips, corners):
        for kind, is_plane, side in ((0, right_plane, above), (1, left_plane, below)):
            @pl.when(jnp.logical_not(is_plane))
            def _(kind=kind, side=side):
                for k, y in ((0, front), (1, back)):
                    remote(corners.at[2 * kind + k], r, "corner", 2 * kind + k, side, y)
                remote(strips.at[kind], r, "side", kind, side, gy)

    def send_around(r, rows):
        @pl.when(any_plane)
        def _():
            for j in range(1, count_y):
                remote(rows, r, "around", j - 1, gx, lax.rem(gy + j, count_y))

    def send_y(r, messages):
        for k, y in ((0, front), (1, back)):
            remote(messages.at[k], r, "y", k, gx, y)

    def wait_for(r, name, sems):
        ref, sem = brought[r][name], sems.at[r, names.index(name)]
        if name in ("side", "corner"):
            step = 1 if name == "side" else 2
            for is_kind, start, size in (
                (left_plane, 1, 1), (right_plane, 0, 1), (jnp.logical_not(any_plane), 0, 2)
            ):
                @pl.when(is_kind)
                def _(start=start, size=size):
                    part = ref.at[pl.ds(step * start, step * size)]
                    pltpu.make_async_copy(part, part, sem).wait()
        else:
            pltpu.make_async_copy(ref, ref, sem).wait()

    def wait_sent(r):
        for name in ("y", "side", "corner"):
            wait_for(r, name, sent)

        @pl.when(any_plane)
        def _():
            for name in ("plane", "around"):
                if name in brought[r]:
                    wait_for(r, name, sent)

    def wait_near(r):
        for name in ("side", "corner", "y"):
            wait_for(r, name, arrived)

    def wait_plane(r):
        for name in ("plane", "around"):
            if name in brought[r]:
                wait_for(r, name, arrived)

    def window_of(held, turn):
        start = ((gy * 16 - turn - 4) & (16 * count_y - 1)) * NZ
        first, offset = start >> 7, start & 127
        window = jnp.concatenate([held[first + i] for i in range(6)], axis=1)
        return pltpu.roll(window, 768 - 4 * NZ - offset, 1)

    def view_b(kind, shift):
        return window_of(ring_b, shift if kind == 0 else -shift - 1)

    def close_ring(r):
        for b in range(blocks + 4):
            row = 7 * (b % 3)
            ring[b, 0:7] = brought[r]["plane"][b % blocks // 3, row:row + 7]

    def view(kind, shift):
        low = shift if kind == 0 else -shift - 1
        near, far = (0.75, 0.25) if kind == 0 else (0.25, 0.75)
        start = ((gy * 16 - low - 3) & (16 * count_y - 1)) * NZ
        first, offset = start >> 7, start & 127
        window = jnp.concatenate([ring[first + i] for i in range(5)], axis=1)
        window = pltpu.roll(window, 640 - 3 * NZ - offset, 1)
        return near * window + far * rolled(window, NZ, 1)

    def patch_y(k, packed):
        cut = slice(0, 128) if k == 0 else slice(256, 384)
        keep = lane1 < NZ if k == 0 else lane1 >= 128 - NZ
        for i, slot in enumerate(plus_y if k == 0 else minus_y):
            part = rolled(packed, -i * NZ if k == 0 else i * NZ, 1)
            f[slot, :, cut] = jnp.where(keep, part, f[slot, :, cut])

    def patch_x(kind, strip):
        edge = 0 if kind == 0 else ROWS - 1
        for i, slot in enumerate(up_slots if kind == 0 else down_slots):
            f[slot, edge:edge + 1, :] = strip[i:i + 1, :WIDE]

    def receive(r, step):
        wait_near(r)
        for k in (0, 1):
            patch_y(k, brought[r]["y"][k])
        ext[0:12, 384:512] = jnp.where(
            lane1 < 64, phase_part(1, brought[r]["y"][1]), phase_part(0, brought[r]["y"][0])
        )[:12]
        for kind, is_plane, _ in sides:
            @pl.when(jnp.logical_not(is_plane))
            def _(kind=kind):
                outer = 14 - 2 * kind
                near_row = 15 - 3 * kind
                e = (0, ROWS - 1)[kind]
                side, corner = brought[r]["side"], brought[r]["corner"]
                strip = jnp.concatenate([side[kind, 7 * b:7 * b + 7] for b in range(3)], axis=1)
                first, last = corner[2 * kind], corner[2 * kind + 1]
                plus = rolled(strip, NZ, 1)
                minus = rolled(strip, -NZ, 1)
                slots = up_slots if kind == 0 else down_slots
                for i in range(3):
                    f[slots[i], e:e + 1, :] = strip[i:i + 1]
                head = jnp.where(lane1[:1] < NZ, first, plus[3:4, 0:128])
                tail = jnp.where(lane1[:1] >= 128 - NZ, last, minus[4:5, 256:384])
                f[slots[3], e:e + 1, 0:128] = head
                f[slots[3], e:e + 1, 128:384] = plus[3:4, 128:384]
                f[slots[4], e:e + 1, 0:256] = minus[4:5, 0:256]
                f[slots[4], e:e + 1, 256:384] = tail
                ext[outer:outer + 2, 0:WIDE] = strip[5:7]
                ext[near_row:near_row + 1, WIDE:512] = jnp.where(lane1[:1] < 64, last, first)

        for kind, is_plane, place_of in sides:
            @pl.when(is_plane)
            def _(kind=kind, place_of=place_of):
                outer = 14 - 2 * kind
                wait_plane(r)
                close_ring(r)
                patch_x(kind, strip_moved(view(kind, shifts[step, place_of])))
                phase = view(kind, shifts[jnp.minimum(step + 1, STEPS - 1), place_of])
                ext[outer:outer + 2, 0:WIDE] = phase[5:7, 0:WIDE]
                ext[outer:outer + 2, WIDE:512] = jnp.where(
                    lane1[:2] < 64, phase[5:7, 384:512], phase[5:7, 512:640]
                )

    def momentum(f):
        density = f[0]
        for slot in range(1, 19):
            density = density + f[slot]
        totals = []
        for axis in range(3):
            total = None
            for slot in range(1, 19, 2):
                sign = lattice_vel[slot][axis]
                if sign != 0:
                    pair = f[slot] - f[slot + 1]
                    if total is None:
                        total = pair
                    else:
                        total = total + pair if sign == 1 else total - pair
            totals.append(total)
        return density, totals

    def advance(r):
        p = ext[...]
        around = differences(p, place4)
        chem = bulk(p, around)
        slope = [0.5 * (a - b)[:, :WIDE] for a, b in around]
        around = [(a[:, :WIDE], b[:, :WIDE]) for a, b in differences(chem, place4)]
        bend = bent(chem[:, :WIDE], around)
        own = p[:, :WIDE]
        density, totals = momentum(f)
        inverse = 1.0 / density
        scaled = (-0.5 * coupling / relax_rate) * own
        next_phase = own + mobility * bend
        drift = []
        for axis in range(3):
            next_phase = next_phase - totals[axis] * inverse * slope[axis]
            drift.append((totals[axis] + scaled * (around[axis][0] - around[axis][1])) * inverse)
        ext[0:12, 0:WIDE] = next_phase[:12]
        if r == 1:
            pack_phase(r)
        collide(density, drift, r, lambda slot: f[slot])

    def collide(density, drift, r, source):
        base = 1.0 - 1.5 * (drift[0] * drift[0] + drift[1] * drift[1] + drift[2] * drift[2])
        weight = relax_rate / 36.0 * density
        keep = 1.0 - relax_rate
        packs = {}

        def put(slot, post):
            step_x, step_y, step_z = lattice_vel[slot]
            if r == 2:
                fx[slot, :, 0:WIDE] = post
                return
            value = rolled(post, step_x, 0)
            moved = moved_yz(value, step_y, step_z, place)
            f[slot] = moved
            if r is None:
                return
            if step_x != 0:
                kind = 0 if step_x == 1 else 1
                i = (up_slots, down_slots)[kind].index(slot)
                line = 12 if step_x == 1 else 15
                shown = value if step_y != 0 else moved
                for b in range(3):
                    to_x[kind, 7 * b + i:7 * b + i + 1, :] = shown[line:line + 1, b * 128:b * 128 + 128]
                if step_y != 0:
                    k = 2 * kind + (0 if step_y == 1 else 1)
                    cut = slice(0, 128) if step_y == 1 else slice(256, 384)
                    edge = 11 if step_x == 1 else 0
                    own = ext[edge:edge + 1, slice(256, 384) if step_y == 1 else slice(0, 128)]
                    post_row = moved[line:line + 1, cut]
                    low = lane1[:1] < 64
                    to_corner[k] = (
                        jnp.where(low, post_row, own) if step_y == 1 else jnp.where(low, own, post_row)
                    )
            if step_y == 1:
                i = plus_y.index(slot)
                part = rolled(moved[:, 0:128], i * NZ, 1)
                mine = (lane1 >= i * NZ) & (lane1 < i * NZ + NZ)
                packs[0] = jnp.where(mine, part, packs[0]) if 0 in packs else part
            if step_y == -1:
                i = minus_y.index(slot)
                part = rolled(moved[:, 256:384], -i * NZ, 1)
                mine = (lane1 < 128 - i * NZ) & (lane1 >= 128 - NZ - i * NZ)
                packs[1] = jnp.where(mine, part, packs[1]) if 1 in packs else part

        def put_pair(slot):
            along = None
            for axis in range(3):
                sign = lattice_vel[slot][axis]
                if sign != 0:
                    if along is None:
                        along = drift[axis]
                    else:
                        along = along + drift[axis] if sign == 1 else along - drift[axis]
            scale = 2.0 * weight if slot < 7 else weight
            even = scale * (base + 4.5 * along * along)
            odd = scale * (3.0 * along)
            here, there = source(slot), source(slot + 1)
            put(slot, keep * here + (even + odd))
            put(slot + 1, keep * there + (even - odd))

        for slot in (1, 7, 9, 11, 13):
            put_pair(slot)
        if r == 1:
            send_x(r, to_x)
            send_sides(r, to_x, to_corner)
        for slot in (3, 15, 17):
            put_pair(slot)
        if r == 1:
            for k in (0, 1):
                to_y[k] = with_phase(k, packs[k], ext[0:16, 256:384] if k == 0 else ext[0:16, 0:128])
            send_y(r, to_y)
        put_pair(5)
        put(0, keep * source(0) + 12.0 * weight * base)

    for slot in range(19):
        f[slot, 0:12, :] = f_in[slot]
        f[slot, 12:16, :] = jnp.ones((4, WIDE), jnp.float32)
    ext[...] = jnp.zeros_like(ext)
    e_p[...] = jnp.zeros_like(e_p)
    e_r[...] = jnp.ones_like(e_r)
    e_u[...] = jnp.zeros_like(e_u)
    e_p[0:12, 0:WIDE] = p_in[...]
    density, totals = momentum(f)
    e_r[0:12, 0:WIDE] = density[:12]
    for axis in range(3):
        e_u[axis, 0:12, 0:WIDE] = (totals[axis] / density)[:12]

    for kind in (0, 1):
        edge, second, low = ((11, 10, 8), (0, 1, 0))[kind]
        for b in range(3):
            cut = slice(b * 128, b * 128 + 128)
            out_x[kind, 16 * b:16 * b + 4, :] = e_p[low:low + 4, cut]
            out_x[kind, 16 * b + 4:16 * b + 5, :] = e_r[edge:edge + 1, cut]
            for axis in range(3):
                out_x[kind, 16 * b + 5 + axis:16 * b + 6 + axis, :] = e_u[axis, edge:edge + 1, cut]
                out_x[kind, 16 * b + 13 + axis:16 * b + 14 + axis, :] = e_u[axis, second:second + 1, cut]
            for i, slot in enumerate(up_slots if kind == 0 else down_slots):
                out_x[kind, 16 * b + 8 + i:16 * b + 9 + i, :] = f[slot, edge:edge + 1, cut]
        for k in (0, 1):
            cut = slice(256, 384) if k == 0 else slice(0, 128)
            slot = (up_slots if kind == 0 else down_slots)[3 + k]
            for i in range(0, len(first_units), 5):
                line = None
                for j, (what, deep_x, deep_y) in enumerate(first_units[i:i + 5]):
                    row = 12 - deep_x if kind == 0 else deep_x - 1
                    if what == "p":
                        part = e_p[row:row + 1, cut]
                    elif what == "r":
                        part = e_r[row:row + 1, cut]
                    elif what == "f":
                        part = f[slot, row:row + 1, cut]
                    else:
                        part = e_u[what, row:row + 1, cut]
                    part = rolled(part, NZ * j - lane_of(k, deep_y), 1)
                    line = part if j == 0 else jnp.where(lane1[:1] >= NZ * j, part, line)
                out_corner[2 * kind + k, i // 5:i // 5 + 1, :] = line
    for k in (0, 1):
        cut = slice(256, 384) if k == 0 else slice(0, 128)
        low = lane1[:12] < 64
        if k == 0:
            pair = lambda a, b: jnp.where(low, pltpu.roll(b, 64, 1), a)
        else:
            pair = lambda a, b: jnp.where(low, a, pltpu.roll(b, 64, 1))
        packed = None
        for i, slot in enumerate(plus_y if k == 0 else minus_y):
            block = f[slot, :, cut]
            part = rolled(block, NZ + i * NZ if k == 0 else -NZ - i * NZ, 1)
            if i == 0:
                packed = part
            else:
                packed = jnp.where(lane1 >= i * NZ if k == 0 else lane1 < 128 - i * NZ, part, packed)
        out_y[k, 0:12, :] = packed[:12]
        out_y[k, 12:24, :] = e_p[0:12, cut]
        out_y[k, 24:36, :] = pair(e_r[0:12, cut], e_u[0, 0:12, cut])
        out_y[k, 36:48, :] = pair(e_u[1, 0:12, cut], e_u[2, 0:12, cut])

    @pl.when(left_plane)
    def _():
        for b in range(3):
            out_a[2 * b:2 * b + 2, :] = e_p[0:2, b * 128:b * 128 + 128]

    @pl.when(right_plane)
    def _():
        for b in range(3):
            out_a[2 * b:2 * b + 2, :] = e_p[10:12, b * 128:b * 128 + 128]

    pl.semaphore_wait(barrier, jnp.where(any_plane, 5 + count_y + max(count_y - 3, 0), 8))

    send_around(0, out_a)
    send_x(0, out_x)
    send_sides(0, out_x, out_corner)
    send_y(0, out_y)

    wait_near(0)
    wide = brought[0]
    for k in (0, 1):
        cut = slice(512, 640) if k == 0 else slice(384, 512)
        e_p[0:12, cut] = wide["y"][k, 12:24]
        e_r[0:12, cut] = wide["y"][k, 24:36]
        e_u[0, 0:12, cut] = pltpu.roll(wide["y"][k, 24:36], 64, 1)
        e_u[1, 0:12, cut] = wide["y"][k, 36:48]
        e_u[2, 0:12, cut] = pltpu.roll(wide["y"][k, 36:48], 64, 1)
    for kind, is_plane, place_of in sides:
        low = (20, 12)[kind]
        edge, second, third = ((23, 22, 21), (12, 13, 12))[kind]

        @pl.when(jnp.logical_not(is_plane))
        def _(kind=kind, low=low, edge=edge, second=second, third=third):
            for k in (0, 1):
                cut = slice(512, 640) if k == 0 else slice(384, 512)
                found = {}
                for i, (what, deep_x, deep_y) in enumerate(first_units):
                    start = lane_of(k, deep_y)
                    part = wide["corner"][2 * kind + k, i // 5:i // 5 + 1]
                    part = rolled(part, start - NZ * (i % 5), 1)
                    here = (lane1[:1] >= start) & (lane1[:1] < start + NZ)
                    key = (what, deep_x)
                    found[key] = jnp.where(here, part, found[key]) if key in found else part
                for (what, deep_x), line in found.items():
                    row = 24 - deep_x if kind == 0 else 11 + deep_x
                    if what == "p":
                        e_p[row:row + 1, cut] = line
                    elif what == "r":
                        e_r[row:row + 1, cut] = line
                    elif what != "f":
                        e_u[what, row:row + 1, cut] = line
            for b in range(3):
                cut = slice(b * 128, b * 128 + 128)
                strip = wide["side"][kind, 16 * b:16 * b + 16]
                e_p[low:low + 4, cut] = strip[0:4]
                e_r[edge:edge + 1, cut] = strip[4:5]
                for axis in range(3):
                    e_u[axis, edge:edge + 1, cut] = strip[5 + axis:6 + axis]
                    e_u[axis, second:second + 1, cut] = strip[13 + axis:14 + axis]

    for kind, is_plane, place_of in sides:
        @pl.when(is_plane)
        def _(kind=kind, place_of=place_of):
            wait_plane(0)
            for b in range(blocks + 5):
                row = 16 * (b % 3)
                ring_b[b] = wide["plane"][b % blocks // 3, row:row + 16]
            a_row = (4, 6)[kind]
            for j in range(count_y):
                source = lax.rem(gy + count_y - j, count_y)
                for b in range(3):
                    rows = slice(2 * b, 2 * b + 2)
                    piece = out_a[rows] if j == 0 else wide["around"][j - 1, rows]
                    ring_a[source * 3 + b, a_row:a_row + 2, :] = piece
            for b in range(5):
                ring_a[blocks + b] = ring_a[b]
            shift = shifts[0, place_of]
            near = view_b(kind, shift)[0:8]
            phase = (near * 0.75 + rolled(near, NZ, 1) * 0.25) if kind == 0 else (
                near * 0.25 + rolled(near, NZ, 1) * 0.75)
            row, at = ((22, 2), (12, 0))[kind]
            e_p[row:row + 2, 0:512] = phase[at:at + 2, 0:512]
            e_p[row:row + 2, 512:640] = phase[at:at + 2, 640:768]

    p = e_p[...]
    around = differences(p, place5)
    chem = bulk(p, around)
    slope = [0.5 * (a - b) for a, b in around]
    around = differences(chem, place5)
    next_phase = p + mobility * bent(chem, around)
    scaled = (-0.5 * coupling / relax_rate) * p / e_r[...]
    drift = []
    for axis in range(3):
        flow = e_u[axis]
        next_phase = next_phase - flow * slope[axis]
        drift.append(flow + scaled * (around[axis][0] - around[axis][1]))
    for top, at, size in ((0, 0, 12), (12, 12, 2), (14, 22, 2)):
        ext[top:top + size, 0:WIDE] = next_phase[at:at + size, 0:WIDE]
        ext[top:top + size, WIDE:512] = jnp.where(
            lane1[:size] < 64, next_phase[at:at + size, 384:512], next_phase[at:at + size, 512:640]
        )
    collide(e_r[0:16, 0:WIDE], [d[0:16, 0:WIDE] for d in drift], None, lambda slot: f[slot])
    for k in (0, 1):
        cut = slice(512, 640) if k == 0 else slice(384, 512)
        patch_y(k, packed_post(k, wide["y"][k, 0:16], e_r[0:16, cut], [d[0:16, cut] for d in drift], lane1))
    for kind, is_plane, place_of in sides:
        @pl.when(is_plane)
        def _(kind=kind, place_of=place_of):
            first = shifts[0, place_of]
            row = lax.broadcasted_iota(jnp.int32, (8, 768), 0)
            edge, at, outer = ((3, 2, 14), (0, 0, 12))[kind]
            weights_of = ((0.75, 0.25), (0.25, 0.75))[kind]
            for step in (0, 1):
                shift = shifts[step, place_of]
                both = view_b(kind, shift)
                turn = shift - first if kind == 0 else first - shift - 1
                own = window_of(ring_a, turn)
                own = 0.75 * own + 0.25 * rolled(own, -NZ if kind == 0 else NZ, 1)
                far_p = jnp.where(row < 4, both[0:8], own)
                around = differences(far_p, place6)
                chem = bulk(far_p, around)
                slope = [0.5 * (a - b) for a, b in around]
                around = differences(chem, place6)
                if step == 0:
                    density = both[4:5]
                    scaled = (-0.5 * coupling / relax_rate) * far_p[edge:edge + 1] / density
                    drift = [
                        both[5 + axis:6 + axis]
                        + scaled * (around[axis][0] - around[axis][1])[edge:edge + 1]
                        for axis in range(3)
                    ]
                    strip = strip_post(kind, both[8:16], density, drift, place6)
                    strip = weights_of[0] * strip + weights_of[1] * rolled(strip, NZ, 1)
                    patch_x(kind, strip_moved(strip))
                else:
                    after = far_p + mobility * bent(chem, around)
                    for axis in range(3):
                        flow = jnp.where(row == edge, both[5 + axis:6 + axis], both[13 + axis:14 + axis])
                        after = after - flow * slope[axis]
                    after = weights_of[0] * after + weights_of[1] * rolled(after, NZ, 1)
                    ext[outer:outer + 2, 0:WIDE] = after[at:at + 2, 0:WIDE]
                    ext[outer:outer + 2, WIDE:512] = jnp.where(
                        lane1[:2] < 64, after[at:at + 2, 384:512], after[at:at + 2, 640:768]
                    )

        @pl.when(jnp.logical_not(is_plane))
        def _(kind=kind):
            edge = (23, 12)[kind]
            at = len(first_units) - 1
            ends = [
                rolled(wide["corner"][2 * kind + k, at // 5:at // 5 + 1], lane_of(k, 1) - NZ * (at % 5), 1)
                for k in (1, 0)
            ]
            strip = jnp.concatenate(
                [wide["side"][kind, 16 * b + 8:16 * b + 16] for b in range(3)]
                + [jnp.broadcast_to(line, (8, 128)) for line in ends],
                axis=1,
            )
            strip = strip_post(
                kind, strip, e_r[edge:edge + 1, :], [d[edge:edge + 1] for d in drift], place5[:8]
            )
            patch_x(kind, strip_moved(strip))

    advance(1)
    wait_sent(0)
    receive(1, 1)

    advance(2)
    y_cut = (slice(256, 384), slice(0, 128))
    lines = [fx[group[0], edge:edge + 1, 0:WIDE] for edge in (11, 0) for group in x_groups]
    halves = 0.5 * jnp.concatenate(lines + lines[:2], axis=0)
    ahead, behind = moved_yz(halves, 0, -1, place[:8]), moved_yz(halves, 0, 1, place[:8])
    for kind in (0, 1):
        edge, second, low = ((11, 10, 9), (0, 1, 0))[kind]
        inward = (up_slots, down_slots)[kind]
        for b in range(3):
            cut = slice(b * 128, b * 128 + 128)
            for i, slot in enumerate(inward):
                last_x[kind, 19 * b + i:19 * b + i + 1, :] = fx[slot, edge:edge + 1, cut]
                last_x[kind, 19 * b + 11 + i:19 * b + 12 + i, :] = fx[slot, second:second + 1, cut]
            for i, (first, slot) in enumerate(folded_x):
                at = x_groups.index(next(g for g in x_groups if g[0] == first)) + 3 * kind
                half = (ahead if lattice_vel[slot][2] == 1 else behind)[at:at + 1, cut]
                last_x[kind, 19 * b + 5 + i:19 * b + 6 + i, :] = fx[slot, edge:edge + 1, cut] + half
            last_x[kind, 19 * b + 16:19 * b + 19, :] = ext[low:low + 3, cut]
        for k in (0, 1):
            units = corner_units(kind, k)
            for i in range(0, len(units), 5):
                line = None
                for j, (slot, deep_x, deep_y) in enumerate(units[i:i + 5]):
                    row = 12 - deep_x if kind == 0 else deep_x - 1
                    part = ext[row:row + 1, y_cut[k]] if slot is None else fx[slot, row:row + 1, y_cut[k]]
                    part = rolled(part, NZ * j - lane_of(k, deep_y), 1)
                    line = part if j == 0 else jnp.where(lane1[:1] >= NZ * j, part, line)
                last_corner[2 * kind + k, i // 5:i // 5 + 1, :] = line
    for is_plane, edge, slots in ((left_plane, 0, down_slots), (right_plane, 11, up_slots)):
        @pl.when(is_plane)
        def _(edge=edge, slots=slots):
            for b in range(3):
                for i, slot in enumerate(slots):
                    last_a[5 * b + i:5 * b + i + 1, :] = fx[slot, edge:edge + 1, b * 128:b * 128 + 128]

    send_around(2, last_a)
    send_x(2, last_x)
    send_sides(2, last_x, last_corner)
    for k in (0, 1):
        spots = lax.rem(lane1 + (16 if k == 0 else 0), NZ)
        for i in range(0, len(y_units[k]), 5):
            line = None
            for j, (slot, deep) in enumerate(y_units[k][i:i + 5]):
                part = ext[0:16, y_cut[k]] if slot is None else fx[slot, :, y_cut[k]]
                for first, folded in folded_y:
                    if folded == slot:
                        part = part + moved_yz(0.5 * fx[first, :, y_cut[k]], 0, -lattice_vel[slot][2], spots)
                part = rolled(part, NZ * j - lane_of(k, deep), 1)
                line = part if j == 0 else jnp.where(lane1 >= NZ * j, part, line)
            last_y[k, 12 * (i // 5):12 * (i // 5) + 12, :] = line[:12]
    send_y(2, last_y)
    e_p[0:12, 0:WIDE] = ext[0:12, 0:WIDE]
    wait_sent(1)

    wait_near(2)
    last = brought[2]

    def unit_of_y(k, slot, deep):
        place = y_units[k].index((slot, deep))
        row = 12 * (place // 5)
        return rolled(last["y"][k, row:row + 12], lane_of(k, deep) - NZ * (place % 5), 1)

    lane12 = lane1[:12]
    for slot in range(19):
        step_y = lattice_vel[slot][1]
        if any(slot == group[0] for group in y_groups):
            rim = jnp.zeros((12, 128), jnp.float32)
        elif step_y == 0:
            rim = jnp.where(lane12 < 64, unit_of_y(1, slot, 1), unit_of_y(0, slot, 1))
        elif step_y == 1:
            rim = jnp.where(lane12 >= 104, unit_of_y(0, slot, 1), unit_of_y(0, slot, 2))
        else:
            rim = jnp.where(lane12 < NZ, unit_of_y(1, slot, 1), unit_of_y(1, slot, 2))
        fx[slot, 0:12, 384:512] = rim
    e_p[0:12, 384:512] = jnp.where(
        lane12 < NZ, unit_of_y(1, None, 1),
        jnp.where(lane12 < 2 * NZ, unit_of_y(1, None, 2), unit_of_y(1, None, 3)),
    )
    e_p[0:12, 512:640] = jnp.where(
        lane12 >= 104, unit_of_y(0, None, 1),
        jnp.where(lane12 >= 80, unit_of_y(0, None, 2), unit_of_y(0, None, 3)),
    )
    for kind, is_plane, place_of in sides:
        @pl.when(jnp.logical_not(is_plane))
        def _(kind=kind):
            rows = ((15, 14), (12, 13))[kind]
            low = (21, 12)[kind]
            inward = (up_slots, down_slots)[kind]
            whole = last["side"][kind]
            for group in x_groups:
                fx[group[0], rows[0]:rows[0] + 1, 0:WIDE] = jnp.zeros((1, WIDE), jnp.float32)
            for b in range(3):
                cut = slice(b * 128, b * 128 + 128)
                strip = whole[19 * b:19 * b + 19]
                for i, slot in enumerate(inward):
                    fx[slot, rows[0]:rows[0] + 1, cut] = strip[i:i + 1]
                    fx[slot, rows[1]:rows[1] + 1, cut] = strip[11 + i:12 + i]
                for i, (_, slot) in enumerate(folded_x):
                    fx[slot, rows[0]:rows[0] + 1, cut] = strip[5 + i:6 + i]
                e_p[low:low + 3, cut] = strip[16:19]
            found = {}
            for k in (0, 1):
                corner = last["corner"][2 * kind + k]
                for i, (slot, deep_x, deep_y) in enumerate(corner_units(kind, k)):
                    part = corner[i // 5:i // 5 + 1]
                    part = rolled(part, lane_of(k, deep_y) - NZ * (i % 5), 1)
                    found.setdefault((slot, deep_x), []).append((k, deep_y, part))
            for (slot, deep_x), parts in found.items():
                line = {}
                for k, deep_y, part in parts:
                    start = lane_of(k, deep_y)
                    here = (lane1[:1] >= start) & (lane1[:1] < start + NZ)
                    at = k if slot is None else 0
                    line[at] = jnp.where(here, part, line[at]) if at in line else part
                if slot is None:
                    row = 24 - deep_x if kind == 0 else 11 + deep_x
                    e_p[row:row + 1, 512:640] = line[0]
                    e_p[row:row + 1, 384:512] = line[1]
                else:
                    row = rows[deep_x - 1]
                    fx[slot, row:row + 1, 384:512] = line[0]

    def mixed(kind, value):
        near, far = ((0.75, 0.25), (0.25, 0.75))[kind]
        return near * value + far * rolled(value, NZ, 1)

    for kind, is_plane, place_of in sides:
        @pl.when(is_plane)
        def _(kind=kind, place_of=place_of):
            wait_plane(2)
            for b in range(blocks + 5):
                row = 19 * (b % 3)
                ring_e[b, 0:19] = last["plane"][b % blocks // 3, row:row + 19]
            for j in range(count_y):
                source = lax.rem(gy + count_y - j, count_y)
                for b in range(3):
                    rows = slice(5 * b, 5 * b + 5)
                    ring_o[source * 3 + b, 0:5] = last_a[rows] if j == 0 else last["around"][j - 1, rows]
            for b in range(5):
                ring_o[blocks + b] = ring_o[b]
            row = (15, 12)[kind]
            shift = shifts[2, place_of]
            strip = mixed(kind, window_of(ring_e, shift if kind == 0 else -shift - 1)[0:8])
            for i, slot in enumerate((up_slots, down_slots)[kind]):
                fx[slot, row:row + 1, 0:384] = strip[i:i + 1, 0:384]
                fx[slot, row:row + 1, 384:512] = jnp.where(
                    lane1[:1] < 64, strip[i:i + 1, 384:512], strip[i:i + 1, 640:768]
                )
            shift = shifts[3, place_of]
            phase = mixed(kind, window_of(ring_e, shift if kind == 0 else -shift - 1)[16:24])
            row, at = ((22, 1), (12, 0))[kind]
            e_p[row:row + 2, 0:512] = phase[at:at + 2, 0:512]
            e_p[row:row + 2, 512:640] = phase[at:at + 2, 640:768]

    def narrowed(to, value):
        for top, at, size in ((0, 0, 12), (12, 12, 2), (14, 22, 2)):
            to[top:top + size, 0:WIDE] = value[at:at + size, 0:WIDE]
            to[top:top + size, WIDE:512] = jnp.where(
                lane1[:size] < 64, value[at:at + size, 384:512], value[at:at + size, 512:640]
            )

    for slot in range(19):
        step_x, step_y, step_z = lattice_vel[slot]
        fx[slot] = moved_yz(rolled(fx[slot], step_x, 0), step_y, step_z, place4)
    p = e_p[...]
    narrowed(ext, p)
    narrowed(chem_x, bulk(p, differences(p, place5)))
    density, totals = momentum(fx)
    inverse = 1.0 / density
    p, chem = ext[...], chem_x[...]
    around = differences(p, place4)
    slope = [0.5 * (a - b)[:, :WIDE] for a, b in around]
    around = differences(chem, place4)
    next_phase = (p + mobility * bent(chem, around))[:, :WIDE]
    scaled = (-0.5 * coupling / relax_rate) * p
    drift = []
    for axis in range(3):
        next_phase = next_phase - (totals[axis] * inverse)[:, :WIDE] * slope[axis]
        drift.append((totals[axis] + scaled * (around[axis][0] - around[axis][1])) * inverse)
    p_out[...] = next_phase[:12]
    collide(density[:, :WIDE], [d[:, :WIDE] for d in drift], None, lambda slot: fx[slot, :, 0:WIDE])
    for k in (0, 1):
        here = None
        for i, slot in enumerate((plus_y, minus_y)[k]):
            part = rolled(fx[slot, :, 384:512], NZ + NZ * i if k == 0 else 104 - NZ * i, 1)
            if i == 0:
                here = part
            else:
                here = jnp.where(lane1 >= NZ * i if k == 0 else lane1 < 128 - NZ * i, part, here)
        rim = [d[:, 384:512] for d in drift]
        patch_y(k, packed_post(k, here, density[:, 384:512], rim, lane1))
    for kind, is_plane, place_of in sides:
        @pl.when(is_plane)
        def _(kind=kind, place_of=place_of):
            before, shift = shifts[2, place_of], shifts[3, place_of]
            edge, top, a_row, own_row = ((3, 1, 4, 0), (0, 0, 6, 10))[kind]
            far = window_of(ring_e, shift if kind == 0 else -shift - 1)
            inner = strip_moved(strip_along_z(kind, far[11:19], place6))
            turn = shift - before if kind == 0 else before - shift - 1
            outer = window_of(ring_o, turn)
            outer = 0.75 * outer + 0.25 * rolled(outer, -NZ if kind == 0 else NZ, 1)
            outer = strip_moved(strip_along_z(1 - kind, outer, place6))
            total = [None] * 4
            sign = 1.0 - 2.0 * kind
            for tile, way in ((inner, sign), (outer, -sign)):
                r = [tile[i:i + 1] for i in range(5)]
                whole = r[0] + r[1] + r[2] + r[3] + r[4]
                found = (whole, way * whole, r[3] - r[4], way * (r[1] - r[2]))
                total = [b if a is None else a + b for a, b in zip(total, found)]
            for i, (_, slot) in enumerate(folded_x):
                _, step_y, step_z = lattice_vel[slot]
                line = moved_yz(far[5 + i:6 + i], step_y, step_z, place6[:1])
                total[0] = total[0] + line
                if step_y != 0:
                    total[2] = total[2] + step_y * line
                if step_z != 0:
                    total[3] = total[3] + step_z * line
            tile_a[...] = jnp.zeros_like(tile_a)
            tile_a[a_row:a_row + 2, 0:512] = e_p[own_row:own_row + 2, 0:512]
            tile_a[a_row:a_row + 2, 640:768] = e_p[own_row:own_row + 2, 512:640]
            own = tile_a[...]
            ahead = rolled(own, -NZ, 1)
            own = 0.75 * own + 0.25 * ahead if kind == 0 else 0.25 * own + 0.75 * ahead
            row = lax.broadcasted_iota(jnp.int32, (8, 768), 0)
            far_p = jnp.where(row < 4, rolled(far[16:24], top, 0), own)
            around = differences(bulk(far_p, differences(far_p, place6)), place6)
            inverse = 1.0 / total[0]
            scaled = (-0.5 * coupling / relax_rate) * far_p[edge:edge + 1]
            drift = [
                (total[1 + axis] + scaled * (around[axis][0] - around[axis][1])[edge:edge + 1]) * inverse
                for axis in range(3)
            ]
            strip = mixed(kind, strip_post(kind, inner, total[0], drift, place6))
            patch_x(kind, strip_moved(strip))

        @pl.when(jnp.logical_not(is_plane))
        def _(kind=kind):
            row = (15, 12)[kind]
            inward = (up_slots, down_slots)[kind]
            lines = [fx[slot, row:row + 1, :] for slot in inward]
            strip = jnp.concatenate(lines + lines[:1] * 3, axis=0)
            strip = strip_post(
                kind, strip, density[row:row + 1], [d[row:row + 1] for d in drift], place4[:8]
            )
            patch_x(kind, strip_moved(strip))

    wait_sent(2)
    for slot in range(19):
        f_out[slot] = f[slot, 0:12, :]


def on_device(populations, phase_field, plane_shifts):
    parts = lax.axis_size("gy")
    blocks = 3 * parts
    rounds = 3
    vmem = pl.BlockSpec(memory_space=pltpu.VMEM)
    return pl.pallas_call(
        kernel,
        out_shape=(
            jax.ShapeDtypeStruct(populations.shape, jnp.float32),
            jax.ShapeDtypeStruct(phase_field.shape, jnp.float32),
        ),
        in_specs=[pl.BlockSpec(memory_space=pltpu.SMEM), vmem, vmem],
        out_specs=(vmem, vmem),
        scratch_shapes=[
            pltpu.VMEM((19, 16, WIDE), jnp.float32),
            pltpu.VMEM((16, 512), jnp.float32),
            pltpu.VMEM((2, 21, 128), jnp.float32),
            pltpu.VMEM((2, 16, 128), jnp.float32),
            pltpu.VMEM((4, 1, 128), jnp.float32),
            pltpu.VMEM((blocks + 4, 8, 128), jnp.float32),
            pltpu.VMEM((24, 640), jnp.float32),
            pltpu.VMEM((24, 640), jnp.float32),
            pltpu.VMEM((3, 24, 640), jnp.float32),
            pltpu.VMEM((blocks + 5, 16, 128), jnp.float32),
            pltpu.VMEM((blocks + 5, 8, 128), jnp.float32),
            pltpu.VMEM((2, 48, 128), jnp.float32),
            pltpu.VMEM((2, 48, 128), jnp.float32),
            pltpu.VMEM((4, 3, 128), jnp.float32),
            pltpu.VMEM((6, 128), jnp.float32),
            pltpu.VMEM((19, 16, 512), jnp.float32),
            pltpu.VMEM((16, 512), jnp.float32),
            pltpu.VMEM((8, 768), jnp.float32),
            pltpu.VMEM((blocks + 5, 24, 128), jnp.float32),
            pltpu.VMEM((blocks + 5, 8, 128), jnp.float32),
            pltpu.VMEM((2, 57, 128), jnp.float32),
            pltpu.VMEM((2, 48, 128), jnp.float32),
            pltpu.VMEM((4, 5, 128), jnp.float32),
            pltpu.VMEM((15, 128), jnp.float32),
        ] + [
            pltpu.VMEM((count, rows, 128), jnp.float32)
            for count, rows in (
                (2, 48), (2, 48), (4, 3), (parts, 48), (parts - 1, 6),
                (2, 16), (2, 21), (4, 1), (parts, 21),
                (2, 48), (2, 57), (4, 5), (parts, 57), (parts - 1, 15),
            )
        ] + [
            pltpu.SemaphoreType.DMA((rounds, 5)),
            pltpu.SemaphoreType.DMA((rounds, 5)),
        ],
        compiler_params=pltpu.CompilerParams(
            collective_id=0, has_side_effects=True, vmem_limit_bytes=32 * 1024 * 1024
        ),
    )(plane_shifts, populations, phase_field)


def solution(mesh):
    return jax.shard_map(
        on_device,
        mesh=mesh,
        in_specs=(P(None, "gx", "gy"), P("gx", "gy"), P()),
        out_specs=(P(None, "gx", "gy"), P("gx", "gy")),
        check_vma=False,
    )
```

```python
import functools

import jax
import jax.numpy as jnp
from jax import lax
from jax.experimental import pallas as pl
from jax.experimental.pallas import tpu as pltpu
from jax.sharding import PartitionSpec as P

STEPS = 4
NZ = 24
ROWS = 12
WIDE = 384
SPAN = 4
MESH = pl.DeviceIdType.MESH

lattice_vel = (
    (0, 0, 0),
    (1, 0, 0),
    (-1, 0, 0),
    (0, 1, 0),
    (0, -1, 0),
    (0, 0, 1),
    (0, 0, -1),
    (1, 1, 0),
    (-1, -1, 0),
    (1, -1, 0),
    (-1, 1, 0),
    (1, 0, 1),
    (-1, 0, -1),
    (1, 0, -1),
    (-1, 0, 1),
    (0, 1, 1),
    (0, -1, -1),
    (0, 1, -1),
    (0, -1, 1),
)
relax_rate = 0.8
coupling = 0.01
mobility = 0.02

up_slots = (1, 11, 13, 7, 9)
down_slots = (2, 12, 14, 10, 8)
plus_y = (3, 7, 10, 15, 17)
minus_y = (4, 8, 9, 16, 18)


x_groups = ((0, 5, 6), (3, 15, 17), (4, 18, 16))
y_groups = ((0, 5, 6), (1, 11, 13), (2, 14, 12))
folded_x = tuple((first, slot) for first, *pair in x_groups for slot in pair)
folded_y = tuple((first, slot) for first, *pair in y_groups for slot in pair)
near_y = tuple(slots + tuple(slot for _, slot in folded_y) for slots in (plus_y, minus_y))
y_units = tuple(
    tuple((slot, 1) for slot in near_y[k]) + tuple((slot, 2) for slot in (plus_y, minus_y)[k])
    + ((None, 1), (None, 2), (None, 3))
    for k in (0, 1)
)


def corner_units(kind, k):
    step = (1 - 2 * kind, 1 - 2 * k)
    units = []
    for deep in ((1, 1), (2, 1), (1, 2), (2, 2)):
        for slot in range(19):
            if all(
                lattice_vel[slot][axis] == step[axis] or (deep[axis] == 1 and lattice_vel[slot][axis] == 0)
                for axis in (0, 1)
            ):
                units.append((slot,) + deep)
    return tuple(units) + tuple((None, x, y) for x in (1, 2, 3) for y in range(1, 5 - x))


first_units = tuple(("p", x, y) for x in (1, 2, 3) for y in range(1, 5 - x)) + tuple(
    (what, 1, 1) for what in ("r", 0, 1, 2, "f")
)


def lane_of(k, depth):
    return 128 - NZ * depth if k == 0 else NZ * (depth - 1)


def rolled(value, shift, axis):
    size = value.shape[axis]
    shift = shift % size
    return value if shift == 0 else pltpu.roll(value, shift, axis)


def moved_yz(value, step_y, step_z, place):
    if step_z == 0:
        return rolled(value, step_y * NZ, 1)
    edge = 0 if step_z == 1 else NZ - 1
    inner = rolled(value, step_y * NZ + step_z, 1)
    wrap = rolled(value, step_y * NZ + step_z - step_z * NZ, 1)
    return jnp.where(place == edge, wrap, inner)


def differences(value, place):
    return (
        (rolled(value, -1, 0), rolled(value, 1, 0)),
        (rolled(value, -NZ, 1), rolled(value, NZ, 1)),
        (moved_yz(value, 0, -1, place), moved_yz(value, 0, 1, place)),
    )


def bulk(p, around):
    total = around[0][0] + around[0][1] + around[1][0] + around[1][1] + around[2][0] + around[2][1]
    return 0.5 * (p * p * p - p) - 0.5 * (total - 6.0 * p)


def bent(chem, around):
    total = around[0][0] + around[0][1] + around[1][0] + around[1][1] + around[2][0] + around[2][1]
    return total - 6.0 * chem


def relaxed(here, weight, along, drift):
    square = drift[0] * drift[0] + drift[1] * drift[1] + drift[2] * drift[2]
    return (1.0 - relax_rate) * here + weight * (
        1.0 - 1.5 * square + 3.0 * along + 4.5 * along * along
    )


def strip_post(kind, here, density, drift, place):
    sign = 1.0 - 2.0 * kind
    row = lax.broadcasted_iota(jnp.int32, here.shape, 0)
    full = [jnp.broadcast_to(d, here.shape) for d in drift]
    along = sign * full[0]
    along = along + jnp.where(row == 3, full[1], jnp.where(row == 4, -full[1], 0.0))
    along = along + jnp.where(row == 1, sign * full[2], jnp.where(row == 2, -sign * full[2], 0.0))
    weight = jnp.where(row == 0, 2.0, 1.0) * (relax_rate / 36.0) * density
    post = relaxed(here, weight, along, full)
    return strip_along_z(kind, post, place)


def strip_along_z(kind, strip, place):
    row = lax.broadcasted_iota(jnp.int32, strip.shape, 0)
    first, second = (1, -1) if kind == 0 else (-1, 1)
    return jnp.where(
        row == 1, moved_yz(strip, 0, first, place), jnp.where(row == 2, moved_yz(strip, 0, second, place), strip)
    )


def strip_moved(strip):
    row = lax.broadcasted_iota(jnp.int32, strip.shape, 0)
    return jnp.where(row == 3, rolled(strip, NZ, 1), jnp.where(row == 4, rolled(strip, -NZ, 1), strip))


def packed_post(k, here, density, drift, lane1):
    def spread(value):
        out = rolled(value, NZ if k == 0 else 104, 1)
        first = out
        for i in range(1, 5):
            if k == 0:
                out = jnp.where(lane1 >= i * NZ, rolled(first, i * NZ, 1), out)
            else:
                out = jnp.where(lane1 < 128 - i * NZ, rolled(first, -i * NZ, 1), out)
        return out

    slots = plus_y if k == 0 else minus_y
    group = lane1 // NZ if k == 0 else (127 - lane1) // NZ
    density, drift = spread(density), [spread(d) for d in drift]

    def chosen(axis, value):
        out = jnp.zeros_like(value)
        for i, slot in enumerate(slots):
            if lattice_vel[slot][axis] != 0:
                out = jnp.where(group == i, lattice_vel[slot][axis] * value, out)
        return out

    along = chosen(0, drift[0]) + chosen(1, drift[1]) + chosen(2, drift[2])
    weight = jnp.where(group == 0, 2.0, 1.0) * (relax_rate / 36.0) * density
    post = relaxed(here, weight, along, drift)
    place = lax.rem(lane1, NZ) if k == 0 else lax.rem(lane1 + 16, NZ)
    out = post
    for i, slot in enumerate(slots):
        step_x, _, step_z = lattice_vel[slot]
        if step_x != 0 or step_z != 0:
            out = jnp.where(group == i, moved_yz(rolled(post, step_x, 0), 0, step_z, place), out)
    return out


def lanes_of_y(k):
    groups = [NZ * i if k == 0 else 104 - NZ * i for i in range(5)]
    return groups, (120 if k == 0 else 0), ((104, 80) if k == 0 else (0, 24))


def with_phase(k, packed, phase):
    groups, spare, (first, second) = lanes_of_y(k)
    lane = lax.broadcasted_iota(jnp.int32, (8, 128), 1)
    upper = lax.broadcasted_iota(jnp.int32, (8, 128), 0) >= 4
    in_spare = (lane >= spare) & (lane < spare + 8)
    top, low = phase[0:8], phase[8:16]
    top_down, low_down = rolled(top, 4, 0), rolled(low, 4, 0)
    head, tail = packed[0:8], packed[8:16]
    pieces = ((top_down, first), (top, first), (low_down, first), (top_down, second), (top, second))
    for start, (piece, at) in zip(groups, pieces):
        here = upper & (lane >= start) & (lane < start + NZ)
        tail = jnp.where(here, rolled(piece, start - at, 1), tail)
    parts = [
        rolled(low, spare - second, 1),
        rolled(low_down, spare - second - 8, 1),
        rolled(low, spare - second - 16, 1),
    ]
    head = jnp.where(in_spare, jnp.where(upper, parts[1], parts[0]), head)
    tail = jnp.where(in_spare & jnp.logical_not(upper), parts[2], tail)
    return jnp.concatenate([head, tail], axis=0)


def phase_part(k, message):
    groups, spare, (first, second) = lanes_of_y(k)
    lane = lax.broadcasted_iota(jnp.int32, (8, 128), 1)
    upper = lax.broadcasted_iota(jnp.int32, (8, 128), 0) >= 4
    in_first = (lane >= first) & (lane < first + NZ)
    head, tail = message[0:8], message[8:16]
    head_up, tail_up = rolled(head, 4, 0), rolled(tail, 4, 0)

    def picked(near, far):
        return jnp.where(in_first, rolled(near[0], first - near[1], 1), rolled(far[0], second - far[1], 1))

    top = jnp.where(
        upper,
        picked((tail, groups[1]), (tail, groups[4])),
        picked((tail_up, groups[0]), (tail_up, groups[3])),
    )
    far = jnp.where(
        lane < second + 8,
        rolled(head, second - spare, 1),
        jnp.where(
            lane < second + 16,
            rolled(head_up, second + 8 - spare, 1),
            rolled(tail, second + 16 - spare, 1),
        ),
    )
    low = jnp.where(in_first, rolled(tail_up, first - groups[2], 1), far)
    return jnp.concatenate([top, low], axis=0)


def kernel(
    shifts, f_in, p_in, f_out, p_out,
    f, ext, to_x, to_y, to_corner, ring,
    e_p, e_r, e_u, ring_b, ring_a, out_x, out_y, out_corner, out_a,
    fx, chem_x, tile_a, ring_e, ring_o, last_x, last_y, last_corner, last_a,
    *landings_and_semaphores,
):
    count_x, count_y = lax.axis_size("gx"), lax.axis_size("gy")
    gx, gy = lax.axis_index("gx"), lax.axis_index("gy")
    above, below = lax.rem(gx + 1, count_x), lax.rem(gx + count_x - 1, count_x)
    front, back = lax.rem(gy + 1, count_y), lax.rem(gy + count_y - 1, count_y)
    planes = count_x // SPAN
    left_plane = lax.rem(gx, SPAN) == 0
    right_plane = lax.rem(gx, SPAN) == SPAN - 1
    left_slot = lax.rem(gx // SPAN + planes - 1, planes)
    right_slot = gx // SPAN
    any_plane = left_plane | right_plane
    blocks = 3 * count_y
    sides = ((0, left_plane, left_slot), (1, right_plane, right_slot))

    def signal(x, y):
        pl.semaphore_signal(barrier, inc=1, device_id=(x, y), device_id_type=MESH)

    barrier = pltpu.get_barrier_semaphore()
    any_plane = left_plane | right_plane
    def far_first():
        half = count_y // 2
        order = [(half // 2, 1), (half // 2, 0)]
        for dx in range(half // 2 - 1, -1, -1):
            order += [(d, z) for z in (1, 0) for d in sorted({dx, (half - dx) % half})]
        return [2 * lax.rem(gy // 2 + dx, half) + lax.rem(gy + dz, 2) for dx, dz in dict.fromkeys(order)]

    for is_plane, side in ((left_plane, below), (right_plane, above)):
        @pl.when(is_plane)
        def _(side=side):
            for y in far_first():
                signal(side, y)
            for j in range(2, count_y - 1):
                signal(gx, lax.rem(gy + j, count_y))

    signal(gx, front)
    signal(gx, back)
    for is_plane, side in ((left_plane, below), (right_plane, above)):
        @pl.when(jnp.logical_not(is_plane))
        def _(side=side):
            signal(side, front)
            signal(side, back)
            signal(side, gy)

    lane = lax.broadcasted_iota(jnp.int32, (16, WIDE), 1)
    place = lax.rem(lane, NZ)
    lane4 = lax.broadcasted_iota(jnp.int32, (16, 512), 1)
    place4 = lax.rem(jnp.where(lane4 < 448, lane4, lane4 - 464), NZ)
    lane1 = lax.broadcasted_iota(jnp.int32, (16, 128), 1)
    lane5 = lax.broadcasted_iota(jnp.int32, (24, 640), 1)
    place5 = lax.rem(jnp.where(lane5 < 512, lane5, lane5 + 8), NZ)
    place6 = lax.rem(lax.broadcasted_iota(jnp.int32, (8, 768), 1), NZ)

    def pack_phase(r):
        for b in range(3):
            cut = slice(b * 128, b * 128 + 128)
            to_x[0, 7 * b + 5:7 * b + 7, :] = ext[10:12, cut]
            to_x[1, 7 * b + 5:7 * b + 7, :] = ext[0:2, cut]

    *landings, sent, arrived = landings_and_semaphores
    brought = (
        dict(zip(("y", "side", "corner", "plane", "around"), landings[0:5])),
        dict(zip(("y", "side", "corner", "plane"), landings[5:9])),
        dict(zip(("y", "side", "corner", "plane", "around"), landings[9:14])),
    )
    names = ("y", "side", "corner", "plane", "around")

    def remote(src, r, name, index, x, y):
        pltpu.make_async_remote_copy(
            src_ref=src, dst_ref=brought[r][name].at[index],
            send_sem=sent.at[r, names.index(name)], recv_sem=arrived.at[r, names.index(name)],
            device_id=(x, y), device_id_type=MESH,
        ).start()

    def send_x(r, strips):
        for kind, is_plane, side in ((0, right_plane, above), (1, left_plane, below)):
            @pl.when(is_plane)
            def _(kind=kind, side=side):
                for y in far_first():
                    remote(strips.at[kind], r, "plane", gy, side, y)

    def send_sides(r, strips, corners):
        for kind, is_plane, side in ((0, right_plane, above), (1, left_plane, below)):
            @pl.when(jnp.logical_not(is_plane))
            def _(kind=kind, side=side):
                for k, y in ((0, front), (1, back)):
                    remote(corners.at[2 * kind + k], r, "corner", 2 * kind + k, side, y)
                remote(strips.at[kind], r, "side", kind, side, gy)

    def send_around(r, rows):
        @pl.when(any_plane)
        def _():
            for j in range(1, count_y):
                remote(rows, r, "around", j - 1, gx, lax.rem(gy + j, count_y))

    def send_y(r, messages):
        for k, y in ((0, front), (1, back)):
            remote(messages.at[k], r, "y", k, gx, y)

    def wait_for(r, name, sems):
        ref, sem = brought[r][name], sems.at[r, names.index(name)]
        if name in ("side", "corner"):
            step = 1 if name == "side" else 2
            for is_kind, start, size in (
                (left_plane, 1, 1), (right_plane, 0, 1), (jnp.logical_not(any_plane), 0, 2)
            ):
                @pl.when(is_kind)
                def _(start=start, size=size):
                    part = ref.at[pl.ds(step * start, step * size)]
                    pltpu.make_async_copy(part, part, sem).wait()
        else:
            pltpu.make_async_copy(ref, ref, sem).wait()

    def wait_sent(r):
        for name in ("y", "side", "corner"):
            wait_for(r, name, sent)

        @pl.when(any_plane)
        def _():
            for name in ("plane", "around"):
                if name in brought[r]:
                    wait_for(r, name, sent)

    def wait_near(r):
        for name in ("side", "corner", "y"):
            wait_for(r, name, arrived)

    def wait_plane(r):
        for name in ("plane", "around"):
            if name in brought[r]:
                wait_for(r, name, arrived)

    def window_of(held, turn):
        start = ((gy * 16 - turn - 4) & (16 * count_y - 1)) * NZ
        first, offset = start >> 7, start & 127
        window = jnp.concatenate([held[first + i] for i in range(6)], axis=1)
        return pltpu.roll(window, 768 - 4 * NZ - offset, 1)

    def view_b(kind, shift):
        return window_of(ring_b, shift if kind == 0 else -shift - 1)

    def close_ring(r):
        for b in range(blocks + 4):
            row = 7 * (b % 3)
            ring[b, 0:7] = brought[r]["plane"][b % blocks // 3, row:row + 7]

    def view(kind, shift):
        low = shift if kind == 0 else -shift - 1
        near, far = (0.75, 0.25) if kind == 0 else (0.25, 0.75)
        start = ((gy * 16 - low - 3) & (16 * count_y - 1)) * NZ
        first, offset = start >> 7, start & 127
        window = jnp.concatenate([ring[first + i] for i in range(5)], axis=1)
        window = pltpu.roll(window, 640 - 3 * NZ - offset, 1)
        return near * window + far * rolled(window, NZ, 1)

    def patch_y(k, packed):
        cut = slice(0, 128) if k == 0 else slice(256, 384)
        keep = lane1 < NZ if k == 0 else lane1 >= 128 - NZ
        for i, slot in enumerate(plus_y if k == 0 else minus_y):
            part = rolled(packed, -i * NZ if k == 0 else i * NZ, 1)
            f[slot, :, cut] = jnp.where(keep, part, f[slot, :, cut])

    def patch_x(kind, strip):
        edge = 0 if kind == 0 else ROWS - 1
        for i, slot in enumerate(up_slots if kind == 0 else down_slots):
            f[slot, edge:edge + 1, :] = strip[i:i + 1, :WIDE]

    def receive(r, step):
        wait_near(r)
        for k in (0, 1):
            patch_y(k, brought[r]["y"][k])
        ext[0:12, 384:512] = jnp.where(
            lane1 < 64, phase_part(1, brought[r]["y"][1]), phase_part(0, brought[r]["y"][0])
        )[:12]
        for kind, is_plane, _ in sides:
            @pl.when(jnp.logical_not(is_plane))
            def _(kind=kind):
                outer = 14 - 2 * kind
                near_row = 15 - 3 * kind
                e = (0, ROWS - 1)[kind]
                side, corner = brought[r]["side"], brought[r]["corner"]
                strip = jnp.concatenate([side[kind, 7 * b:7 * b + 7] for b in range(3)], axis=1)
                first, last = corner[2 * kind], corner[2 * kind + 1]
                plus = rolled(strip, NZ, 1)
                minus = rolled(strip, -NZ, 1)
                slots = up_slots if kind == 0 else down_slots
                for i in range(3):
                    f[slots[i], e:e + 1, :] = strip[i:i + 1]
                head = jnp.where(lane1[:1] < NZ, first, plus[3:4, 0:128])
                tail = jnp.where(lane1[:1] >= 128 - NZ, last, minus[4:5, 256:384])
                f[slots[3], e:e + 1, 0:128] = head
                f[slots[3], e:e + 1, 128:384] = plus[3:4, 128:384]
                f[slots[4], e:e + 1, 0:256] = minus[4:5, 0:256]
                f[slots[4], e:e + 1, 256:384] = tail
                ext[outer:outer + 2, 0:WIDE] = strip[5:7]
                ext[near_row:near_row + 1, WIDE:512] = jnp.where(lane1[:1] < 64, last, first)

        for kind, is_plane, place_of in sides:
            @pl.when(is_plane)
            def _(kind=kind, place_of=place_of):
                outer = 14 - 2 * kind
                wait_plane(r)
                close_ring(r)
                patch_x(kind, strip_moved(view(kind, shifts[step, place_of])))
                phase = view(kind, shifts[jnp.minimum(step + 1, STEPS - 1), place_of])
                ext[outer:outer + 2, 0:WIDE] = phase[5:7, 0:WIDE]
                ext[outer:outer + 2, WIDE:512] = jnp.where(
                    lane1[:2] < 64, phase[5:7, 384:512], phase[5:7, 512:640]
                )

    def momentum(f):
        density = f[0]
        for slot in range(1, 19):
            density = density + f[slot]
        totals = []
        for axis in range(3):
            total = None
            for slot in range(1, 19, 2):
                sign = lattice_vel[slot][axis]
                if sign != 0:
                    pair = f[slot] - f[slot + 1]
                    if total is None:
                        total = pair
                    else:
                        total = total + pair if sign == 1 else total - pair
            totals.append(total)
        return density, totals

    def advance(r):
        p = ext[...]
        around = differences(p, place4)
        chem = bulk(p, around)
        slope = [0.5 * (a - b)[:, :WIDE] for a, b in around]
        around = [(a[:, :WIDE], b[:, :WIDE]) for a, b in differences(chem, place4)]
        bend = bent(chem[:, :WIDE], around)
        own = p[:, :WIDE]
        density, totals = momentum(f)
        inverse = 1.0 / density
        scaled = (-0.5 * coupling / relax_rate) * own
        next_phase = own + mobility * bend
        drift = []
        for axis in range(3):
            next_phase = next_phase - totals[axis] * inverse * slope[axis]
            drift.append((totals[axis] + scaled * (around[axis][0] - around[axis][1])) * inverse)
        ext[0:12, 0:WIDE] = next_phase[:12]
        if r == 1:
            pack_phase(r)
        collide(density, drift, r, lambda slot: f[slot])

    def collide(density, drift, r, source):
        base = 1.0 - 1.5 * (drift[0] * drift[0] + drift[1] * drift[1] + drift[2] * drift[2])
        weight = relax_rate / 36.0 * density
        keep = 1.0 - relax_rate
        packs = {}

        def put(slot, post):
            step_x, step_y, step_z = lattice_vel[slot]
            if r == 2:
                fx[slot, :, 0:WIDE] = post
                return
            value = rolled(post, step_x, 0)
            moved = moved_yz(value, step_y, step_z, place)
            f[slot] = moved
            if r is None:
                return
            if step_x != 0:
                kind = 0 if step_x == 1 else 1
                i = (up_slots, down_slots)[kind].index(slot)
                line = 12 if step_x == 1 else 15
                shown = value if step_y != 0 else moved
                for b in range(3):
                    to_x[kind, 7 * b + i:7 * b + i + 1, :] = shown[line:line + 1, b * 128:b * 128 + 128]
                if step_y != 0:
                    k = 2 * kind + (0 if step_y == 1 else 1)
                    cut = slice(0, 128) if step_y == 1 else slice(256, 384)
                    edge = 11 if step_x == 1 else 0
                    own = ext[edge:edge + 1, slice(256, 384) if step_y == 1 else slice(0, 128)]
                    post_row = moved[line:line + 1, cut]
                    low = lane1[:1] < 64
                    to_corner[k] = (
                        jnp.where(low, post_row, own) if step_y == 1 else jnp.where(low, own, post_row)
                    )
            if step_y == 1:
                i = plus_y.index(slot)
                part = rolled(moved[:, 0:128], i * NZ, 1)
                mine = (lane1 >= i * NZ) & (lane1 < i * NZ + NZ)
                packs[0] = jnp.where(mine, part, packs[0]) if 0 in packs else part
            if step_y == -1:
                i = minus_y.index(slot)
                part = rolled(moved[:, 256:384], -i * NZ, 1)
                mine = (lane1 < 128 - i * NZ) & (lane1 >= 128 - NZ - i * NZ)
                packs[1] = jnp.where(mine, part, packs[1]) if 1 in packs else part

        def put_pair(slot):
            along = None
            for axis in range(3):
                sign = lattice_vel[slot][axis]
                if sign != 0:
                    if along is None:
                        along = drift[axis]
                    else:
                        along = along + drift[axis] if sign == 1 else along - drift[axis]
            scale = 2.0 * weight if slot < 7 else weight
            even = scale * (base + 4.5 * along * along)
            odd = scale * (3.0 * along)
            here, there = source(slot), source(slot + 1)
            put(slot, keep * here + (even + odd))
            put(slot + 1, keep * there + (even - odd))

        for slot in (1, 7, 9, 11, 13):
            put_pair(slot)
        if r == 1:
            send_x(r, to_x)
            send_sides(r, to_x, to_corner)
        for slot in (3, 15, 17):
            put_pair(slot)
        if r == 1:
            for k in (0, 1):
                to_y[k] = with_phase(k, packs[k], ext[0:16, 256:384] if k == 0 else ext[0:16, 0:128])
            send_y(r, to_y)
        put_pair(5)
        put(0, keep * source(0) + 12.0 * weight * base)

    for slot in range(19):
        f[slot, 0:12, :] = f_in[slot]
        f[slot, 12:16, :] = jnp.ones((4, WIDE), jnp.float32)
    ext[...] = jnp.zeros_like(ext)
    e_p[...] = jnp.zeros_like(e_p)
    e_r[...] = jnp.ones_like(e_r)
    e_u[...] = jnp.zeros_like(e_u)
    e_p[0:12, 0:WIDE] = p_in[...]
    density, totals = momentum(f)
    e_r[0:12, 0:WIDE] = density[:12]
    for axis in range(3):
        e_u[axis, 0:12, 0:WIDE] = (totals[axis] / density)[:12]

    for kind in (0, 1):
        edge, second, low = ((11, 10, 8), (0, 1, 0))[kind]
        for b in range(3):
            cut = slice(b * 128, b * 128 + 128)
            out_x[kind, 16 * b:16 * b + 4, :] = e_p[low:low + 4, cut]
            out_x[kind, 16 * b + 4:16 * b + 5, :] = e_r[edge:edge + 1, cut]
            for axis in range(3):
                out_x[kind, 16 * b + 5 + axis:16 * b + 6 + axis, :] = e_u[axis, edge:edge + 1, cut]
                out_x[kind, 16 * b + 13 + axis:16 * b + 14 + axis, :] = e_u[axis, second:second + 1, cut]
            for i, slot in enumerate(up_slots if kind == 0 else down_slots):
                out_x[kind, 16 * b + 8 + i:16 * b + 9 + i, :] = f[slot, edge:edge + 1, cut]
        for k in (0, 1):
            cut = slice(256, 384) if k == 0 else slice(0, 128)
            slot = (up_slots if kind == 0 else down_slots)[3 + k]
            for i in range(0, len(first_units), 5):
                line = None
                for j, (what, deep_x, deep_y) in enumerate(first_units[i:i + 5]):
                    row = 12 - deep_x if kind == 0 else deep_x - 1
                    if what == "p":
                        part = e_p[row:row + 1, cut]
                    elif what == "r":
                        part = e_r[row:row + 1, cut]
                    elif what == "f":
                        part = f[slot, row:row + 1, cut]
                    else:
                        part = e_u[what, row:row + 1, cut]
                    part = rolled(part, NZ * j - lane_of(k, deep_y), 1)
                    line = part if j == 0 else jnp.where(lane1[:1] >= NZ * j, part, line)
                out_corner[2 * kind + k, i // 5:i // 5 + 1, :] = line
    for k in (0, 1):
        cut = slice(256, 384) if k == 0 else slice(0, 128)
        low = lane1[:12] < 64
        if k == 0:
            pair = lambda a, b: jnp.where(low, pltpu.roll(b, 64, 1), a)
        else:
            pair = lambda a, b: jnp.where(low, a, pltpu.roll(b, 64, 1))
        packed = None
        for i, slot in enumerate(plus_y if k == 0 else minus_y):
            block = f[slot, :, cut]
            part = rolled(block, NZ + i * NZ if k == 0 else -NZ - i * NZ, 1)
            if i == 0:
                packed = part
            else:
                packed = jnp.where(lane1 >= i * NZ if k == 0 else lane1 < 128 - i * NZ, part, packed)
        out_y[k, 0:12, :] = packed[:12]
        out_y[k, 12:24, :] = e_p[0:12, cut]
        out_y[k, 24:36, :] = pair(e_r[0:12, cut], e_u[0, 0:12, cut])
        out_y[k, 36:48, :] = pair(e_u[1, 0:12, cut], e_u[2, 0:12, cut])

    @pl.when(left_plane)
    def _():
        for b in range(3):
            out_a[2 * b:2 * b + 2, :] = e_p[0:2, b * 128:b * 128 + 128]

    @pl.when(right_plane)
    def _():
        for b in range(3):
            out_a[2 * b:2 * b + 2, :] = e_p[10:12, b * 128:b * 128 + 128]

    pl.semaphore_wait(barrier, jnp.where(any_plane, 5 + count_y + max(count_y - 3, 0), 8))

    send_around(0, out_a)
    send_x(0, out_x)
    send_sides(0, out_x, out_corner)
    send_y(0, out_y)

    wait_near(0)
    wide = brought[0]
    for k in (0, 1):
        cut = slice(512, 640) if k == 0 else slice(384, 512)
        e_p[0:12, cut] = wide["y"][k, 12:24]
        e_r[0:12, cut] = wide["y"][k, 24:36]
        e_u[0, 0:12, cut] = pltpu.roll(wide["y"][k, 24:36], 64, 1)
        e_u[1, 0:12, cut] = wide["y"][k, 36:48]
        e_u[2, 0:12, cut] = pltpu.roll(wide["y"][k, 36:48], 64, 1)
    for kind, is_plane, place_of in sides:
        low = (20, 12)[kind]
        edge, second, third = ((23, 22, 21), (12, 13, 12))[kind]

        @pl.when(jnp.logical_not(is_plane))
        def _(kind=kind, low=low, edge=edge, second=second, third=third):
            for k in (0, 1):
                cut = slice(512, 640) if k == 0 else slice(384, 512)
                found = {}
                for i, (what, deep_x, deep_y) in enumerate(first_units):
                    start = lane_of(k, deep_y)
                    part = wide["corner"][2 * kind + k, i // 5:i // 5 + 1]
                    part = rolled(part, start - NZ * (i % 5), 1)
                    here = (lane1[:1] >= start) & (lane1[:1] < start + NZ)
                    key = (what, deep_x)
                    found[key] = jnp.where(here, part, found[key]) if key in found else part
                for (what, deep_x), line in found.items():
                    row = 24 - deep_x if kind == 0 else 11 + deep_x
                    if what == "p":
                        e_p[row:row + 1, cut] = line
                    elif what == "r":
                        e_r[row:row + 1, cut] = line
                    elif what != "f":
                        e_u[what, row:row + 1, cut] = line
            for b in range(3):
                cut = slice(b * 128, b * 128 + 128)
                strip = wide["side"][kind, 16 * b:16 * b + 16]
                e_p[low:low + 4, cut] = strip[0:4]
                e_r[edge:edge + 1, cut] = strip[4:5]
                for axis in range(3):
                    e_u[axis, edge:edge + 1, cut] = strip[5 + axis:6 + axis]
                    e_u[axis, second:second + 1, cut] = strip[13 + axis:14 + axis]

    for kind, is_plane, place_of in sides:
        @pl.when(is_plane)
        def _(kind=kind, place_of=place_of):
            wait_plane(0)
            for b in range(blocks + 5):
                row = 16 * (b % 3)
                ring_b[b] = wide["plane"][b % blocks // 3, row:row + 16]
            a_row = (4, 6)[kind]
            for j in range(count_y):
                source = lax.rem(gy + count_y - j, count_y)
                for b in range(3):
                    rows = slice(2 * b, 2 * b + 2)
                    piece = out_a[rows] if j == 0 else wide["around"][j - 1, rows]
                    ring_a[source * 3 + b, a_row:a_row + 2, :] = piece
            for b in range(5):
                ring_a[blocks + b] = ring_a[b]
            shift = shifts[0, place_of]
            near = view_b(kind, shift)[0:8]
            phase = (near * 0.75 + rolled(near, NZ, 1) * 0.25) if kind == 0 else (
                near * 0.25 + rolled(near, NZ, 1) * 0.75)
            row, at = ((22, 2), (12, 0))[kind]
            e_p[row:row + 2, 0:512] = phase[at:at + 2, 0:512]
            e_p[row:row + 2, 512:640] = phase[at:at + 2, 640:768]

    p = e_p[...]
    around = differences(p, place5)
    chem = bulk(p, around)
    slope = [0.5 * (a - b) for a, b in around]
    around = differences(chem, place5)
    next_phase = p + mobility * bent(chem, around)
    scaled = (-0.5 * coupling / relax_rate) * p / e_r[...]
    drift = []
    for axis in range(3):
        flow = e_u[axis]
        next_phase = next_phase - flow * slope[axis]
        drift.append(flow + scaled * (around[axis][0] - around[axis][1]))
    for top, at, size in ((0, 0, 12), (12, 12, 2), (14, 22, 2)):
        ext[top:top + size, 0:WIDE] = next_phase[at:at + size, 0:WIDE]
        ext[top:top + size, WIDE:512] = jnp.where(
            lane1[:size] < 64, next_phase[at:at + size, 384:512], next_phase[at:at + size, 512:640]
        )
    collide(e_r[0:16, 0:WIDE], [d[0:16, 0:WIDE] for d in drift], None, lambda slot: f[slot])
    for k in (0, 1):
        cut = slice(512, 640) if k == 0 else slice(384, 512)
        patch_y(k, packed_post(k, wide["y"][k, 0:16], e_r[0:16, cut], [d[0:16, cut] for d in drift], lane1))
    for kind, is_plane, place_of in sides:
        @pl.when(is_plane)
        def _(kind=kind, place_of=place_of):
            first = shifts[0, place_of]
            row = lax.broadcasted_iota(jnp.int32, (8, 768), 0)
            edge, at, outer = ((3, 2, 14), (0, 0, 12))[kind]
            weights_of = ((0.75, 0.25), (0.25, 0.75))[kind]
            for step in (0, 1):
                shift = shifts[step, place_of]
                both = view_b(kind, shift)
                turn = shift - first if kind == 0 else first - shift - 1
                own = window_of(ring_a, turn)
                own = 0.75 * own + 0.25 * rolled(own, -NZ if kind == 0 else NZ, 1)
                far_p = jnp.where(row < 4, both[0:8], own)
                around = differences(far_p, place6)
                chem = bulk(far_p, around)
                slope = [0.5 * (a - b) for a, b in around]
                around = differences(chem, place6)
                if step == 0:
                    density = both[4:5]
                    scaled = (-0.5 * coupling / relax_rate) * far_p[edge:edge + 1] / density
                    drift = [
                        both[5 + axis:6 + axis]
                        + scaled * (around[axis][0] - around[axis][1])[edge:edge + 1]
                        for axis in range(3)
                    ]
                    strip = strip_post(kind, both[8:16], density, drift, place6)
                    strip = weights_of[0] * strip + weights_of[1] * rolled(strip, NZ, 1)
                    patch_x(kind, strip_moved(strip))
                else:
                    after = far_p + mobility * bent(chem, around)
                    for axis in range(3):
                        flow = jnp.where(row == edge, both[5 + axis:6 + axis], both[13 + axis:14 + axis])
                        after = after - flow * slope[axis]
                    after = weights_of[0] * after + weights_of[1] * rolled(after, NZ, 1)
                    ext[outer:outer + 2, 0:WIDE] = after[at:at + 2, 0:WIDE]
                    ext[outer:outer + 2, WIDE:512] = jnp.where(
                        lane1[:2] < 64, after[at:at + 2, 384:512], after[at:at + 2, 640:768]
                    )

        @pl.when(jnp.logical_not(is_plane))
        def _(kind=kind):
            edge = (23, 12)[kind]
            at = len(first_units) - 1
            ends = [
                rolled(wide["corner"][2 * kind + k, at // 5:at // 5 + 1], lane_of(k, 1) - NZ * (at % 5), 1)
                for k in (1, 0)
            ]
            strip = jnp.concatenate(
                [wide["side"][kind, 16 * b + 8:16 * b + 16] for b in range(3)]
                + [jnp.broadcast_to(line, (8, 128)) for line in ends],
                axis=1,
            )
            strip = strip_post(
                kind, strip, e_r[edge:edge + 1, :], [d[edge:edge + 1] for d in drift], place5[:8]
            )
            patch_x(kind, strip_moved(strip))

    advance(1)
    wait_sent(0)
    receive(1, 1)

    advance(2)
    y_cut = (slice(256, 384), slice(0, 128))
    lines = [fx[group[0], edge:edge + 1, 0:WIDE] for edge in (11, 0) for group in x_groups]
    lines += [fx[1, 11:12, 0:WIDE], fx[2, 0:1, 0:WIDE]]
    halves = 0.5 * jnp.concatenate(lines, axis=0)
    ahead, behind = moved_yz(halves, 0, -1, place[:8]), moved_yz(halves, 0, 1, place[:8])
    for kind in (0, 1):
        edge, second, low = ((11, 10, 9), (0, 1, 0))[kind]
        inward = (up_slots, down_slots)[kind]
        for b in range(3):
            cut = slice(b * 128, b * 128 + 128)
            for i, slot in enumerate(inward):
                last_x[kind, 19 * b + i:19 * b + i + 1, :] = fx[slot, edge:edge + 1, cut]
                last_x[kind, 19 * b + 11 + i:19 * b + 12 + i, :] = fx[slot, second:second + 1, cut]
            for i, (first, slot) in enumerate(folded_x):
                at = x_groups.index(next(g for g in x_groups if g[0] == first)) + 3 * kind
                half = (ahead if lattice_vel[slot][2] == 1 else behind)[at:at + 1, cut]
                last_x[kind, 19 * b + 5 + i:19 * b + 6 + i, :] = fx[slot, edge:edge + 1, cut] + half
            last_x[kind, 19 * b + 16:19 * b + 19, :] = ext[low:low + 3, cut]
        for k in (0, 1):
            units = corner_units(kind, k)
            for i in range(0, len(units), 5):
                line = None
                for j, (slot, deep_x, deep_y) in enumerate(units[i:i + 5]):
                    row = 12 - deep_x if kind == 0 else deep_x - 1
                    part = ext[row:row + 1, y_cut[k]] if slot is None else fx[slot, row:row + 1, y_cut[k]]
                    part = rolled(part, NZ * j - lane_of(k, deep_y), 1)
                    line = part if j == 0 else jnp.where(lane1[:1] >= NZ * j, part, line)
                last_corner[2 * kind + k, i // 5:i // 5 + 1, :] = line
    for is_plane, edge, slots in ((left_plane, 0, down_slots), (right_plane, 11, up_slots)):
        @pl.when(is_plane)
        def _(edge=edge, slots=slots):
            at = 6 if edge == 11 else 7
            for b in range(3):
                cut = slice(b * 128, b * 128 + 128)
                for i, slot in enumerate(slots[1:]):
                    line = fx[slot, edge:edge + 1, cut]
                    if lattice_vel[slot][2] != 0:
                        line = line + (ahead if lattice_vel[slot][2] == 1 else behind)[at:at + 1, cut]
                    last_a[4 * b + i:4 * b + i + 1, :] = line

    send_around(2, last_a)
    send_x(2, last_x)
    send_sides(2, last_x, last_corner)
    for k in (0, 1):
        spots = lax.rem(lane1 + (16 if k == 0 else 0), NZ)
        for i in range(0, len(y_units[k]), 5):
            line = None
            for j, (slot, deep) in enumerate(y_units[k][i:i + 5]):
                part = ext[0:16, y_cut[k]] if slot is None else fx[slot, :, y_cut[k]]
                for first, folded in folded_y:
                    if folded == slot:
                        part = part + moved_yz(0.5 * fx[first, :, y_cut[k]], 0, -lattice_vel[slot][2], spots)
                part = rolled(part, NZ * j - lane_of(k, deep), 1)
                line = part if j == 0 else jnp.where(lane1 >= NZ * j, part, line)
            last_y[k, 12 * (i // 5):12 * (i // 5) + 12, :] = line[:12]
    send_y(2, last_y)
    e_p[0:12, 0:WIDE] = ext[0:12, 0:WIDE]
    wait_sent(1)

    wait_near(2)
    last = brought[2]

    def unit_of_y(k, slot, deep):
        place = y_units[k].index((slot, deep))
        row = 12 * (place // 5)
        return rolled(last["y"][k, row:row + 12], lane_of(k, deep) - NZ * (place % 5), 1)

    lane12 = lane1[:12]
    for slot in range(19):
        step_y = lattice_vel[slot][1]
        if any(slot == group[0] for group in y_groups):
            rim = jnp.zeros((12, 128), jnp.float32)
        elif step_y == 0:
            rim = jnp.where(lane12 < 64, unit_of_y(1, slot, 1), unit_of_y(0, slot, 1))
        elif step_y == 1:
            rim = jnp.where(lane12 >= 104, unit_of_y(0, slot, 1), unit_of_y(0, slot, 2))
        else:
            rim = jnp.where(lane12 < NZ, unit_of_y(1, slot, 1), unit_of_y(1, slot, 2))
        fx[slot, 0:12, 384:512] = rim
    e_p[0:12, 384:512] = jnp.where(
        lane12 < NZ, unit_of_y(1, None, 1),
        jnp.where(lane12 < 2 * NZ, unit_of_y(1, None, 2), unit_of_y(1, None, 3)),
    )
    e_p[0:12, 512:640] = jnp.where(
        lane12 >= 104, unit_of_y(0, None, 1),
        jnp.where(lane12 >= 80, unit_of_y(0, None, 2), unit_of_y(0, None, 3)),
    )
    for kind, is_plane, place_of in sides:
        @pl.when(jnp.logical_not(is_plane))
        def _(kind=kind):
            rows = ((15, 14), (12, 13))[kind]
            low = (21, 12)[kind]
            inward = (up_slots, down_slots)[kind]
            whole = last["side"][kind]
            for group in x_groups:
                fx[group[0], rows[0]:rows[0] + 1, 0:WIDE] = jnp.zeros((1, WIDE), jnp.float32)
            for b in range(3):
                cut = slice(b * 128, b * 128 + 128)
                strip = whole[19 * b:19 * b + 19]
                for i, slot in enumerate(inward):
                    fx[slot, rows[0]:rows[0] + 1, cut] = strip[i:i + 1]
                    fx[slot, rows[1]:rows[1] + 1, cut] = strip[11 + i:12 + i]
                for i, (_, slot) in enumerate(folded_x):
                    fx[slot, rows[0]:rows[0] + 1, cut] = strip[5 + i:6 + i]
                e_p[low:low + 3, cut] = strip[16:19]
            found = {}
            for k in (0, 1):
                corner = last["corner"][2 * kind + k]
                for i, (slot, deep_x, deep_y) in enumerate(corner_units(kind, k)):
                    part = corner[i // 5:i // 5 + 1]
                    part = rolled(part, lane_of(k, deep_y) - NZ * (i % 5), 1)
                    found.setdefault((slot, deep_x), []).append((k, deep_y, part))
            for (slot, deep_x), parts in found.items():
                line = {}
                for k, deep_y, part in parts:
                    start = lane_of(k, deep_y)
                    here = (lane1[:1] >= start) & (lane1[:1] < start + NZ)
                    at = k if slot is None else 0
                    line[at] = jnp.where(here, part, line[at]) if at in line else part
                if slot is None:
                    row = 24 - deep_x if kind == 0 else 11 + deep_x
                    e_p[row:row + 1, 512:640] = line[0]
                    e_p[row:row + 1, 384:512] = line[1]
                else:
                    row = rows[deep_x - 1]
                    fx[slot, row:row + 1, 384:512] = line[0]

    for slot in range(19):
        step_x, step_y, step_z = lattice_vel[slot]
        if step_x == 0:
            fx[slot] = moved_yz(fx[slot], step_y, step_z, place4)

    def mixed(kind, value):
        near, far = ((0.75, 0.25), (0.25, 0.75))[kind]
        return near * value + far * rolled(value, NZ, 1)

    for kind, is_plane, place_of in sides:
        @pl.when(is_plane)
        def _(kind=kind, place_of=place_of):
            wait_plane(2)
            for b in range(blocks + 5):
                row = 19 * (b % 3)
                ring_e[b, 0:19] = last["plane"][b % blocks // 3, row:row + 19]
            for j in range(count_y):
                source = lax.rem(gy + count_y - j, count_y)
                for b in range(3):
                    rows = slice(4 * b, 4 * b + 4)
                    ring_o[source * 3 + b, 1:5] = last_a[rows] if j == 0 else last["around"][j - 1, rows]
            for b in range(5):
                ring_o[blocks + b] = ring_o[b]
            row = (15, 12)[kind]
            shift = shifts[2, place_of]
            strip = mixed(kind, window_of(ring_e, shift if kind == 0 else -shift - 1)[0:8])
            for i, slot in enumerate((up_slots, down_slots)[kind]):
                fx[slot, row:row + 1, 0:384] = strip[i:i + 1, 0:384]
                fx[slot, row:row + 1, 384:512] = jnp.where(
                    lane1[:1] < 64, strip[i:i + 1, 384:512], strip[i:i + 1, 640:768]
                )
            shift = shifts[3, place_of]
            phase = mixed(kind, window_of(ring_e, shift if kind == 0 else -shift - 1)[16:24])
            row, at = ((22, 1), (12, 0))[kind]
            e_p[row:row + 2, 0:512] = phase[at:at + 2, 0:512]
            e_p[row:row + 2, 512:640] = phase[at:at + 2, 640:768]

    def narrowed(to, value):
        for top, at, size in ((0, 0, 12), (12, 12, 2), (14, 22, 2)):
            to[top:top + size, 0:WIDE] = value[at:at + size, 0:WIDE]
            to[top:top + size, WIDE:512] = jnp.where(
                lane1[:size] < 64, value[at:at + size, 384:512], value[at:at + size, 512:640]
            )

    for slot in up_slots + down_slots:
        step_x, step_y, step_z = lattice_vel[slot]
        fx[slot] = moved_yz(rolled(fx[slot], step_x, 0), step_y, step_z, place4)
    p = e_p[...]
    narrowed(ext, p)
    narrowed(chem_x, bulk(p, differences(p, place5)))
    density, totals = momentum(fx)
    inverse = 1.0 / density
    p, chem = ext[...], chem_x[...]
    around = differences(p, place4)
    slope = [0.5 * (a - b)[:, :WIDE] for a, b in around]
    around = differences(chem, place4)
    next_phase = (p + mobility * bent(chem, around))[:, :WIDE]
    scaled = (-0.5 * coupling / relax_rate) * p
    drift = []
    for axis in range(3):
        next_phase = next_phase - (totals[axis] * inverse)[:, :WIDE] * slope[axis]
        drift.append((totals[axis] + scaled * (around[axis][0] - around[axis][1])) * inverse)
    p_out[...] = next_phase[:12]
    collide(density[:, :WIDE], [d[:, :WIDE] for d in drift], None, lambda slot: fx[slot, :, 0:WIDE])
    for k in (0, 1):
        here = None
        for i, slot in enumerate((plus_y, minus_y)[k]):
            part = rolled(fx[slot, :, 384:512], NZ + NZ * i if k == 0 else 104 - NZ * i, 1)
            if i == 0:
                here = part
            else:
                here = jnp.where(lane1 >= NZ * i if k == 0 else lane1 < 128 - NZ * i, part, here)
        rim = [d[:, 384:512] for d in drift]
        patch_y(k, packed_post(k, here, density[:, 384:512], rim, lane1))
    for kind, is_plane, place_of in sides:
        @pl.when(is_plane)
        def _(kind=kind, place_of=place_of):
            before, shift = shifts[2, place_of], shifts[3, place_of]
            edge, top, a_row, own_row = ((3, 1, 4, 0), (0, 0, 6, 10))[kind]
            far = window_of(ring_e, shift if kind == 0 else -shift - 1)
            inner = strip_moved(strip_along_z(kind, far[11:19], place6))
            turn = shift - before if kind == 0 else before - shift - 1
            outer = window_of(ring_o, turn)
            outer = 0.75 * outer + 0.25 * rolled(outer, -NZ if kind == 0 else NZ, 1)
            outer = strip_moved(strip_along_z(1 - kind, outer, place6))
            total = [None] * 4
            sign = 1.0 - 2.0 * kind
            for tile, way in ((inner, sign), (outer, -sign)):
                r = [tile[i:i + 1] for i in range(5)]
                whole = r[1] + r[2] + r[3] + r[4]
                if tile is inner:
                    whole = whole + r[0]
                found = (whole, way * whole, r[3] - r[4], way * (r[1] - r[2]))
                total = [b if a is None else a + b for a, b in zip(total, found)]
            for i, (_, slot) in enumerate(folded_x):
                _, step_y, step_z = lattice_vel[slot]
                line = moved_yz(far[5 + i:6 + i], step_y, step_z, place6[:1])
                total[0] = total[0] + line
                if step_y != 0:
                    total[2] = total[2] + step_y * line
                if step_z != 0:
                    total[3] = total[3] + step_z * line
            tile_a[...] = jnp.zeros_like(tile_a)
            tile_a[a_row:a_row + 2, 0:512] = e_p[own_row:own_row + 2, 0:512]
            tile_a[a_row:a_row + 2, 640:768] = e_p[own_row:own_row + 2, 512:640]
            own = tile_a[...]
            ahead = rolled(own, -NZ, 1)
            own = 0.75 * own + 0.25 * ahead if kind == 0 else 0.25 * own + 0.75 * ahead
            row = lax.broadcasted_iota(jnp.int32, (8, 768), 0)
            far_p = jnp.where(row < 4, rolled(far[16:24], top, 0), own)
            around = differences(bulk(far_p, differences(far_p, place6)), place6)
            inverse = 1.0 / total[0]
            scaled = (-0.5 * coupling / relax_rate) * far_p[edge:edge + 1]
            drift = [
                (total[1 + axis] + scaled * (around[axis][0] - around[axis][1])[edge:edge + 1]) * inverse
                for axis in range(3)
            ]
            strip = mixed(kind, strip_post(kind, inner, total[0], drift, place6))
            patch_x(kind, strip_moved(strip))

        @pl.when(jnp.logical_not(is_plane))
        def _(kind=kind):
            row = (15, 12)[kind]
            inward = (up_slots, down_slots)[kind]
            lines = [fx[slot, row:row + 1, :] for slot in inward]
            strip = jnp.concatenate(lines + lines[:1] * 3, axis=0)
            strip = strip_post(
                kind, strip, density[row:row + 1], [d[row:row + 1] for d in drift], place4[:8]
            )
            patch_x(kind, strip_moved(strip))

    wait_sent(2)
    for slot in range(19):
        f_out[slot] = f[slot, 0:12, :]


def on_device(populations, phase_field, plane_shifts):
    parts = lax.axis_size("gy")
    blocks = 3 * parts
    rounds = 3
    vmem = pl.BlockSpec(memory_space=pltpu.VMEM)
    return pl.pallas_call(
        kernel,
        out_shape=(
            jax.ShapeDtypeStruct(populations.shape, jnp.float32),
            jax.ShapeDtypeStruct(phase_field.shape, jnp.float32),
        ),
        in_specs=[pl.BlockSpec(memory_space=pltpu.SMEM), vmem, vmem],
        out_specs=(vmem, vmem),
        scratch_shapes=[
            pltpu.VMEM((19, 16, WIDE), jnp.float32),
            pltpu.VMEM((16, 512), jnp.float32),
            pltpu.VMEM((2, 21, 128), jnp.float32),
            pltpu.VMEM((2, 16, 128), jnp.float32),
            pltpu.VMEM((4, 1, 128), jnp.float32),
            pltpu.VMEM((blocks + 4, 8, 128), jnp.float32),
            pltpu.VMEM((24, 640), jnp.float32),
            pltpu.VMEM((24, 640), jnp.float32),
            pltpu.VMEM((3, 24, 640), jnp.float32),
            pltpu.VMEM((blocks + 5, 16, 128), jnp.float32),
            pltpu.VMEM((blocks + 5, 8, 128), jnp.float32),
            pltpu.VMEM((2, 48, 128), jnp.float32),
            pltpu.VMEM((2, 48, 128), jnp.float32),
            pltpu.VMEM((4, 3, 128), jnp.float32),
            pltpu.VMEM((6, 128), jnp.float32),
            pltpu.VMEM((19, 16, 512), jnp.float32),
            pltpu.VMEM((16, 512), jnp.float32),
            pltpu.VMEM((8, 768), jnp.float32),
            pltpu.VMEM((blocks + 5, 24, 128), jnp.float32),
            pltpu.VMEM((blocks + 5, 8, 128), jnp.float32),
            pltpu.VMEM((2, 57, 128), jnp.float32),
            pltpu.VMEM((2, 48, 128), jnp.float32),
            pltpu.VMEM((4, 5, 128), jnp.float32),
            pltpu.VMEM((12, 128), jnp.float32),
        ] + [
            pltpu.VMEM((count, rows, 128), jnp.float32)
            for count, rows in (
                (2, 48), (2, 48), (4, 3), (parts, 48), (parts - 1, 6),
                (2, 16), (2, 21), (4, 1), (parts, 21),
                (2, 48), (2, 57), (4, 5), (parts, 57), (parts - 1, 12),
            )
        ] + [
            pltpu.SemaphoreType.DMA((rounds, 5)),
            pltpu.SemaphoreType.DMA((rounds, 5)),
        ],
        compiler_params=pltpu.CompilerParams(
            collective_id=0, has_side_effects=True, vmem_limit_bytes=32 * 1024 * 1024
        ),
    )(plane_shifts, populations, phase_field)


def solution(mesh):
    return jax.shard_map(
        on_device,
        mesh=mesh,
        in_specs=(P(None, "gx", "gy"), P("gx", "gy"), P()),
        out_specs=(P(None, "gx", "gy"), P("gx", "gy")),
        check_vma=False,
    )
```

```python
import functools

import jax
import jax.numpy as jnp
from jax import lax
from jax.experimental import pallas as pl
from jax.experimental.pallas import tpu as pltpu
from jax.sharding import PartitionSpec as P

STEPS = 4
NZ = 24
ROWS = 12
WIDE = 384
SPAN = 4
MESH = pl.DeviceIdType.MESH

lattice_vel = (
    (0, 0, 0),
    (1, 0, 0),
    (-1, 0, 0),
    (0, 1, 0),
    (0, -1, 0),
    (0, 0, 1),
    (0, 0, -1),
    (1, 1, 0),
    (-1, -1, 0),
    (1, -1, 0),
    (-1, 1, 0),
    (1, 0, 1),
    (-1, 0, -1),
    (1, 0, -1),
    (-1, 0, 1),
    (0, 1, 1),
    (0, -1, -1),
    (0, 1, -1),
    (0, -1, 1),
)
relax_rate = 0.8
coupling = 0.01
mobility = 0.02

up_slots = (1, 11, 13, 7, 9)
down_slots = (2, 12, 14, 10, 8)
plus_y = (3, 7, 10, 15, 17)
minus_y = (4, 8, 9, 16, 18)


x_groups = ((0, 5, 6), (3, 15, 17), (4, 18, 16))
y_groups = ((0, 5, 6), (1, 11, 13), (2, 14, 12))
folded_x = tuple((first, slot) for first, *pair in x_groups for slot in pair)
folded_y = tuple((first, slot) for first, *pair in y_groups for slot in pair)
near_y = tuple(slots + tuple(slot for _, slot in folded_y) for slots in (plus_y, minus_y))
y_units = tuple(
    tuple((slot, 1) for slot in near_y[k]) + tuple((slot, 2) for slot in (plus_y, minus_y)[k])
    + ((None, 1), (None, 2), (None, 3))
    for k in (0, 1)
)


def corner_units(kind, k):
    step = (1 - 2 * kind, 1 - 2 * k)
    units = []
    for deep in ((1, 1), (2, 1), (1, 2), (2, 2)):
        for slot in range(19):
            if all(
                lattice_vel[slot][axis] == step[axis] or (deep[axis] == 1 and lattice_vel[slot][axis] == 0)
                for axis in (0, 1)
            ):
                units.append((slot,) + deep)
    return tuple(units) + tuple((None, x, y) for x in (1, 2, 3) for y in range(1, 5 - x))


first_units = tuple(("p", x, y) for x in (1, 2, 3) for y in range(1, 5 - x)) + tuple(
    (what, 1, 1) for what in ("r", 0, 1, 2, "f")
)


def lane_of(k, depth):
    return 128 - NZ * depth if k == 0 else NZ * (depth - 1)


def rolled(value, shift, axis):
    size = value.shape[axis]
    shift = shift % size
    return value if shift == 0 else pltpu.roll(value, shift, axis)


def moved_yz(value, step_y, step_z, place):
    if step_z == 0:
        return rolled(value, step_y * NZ, 1)
    edge = 0 if step_z == 1 else NZ - 1
    inner = rolled(value, step_y * NZ + step_z, 1)
    wrap = rolled(value, step_y * NZ + step_z - step_z * NZ, 1)
    return jnp.where(place == edge, wrap, inner)


def differences(value, place):
    return (
        (rolled(value, -1, 0), rolled(value, 1, 0)),
        (rolled(value, -NZ, 1), rolled(value, NZ, 1)),
        (moved_yz(value, 0, -1, place), moved_yz(value, 0, 1, place)),
    )


def bulk(p, around):
    total = around[0][0] + around[0][1] + around[1][0] + around[1][1] + around[2][0] + around[2][1]
    return 0.5 * (p * p * p - p) - 0.5 * (total - 6.0 * p)


def bent(chem, around):
    total = around[0][0] + around[0][1] + around[1][0] + around[1][1] + around[2][0] + around[2][1]
    return total - 6.0 * chem


def relaxed(here, weight, along, drift):
    square = drift[0] * drift[0] + drift[1] * drift[1] + drift[2] * drift[2]
    return (1.0 - relax_rate) * here + weight * (
        1.0 - 1.5 * square + 3.0 * along + 4.5 * along * along
    )


def strip_post(kind, here, density, drift, place):
    sign = 1.0 - 2.0 * kind
    row = lax.broadcasted_iota(jnp.int32, here.shape, 0)
    full = [jnp.broadcast_to(d, here.shape) for d in drift]
    along = sign * full[0]
    along = along + jnp.where(row == 3, full[1], jnp.where(row == 4, -full[1], 0.0))
    along = along + jnp.where(row == 1, sign * full[2], jnp.where(row == 2, -sign * full[2], 0.0))
    weight = jnp.where(row == 0, 2.0, 1.0) * (relax_rate / 36.0) * density
    post = relaxed(here, weight, along, full)
    return strip_along_z(kind, post, place)


def strip_along_z(kind, strip, place):
    row = lax.broadcasted_iota(jnp.int32, strip.shape, 0)
    first, second = (1, -1) if kind == 0 else (-1, 1)
    return jnp.where(
        row == 1, moved_yz(strip, 0, first, place), jnp.where(row == 2, moved_yz(strip, 0, second, place), strip)
    )


def strip_moved(strip):
    row = lax.broadcasted_iota(jnp.int32, strip.shape, 0)
    return jnp.where(row == 3, rolled(strip, NZ, 1), jnp.where(row == 4, rolled(strip, -NZ, 1), strip))


def packed_post(k, here, density, drift, lane1):
    def spread(value):
        out = rolled(value, NZ if k == 0 else 104, 1)
        first = out
        for i in range(1, 5):
            if k == 0:
                out = jnp.where(lane1 >= i * NZ, rolled(first, i * NZ, 1), out)
            else:
                out = jnp.where(lane1 < 128 - i * NZ, rolled(first, -i * NZ, 1), out)
        return out

    slots = plus_y if k == 0 else minus_y
    group = lane1 // NZ if k == 0 else (127 - lane1) // NZ
    density, drift = spread(density), [spread(d) for d in drift]

    def chosen(axis, value):
        out = jnp.zeros_like(value)
        for i, slot in enumerate(slots):
            if lattice_vel[slot][axis] != 0:
                out = jnp.where(group == i, lattice_vel[slot][axis] * value, out)
        return out

    along = chosen(0, drift[0]) + chosen(1, drift[1]) + chosen(2, drift[2])
    weight = jnp.where(group == 0, 2.0, 1.0) * (relax_rate / 36.0) * density
    post = relaxed(here, weight, along, drift)
    place = lax.rem(lane1, NZ) if k == 0 else lax.rem(lane1 + 16, NZ)
    out = post
    for i, slot in enumerate(slots):
        step_x, _, step_z = lattice_vel[slot]
        if step_x != 0 or step_z != 0:
            out = jnp.where(group == i, moved_yz(rolled(post, step_x, 0), 0, step_z, place), out)
    return out


def lanes_of_y(k):
    groups = [NZ * i if k == 0 else 104 - NZ * i for i in range(5)]
    return groups, (120 if k == 0 else 0), ((104, 80) if k == 0 else (0, 24))


def with_phase(k, packed, phase):
    groups, spare, (first, second) = lanes_of_y(k)
    lane = lax.broadcasted_iota(jnp.int32, (8, 128), 1)
    upper = lax.broadcasted_iota(jnp.int32, (8, 128), 0) >= 4
    in_spare = (lane >= spare) & (lane < spare + 8)
    top, low = phase[0:8], phase[8:16]
    top_down, low_down = rolled(top, 4, 0), rolled(low, 4, 0)
    head, tail = packed[0:8], packed[8:16]
    pieces = ((top_down, first), (top, first), (low_down, first), (top_down, second), (top, second))
    for start, (piece, at) in zip(groups, pieces):
        here = upper & (lane >= start) & (lane < start + NZ)
        tail = jnp.where(here, rolled(piece, start - at, 1), tail)
    parts = [
        rolled(low, spare - second, 1),
        rolled(low_down, spare - second - 8, 1),
        rolled(low, spare - second - 16, 1),
    ]
    head = jnp.where(in_spare, jnp.where(upper, parts[1], parts[0]), head)
    tail = jnp.where(in_spare & jnp.logical_not(upper), parts[2], tail)
    return jnp.concatenate([head, tail], axis=0)


def phase_part(k, message):
    groups, spare, (first, second) = lanes_of_y(k)
    lane = lax.broadcasted_iota(jnp.int32, (8, 128), 1)
    upper = lax.broadcasted_iota(jnp.int32, (8, 128), 0) >= 4
    in_first = (lane >= first) & (lane < first + NZ)
    head, tail = message[0:8], message[8:16]
    head_up, tail_up = rolled(head, 4, 0), rolled(tail, 4, 0)

    def picked(near, far):
        return jnp.where(in_first, rolled(near[0], first - near[1], 1), rolled(far[0], second - far[1], 1))

    top = jnp.where(
        upper,
        picked((tail, groups[1]), (tail, groups[4])),
        picked((tail_up, groups[0]), (tail_up, groups[3])),
    )
    far = jnp.where(
        lane < second + 8,
        rolled(head, second - spare, 1),
        jnp.where(
            lane < second + 16,
            rolled(head_up, second + 8 - spare, 1),
            rolled(tail, second + 16 - spare, 1),
        ),
    )
    low = jnp.where(in_first, rolled(tail_up, first - groups[2], 1), far)
    return jnp.concatenate([top, low], axis=0)


def kernel(
    shifts, f_in, p_in, f_out, p_out,
    f, ext, to_x, to_y, to_corner, ring,
    e_p, e_r, e_u, ring_b, ring_a, out_x, out_y, out_corner, out_a,
    fx, chem_x, tile_a, ring_e, ring_o, last_x, last_y, last_corner, last_a,
    *landings_and_semaphores,
):
    count_x, count_y = lax.axis_size("gx"), lax.axis_size("gy")
    gx, gy = lax.axis_index("gx"), lax.axis_index("gy")
    above, below = lax.rem(gx + 1, count_x), lax.rem(gx + count_x - 1, count_x)
    front, back = lax.rem(gy + 1, count_y), lax.rem(gy + count_y - 1, count_y)
    planes = count_x // SPAN
    left_plane = lax.rem(gx, SPAN) == 0
    right_plane = lax.rem(gx, SPAN) == SPAN - 1
    left_slot = lax.rem(gx // SPAN + planes - 1, planes)
    right_slot = gx // SPAN
    any_plane = left_plane | right_plane
    blocks = 3 * count_y
    sides = ((0, left_plane, left_slot), (1, right_plane, right_slot))

    def signal(x, y):
        pl.semaphore_signal(barrier, inc=1, device_id=(x, y), device_id_type=MESH)

    barrier = pltpu.get_barrier_semaphore()
    any_plane = left_plane | right_plane
    def far_first():
        half = count_y // 2
        order = [(half // 2, 1), (half // 2, 0)]
        for dx in range(half // 2 - 1, -1, -1):
            order += [(d, z) for z in (1, 0) for d in sorted({dx, (half - dx) % half})]
        return [2 * lax.rem(gy // 2 + dx, half) + lax.rem(gy + dz, 2) for dx, dz in dict.fromkeys(order)]

    for is_plane, side in ((left_plane, below), (right_plane, above)):
        @pl.when(is_plane)
        def _(side=side):
            for y in far_first():
                signal(side, y)
            for j in range(2, count_y - 1):
                signal(gx, lax.rem(gy + j, count_y))

    signal(gx, front)
    signal(gx, back)
    for is_plane, side in ((left_plane, below), (right_plane, above)):
        @pl.when(jnp.logical_not(is_plane))
        def _(side=side):
            signal(side, front)
            signal(side, back)
            signal(side, gy)

    lane = lax.broadcasted_iota(jnp.int32, (16, WIDE), 1)
    place = lax.rem(lane, NZ)
    lane4 = lax.broadcasted_iota(jnp.int32, (16, 512), 1)
    place4 = lax.rem(jnp.where(lane4 < 448, lane4, lane4 - 464), NZ)
    lane1 = lax.broadcasted_iota(jnp.int32, (16, 128), 1)
    lane5 = lax.broadcasted_iota(jnp.int32, (24, 640), 1)
    place5 = lax.rem(jnp.where(lane5 < 512, lane5, lane5 + 8), NZ)
    place6 = lax.rem(lax.broadcasted_iota(jnp.int32, (8, 768), 1), NZ)

    def pack_phase(r):
        for b in range(3):
            cut = slice(b * 128, b * 128 + 128)
            to_x[0, 7 * b + 5:7 * b + 7, :] = ext[10:12, cut]
            to_x[1, 7 * b + 5:7 * b + 7, :] = ext[0:2, cut]

    *landings, sent, arrived = landings_and_semaphores
    brought = (
        dict(zip(("y", "side", "corner", "plane", "around"), landings[0:5])),
        dict(zip(("y", "side", "corner", "plane"), landings[5:9])),
        dict(zip(("y", "side", "corner", "plane", "around"), landings[9:14])),
    )
    names = ("y", "side", "corner", "plane", "around")

    def remote(src, r, name, index, x, y):
        pltpu.make_async_remote_copy(
            src_ref=src, dst_ref=brought[r][name].at[index],
            send_sem=sent.at[r, names.index(name)], recv_sem=arrived.at[r, names.index(name)],
            device_id=(x, y), device_id_type=MESH,
        ).start()

    def send_x(r, strips):
        for kind, is_plane, side in ((0, right_plane, above), (1, left_plane, below)):
            @pl.when(is_plane)
            def _(kind=kind, side=side):
                for y in far_first():
                    remote(strips.at[kind], r, "plane", gy, side, y)

    def send_sides(r, strips, corners):
        for kind, is_plane, side in ((0, right_plane, above), (1, left_plane, below)):
            @pl.when(jnp.logical_not(is_plane))
            def _(kind=kind, side=side):
                for k, y in ((0, front), (1, back)):
                    remote(corners.at[2 * kind + k], r, "corner", 2 * kind + k, side, y)
                remote(strips.at[kind], r, "side", kind, side, gy)

    def send_around(r, rows):
        @pl.when(any_plane)
        def _():
            for j in range(1, count_y):
                remote(rows, r, "around", j - 1, gx, lax.rem(gy + j, count_y))

    def send_y(r, messages):
        for k, y in ((0, front), (1, back)):
            remote(messages.at[k], r, "y", k, gx, y)

    def wait_for(r, name, sems):
        ref, sem = brought[r][name], sems.at[r, names.index(name)]
        if name in ("side", "corner"):
            step = 1 if name == "side" else 2
            for is_kind, start, size in (
                (left_plane, 1, 1), (right_plane, 0, 1), (jnp.logical_not(any_plane), 0, 2)
            ):
                @pl.when(is_kind)
                def _(start=start, size=size):
                    part = ref.at[pl.ds(step * start, step * size)]
                    pltpu.make_async_copy(part, part, sem).wait()
        else:
            pltpu.make_async_copy(ref, ref, sem).wait()

    def wait_sent(r):
        for name in ("y", "side", "corner"):
            wait_for(r, name, sent)

        @pl.when(any_plane)
        def _():
            for name in ("plane", "around"):
                if name in brought[r]:
                    wait_for(r, name, sent)

    def wait_near(r):
        for name in ("side", "corner", "y"):
            wait_for(r, name, arrived)

    def wait_plane(r):
        for name in ("plane", "around"):
            if name in brought[r]:
                wait_for(r, name, arrived)

    def window_of(held, turn):
        start = ((gy * 16 - turn - 4) & (16 * count_y - 1)) * NZ
        first, offset = start >> 7, start & 127
        window = jnp.concatenate([held[first + i] for i in range(6)], axis=1)
        return pltpu.roll(window, 768 - 4 * NZ - offset, 1)

    def view_b(kind, shift):
        return window_of(ring_b, shift if kind == 0 else -shift - 1)

    def close_ring(r):
        for b in range(blocks + 4):
            row = 7 * (b % 3)
            ring[b, 0:7] = brought[r]["plane"][b % blocks // 3, row:row + 7]

    def view(kind, shift):
        low = shift if kind == 0 else -shift - 1
        near, far = (0.75, 0.25) if kind == 0 else (0.25, 0.75)
        start = ((gy * 16 - low - 3) & (16 * count_y - 1)) * NZ
        first, offset = start >> 7, start & 127
        window = jnp.concatenate([ring[first + i] for i in range(5)], axis=1)
        window = pltpu.roll(window, 640 - 3 * NZ - offset, 1)
        return near * window + far * rolled(window, NZ, 1)

    def patch_y(k, packed):
        cut = slice(0, 128) if k == 0 else slice(256, 384)
        keep = lane1 < NZ if k == 0 else lane1 >= 128 - NZ
        for i, slot in enumerate(plus_y if k == 0 else minus_y):
            part = rolled(packed, -i * NZ if k == 0 else i * NZ, 1)
            f[slot, :, cut] = jnp.where(keep, part, f[slot, :, cut])

    def patch_x(kind, strip):
        edge = 0 if kind == 0 else ROWS - 1
        for i, slot in enumerate(up_slots if kind == 0 else down_slots):
            f[slot, edge:edge + 1, :] = strip[i:i + 1, :WIDE]

    def receive(r, step):
        wait_near(r)
        for k in (0, 1):
            patch_y(k, brought[r]["y"][k])
        ext[0:12, 384:512] = jnp.where(
            lane1 < 64, phase_part(1, brought[r]["y"][1]), phase_part(0, brought[r]["y"][0])
        )[:12]
        for kind, is_plane, _ in sides:
            @pl.when(jnp.logical_not(is_plane))
            def _(kind=kind):
                outer = 14 - 2 * kind
                near_row = 15 - 3 * kind
                e = (0, ROWS - 1)[kind]
                side, corner = brought[r]["side"], brought[r]["corner"]
                strip = jnp.concatenate([side[kind, 7 * b:7 * b + 7] for b in range(3)], axis=1)
                first, last = corner[2 * kind], corner[2 * kind + 1]
                plus = rolled(strip, NZ, 1)
                minus = rolled(strip, -NZ, 1)
                slots = up_slots if kind == 0 else down_slots
                for i in range(3):
                    f[slots[i], e:e + 1, :] = strip[i:i + 1]
                head = jnp.where(lane1[:1] < NZ, first, plus[3:4, 0:128])
                tail = jnp.where(lane1[:1] >= 128 - NZ, last, minus[4:5, 256:384])
                f[slots[3], e:e + 1, 0:128] = head
                f[slots[3], e:e + 1, 128:384] = plus[3:4, 128:384]
                f[slots[4], e:e + 1, 0:256] = minus[4:5, 0:256]
                f[slots[4], e:e + 1, 256:384] = tail
                ext[outer:outer + 2, 0:WIDE] = strip[5:7]
                ext[near_row:near_row + 1, WIDE:512] = jnp.where(lane1[:1] < 64, last, first)

        for kind, is_plane, place_of in sides:
            @pl.when(is_plane)
            def _(kind=kind, place_of=place_of):
                outer = 14 - 2 * kind
                wait_plane(r)
                close_ring(r)
                patch_x(kind, strip_moved(view(kind, shifts[step, place_of])))
                phase = view(kind, shifts[jnp.minimum(step + 1, STEPS - 1), place_of])
                ext[outer:outer + 2, 0:WIDE] = phase[5:7, 0:WIDE]
                ext[outer:outer + 2, WIDE:512] = jnp.where(
                    lane1[:2] < 64, phase[5:7, 384:512], phase[5:7, 512:640]
                )

    def momentum(f):
        density = f[0]
        for slot in range(1, 19):
            density = density + f[slot]
        totals = []
        for axis in range(3):
            total = None
            for slot in range(1, 19, 2):
                sign = lattice_vel[slot][axis]
                if sign != 0:
                    pair = f[slot] - f[slot + 1]
                    if total is None:
                        total = pair
                    else:
                        total = total + pair if sign == 1 else total - pair
            totals.append(total)
        return density, totals

    def advance(r):
        p = ext[...]
        around = differences(p, place4)
        chem = bulk(p, around)
        slope = [0.5 * (a - b)[:, :WIDE] for a, b in around]
        around = [(a[:, :WIDE], b[:, :WIDE]) for a, b in differences(chem, place4)]
        bend = bent(chem[:, :WIDE], around)
        own = p[:, :WIDE]
        density, totals = momentum(f)
        inverse = 1.0 / density
        scaled = (-0.5 * coupling / relax_rate) * own
        next_phase = own + mobility * bend
        drift = []
        for axis in range(3):
            next_phase = next_phase - totals[axis] * inverse * slope[axis]
            drift.append((totals[axis] + scaled * (around[axis][0] - around[axis][1])) * inverse)
        ext[0:12, 0:WIDE] = next_phase[:12]
        if r == 1:
            pack_phase(r)
        collide(density, drift, r, lambda slot: f[slot])

    def collide(density, drift, r, source):
        base = 1.0 - 1.5 * (drift[0] * drift[0] + drift[1] * drift[1] + drift[2] * drift[2])
        weight = relax_rate / 36.0 * density
        keep = 1.0 - relax_rate
        packs = {}

        def put(slot, post):
            step_x, step_y, step_z = lattice_vel[slot]
            if r == 2:
                fx[slot, :, 0:WIDE] = post
                return
            value = rolled(post, step_x, 0)
            moved = moved_yz(value, step_y, step_z, place)
            f[slot] = moved
            if r is None:
                return
            if step_x != 0:
                kind = 0 if step_x == 1 else 1
                i = (up_slots, down_slots)[kind].index(slot)
                line = 12 if step_x == 1 else 15
                shown = value if step_y != 0 else moved
                for b in range(3):
                    to_x[kind, 7 * b + i:7 * b + i + 1, :] = shown[line:line + 1, b * 128:b * 128 + 128]
                if step_y != 0:
                    k = 2 * kind + (0 if step_y == 1 else 1)
                    cut = slice(0, 128) if step_y == 1 else slice(256, 384)
                    edge = 11 if step_x == 1 else 0
                    own = ext[edge:edge + 1, slice(256, 384) if step_y == 1 else slice(0, 128)]
                    post_row = moved[line:line + 1, cut]
                    low = lane1[:1] < 64
                    to_corner[k] = (
                        jnp.where(low, post_row, own) if step_y == 1 else jnp.where(low, own, post_row)
                    )
            if step_y == 1:
                i = plus_y.index(slot)
                part = rolled(moved[:, 0:128], i * NZ, 1)
                mine = (lane1 >= i * NZ) & (lane1 < i * NZ + NZ)
                packs[0] = jnp.where(mine, part, packs[0]) if 0 in packs else part
            if step_y == -1:
                i = minus_y.index(slot)
                part = rolled(moved[:, 256:384], -i * NZ, 1)
                mine = (lane1 < 128 - i * NZ) & (lane1 >= 128 - NZ - i * NZ)
                packs[1] = jnp.where(mine, part, packs[1]) if 1 in packs else part

        def put_pair(slot):
            along = None
            for axis in range(3):
                sign = lattice_vel[slot][axis]
                if sign != 0:
                    if along is None:
                        along = drift[axis]
                    else:
                        along = along + drift[axis] if sign == 1 else along - drift[axis]
            scale = 2.0 * weight if slot < 7 else weight
            even = scale * (base + 4.5 * along * along)
            odd = scale * (3.0 * along)
            here, there = source(slot), source(slot + 1)
            put(slot, keep * here + (even + odd))
            put(slot + 1, keep * there + (even - odd))

        for slot in (1, 7, 9, 11, 13):
            put_pair(slot)
        if r == 1:
            send_x(r, to_x)
            send_sides(r, to_x, to_corner)
        for slot in (3, 15, 17):
            put_pair(slot)
        if r == 1:
            for k in (0, 1):
                to_y[k] = with_phase(k, packs[k], ext[0:16, 256:384] if k == 0 else ext[0:16, 0:128])
            send_y(r, to_y)
        put_pair(5)
        put(0, keep * source(0) + 12.0 * weight * base)

    for slot in range(19):
        f[slot, 0:12, :] = f_in[slot]
        f[slot, 12:16, :] = jnp.ones((4, WIDE), jnp.float32)
    ext[...] = jnp.zeros_like(ext)
    e_p[...] = jnp.zeros_like(e_p)
    e_r[...] = jnp.ones_like(e_r)
    e_u[...] = jnp.zeros_like(e_u)
    e_p[0:12, 0:WIDE] = p_in[...]
    density, totals = momentum(f)
    e_r[0:12, 0:WIDE] = density[:12]
    for axis in range(3):
        e_u[axis, 0:12, 0:WIDE] = (totals[axis] / density)[:12]

    for kind in (0, 1):
        edge, second, low = ((11, 10, 8), (0, 1, 0))[kind]
        for b in range(3):
            cut = slice(b * 128, b * 128 + 128)
            out_x[kind, 16 * b:16 * b + 4, :] = e_p[low:low + 4, cut]
            out_x[kind, 16 * b + 4:16 * b + 5, :] = e_r[edge:edge + 1, cut]
            for axis in range(3):
                out_x[kind, 16 * b + 5 + axis:16 * b + 6 + axis, :] = e_u[axis, edge:edge + 1, cut]
                out_x[kind, 16 * b + 13 + axis:16 * b + 14 + axis, :] = e_u[axis, second:second + 1, cut]
            for i, slot in enumerate(up_slots if kind == 0 else down_slots):
                out_x[kind, 16 * b + 8 + i:16 * b + 9 + i, :] = f[slot, edge:edge + 1, cut]
        for k in (0, 1):
            cut = slice(256, 384) if k == 0 else slice(0, 128)
            slot = (up_slots if kind == 0 else down_slots)[3 + k]
            for i in range(0, len(first_units), 5):
                line = None
                for j, (what, deep_x, deep_y) in enumerate(first_units[i:i + 5]):
                    row = 12 - deep_x if kind == 0 else deep_x - 1
                    if what == "p":
                        part = e_p[row:row + 1, cut]
                    elif what == "r":
                        part = e_r[row:row + 1, cut]
                    elif what == "f":
                        part = f[slot, row:row + 1, cut]
                    else:
                        part = e_u[what, row:row + 1, cut]
                    part = rolled(part, NZ * j - lane_of(k, deep_y), 1)
                    line = part if j == 0 else jnp.where(lane1[:1] >= NZ * j, part, line)
                out_corner[2 * kind + k, i // 5:i // 5 + 1, :] = line
    for k in (0, 1):
        cut = slice(256, 384) if k == 0 else slice(0, 128)
        packed = None
        for i, slot in enumerate(plus_y if k == 0 else minus_y):
            block = f[slot, :, cut]
            part = rolled(block, NZ + i * NZ if k == 0 else -NZ - i * NZ, 1)
            if i == 0:
                packed = part
            else:
                packed = jnp.where(lane1 >= i * NZ if k == 0 else lane1 < 128 - i * NZ, part, packed)
        out_y[k, 0:12, :] = packed[:12]
        lane12 = lane1[:12]
        free = lane12 < 32 if k == 0 else lane12 >= 96
        second = (lane12 >= 32) & (lane12 < 80) if k == 0 else (lane12 >= 48) & (lane12 < 96)
        density_at, flow_at, deep_at = ((NZ, 32, 80), (96, 96, NZ))[k]
        out_y[k, 12:24, :] = jnp.where(free, rolled(e_r[0:12, cut], density_at, 1), e_p[0:12, cut])
        u_z = e_u[2, 0:12, cut]
        out_y[k, 24:36, :] = jnp.where(
            free, rolled(u_z, flow_at, 1),
            jnp.where(second, rolled(e_u[1, 0:12, cut], -48 if k == 0 else 48, 1), e_u[0, 0:12, cut]),
        )
        deep = [rolled(u_z[4 * g:4 * g + 4], NZ * g - deep_at, 1) for g in range(3)]
        out_y[k, 36:40, :] = jnp.where(
            lane1[:4] < NZ, deep[0], jnp.where(lane1[:4] < 2 * NZ, deep[1], deep[2])
        )

    @pl.when(left_plane)
    def _():
        for b in range(3):
            out_a[2 * b:2 * b + 2, :] = e_p[0:2, b * 128:b * 128 + 128]

    @pl.when(right_plane)
    def _():
        for b in range(3):
            out_a[2 * b:2 * b + 2, :] = e_p[10:12, b * 128:b * 128 + 128]

    pl.semaphore_wait(barrier, jnp.where(any_plane, 5 + count_y + max(count_y - 3, 0), 8))

    send_around(0, out_a)
    send_x(0, out_x)
    send_sides(0, out_x, out_corner)
    send_y(0, out_y)

    wait_near(0)
    wide = brought[0]
    for k in (0, 1):
        cut = slice(512, 640) if k == 0 else slice(384, 512)
        e_p[0:12, cut] = wide["y"][k, 12:24]
        density_at, flow_at, deep_at = ((NZ, 32, 80), (96, 96, NZ))[k]
        flow = wide["y"][k, 24:36]
        e_r[0:12, cut] = rolled(wide["y"][k, 12:24], -density_at, 1)
        e_u[0, 0:12, cut] = flow
        e_u[1, 0:12, cut] = rolled(flow, 48 if k == 0 else -48, 1)
        e_u[2, 0:12, cut] = rolled(flow, -flow_at, 1)
        here = (lane1[:4] >= deep_at) & (lane1[:4] < deep_at + NZ)
        for g in range(3):
            rows = slice(4 * g, 4 * g + 4)
            deep = rolled(wide["y"][k, 36:40], deep_at - NZ * g, 1)
            e_u[2, rows, cut] = jnp.where(here, deep, e_u[2, rows, cut])
    for kind, is_plane, place_of in sides:
        low = (20, 12)[kind]
        edge, second, third = ((23, 22, 21), (12, 13, 12))[kind]

        @pl.when(jnp.logical_not(is_plane))
        def _(kind=kind, low=low, edge=edge, second=second, third=third):
            for k in (0, 1):
                cut = slice(512, 640) if k == 0 else slice(384, 512)
                found = {}
                for i, (what, deep_x, deep_y) in enumerate(first_units):
                    start = lane_of(k, deep_y)
                    part = wide["corner"][2 * kind + k, i // 5:i // 5 + 1]
                    part = rolled(part, start - NZ * (i % 5), 1)
                    here = (lane1[:1] >= start) & (lane1[:1] < start + NZ)
                    key = (what, deep_x)
                    found[key] = jnp.where(here, part, found[key]) if key in found else part
                for (what, deep_x), line in found.items():
                    row = 24 - deep_x if kind == 0 else 11 + deep_x
                    if what == "p":
                        e_p[row:row + 1, cut] = line
                    elif what == "r":
                        e_r[row:row + 1, cut] = line
                    elif what != "f":
                        e_u[what, row:row + 1, cut] = line
            for b in range(3):
                cut = slice(b * 128, b * 128 + 128)
                strip = wide["side"][kind, 16 * b:16 * b + 16]
                e_p[low:low + 4, cut] = strip[0:4]
                e_r[edge:edge + 1, cut] = strip[4:5]
                for axis in range(3):
                    e_u[axis, edge:edge + 1, cut] = strip[5 + axis:6 + axis]
                    e_u[axis, second:second + 1, cut] = strip[13 + axis:14 + axis]

    for kind, is_plane, place_of in sides:
        @pl.when(is_plane)
        def _(kind=kind, place_of=place_of):
            wait_plane(0)
            for b in range(blocks + 5):
                row = 16 * (b % 3)
                ring_b[b] = wide["plane"][b % blocks // 3, row:row + 16]
            a_row = (4, 6)[kind]
            for j in range(count_y):
                source = lax.rem(gy + count_y - j, count_y)
                for b in range(3):
                    rows = slice(2 * b, 2 * b + 2)
                    piece = out_a[rows] if j == 0 else wide["around"][j - 1, rows]
                    ring_a[source * 3 + b, a_row:a_row + 2, :] = piece
            for b in range(5):
                ring_a[blocks + b] = ring_a[b]
            shift = shifts[0, place_of]
            near = view_b(kind, shift)[0:8]
            phase = (near * 0.75 + rolled(near, NZ, 1) * 0.25) if kind == 0 else (
                near * 0.25 + rolled(near, NZ, 1) * 0.75)
            row, at = ((22, 2), (12, 0))[kind]
            e_p[row:row + 2, 0:512] = phase[at:at + 2, 0:512]
            e_p[row:row + 2, 512:640] = phase[at:at + 2, 640:768]

    p = e_p[...]
    around = differences(p, place5)
    chem = bulk(p, around)
    slope = [0.5 * (a - b) for a, b in around]
    around = differences(chem, place5)
    next_phase = p + mobility * bent(chem, around)
    scaled = (-0.5 * coupling / relax_rate) * p / e_r[...]
    drift = []
    for axis in range(3):
        flow = e_u[axis]
        next_phase = next_phase - flow * slope[axis]
        drift.append(flow + scaled * (around[axis][0] - around[axis][1]))
    for top, at, size in ((0, 0, 12), (12, 12, 2), (14, 22, 2)):
        ext[top:top + size, 0:WIDE] = next_phase[at:at + size, 0:WIDE]
        ext[top:top + size, WIDE:512] = jnp.where(
            lane1[:size] < 64, next_phase[at:at + size, 384:512], next_phase[at:at + size, 512:640]
        )
    collide(e_r[0:16, 0:WIDE], [d[0:16, 0:WIDE] for d in drift], None, lambda slot: f[slot])
    for k in (0, 1):
        cut = slice(512, 640) if k == 0 else slice(384, 512)
        patch_y(k, packed_post(k, wide["y"][k, 0:16], e_r[0:16, cut], [d[0:16, cut] for d in drift], lane1))
    for kind, is_plane, place_of in sides:
        @pl.when(is_plane)
        def _(kind=kind, place_of=place_of):
            first = shifts[0, place_of]
            row = lax.broadcasted_iota(jnp.int32, (8, 768), 0)
            edge, at, outer = ((3, 2, 14), (0, 0, 12))[kind]
            weights_of = ((0.75, 0.25), (0.25, 0.75))[kind]
            for step in (0, 1):
                shift = shifts[step, place_of]
                both = view_b(kind, shift)
                turn = shift - first if kind == 0 else first - shift - 1
                own = window_of(ring_a, turn)
                own = 0.75 * own + 0.25 * rolled(own, -NZ if kind == 0 else NZ, 1)
                far_p = jnp.where(row < 4, both[0:8], own)
                around = differences(far_p, place6)
                chem = bulk(far_p, around)
                slope = [0.5 * (a - b) for a, b in around]
                around = differences(chem, place6)
                if step == 0:
                    density = both[4:5]
                    scaled = (-0.5 * coupling / relax_rate) * far_p[edge:edge + 1] / density
                    drift = [
                        both[5 + axis:6 + axis]
                        + scaled * (around[axis][0] - around[axis][1])[edge:edge + 1]
                        for axis in range(3)
                    ]
                    strip = strip_post(kind, both[8:16], density, drift, place6)
                    strip = weights_of[0] * strip + weights_of[1] * rolled(strip, NZ, 1)
                    patch_x(kind, strip_moved(strip))
                else:
                    after = far_p + mobility * bent(chem, around)
                    for axis in range(3):
                        flow = jnp.where(row == edge, both[5 + axis:6 + axis], both[13 + axis:14 + axis])
                        after = after - flow * slope[axis]
                    after = weights_of[0] * after + weights_of[1] * rolled(after, NZ, 1)
                    ext[outer:outer + 2, 0:WIDE] = after[at:at + 2, 0:WIDE]
                    ext[outer:outer + 2, WIDE:512] = jnp.where(
                        lane1[:2] < 64, after[at:at + 2, 384:512], after[at:at + 2, 640:768]
                    )

        @pl.when(jnp.logical_not(is_plane))
        def _(kind=kind):
            edge = (23, 12)[kind]
            at = len(first_units) - 1
            ends = [
                rolled(wide["corner"][2 * kind + k, at // 5:at // 5 + 1], lane_of(k, 1) - NZ * (at % 5), 1)
                for k in (1, 0)
            ]
            strip = jnp.concatenate(
                [wide["side"][kind, 16 * b + 8:16 * b + 16] for b in range(3)]
                + [jnp.broadcast_to(line, (8, 128)) for line in ends],
                axis=1,
            )
            strip = strip_post(
                kind, strip, e_r[edge:edge + 1, :], [d[edge:edge + 1] for d in drift], place5[:8]
            )
            patch_x(kind, strip_moved(strip))

    advance(1)
    wait_sent(0)
    receive(1, 1)

    advance(2)
    y_cut = (slice(256, 384), slice(0, 128))
    lines = [fx[group[0], edge:edge + 1, 0:WIDE] for edge in (11, 0) for group in x_groups]
    lines += [fx[1, 11:12, 0:WIDE], fx[2, 0:1, 0:WIDE]]
    halves = 0.5 * jnp.concatenate(lines, axis=0)
    ahead, behind = moved_yz(halves, 0, -1, place[:8]), moved_yz(halves, 0, 1, place[:8])
    for kind in (0, 1):
        edge, second, low = ((11, 10, 9), (0, 1, 0))[kind]
        inward = (up_slots, down_slots)[kind]
        for b in range(3):
            cut = slice(b * 128, b * 128 + 128)
            for i, slot in enumerate(inward):
                last_x[kind, 19 * b + i:19 * b + i + 1, :] = fx[slot, edge:edge + 1, cut]
                last_x[kind, 19 * b + 11 + i:19 * b + 12 + i, :] = fx[slot, second:second + 1, cut]
            for i, (first, slot) in enumerate(folded_x):
                at = x_groups.index(next(g for g in x_groups if g[0] == first)) + 3 * kind
                half = (ahead if lattice_vel[slot][2] == 1 else behind)[at:at + 1, cut]
                last_x[kind, 19 * b + 5 + i:19 * b + 6 + i, :] = fx[slot, edge:edge + 1, cut] + half
            last_x[kind, 19 * b + 16:19 * b + 19, :] = ext[low:low + 3, cut]
        for k in (0, 1):
            units = corner_units(kind, k)
            for i in range(0, len(units), 5):
                line = None
                for j, (slot, deep_x, deep_y) in enumerate(units[i:i + 5]):
                    row = 12 - deep_x if kind == 0 else deep_x - 1
                    part = ext[row:row + 1, y_cut[k]] if slot is None else fx[slot, row:row + 1, y_cut[k]]
                    part = rolled(part, NZ * j - lane_of(k, deep_y), 1)
                    line = part if j == 0 else jnp.where(lane1[:1] >= NZ * j, part, line)
                last_corner[2 * kind + k, i // 5:i // 5 + 1, :] = line
    for is_plane, edge, slots in ((left_plane, 0, down_slots), (right_plane, 11, up_slots)):
        @pl.when(is_plane)
        def _(edge=edge, slots=slots):
            at = 6 if edge == 11 else 7
            for b in range(3):
                cut = slice(b * 128, b * 128 + 128)
                for i, slot in enumerate(slots[1:]):
                    line = fx[slot, edge:edge + 1, cut]
                    if lattice_vel[slot][2] != 0:
                        line = line + (ahead if lattice_vel[slot][2] == 1 else behind)[at:at + 1, cut]
                    last_a[4 * b + i:4 * b + i + 1, :] = line

    send_around(2, last_a)
    send_x(2, last_x)
    send_sides(2, last_x, last_corner)
    for k in (0, 1):
        spots = lax.rem(lane1 + (16 if k == 0 else 0), NZ)
        for i in range(0, len(y_units[k]), 5):
            line = None
            for j, (slot, deep) in enumerate(y_units[k][i:i + 5]):
                part = ext[0:16, y_cut[k]] if slot is None else fx[slot, :, y_cut[k]]
                for first, folded in folded_y:
                    if folded == slot:
                        part = part + moved_yz(0.5 * fx[first, :, y_cut[k]], 0, -lattice_vel[slot][2], spots)
                part = rolled(part, NZ * j - lane_of(k, deep), 1)
                line = part if j == 0 else jnp.where(lane1 >= NZ * j, part, line)
            last_y[k, 12 * (i // 5):12 * (i // 5) + 12, :] = line[:12]
    send_y(2, last_y)
    e_p[0:12, 0:WIDE] = ext[0:12, 0:WIDE]
    wait_sent(1)

    wait_near(2)
    last = brought[2]

    def unit_of_y(k, slot, deep):
        place = y_units[k].index((slot, deep))
        row = 12 * (place // 5)
        return rolled(last["y"][k, row:row + 12], lane_of(k, deep) - NZ * (place % 5), 1)

    lane12 = lane1[:12]
    for slot in range(19):
        step_y = lattice_vel[slot][1]
        if any(slot == group[0] for group in y_groups):
            rim = jnp.zeros((12, 128), jnp.float32)
        elif step_y == 0:
            rim = jnp.where(lane12 < 64, unit_of_y(1, slot, 1), unit_of_y(0, slot, 1))
        elif step_y == 1:
            rim = jnp.where(lane12 >= 104, unit_of_y(0, slot, 1), unit_of_y(0, slot, 2))
        else:
            rim = jnp.where(lane12 < NZ, unit_of_y(1, slot, 1), unit_of_y(1, slot, 2))
        fx[slot, 0:12, 384:512] = rim
    e_p[0:12, 384:512] = jnp.where(
        lane12 < NZ, unit_of_y(1, None, 1),
        jnp.where(lane12 < 2 * NZ, unit_of_y(1, None, 2), unit_of_y(1, None, 3)),
    )
    e_p[0:12, 512:640] = jnp.where(
        lane12 >= 104, unit_of_y(0, None, 1),
        jnp.where(lane12 >= 80, unit_of_y(0, None, 2), unit_of_y(0, None, 3)),
    )
    for kind, is_plane, place_of in sides:
        @pl.when(jnp.logical_not(is_plane))
        def _(kind=kind):
            rows = ((15, 14), (12, 13))[kind]
            low = (21, 12)[kind]
            inward = (up_slots, down_slots)[kind]
            whole = last["side"][kind]
            for group in x_groups:
                fx[group[0], rows[0]:rows[0] + 1, 0:WIDE] = jnp.zeros((1, WIDE), jnp.float32)
            for b in range(3):
                cut = slice(b * 128, b * 128 + 128)
                strip = whole[19 * b:19 * b + 19]
                for i, slot in enumerate(inward):
                    fx[slot, rows[0]:rows[0] + 1, cut] = strip[i:i + 1]
                    fx[slot, rows[1]:rows[1] + 1, cut] = strip[11 + i:12 + i]
                for i, (_, slot) in enumerate(folded_x):
                    fx[slot, rows[0]:rows[0] + 1, cut] = strip[5 + i:6 + i]
                e_p[low:low + 3, cut] = strip[16:19]
            found = {}
            for k in (0, 1):
                corner = last["corner"][2 * kind + k]
                for i, (slot, deep_x, deep_y) in enumerate(corner_units(kind, k)):
                    part = corner[i // 5:i // 5 + 1]
                    part = rolled(part, lane_of(k, deep_y) - NZ * (i % 5), 1)
                    found.setdefault((slot, deep_x), []).append((k, deep_y, part))
            for (slot, deep_x), parts in found.items():
                line = {}
                for k, deep_y, part in parts:
                    start = lane_of(k, deep_y)
                    here = (lane1[:1] >= start) & (lane1[:1] < start + NZ)
                    at = k if slot is None else 0
                    line[at] = jnp.where(here, part, line[at]) if at in line else part
                if slot is None:
                    row = 24 - deep_x if kind == 0 else 11 + deep_x
                    e_p[row:row + 1, 512:640] = line[0]
                    e_p[row:row + 1, 384:512] = line[1]
                else:
                    row = rows[deep_x - 1]
                    fx[slot, row:row + 1, 384:512] = line[0]

    for slot in range(19):
        step_x, step_y, step_z = lattice_vel[slot]
        if step_x == 0:
            fx[slot] = moved_yz(fx[slot], step_y, step_z, place4)

    def mixed(kind, value):
        near, far = ((0.75, 0.25), (0.25, 0.75))[kind]
        return near * value + far * rolled(value, NZ, 1)

    for kind, is_plane, place_of in sides:
        @pl.when(is_plane)
        def _(kind=kind, place_of=place_of):
            wait_plane(2)
            for b in range(blocks + 5):
                row = 19 * (b % 3)
                ring_e[b, 0:19] = last["plane"][b % blocks // 3, row:row + 19]
            for j in range(count_y):
                source = lax.rem(gy + count_y - j, count_y)
                for b in range(3):
                    rows = slice(4 * b, 4 * b + 4)
                    ring_o[source * 3 + b, 1:5] = last_a[rows] if j == 0 else last["around"][j - 1, rows]
            for b in range(5):
                ring_o[blocks + b] = ring_o[b]
            row = (15, 12)[kind]
            shift = shifts[2, place_of]
            strip = mixed(kind, window_of(ring_e, shift if kind == 0 else -shift - 1)[0:8])
            for i, slot in enumerate((up_slots, down_slots)[kind]):
                fx[slot, row:row + 1, 0:384] = strip[i:i + 1, 0:384]
                fx[slot, row:row + 1, 384:512] = jnp.where(
                    lane1[:1] < 64, strip[i:i + 1, 384:512], strip[i:i + 1, 640:768]
                )
            shift = shifts[3, place_of]
            phase = mixed(kind, window_of(ring_e, shift if kind == 0 else -shift - 1)[16:24])
            row, at = ((22, 1), (12, 0))[kind]
            e_p[row:row + 2, 0:512] = phase[at:at + 2, 0:512]
            e_p[row:row + 2, 512:640] = phase[at:at + 2, 640:768]

    def narrowed(to, value):
        for top, at, size in ((0, 0, 12), (12, 12, 2), (14, 22, 2)):
            to[top:top + size, 0:WIDE] = value[at:at + size, 0:WIDE]
            to[top:top + size, WIDE:512] = jnp.where(
                lane1[:size] < 64, value[at:at + size, 384:512], value[at:at + size, 512:640]
            )

    for slot in up_slots + down_slots:
        step_x, step_y, step_z = lattice_vel[slot]
        fx[slot] = moved_yz(rolled(fx[slot], step_x, 0), step_y, step_z, place4)
    p = e_p[...]
    narrowed(ext, p)
    narrowed(chem_x, bulk(p, differences(p, place5)))
    density, totals = momentum(fx)
    inverse = 1.0 / density
    p, chem = ext[...], chem_x[...]
    around = differences(p, place4)
    slope = [0.5 * (a - b)[:, :WIDE] for a, b in around]
    around = differences(chem, place4)
    next_phase = (p + mobility * bent(chem, around))[:, :WIDE]
    scaled = (-0.5 * coupling / relax_rate) * p
    drift = []
    for axis in range(3):
        next_phase = next_phase - (totals[axis] * inverse)[:, :WIDE] * slope[axis]
        drift.append((totals[axis] + scaled * (around[axis][0] - around[axis][1])) * inverse)
    p_out[...] = next_phase[:12]
    collide(density[:, :WIDE], [d[:, :WIDE] for d in drift], None, lambda slot: fx[slot, :, 0:WIDE])
    for k in (0, 1):
        here = None
        for i, slot in enumerate((plus_y, minus_y)[k]):
            part = rolled(fx[slot, :, 384:512], NZ + NZ * i if k == 0 else 104 - NZ * i, 1)
            if i == 0:
                here = part
            else:
                here = jnp.where(lane1 >= NZ * i if k == 0 else lane1 < 128 - NZ * i, part, here)
        rim = [d[:, 384:512] for d in drift]
        patch_y(k, packed_post(k, here, density[:, 384:512], rim, lane1))
    for kind, is_plane, place_of in sides:
        @pl.when(is_plane)
        def _(kind=kind, place_of=place_of):
            before, shift = shifts[2, place_of], shifts[3, place_of]
            edge, top, a_row, own_row = ((3, 1, 4, 0), (0, 0, 6, 10))[kind]
            far = window_of(ring_e, shift if kind == 0 else -shift - 1)
            inner = strip_moved(strip_along_z(kind, far[11:19], place6))
            turn = shift - before if kind == 0 else before - shift - 1
            outer = window_of(ring_o, turn)
            outer = 0.75 * outer + 0.25 * rolled(outer, -NZ if kind == 0 else NZ, 1)
            outer = strip_moved(strip_along_z(1 - kind, outer, place6))
            total = [None] * 4
            sign = 1.0 - 2.0 * kind
            for tile, way in ((inner, sign), (outer, -sign)):
                r = [tile[i:i + 1] for i in range(5)]
                whole = r[1] + r[2] + r[3] + r[4]
                if tile is inner:
                    whole = whole + r[0]
                found = (whole, way * whole, r[3] - r[4], way * (r[1] - r[2]))
                total = [b if a is None else a + b for a, b in zip(total, found)]
            for i, (_, slot) in enumerate(folded_x):
                _, step_y, step_z = lattice_vel[slot]
                line = moved_yz(far[5 + i:6 + i], step_y, step_z, place6[:1])
                total[0] = total[0] + line
                if step_y != 0:
                    total[2] = total[2] + step_y * line
                if step_z != 0:
                    total[3] = total[3] + step_z * line
            tile_a[...] = jnp.zeros_like(tile_a)
            tile_a[a_row:a_row + 2, 0:512] = e_p[own_row:own_row + 2, 0:512]
            tile_a[a_row:a_row + 2, 640:768] = e_p[own_row:own_row + 2, 512:640]
            own = tile_a[...]
            ahead = rolled(own, -NZ, 1)
            own = 0.75 * own + 0.25 * ahead if kind == 0 else 0.25 * own + 0.75 * ahead
            row = lax.broadcasted_iota(jnp.int32, (8, 768), 0)
            far_p = jnp.where(row < 4, rolled(far[16:24], top, 0), own)
            around = differences(bulk(far_p, differences(far_p, place6)), place6)
            inverse = 1.0 / total[0]
            scaled = (-0.5 * coupling / relax_rate) * far_p[edge:edge + 1]
            drift = [
                (total[1 + axis] + scaled * (around[axis][0] - around[axis][1])[edge:edge + 1]) * inverse
                for axis in range(3)
            ]
            strip = mixed(kind, strip_post(kind, inner, total[0], drift, place6))
            patch_x(kind, strip_moved(strip))

        @pl.when(jnp.logical_not(is_plane))
        def _(kind=kind):
            row = (15, 12)[kind]
            inward = (up_slots, down_slots)[kind]
            lines = [fx[slot, row:row + 1, :] for slot in inward]
            strip = jnp.concatenate(lines + lines[:1] * 3, axis=0)
            strip = strip_post(
                kind, strip, density[row:row + 1], [d[row:row + 1] for d in drift], place4[:8]
            )
            patch_x(kind, strip_moved(strip))

    wait_sent(2)
    for slot in range(19):
        f_out[slot] = f[slot, 0:12, :]


def on_device(populations, phase_field, plane_shifts):
    parts = lax.axis_size("gy")
    blocks = 3 * parts
    rounds = 3
    vmem = pl.BlockSpec(memory_space=pltpu.VMEM)
    return pl.pallas_call(
        kernel,
        out_shape=(
            jax.ShapeDtypeStruct(populations.shape, jnp.float32),
            jax.ShapeDtypeStruct(phase_field.shape, jnp.float32),
        ),
        in_specs=[pl.BlockSpec(memory_space=pltpu.SMEM), vmem, vmem],
        out_specs=(vmem, vmem),
        scratch_shapes=[
            pltpu.VMEM((19, 16, WIDE), jnp.float32),
            pltpu.VMEM((16, 512), jnp.float32),
            pltpu.VMEM((2, 21, 128), jnp.float32),
            pltpu.VMEM((2, 16, 128), jnp.float32),
            pltpu.VMEM((4, 1, 128), jnp.float32),
            pltpu.VMEM((blocks + 4, 8, 128), jnp.float32),
            pltpu.VMEM((24, 640), jnp.float32),
            pltpu.VMEM((24, 640), jnp.float32),
            pltpu.VMEM((3, 24, 640), jnp.float32),
            pltpu.VMEM((blocks + 5, 16, 128), jnp.float32),
            pltpu.VMEM((blocks + 5, 8, 128), jnp.float32),
            pltpu.VMEM((2, 48, 128), jnp.float32),
            pltpu.VMEM((2, 40, 128), jnp.float32),
            pltpu.VMEM((4, 3, 128), jnp.float32),
            pltpu.VMEM((6, 128), jnp.float32),
            pltpu.VMEM((19, 16, 512), jnp.float32),
            pltpu.VMEM((16, 512), jnp.float32),
            pltpu.VMEM((8, 768), jnp.float32),
            pltpu.VMEM((blocks + 5, 24, 128), jnp.float32),
            pltpu.VMEM((blocks + 5, 8, 128), jnp.float32),
            pltpu.VMEM((2, 57, 128), jnp.float32),
            pltpu.VMEM((2, 48, 128), jnp.float32),
            pltpu.VMEM((4, 5, 128), jnp.float32),
            pltpu.VMEM((12, 128), jnp.float32),
        ] + [
            pltpu.VMEM((count, rows, 128), jnp.float32)
            for count, rows in (
                (2, 40), (2, 48), (4, 3), (parts, 48), (parts - 1, 6),
                (2, 16), (2, 21), (4, 1), (parts, 21),
                (2, 48), (2, 57), (4, 5), (parts, 57), (parts - 1, 12),
            )
        ] + [
            pltpu.SemaphoreType.DMA((rounds, 5)),
            pltpu.SemaphoreType.DMA((rounds, 5)),
        ],
        compiler_params=pltpu.CompilerParams(
            collective_id=0, has_side_effects=True, vmem_limit_bytes=32 * 1024 * 1024
        ),
    )(plane_shifts, populations, phase_field)


def solution(mesh):
    return jax.shard_map(
        on_device,
        mesh=mesh,
        in_specs=(P(None, "gx", "gy"), P("gx", "gy"), P()),
        out_specs=(P(None, "gx", "gy"), P("gx", "gy")),
        check_vma=False,
    )
```

```python
import functools

import jax
import jax.numpy as jnp
from jax import lax
from jax.experimental import pallas as pl
from jax.experimental.pallas import tpu as pltpu
from jax.sharding import PartitionSpec as P

STEPS = 4
NZ = 24
ROWS = 12
WIDE = 384
SPAN = 4
MESH = pl.DeviceIdType.MESH

lattice_vel = (
    (0, 0, 0),
    (1, 0, 0),
    (-1, 0, 0),
    (0, 1, 0),
    (0, -1, 0),
    (0, 0, 1),
    (0, 0, -1),
    (1, 1, 0),
    (-1, -1, 0),
    (1, -1, 0),
    (-1, 1, 0),
    (1, 0, 1),
    (-1, 0, -1),
    (1, 0, -1),
    (-1, 0, 1),
    (0, 1, 1),
    (0, -1, -1),
    (0, 1, -1),
    (0, -1, 1),
)
relax_rate = 0.8
coupling = 0.01
mobility = 0.02

up_slots = (1, 11, 13, 7, 9)
down_slots = (2, 12, 14, 10, 8)
plus_y = (3, 7, 10, 15, 17)
minus_y = (4, 8, 9, 16, 18)


x_groups = ((0, 5, 6), (3, 15, 17), (4, 18, 16))
y_groups = ((0, 5, 6), (1, 11, 13), (2, 14, 12))
folded_x = tuple((first, slot) for first, *pair in x_groups for slot in pair)
folded_y = tuple((first, slot) for first, *pair in y_groups for slot in pair)
near_y = tuple(slots + tuple(slot for _, slot in folded_y) for slots in (plus_y, minus_y))
y_units = tuple(
    tuple((slot, 1) for slot in near_y[k]) + tuple((slot, 2) for slot in (plus_y, minus_y)[k])
    + ((None, 1), (None, 2), (None, 3))
    for k in (0, 1)
)


def corner_units(kind, k):
    step = (1 - 2 * kind, 1 - 2 * k)
    units = []
    for deep in ((1, 1), (2, 1), (1, 2), (2, 2)):
        for slot in range(19):
            if all(
                lattice_vel[slot][axis] == step[axis] or (deep[axis] == 1 and lattice_vel[slot][axis] == 0)
                for axis in (0, 1)
            ):
                units.append((slot,) + deep)
    return tuple(units) + tuple((None, x, y) for x in (1, 2, 3) for y in range(1, 5 - x))


first_units = tuple(("p", x, y) for x in (1, 2, 3) for y in range(1, 5 - x)) + tuple(
    (what, 1, 1) for what in ("r", 0, 1, 2, "f")
)


def lane_of(k, depth):
    return 128 - NZ * depth if k == 0 else NZ * (depth - 1)


def rolled(value, shift, axis):
    size = value.shape[axis]
    shift = shift % size
    return value if shift == 0 else pltpu.roll(value, shift, axis)


def moved_yz(value, step_y, step_z, place):
    if step_z == 0:
        return rolled(value, step_y * NZ, 1)
    edge = 0 if step_z == 1 else NZ - 1
    inner = rolled(value, step_y * NZ + step_z, 1)
    wrap = rolled(value, step_y * NZ + step_z - step_z * NZ, 1)
    return jnp.where(place == edge, wrap, inner)


def differences(value, place):
    return (
        (rolled(value, -1, 0), rolled(value, 1, 0)),
        (rolled(value, -NZ, 1), rolled(value, NZ, 1)),
        (moved_yz(value, 0, -1, place), moved_yz(value, 0, 1, place)),
    )


def bulk(p, around):
    total = around[0][0] + around[0][1] + around[1][0] + around[1][1] + around[2][0] + around[2][1]
    return 0.5 * (p * p * p - p) - 0.5 * (total - 6.0 * p)


def bent(chem, around):
    total = around[0][0] + around[0][1] + around[1][0] + around[1][1] + around[2][0] + around[2][1]
    return total - 6.0 * chem


def relaxed(here, weight, along, drift):
    square = drift[0] * drift[0] + drift[1] * drift[1] + drift[2] * drift[2]
    return (1.0 - relax_rate) * here + weight * (
        1.0 - 1.5 * square + 3.0 * along + 4.5 * along * along
    )


def strip_post(kind, here, density, drift, place):
    sign = 1.0 - 2.0 * kind
    row = lax.broadcasted_iota(jnp.int32, here.shape, 0)
    full = [jnp.broadcast_to(d, here.shape) for d in drift]
    along = sign * full[0]
    along = along + jnp.where(row == 3, full[1], jnp.where(row == 4, -full[1], 0.0))
    along = along + jnp.where(row == 1, sign * full[2], jnp.where(row == 2, -sign * full[2], 0.0))
    weight = jnp.where(row == 0, 2.0, 1.0) * (relax_rate / 36.0) * density
    post = relaxed(here, weight, along, full)
    return strip_along_z(kind, post, place)


def strip_along_z(kind, strip, place):
    row = lax.broadcasted_iota(jnp.int32, strip.shape, 0)
    first, second = (1, -1) if kind == 0 else (-1, 1)
    return jnp.where(
        row == 1, moved_yz(strip, 0, first, place), jnp.where(row == 2, moved_yz(strip, 0, second, place), strip)
    )


def strip_moved(strip):
    row = lax.broadcasted_iota(jnp.int32, strip.shape, 0)
    return jnp.where(row == 3, rolled(strip, NZ, 1), jnp.where(row == 4, rolled(strip, -NZ, 1), strip))


def packed_post(k, here, density, drift, lane1):
    def spread(value):
        out = rolled(value, NZ if k == 0 else 104, 1)
        first = out
        for i in range(1, 5):
            if k == 0:
                out = jnp.where(lane1 >= i * NZ, rolled(first, i * NZ, 1), out)
            else:
                out = jnp.where(lane1 < 128 - i * NZ, rolled(first, -i * NZ, 1), out)
        return out

    slots = plus_y if k == 0 else minus_y
    group = lane1 // NZ if k == 0 else (127 - lane1) // NZ
    density, drift = spread(density), [spread(d) for d in drift]

    def chosen(axis, value):
        out = jnp.zeros_like(value)
        for i, slot in enumerate(slots):
            if lattice_vel[slot][axis] != 0:
                out = jnp.where(group == i, lattice_vel[slot][axis] * value, out)
        return out

    along = chosen(0, drift[0]) + chosen(1, drift[1]) + chosen(2, drift[2])
    weight = jnp.where(group == 0, 2.0, 1.0) * (relax_rate / 36.0) * density
    post = relaxed(here, weight, along, drift)
    place = lax.rem(lane1, NZ) if k == 0 else lax.rem(lane1 + 16, NZ)
    out = post
    for i, slot in enumerate(slots):
        step_x, _, step_z = lattice_vel[slot]
        if step_x != 0 or step_z != 0:
            out = jnp.where(group == i, moved_yz(rolled(post, step_x, 0), 0, step_z, place), out)
    return out


def lanes_of_y(k):
    groups = [NZ * i if k == 0 else 104 - NZ * i for i in range(5)]
    return groups, (120 if k == 0 else 0), ((104, 80) if k == 0 else (0, 24))


def with_phase(k, packed, phase):
    groups, spare, (first, second) = lanes_of_y(k)
    lane = lax.broadcasted_iota(jnp.int32, (8, 128), 1)
    upper = lax.broadcasted_iota(jnp.int32, (8, 128), 0) >= 4
    in_spare = (lane >= spare) & (lane < spare + 8)
    top, low = phase[0:8], phase[8:16]
    top_down, low_down = rolled(top, 4, 0), rolled(low, 4, 0)
    head, tail = packed[0:8], packed[8:16]
    pieces = ((top_down, first), (top, first), (low_down, first), (top_down, second), (top, second))
    for start, (piece, at) in zip(groups, pieces):
        here = upper & (lane >= start) & (lane < start + NZ)
        tail = jnp.where(here, rolled(piece, start - at, 1), tail)
    parts = [
        rolled(low, spare - second, 1),
        rolled(low_down, spare - second - 8, 1),
        rolled(low, spare - second - 16, 1),
    ]
    head = jnp.where(in_spare, jnp.where(upper, parts[1], parts[0]), head)
    tail = jnp.where(in_spare & jnp.logical_not(upper), parts[2], tail)
    return jnp.concatenate([head, tail], axis=0)


def phase_part(k, message):
    groups, spare, (first, second) = lanes_of_y(k)
    lane = lax.broadcasted_iota(jnp.int32, (8, 128), 1)
    upper = lax.broadcasted_iota(jnp.int32, (8, 128), 0) >= 4
    in_first = (lane >= first) & (lane < first + NZ)
    head, tail = message[0:8], message[8:16]
    head_up, tail_up = rolled(head, 4, 0), rolled(tail, 4, 0)

    def picked(near, far):
        return jnp.where(in_first, rolled(near[0], first - near[1], 1), rolled(far[0], second - far[1], 1))

    top = jnp.where(
        upper,
        picked((tail, groups[1]), (tail, groups[4])),
        picked((tail_up, groups[0]), (tail_up, groups[3])),
    )
    far = jnp.where(
        lane < second + 8,
        rolled(head, second - spare, 1),
        jnp.where(
            lane < second + 16,
            rolled(head_up, second + 8 - spare, 1),
            rolled(tail, second + 16 - spare, 1),
        ),
    )
    low = jnp.where(in_first, rolled(tail_up, first - groups[2], 1), far)
    return jnp.concatenate([top, low], axis=0)


def kernel(
    shifts, f_in, p_in, f_out, p_out,
    f, ext, to_x, to_y, to_corner, ring,
    e_p, e_r, e_u, ring_b, ring_a, out_x, out_y, out_corner, out_a,
    fx, chem_x, tile_a, ring_e, ring_o, last_x, last_y, last_corner, last_a,
    *landings_and_semaphores,
):
    count_x, count_y = lax.axis_size("gx"), lax.axis_size("gy")
    gx, gy = lax.axis_index("gx"), lax.axis_index("gy")
    above, below = lax.rem(gx + 1, count_x), lax.rem(gx + count_x - 1, count_x)
    front, back = lax.rem(gy + 1, count_y), lax.rem(gy + count_y - 1, count_y)
    planes = count_x // SPAN
    left_plane = lax.rem(gx, SPAN) == 0
    right_plane = lax.rem(gx, SPAN) == SPAN - 1
    left_slot = lax.rem(gx // SPAN + planes - 1, planes)
    right_slot = gx // SPAN
    any_plane = left_plane | right_plane
    blocks = 3 * count_y
    sides = ((0, left_plane, left_slot), (1, right_plane, right_slot))

    def signal(x, y):
        pl.semaphore_signal(barrier, inc=1, device_id=(x, y), device_id_type=MESH)

    barrier = pltpu.get_barrier_semaphore()
    any_plane = left_plane | right_plane
    def far_first():
        half = count_y // 2
        order = [(half // 2, 1), (half // 2, 0)]
        for dx in range(half // 2 - 1, -1, -1):
            order += [(d, z) for z in (1, 0) for d in sorted({dx, (half - dx) % half})]
        place = lax.rem(gx, 2 * SPAN)
        turn = jnp.where((place == 0) | (place == 2 * SPAN - 1), 1, 0)
        return [2 * lax.rem(gy // 2 + dx, half) + lax.rem(gy + dz + turn, 2) for dx, dz in dict.fromkeys(order)]

    for is_plane, side in ((left_plane, below), (right_plane, above)):
        @pl.when(is_plane)
        def _(side=side):
            for y in far_first():
                signal(side, y)
            for j in range(2, count_y - 1):
                signal(gx, lax.rem(gy + j, count_y))

    signal(gx, front)
    signal(gx, back)
    for is_plane, side in ((left_plane, below), (right_plane, above)):
        @pl.when(jnp.logical_not(is_plane))
        def _(side=side):
            signal(side, front)
            signal(side, back)
            signal(side, gy)

    lane = lax.broadcasted_iota(jnp.int32, (16, WIDE), 1)
    place = lax.rem(lane, NZ)
    lane4 = lax.broadcasted_iota(jnp.int32, (16, 512), 1)
    place4 = lax.rem(jnp.where(lane4 < 448, lane4, lane4 - 464), NZ)
    lane1 = lax.broadcasted_iota(jnp.int32, (16, 128), 1)
    lane5 = lax.broadcasted_iota(jnp.int32, (24, 640), 1)
    place5 = lax.rem(jnp.where(lane5 < 512, lane5, lane5 + 8), NZ)
    place6 = lax.rem(lax.broadcasted_iota(jnp.int32, (8, 768), 1), NZ)

    def pack_phase(r):
        for b in range(3):
            cut = slice(b * 128, b * 128 + 128)
            to_x[0, 7 * b + 5:7 * b + 7, :] = ext[10:12, cut]
            to_x[1, 7 * b + 5:7 * b + 7, :] = ext[0:2, cut]

    *landings, sent, arrived = landings_and_semaphores
    brought = (
        dict(zip(("y", "side", "corner", "plane", "around"), landings[0:5])),
        dict(zip(("y", "side", "corner", "plane"), landings[5:9])),
        dict(zip(("y", "side", "corner", "plane", "around"), landings[9:14])),
    )
    names = ("y", "side", "corner", "plane", "around")

    def remote(src, r, name, index, x, y):
        pltpu.make_async_remote_copy(
            src_ref=src, dst_ref=brought[r][name].at[index],
            send_sem=sent.at[r, names.index(name)], recv_sem=arrived.at[r, names.index(name)],
            device_id=(x, y), device_id_type=MESH,
        ).start()

    def send_x(r, strips):
        for kind, is_plane, side in ((0, right_plane, above), (1, left_plane, below)):
            @pl.when(is_plane)
            def _(kind=kind, side=side):
                for y in far_first():
                    remote(strips.at[kind], r, "plane", gy, side, y)

    def send_sides(r, strips, corners):
        for kind, is_plane, side in ((0, right_plane, above), (1, left_plane, below)):
            @pl.when(jnp.logical_not(is_plane))
            def _(kind=kind, side=side):
                for k, y in ((0, front), (1, back)):
                    remote(corners.at[2 * kind + k], r, "corner", 2 * kind + k, side, y)
                remote(strips.at[kind], r, "side", kind, side, gy)

    def send_around(r, rows):
        @pl.when(any_plane)
        def _():
            for j in range(1, count_y):
                remote(rows, r, "around", j - 1, gx, lax.rem(gy + j, count_y))

    def send_y(r, messages):
        for k, y in ((0, front), (1, back)):
            remote(messages.at[k], r, "y", k, gx, y)

    def wait_for(r, name, sems):
        ref, sem = brought[r][name], sems.at[r, names.index(name)]
        if name in ("side", "corner"):
            step = 1 if name == "side" else 2
            for is_kind, start, size in (
                (left_plane, 1, 1), (right_plane, 0, 1), (jnp.logical_not(any_plane), 0, 2)
            ):
                @pl.when(is_kind)
                def _(start=start, size=size):
                    part = ref.at[pl.ds(step * start, step * size)]
                    pltpu.make_async_copy(part, part, sem).wait()
        else:
            pltpu.make_async_copy(ref, ref, sem).wait()

    def wait_sent(r):
        for name in ("y", "side", "corner"):
            wait_for(r, name, sent)

        @pl.when(any_plane)
        def _():
            for name in ("plane", "around"):
                if name in brought[r]:
                    wait_for(r, name, sent)

    def wait_near(r):
        for name in ("side", "corner", "y"):
            wait_for(r, name, arrived)

    def wait_plane(r):
        for name in ("plane", "around"):
            if name in brought[r]:
                wait_for(r, name, arrived)

    def window_of(held, turn):
        start = ((gy * 16 - turn - 4) & (16 * count_y - 1)) * NZ
        first, offset = start >> 7, start & 127
        window = jnp.concatenate([held[first + i] for i in range(6)], axis=1)
        return pltpu.roll(window, 768 - 4 * NZ - offset, 1)

    def view_b(kind, shift):
        return window_of(ring_b, shift if kind == 0 else -shift - 1)

    def close_ring(r):
        for b in range(blocks + 4):
            row = 7 * (b % 3)
            ring[b, 0:7] = brought[r]["plane"][b % blocks // 3, row:row + 7]

    def view(kind, shift):
        low = shift if kind == 0 else -shift - 1
        near, far = (0.75, 0.25) if kind == 0 else (0.25, 0.75)
        start = ((gy * 16 - low - 3) & (16 * count_y - 1)) * NZ
        first, offset = start >> 7, start & 127
        window = jnp.concatenate([ring[first + i] for i in range(5)], axis=1)
        window = pltpu.roll(window, 640 - 3 * NZ - offset, 1)
        return near * window + far * rolled(window, NZ, 1)

    def patch_y(k, packed):
        cut = slice(0, 128) if k == 0 else slice(256, 384)
        keep = lane1 < NZ if k == 0 else lane1 >= 128 - NZ
        for i, slot in enumerate(plus_y if k == 0 else minus_y):
            part = rolled(packed, -i * NZ if k == 0 else i * NZ, 1)
            f[slot, :, cut] = jnp.where(keep, part, f[slot, :, cut])

    def patch_x(kind, strip):
        edge = 0 if kind == 0 else ROWS - 1
        for i, slot in enumerate(up_slots if kind == 0 else down_slots):
            f[slot, edge:edge + 1, :] = strip[i:i + 1, :WIDE]

    def receive(r, step):
        wait_near(r)
        for k in (0, 1):
            patch_y(k, brought[r]["y"][k])
        ext[0:12, 384:512] = jnp.where(
            lane1 < 64, phase_part(1, brought[r]["y"][1]), phase_part(0, brought[r]["y"][0])
        )[:12]
        for kind, is_plane, _ in sides:
            @pl.when(jnp.logical_not(is_plane))
            def _(kind=kind):
                outer = 14 - 2 * kind
                near_row = 15 - 3 * kind
                e = (0, ROWS - 1)[kind]
                side, corner = brought[r]["side"], brought[r]["corner"]
                strip = jnp.concatenate([side[kind, 7 * b:7 * b + 7] for b in range(3)], axis=1)
                first, last = corner[2 * kind], corner[2 * kind + 1]
                plus = rolled(strip, NZ, 1)
                minus = rolled(strip, -NZ, 1)
                slots = up_slots if kind == 0 else down_slots
                for i in range(3):
                    f[slots[i], e:e + 1, :] = strip[i:i + 1]
                head = jnp.where(lane1[:1] < NZ, first, plus[3:4, 0:128])
                tail = jnp.where(lane1[:1] >= 128 - NZ, last, minus[4:5, 256:384])
                f[slots[3], e:e + 1, 0:128] = head
                f[slots[3], e:e + 1, 128:384] = plus[3:4, 128:384]
                f[slots[4], e:e + 1, 0:256] = minus[4:5, 0:256]
                f[slots[4], e:e + 1, 256:384] = tail
                ext[outer:outer + 2, 0:WIDE] = strip[5:7]
                ext[near_row:near_row + 1, WIDE:512] = jnp.where(lane1[:1] < 64, last, first)

        for kind, is_plane, place_of in sides:
            @pl.when(is_plane)
            def _(kind=kind, place_of=place_of):
                outer = 14 - 2 * kind
                wait_plane(r)
                close_ring(r)
                patch_x(kind, strip_moved(view(kind, shifts[step, place_of])))
                phase = view(kind, shifts[jnp.minimum(step + 1, STEPS - 1), place_of])
                ext[outer:outer + 2, 0:WIDE] = phase[5:7, 0:WIDE]
                ext[outer:outer + 2, WIDE:512] = jnp.where(
                    lane1[:2] < 64, phase[5:7, 384:512], phase[5:7, 512:640]
                )

    def momentum(f):
        density = f[0]
        for slot in range(1, 19):
            density = density + f[slot]
        totals = []
        for axis in range(3):
            total = None
            for slot in range(1, 19, 2):
                sign = lattice_vel[slot][axis]
                if sign != 0:
                    pair = f[slot] - f[slot + 1]
                    if total is None:
                        total = pair
                    else:
                        total = total + pair if sign == 1 else total - pair
            totals.append(total)
        return density, totals

    def advance(r):
        p = ext[...]
        around = differences(p, place4)
        chem = bulk(p, around)
        slope = [0.5 * (a - b)[:, :WIDE] for a, b in around]
        around = [(a[:, :WIDE], b[:, :WIDE]) for a, b in differences(chem, place4)]
        bend = bent(chem[:, :WIDE], around)
        own = p[:, :WIDE]
        density, totals = momentum(f)
        inverse = 1.0 / density
        scaled = (-0.5 * coupling / relax_rate) * own
        next_phase = own + mobility * bend
        drift = []
        for axis in range(3):
            next_phase = next_phase - totals[axis] * inverse * slope[axis]
            drift.append((totals[axis] + scaled * (around[axis][0] - around[axis][1])) * inverse)
        ext[0:12, 0:WIDE] = next_phase[:12]
        if r == 1:
            pack_phase(r)
        collide(density, drift, r, lambda slot: f[slot])

    def collide(density, drift, r, source):
        base = 1.0 - 1.5 * (drift[0] * drift[0] + drift[1] * drift[1] + drift[2] * drift[2])
        weight = relax_rate / 36.0 * density
        keep = 1.0 - relax_rate
        packs = {}

        def put(slot, post):
            step_x, step_y, step_z = lattice_vel[slot]
            if r == 2:
                fx[slot, :, 0:WIDE] = post
                return
            value = rolled(post, step_x, 0)
            moved = moved_yz(value, step_y, step_z, place)
            f[slot] = moved
            if r is None:
                return
            if step_x != 0:
                kind = 0 if step_x == 1 else 1
                i = (up_slots, down_slots)[kind].index(slot)
                line = 12 if step_x == 1 else 15
                shown = value if step_y != 0 else moved
                for b in range(3):
                    to_x[kind, 7 * b + i:7 * b + i + 1, :] = shown[line:line + 1, b * 128:b * 128 + 128]
                if step_y != 0:
                    k = 2 * kind + (0 if step_y == 1 else 1)
                    cut = slice(0, 128) if step_y == 1 else slice(256, 384)
                    edge = 11 if step_x == 1 else 0
                    own = ext[edge:edge + 1, slice(256, 384) if step_y == 1 else slice(0, 128)]
                    post_row = moved[line:line + 1, cut]
                    low = lane1[:1] < 64
                    to_corner[k] = (
                        jnp.where(low, post_row, own) if step_y == 1 else jnp.where(low, own, post_row)
                    )
            if step_y == 1:
                i = plus_y.index(slot)
                part = rolled(moved[:, 0:128], i * NZ, 1)
                mine = (lane1 >= i * NZ) & (lane1 < i * NZ + NZ)
                packs[0] = jnp.where(mine, part, packs[0]) if 0 in packs else part
            if step_y == -1:
                i = minus_y.index(slot)
                part = rolled(moved[:, 256:384], -i * NZ, 1)
                mine = (lane1 < 128 - i * NZ) & (lane1 >= 128 - NZ - i * NZ)
                packs[1] = jnp.where(mine, part, packs[1]) if 1 in packs else part

        def put_pair(slot):
            along = None
            for axis in range(3):
                sign = lattice_vel[slot][axis]
                if sign != 0:
                    if along is None:
                        along = drift[axis]
                    else:
                        along = along + drift[axis] if sign == 1 else along - drift[axis]
            scale = 2.0 * weight if slot < 7 else weight
            even = scale * (base + 4.5 * along * along)
            odd = scale * (3.0 * along)
            here, there = source(slot), source(slot + 1)
            put(slot, keep * here + (even + odd))
            put(slot + 1, keep * there + (even - odd))

        for slot in (1, 7, 9, 11, 13):
            put_pair(slot)
        if r == 1:
            send_x(r, to_x)
            send_sides(r, to_x, to_corner)
        for slot in (3, 15, 17):
            put_pair(slot)
        if r == 1:
            for k in (0, 1):
                to_y[k] = with_phase(k, packs[k], ext[0:16, 256:384] if k == 0 else ext[0:16, 0:128])
            send_y(r, to_y)
        put_pair(5)
        put(0, keep * source(0) + 12.0 * weight * base)

    for slot in range(19):
        f[slot, 0:12, :] = f_in[slot]
        f[slot, 12:16, :] = jnp.ones((4, WIDE), jnp.float32)
    ext[...] = jnp.zeros_like(ext)
    e_p[...] = jnp.zeros_like(e_p)
    e_r[...] = jnp.ones_like(e_r)
    e_u[...] = jnp.zeros_like(e_u)
    e_p[0:12, 0:WIDE] = p_in[...]
    density, totals = momentum(f)
    e_r[0:12, 0:WIDE] = density[:12]
    for axis in range(3):
        e_u[axis, 0:12, 0:WIDE] = (totals[axis] / density)[:12]

    for kind in (0, 1):
        edge, second, low = ((11, 10, 8), (0, 1, 0))[kind]
        for b in range(3):
            cut = slice(b * 128, b * 128 + 128)
            out_x[kind, 16 * b:16 * b + 4, :] = e_p[low:low + 4, cut]
            out_x[kind, 16 * b + 4:16 * b + 5, :] = e_r[edge:edge + 1, cut]
            for axis in range(3):
                out_x[kind, 16 * b + 5 + axis:16 * b + 6 + axis, :] = e_u[axis, edge:edge + 1, cut]
                out_x[kind, 16 * b + 13 + axis:16 * b + 14 + axis, :] = e_u[axis, second:second + 1, cut]
            for i, slot in enumerate(up_slots if kind == 0 else down_slots):
                out_x[kind, 16 * b + 8 + i:16 * b + 9 + i, :] = f[slot, edge:edge + 1, cut]
        for k in (0, 1):
            cut = slice(256, 384) if k == 0 else slice(0, 128)
            slot = (up_slots if kind == 0 else down_slots)[3 + k]
            for i in range(0, len(first_units), 5):
                line = None
                for j, (what, deep_x, deep_y) in enumerate(first_units[i:i + 5]):
                    row = 12 - deep_x if kind == 0 else deep_x - 1
                    if what == "p":
                        part = e_p[row:row + 1, cut]
                    elif what == "r":
                        part = e_r[row:row + 1, cut]
                    elif what == "f":
                        part = f[slot, row:row + 1, cut]
                    else:
                        part = e_u[what, row:row + 1, cut]
                    part = rolled(part, NZ * j - lane_of(k, deep_y), 1)
                    line = part if j == 0 else jnp.where(lane1[:1] >= NZ * j, part, line)
                out_corner[2 * kind + k, i // 5:i // 5 + 1, :] = line
    for k in (0, 1):
        cut = slice(256, 384) if k == 0 else slice(0, 128)
        packed = None
        for i, slot in enumerate(plus_y if k == 0 else minus_y):
            block = f[slot, :, cut]
            part = rolled(block, NZ + i * NZ if k == 0 else -NZ - i * NZ, 1)
            if i == 0:
                packed = part
            else:
                packed = jnp.where(lane1 >= i * NZ if k == 0 else lane1 < 128 - i * NZ, part, packed)
        out_y[k, 0:12, :] = packed[:12]
        lane12 = lane1[:12]
        free = lane12 < 32 if k == 0 else lane12 >= 96
        second = (lane12 >= 32) & (lane12 < 80) if k == 0 else (lane12 >= 48) & (lane12 < 96)
        density_at, flow_at, deep_at = ((NZ, 32, 80), (96, 96, NZ))[k]
        out_y[k, 12:24, :] = jnp.where(free, rolled(e_r[0:12, cut], density_at, 1), e_p[0:12, cut])
        u_z = e_u[2, 0:12, cut]
        out_y[k, 24:36, :] = jnp.where(
            free, rolled(u_z, flow_at, 1),
            jnp.where(second, rolled(e_u[1, 0:12, cut], -48 if k == 0 else 48, 1), e_u[0, 0:12, cut]),
        )
        deep = [rolled(u_z[4 * g:4 * g + 4], NZ * g - deep_at, 1) for g in range(3)]
        out_y[k, 36:40, :] = jnp.where(
            lane1[:4] < NZ, deep[0], jnp.where(lane1[:4] < 2 * NZ, deep[1], deep[2])
        )

    @pl.when(left_plane)
    def _():
        for b in range(3):
            out_a[2 * b:2 * b + 2, :] = e_p[0:2, b * 128:b * 128 + 128]

    @pl.when(right_plane)
    def _():
        for b in range(3):
            out_a[2 * b:2 * b + 2, :] = e_p[10:12, b * 128:b * 128 + 128]

    pl.semaphore_wait(barrier, jnp.where(any_plane, 5 + count_y + max(count_y - 3, 0), 8))

    send_around(0, out_a)
    send_x(0, out_x)
    send_sides(0, out_x, out_corner)
    send_y(0, out_y)

    wait_near(0)
    wide = brought[0]
    for k in (0, 1):
        cut = slice(512, 640) if k == 0 else slice(384, 512)
        e_p[0:12, cut] = wide["y"][k, 12:24]
        density_at, flow_at, deep_at = ((NZ, 32, 80), (96, 96, NZ))[k]
        flow = wide["y"][k, 24:36]
        e_r[0:12, cut] = rolled(wide["y"][k, 12:24], -density_at, 1)
        e_u[0, 0:12, cut] = flow
        e_u[1, 0:12, cut] = rolled(flow, 48 if k == 0 else -48, 1)
        e_u[2, 0:12, cut] = rolled(flow, -flow_at, 1)
        here = (lane1[:4] >= deep_at) & (lane1[:4] < deep_at + NZ)
        for g in range(3):
            rows = slice(4 * g, 4 * g + 4)
            deep = rolled(wide["y"][k, 36:40], deep_at - NZ * g, 1)
            e_u[2, rows, cut] = jnp.where(here, deep, e_u[2, rows, cut])
    for kind, is_plane, place_of in sides:
        low = (20, 12)[kind]
        edge, second, third = ((23, 22, 21), (12, 13, 12))[kind]

        @pl.when(jnp.logical_not(is_plane))
        def _(kind=kind, low=low, edge=edge, second=second, third=third):
            for k in (0, 1):
                cut = slice(512, 640) if k == 0 else slice(384, 512)
                found = {}
                for i, (what, deep_x, deep_y) in enumerate(first_units):
                    start = lane_of(k, deep_y)
                    part = wide["corner"][2 * kind + k, i // 5:i // 5 + 1]
                    part = rolled(part, start - NZ * (i % 5), 1)
                    here = (lane1[:1] >= start) & (lane1[:1] < start + NZ)
                    key = (what, deep_x)
                    found[key] = jnp.where(here, part, found[key]) if key in found else part
                for (what, deep_x), line in found.items():
                    row = 24 - deep_x if kind == 0 else 11 + deep_x
                    if what == "p":
                        e_p[row:row + 1, cut] = line
                    elif what == "r":
                        e_r[row:row + 1, cut] = line
                    elif what != "f":
                        e_u[what, row:row + 1, cut] = line
            for b in range(3):
                cut = slice(b * 128, b * 128 + 128)
                strip = wide["side"][kind, 16 * b:16 * b + 16]
                e_p[low:low + 4, cut] = strip[0:4]
                e_r[edge:edge + 1, cut] = strip[4:5]
                for axis in range(3):
                    e_u[axis, edge:edge + 1, cut] = strip[5 + axis:6 + axis]
                    e_u[axis, second:second + 1, cut] = strip[13 + axis:14 + axis]

    for kind, is_plane, place_of in sides:
        @pl.when(is_plane)
        def _(kind=kind, place_of=place_of):
            wait_plane(0)
            for b in range(blocks + 5):
                row = 16 * (b % 3)
                ring_b[b] = wide["plane"][b % blocks // 3, row:row + 16]
            a_row = (4, 6)[kind]
            for j in range(count_y):
                source = lax.rem(gy + count_y - j, count_y)
                for b in range(3):
                    rows = slice(2 * b, 2 * b + 2)
                    piece = out_a[rows] if j == 0 else wide["around"][j - 1, rows]
                    ring_a[source * 3 + b, a_row:a_row + 2, :] = piece
            for b in range(5):
                ring_a[blocks + b] = ring_a[b]
            shift = shifts[0, place_of]
            near = view_b(kind, shift)[0:8]
            phase = (near * 0.75 + rolled(near, NZ, 1) * 0.25) if kind == 0 else (
                near * 0.25 + rolled(near, NZ, 1) * 0.75)
            row, at = ((22, 2), (12, 0))[kind]
            e_p[row:row + 2, 0:512] = phase[at:at + 2, 0:512]
            e_p[row:row + 2, 512:640] = phase[at:at + 2, 640:768]

    p = e_p[...]
    around = differences(p, place5)
    chem = bulk(p, around)
    slope = [0.5 * (a - b) for a, b in around]
    around = differences(chem, place5)
    next_phase = p + mobility * bent(chem, around)
    scaled = (-0.5 * coupling / relax_rate) * p / e_r[...]
    drift = []
    for axis in range(3):
        flow = e_u[axis]
        next_phase = next_phase - flow * slope[axis]
        drift.append(flow + scaled * (around[axis][0] - around[axis][1]))
    for top, at, size in ((0, 0, 12), (12, 12, 2), (14, 22, 2)):
        ext[top:top + size, 0:WIDE] = next_phase[at:at + size, 0:WIDE]
        ext[top:top + size, WIDE:512] = jnp.where(
            lane1[:size] < 64, next_phase[at:at + size, 384:512], next_phase[at:at + size, 512:640]
        )
    collide(e_r[0:16, 0:WIDE], [d[0:16, 0:WIDE] for d in drift], None, lambda slot: f[slot])
    for k in (0, 1):
        cut = slice(512, 640) if k == 0 else slice(384, 512)
        patch_y(k, packed_post(k, wide["y"][k, 0:16], e_r[0:16, cut], [d[0:16, cut] for d in drift], lane1))
    for kind, is_plane, place_of in sides:
        @pl.when(is_plane)
        def _(kind=kind, place_of=place_of):
            first = shifts[0, place_of]
            row = lax.broadcasted_iota(jnp.int32, (8, 768), 0)
            edge, at, outer = ((3, 2, 14), (0, 0, 12))[kind]
            weights_of = ((0.75, 0.25), (0.25, 0.75))[kind]
            for step in (0, 1):
                shift = shifts[step, place_of]
                both = view_b(kind, shift)
                turn = shift - first if kind == 0 else first - shift - 1
                own = window_of(ring_a, turn)
                own = 0.75 * own + 0.25 * rolled(own, -NZ if kind == 0 else NZ, 1)
                far_p = jnp.where(row < 4, both[0:8], own)
                around = differences(far_p, place6)
                chem = bulk(far_p, around)
                slope = [0.5 * (a - b) for a, b in around]
                around = differences(chem, place6)
                if step == 0:
                    density = both[4:5]
                    scaled = (-0.5 * coupling / relax_rate) * far_p[edge:edge + 1] / density
                    drift = [
                        both[5 + axis:6 + axis]
                        + scaled * (around[axis][0] - around[axis][1])[edge:edge + 1]
                        for axis in range(3)
                    ]
                    strip = strip_post(kind, both[8:16], density, drift, place6)
                    strip = weights_of[0] * strip + weights_of[1] * rolled(strip, NZ, 1)
                    patch_x(kind, strip_moved(strip))
                else:
                    after = far_p + mobility * bent(chem, around)
                    for axis in range(3):
                        flow = jnp.where(row == edge, both[5 + axis:6 + axis], both[13 + axis:14 + axis])
                        after = after - flow * slope[axis]
                    after = weights_of[0] * after + weights_of[1] * rolled(after, NZ, 1)
                    ext[outer:outer + 2, 0:WIDE] = after[at:at + 2, 0:WIDE]
                    ext[outer:outer + 2, WIDE:512] = jnp.where(
                        lane1[:2] < 64, after[at:at + 2, 384:512], after[at:at + 2, 640:768]
                    )

        @pl.when(jnp.logical_not(is_plane))
        def _(kind=kind):
            edge = (23, 12)[kind]
            at = len(first_units) - 1
            ends = [
                rolled(wide["corner"][2 * kind + k, at // 5:at // 5 + 1], lane_of(k, 1) - NZ * (at % 5), 1)
                for k in (1, 0)
            ]
            strip = jnp.concatenate(
                [wide["side"][kind, 16 * b + 8:16 * b + 16] for b in range(3)]
                + [jnp.broadcast_to(line, (8, 128)) for line in ends],
                axis=1,
            )
            strip = strip_post(
                kind, strip, e_r[edge:edge + 1, :], [d[edge:edge + 1] for d in drift], place5[:8]
            )
            patch_x(kind, strip_moved(strip))

    advance(1)
    wait_sent(0)
    receive(1, 1)

    advance(2)
    y_cut = (slice(256, 384), slice(0, 128))
    lines = [fx[group[0], edge:edge + 1, 0:WIDE] for edge in (11, 0) for group in x_groups]
    lines += [fx[1, 11:12, 0:WIDE], fx[2, 0:1, 0:WIDE]]
    halves = 0.5 * jnp.concatenate(lines, axis=0)
    ahead, behind = moved_yz(halves, 0, -1, place[:8]), moved_yz(halves, 0, 1, place[:8])
    for kind in (0, 1):
        edge, second, low = ((11, 10, 9), (0, 1, 0))[kind]
        inward = (up_slots, down_slots)[kind]
        for b in range(3):
            cut = slice(b * 128, b * 128 + 128)
            for i, slot in enumerate(inward):
                last_x[kind, 19 * b + i:19 * b + i + 1, :] = fx[slot, edge:edge + 1, cut]
                last_x[kind, 19 * b + 11 + i:19 * b + 12 + i, :] = fx[slot, second:second + 1, cut]
            for i, (first, slot) in enumerate(folded_x):
                at = x_groups.index(next(g for g in x_groups if g[0] == first)) + 3 * kind
                half = (ahead if lattice_vel[slot][2] == 1 else behind)[at:at + 1, cut]
                last_x[kind, 19 * b + 5 + i:19 * b + 6 + i, :] = fx[slot, edge:edge + 1, cut] + half
            last_x[kind, 19 * b + 16:19 * b + 19, :] = ext[low:low + 3, cut]
        for k in (0, 1):
            units = corner_units(kind, k)
            for i in range(0, len(units), 5):
                line = None
                for j, (slot, deep_x, deep_y) in enumerate(units[i:i + 5]):
                    row = 12 - deep_x if kind == 0 else deep_x - 1
                    part = ext[row:row + 1, y_cut[k]] if slot is None else fx[slot, row:row + 1, y_cut[k]]
                    part = rolled(part, NZ * j - lane_of(k, deep_y), 1)
                    line = part if j == 0 else jnp.where(lane1[:1] >= NZ * j, part, line)
                last_corner[2 * kind + k, i // 5:i // 5 + 1, :] = line
    for is_plane, edge, slots in ((left_plane, 0, down_slots), (right_plane, 11, up_slots)):
        @pl.when(is_plane)
        def _(edge=edge, slots=slots):
            at = 6 if edge == 11 else 7
            for b in range(3):
                cut = slice(b * 128, b * 128 + 128)
                for i, slot in enumerate(slots[1:]):
                    line = fx[slot, edge:edge + 1, cut]
                    if lattice_vel[slot][2] != 0:
                        line = line + (ahead if lattice_vel[slot][2] == 1 else behind)[at:at + 1, cut]
                    last_a[4 * b + i:4 * b + i + 1, :] = line

    send_around(2, last_a)
    send_x(2, last_x)
    send_sides(2, last_x, last_corner)
    for k in (0, 1):
        spots = lax.rem(lane1 + (16 if k == 0 else 0), NZ)
        for i in range(0, len(y_units[k]), 5):
            line = None
            for j, (slot, deep) in enumerate(y_units[k][i:i + 5]):
                part = ext[0:16, y_cut[k]] if slot is None else fx[slot, :, y_cut[k]]
                for first, folded in folded_y:
                    if folded == slot:
                        part = part + moved_yz(0.5 * fx[first, :, y_cut[k]], 0, -lattice_vel[slot][2], spots)
                part = rolled(part, NZ * j - lane_of(k, deep), 1)
                line = part if j == 0 else jnp.where(lane1 >= NZ * j, part, line)
            last_y[k, 12 * (i // 5):12 * (i // 5) + 12, :] = line[:12]
    send_y(2, last_y)
    e_p[0:12, 0:WIDE] = ext[0:12, 0:WIDE]
    wait_sent(1)

    wait_near(2)
    last = brought[2]

    def unit_of_y(k, slot, deep):
        place = y_units[k].index((slot, deep))
        row = 12 * (place // 5)
        return rolled(last["y"][k, row:row + 12], lane_of(k, deep) - NZ * (place % 5), 1)

    lane12 = lane1[:12]
    for slot in range(19):
        step_y = lattice_vel[slot][1]
        if any(slot == group[0] for group in y_groups):
            rim = jnp.zeros((12, 128), jnp.float32)
        elif step_y == 0:
            rim = jnp.where(lane12 < 64, unit_of_y(1, slot, 1), unit_of_y(0, slot, 1))
        elif step_y == 1:
            rim = jnp.where(lane12 >= 104, unit_of_y(0, slot, 1), unit_of_y(0, slot, 2))
        else:
            rim = jnp.where(lane12 < NZ, unit_of_y(1, slot, 1), unit_of_y(1, slot, 2))
        fx[slot, 0:12, 384:512] = rim
    e_p[0:12, 384:512] = jnp.where(
        lane12 < NZ, unit_of_y(1, None, 1),
        jnp.where(lane12 < 2 * NZ, unit_of_y(1, None, 2), unit_of_y(1, None, 3)),
    )
    e_p[0:12, 512:640] = jnp.where(
        lane12 >= 104, unit_of_y(0, None, 1),
        jnp.where(lane12 >= 80, unit_of_y(0, None, 2), unit_of_y(0, None, 3)),
    )
    for kind, is_plane, place_of in sides:
        @pl.when(jnp.logical_not(is_plane))
        def _(kind=kind):
            rows = ((15, 14), (12, 13))[kind]
            low = (21, 12)[kind]
            inward = (up_slots, down_slots)[kind]
            whole = last["side"][kind]
            for group in x_groups:
                fx[group[0], rows[0]:rows[0] + 1, 0:WIDE] = jnp.zeros((1, WIDE), jnp.float32)
            for b in range(3):
                cut = slice(b * 128, b * 128 + 128)
                strip = whole[19 * b:19 * b + 19]
                for i, slot in enumerate(inward):
                    fx[slot, rows[0]:rows[0] + 1, cut] = strip[i:i + 1]
                    fx[slot, rows[1]:rows[1] + 1, cut] = strip[11 + i:12 + i]
                for i, (_, slot) in enumerate(folded_x):
                    fx[slot, rows[0]:rows[0] + 1, cut] = strip[5 + i:6 + i]
                e_p[low:low + 3, cut] = strip[16:19]
            found = {}
            for k in (0, 1):
                corner = last["corner"][2 * kind + k]
                for i, (slot, deep_x, deep_y) in enumerate(corner_units(kind, k)):
                    part = corner[i // 5:i // 5 + 1]
                    part = rolled(part, lane_of(k, deep_y) - NZ * (i % 5), 1)
                    found.setdefault((slot, deep_x), []).append((k, deep_y, part))
            for (slot, deep_x), parts in found.items():
                line = {}
                for k, deep_y, part in parts:
                    start = lane_of(k, deep_y)
                    here = (lane1[:1] >= start) & (lane1[:1] < start + NZ)
                    at = k if slot is None else 0
                    line[at] = jnp.where(here, part, line[at]) if at in line else part
                if slot is None:
                    row = 24 - deep_x if kind == 0 else 11 + deep_x
                    e_p[row:row + 1, 512:640] = line[0]
                    e_p[row:row + 1, 384:512] = line[1]
                else:
                    row = rows[deep_x - 1]
                    fx[slot, row:row + 1, 384:512] = line[0]

    for slot in range(19):
        step_x, step_y, step_z = lattice_vel[slot]
        if step_x == 0:
            fx[slot] = moved_yz(fx[slot], step_y, step_z, place4)

    def mixed(kind, value):
        near, far = ((0.75, 0.25), (0.25, 0.75))[kind]
        return near * value + far * rolled(value, NZ, 1)

    for kind, is_plane, place_of in sides:
        @pl.when(is_plane)
        def _(kind=kind, place_of=place_of):
            wait_plane(2)
            for b in range(blocks + 5):
                row = 19 * (b % 3)
                ring_e[b, 0:19] = last["plane"][b % blocks // 3, row:row + 19]
            for j in range(count_y):
                source = lax.rem(gy + count_y - j, count_y)
                for b in range(3):
                    rows = slice(4 * b, 4 * b + 4)
                    ring_o[source * 3 + b, 1:5] = last_a[rows] if j == 0 else last["around"][j - 1, rows]
            for b in range(5):
                ring_o[blocks + b] = ring_o[b]
            row = (15, 12)[kind]
            shift = shifts[2, place_of]
            strip = mixed(kind, window_of(ring_e, shift if kind == 0 else -shift - 1)[0:8])
            for i, slot in enumerate((up_slots, down_slots)[kind]):
                fx[slot, row:row + 1, 0:384] = strip[i:i + 1, 0:384]
                fx[slot, row:row + 1, 384:512] = jnp.where(
                    lane1[:1] < 64, strip[i:i + 1, 384:512], strip[i:i + 1, 640:768]
                )
            shift = shifts[3, place_of]
            phase = mixed(kind, window_of(ring_e, shift if kind == 0 else -shift - 1)[16:24])
            row, at = ((22, 1), (12, 0))[kind]
            e_p[row:row + 2, 0:512] = phase[at:at + 2, 0:512]
            e_p[row:row + 2, 512:640] = phase[at:at + 2, 640:768]

    def narrowed(to, value):
        for top, at, size in ((0, 0, 12), (12, 12, 2), (14, 22, 2)):
            to[top:top + size, 0:WIDE] = value[at:at + size, 0:WIDE]
            to[top:top + size, WIDE:512] = jnp.where(
                lane1[:size] < 64, value[at:at + size, 384:512], value[at:at + size, 512:640]
            )

    for slot in up_slots + down_slots:
        step_x, step_y, step_z = lattice_vel[slot]
        fx[slot] = moved_yz(rolled(fx[slot], step_x, 0), step_y, step_z, place4)
    p = e_p[...]
    narrowed(ext, p)
    narrowed(chem_x, bulk(p, differences(p, place5)))
    density, totals = momentum(fx)
    inverse = 1.0 / density
    p, chem = ext[...], chem_x[...]
    around = differences(p, place4)
    slope = [0.5 * (a - b)[:, :WIDE] for a, b in around]
    around = differences(chem, place4)
    next_phase = (p + mobility * bent(chem, around))[:, :WIDE]
    scaled = (-0.5 * coupling / relax_rate) * p
    drift = []
    for axis in range(3):
        next_phase = next_phase - (totals[axis] * inverse)[:, :WIDE] * slope[axis]
        drift.append((totals[axis] + scaled * (around[axis][0] - around[axis][1])) * inverse)
    p_out[...] = next_phase[:12]
    collide(density[:, :WIDE], [d[:, :WIDE] for d in drift], None, lambda slot: fx[slot, :, 0:WIDE])
    for k in (0, 1):
        here = None
        for i, slot in enumerate((plus_y, minus_y)[k]):
            part = rolled(fx[slot, :, 384:512], NZ + NZ * i if k == 0 else 104 - NZ * i, 1)
            if i == 0:
                here = part
            else:
                here = jnp.where(lane1 >= NZ * i if k == 0 else lane1 < 128 - NZ * i, part, here)
        rim = [d[:, 384:512] for d in drift]
        patch_y(k, packed_post(k, here, density[:, 384:512], rim, lane1))
    for kind, is_plane, place_of in sides:
        @pl.when(is_plane)
        def _(kind=kind, place_of=place_of):
            before, shift = shifts[2, place_of], shifts[3, place_of]
            edge, top, a_row, own_row = ((3, 1, 4, 0), (0, 0, 6, 10))[kind]
            far = window_of(ring_e, shift if kind == 0 else -shift - 1)
            inner = strip_moved(strip_along_z(kind, far[11:19], place6))
            turn = shift - before if kind == 0 else before - shift - 1
            outer = window_of(ring_o, turn)
            outer = 0.75 * outer + 0.25 * rolled(outer, -NZ if kind == 0 else NZ, 1)
            outer = strip_moved(strip_along_z(1 - kind, outer, place6))
            total = [None] * 4
            sign = 1.0 - 2.0 * kind
            for tile, way in ((inner, sign), (outer, -sign)):
                r = [tile[i:i + 1] for i in range(5)]
                whole = r[1] + r[2] + r[3] + r[4]
                if tile is inner:
                    whole = whole + r[0]
                found = (whole, way * whole, r[3] - r[4], way * (r[1] - r[2]))
                total = [b if a is None else a + b for a, b in zip(total, found)]
            for i, (_, slot) in enumerate(folded_x):
                _, step_y, step_z = lattice_vel[slot]
                line = moved_yz(far[5 + i:6 + i], step_y, step_z, place6[:1])
                total[0] = total[0] + line
                if step_y != 0:
                    total[2] = total[2] + step_y * line
                if step_z != 0:
                    total[3] = total[3] + step_z * line
            tile_a[...] = jnp.zeros_like(tile_a)
            tile_a[a_row:a_row + 2, 0:512] = e_p[own_row:own_row + 2, 0:512]
            tile_a[a_row:a_row + 2, 640:768] = e_p[own_row:own_row + 2, 512:640]
            own = tile_a[...]
            ahead = rolled(own, -NZ, 1)
            own = 0.75 * own + 0.25 * ahead if kind == 0 else 0.25 * own + 0.75 * ahead
            row = lax.broadcasted_iota(jnp.int32, (8, 768), 0)
            far_p = jnp.where(row < 4, rolled(far[16:24], top, 0), own)
            around = differences(bulk(far_p, differences(far_p, place6)), place6)
            inverse = 1.0 / total[0]
            scaled = (-0.5 * coupling / relax_rate) * far_p[edge:edge + 1]
            drift = [
                (total[1 + axis] + scaled * (around[axis][0] - around[axis][1])[edge:edge + 1]) * inverse
                for axis in range(3)
            ]
            strip = mixed(kind, strip_post(kind, inner, total[0], drift, place6))
            patch_x(kind, strip_moved(strip))

        @pl.when(jnp.logical_not(is_plane))
        def _(kind=kind):
            row = (15, 12)[kind]
            inward = (up_slots, down_slots)[kind]
            lines = [fx[slot, row:row + 1, :] for slot in inward]
            strip = jnp.concatenate(lines + lines[:1] * 3, axis=0)
            strip = strip_post(
                kind, strip, density[row:row + 1], [d[row:row + 1] for d in drift], place4[:8]
            )
            patch_x(kind, strip_moved(strip))

    wait_sent(2)
    for slot in range(19):
        f_out[slot] = f[slot, 0:12, :]


def on_device(populations, phase_field, plane_shifts):
    parts = lax.axis_size("gy")
    blocks = 3 * parts
    rounds = 3
    vmem = pl.BlockSpec(memory_space=pltpu.VMEM)
    return pl.pallas_call(
        kernel,
        out_shape=(
            jax.ShapeDtypeStruct(populations.shape, jnp.float32),
            jax.ShapeDtypeStruct(phase_field.shape, jnp.float32),
        ),
        in_specs=[pl.BlockSpec(memory_space=pltpu.SMEM), vmem, vmem],
        out_specs=(vmem, vmem),
        scratch_shapes=[
            pltpu.VMEM((19, 16, WIDE), jnp.float32),
            pltpu.VMEM((16, 512), jnp.float32),
            pltpu.VMEM((2, 21, 128), jnp.float32),
            pltpu.VMEM((2, 16, 128), jnp.float32),
            pltpu.VMEM((4, 1, 128), jnp.float32),
            pltpu.VMEM((blocks + 4, 8, 128), jnp.float32),
            pltpu.VMEM((24, 640), jnp.float32),
            pltpu.VMEM((24, 640), jnp.float32),
            pltpu.VMEM((3, 24, 640), jnp.float32),
            pltpu.VMEM((blocks + 5, 16, 128), jnp.float32),
            pltpu.VMEM((blocks + 5, 8, 128), jnp.float32),
            pltpu.VMEM((2, 48, 128), jnp.float32),
            pltpu.VMEM((2, 40, 128), jnp.float32),
            pltpu.VMEM((4, 3, 128), jnp.float32),
            pltpu.VMEM((6, 128), jnp.float32),
            pltpu.VMEM((19, 16, 512), jnp.float32),
            pltpu.VMEM((16, 512), jnp.float32),
            pltpu.VMEM((8, 768), jnp.float32),
            pltpu.VMEM((blocks + 5, 24, 128), jnp.float32),
            pltpu.VMEM((blocks + 5, 8, 128), jnp.float32),
            pltpu.VMEM((2, 57, 128), jnp.float32),
            pltpu.VMEM((2, 48, 128), jnp.float32),
            pltpu.VMEM((4, 5, 128), jnp.float32),
            pltpu.VMEM((12, 128), jnp.float32),
        ] + [
            pltpu.VMEM((count, rows, 128), jnp.float32)
            for count, rows in (
                (2, 40), (2, 48), (4, 3), (parts, 48), (parts - 1, 6),
                (2, 16), (2, 21), (4, 1), (parts, 21),
                (2, 48), (2, 57), (4, 5), (parts, 57), (parts - 1, 12),
            )
        ] + [
            pltpu.SemaphoreType.DMA((rounds, 5)),
            pltpu.SemaphoreType.DMA((rounds, 5)),
        ],
        compiler_params=pltpu.CompilerParams(
            collective_id=0, has_side_effects=True, vmem_limit_bytes=32 * 1024 * 1024
        ),
    )(plane_shifts, populations, phase_field)


def solution(mesh):
    return jax.shard_map(
        on_device,
        mesh=mesh,
        in_specs=(P(None, "gx", "gy"), P("gx", "gy"), P()),
        out_specs=(P(None, "gx", "gy"), P("gx", "gy")),
        check_vma=False,
    )
```
